32 devices in a mesh: dp: 8 (over y, x, core), tensor: 4 (over z).
Axes of the slice: x: 2, y: 2, z: 4, core: 2. Of those that a mesh axis runs over, the one named last changes fastest.
Arguments:
- tokens: bfloat16 [4096, 8192], P('dp', 'tensor'), may hold values from -6 to 6
- ref_gain: float32 [8192], P('tensor'), may hold values from 0.1 to 1.9
- ref_weight: bfloat16 [8192, 512], P('tensor'), may hold values from -0.0625 to 0.0625
- pol_gain: float32 [8192], replicated, may hold values from 0.1 to 1.9
- pol_weight: bfloat16 [8192, 512], P('dp'), may hold values from -0.0625 to 0.0625
- lengths: int32 [8, 4, 8], P('dp', 'tensor'), may hold values from 1 to 32, 128 in all within a row
- bins: int32 [8, 4, 8], P('dp', 'tensor'), may hold values from 0 to 7, each once within a row
- advantage: float32 [8, 4, 8], P('dp', 'tensor'), may hold values from -4 to 4
- logprob_gap: float32 [4096], P(('dp', 'tensor')), may hold values from -1 to 1
- cotangent: bfloat16 [8, 4, 256, 512], P('dp', 'tensor'), may hold values from -6 to 6
Outputs:
- policy_values: bfloat16 [8, 4, 256, 512], P('dp', 'tensor')
- grad_weight: float32 [8192, 512], P(('dp', 'tensor'))
The draws below stay inside these ranges and needn't reach their ends.
Inputs may be any that keep to these rules, and one draw needn't show every extreme that they name: `lengths`: lengths of the 8 sequences of one run, in the order in which they lie in it; they sum to 128, and the longest of every run is exactly 32. The sequences of one run go to distinct bins: each bin takes exactly one sequence of every run.
All inputs are finite; a program needn't handle non-finite values.
Results may differ from the reference program's by a relative error of at most 0.015.
Values may be sent and summed in bfloat16 or wider, within the bound.
No kernel may reach another device: no remote copies, remote signals or barrier semaphores. Data moves between devices by JAX's collectives and lax.ppermute only.
A program may use at most 64 MiB of HBM per device.

```python
import math
import jax
import jax.numpy as jnp
import numpy as np
from jax import lax

D = 8192
VW = 512
TOK_DEV = 128
BINS = 8
TP_WAYS = 4
BLOCK = 2048
SPAN = 32
SLOTS = 256
SEQS = 256
TOKENS = 4096


def spiked(entries, key, source, target, blocks, factor):
    owner, partner = [(jnp.arange(entries.shape[position]) // (entries.shape[position] // blocks)).reshape([-1 if axis == position else 1 for axis in range(entries.ndim)]) for position in (source, target)]
    chosen = jax.random.permutation(key, blocks)[partner]
    strong = (owner == chosen) | (owner == (partner + blocks // 2) % blocks)
    return jnp.where(strong, factor * entries, entries)


def block_levels(rng, extent, split, smallest, largest):
    def one(dim, blocks):
        steps = jax.random.uniform(jax.random.fold_in(jax.random.fold_in(rng, 6), dim), (blocks,), jnp.float32, smallest / len(split), largest / len(split))
        return jnp.repeat(jnp.exp(steps), extent[dim] // blocks).reshape((-1,) + (1,) * (len(extent) - dim - 1))

    factor_of = one(*split[0])
    for cut in split[1:]:
        factor_of = factor_of * one(*cut)
    return factor_of


def split_up(count, total, reach, skew):
    weights = [(1 << 20) // math.isqrt(standing ** skew) + 1 for standing in range(2, count + 1)]
    surplus, counts = total - reach - (count - 1), [1] * (count - 1)
    while surplus > 0:
        free = [i for i in range(count - 1) if counts[i] < reach]
        pool, budget = sum([weights[i] for i in free]), surplus
        for i in free:
            extra = min(reach - counts[i], max(1, budget * weights[i] // pool), surplus)
            counts[i] = counts[i] + extra
            surplus = surplus - extra
    return np.array([reach] + counts)


def uneven(key, number_of, total, reach, skew):
    if number_of == 2:
        one = jax.random.randint(key, (), max(1, total - reach), min(reach, total - 1) + 1)
        return jnp.stack([one, total - one])
    sizes = jnp.asarray(split_up(number_of, total, reach, skew), jnp.int32)
    pairs = (number_of - 1) // 2
    giver, sink = sizes[1:1 + 2 * pairs:2], sizes[2:2 + 2 * pairs:2]
    slack = jnp.minimum(giver - 1, reach - sink)
    moved = jax.random.randint(jax.random.fold_in(key, 1), (pairs,), 0, 1 << 20) % (slack + 1)
    sizes = sizes.at[1:1 + 2 * pairs:2].set(giver - moved).at[2:2 + 2 * pairs:2].set(sink + moved)
    return sizes[jax.random.permutation(jax.random.fold_in(key, 2), number_of)]


def scatter_about(own_key, shape, width, most, cuts=(), kind=jnp.bfloat16):
    level = block_levels(own_key, shape, cuts, -0.22, 0.18) if cuts else 1.0
    result = jax.random.normal(own_key, shape, jnp.float32) * width * level
    return jnp.minimum(jnp.maximum(result, -most), most).astype(kind)


def noise_with(key, dims, deviation, most, cuts, heavy, kind=jnp.bfloat16):
    drawn = deviation * jax.random.normal(key, dims, jnp.float32)
    if cuts:
        drawn = drawn * block_levels(key, dims, cuts, -0.22, 0.18)
    return jnp.clip(spiked(drawn, jax.random.fold_in(key, 3), *heavy), -most, most).astype(kind)


def setup_inputs(seed: int = 0) -> dict:
    arg_keys = jax.random.split(jax.random.key(seed), 11)
    return {
        "tokens": noise_with(arg_keys[0], (TOKENS, D), 1.0, 6.0, ((0, 8), (1, 4)), (0, 1, 8, 2.0)),
        "ref_gain": jnp.clip(1.0 + 0.18 * jax.random.normal(arg_keys[1], (D,), jnp.float32), 0.1, 1.9),
        "ref_weight": scatter_about(arg_keys[2], (D, VW), D ** -0.5, 0.0625, ((0, 4),)),
        "pol_gain": jnp.clip(1.0 + 0.18 * jax.random.normal(arg_keys[3], (D,), jnp.float32), 0.1, 1.9),
        "pol_weight": scatter_about(arg_keys[4], (D, VW), D ** -0.5, 0.0625, ((0, 8),)),
        "lengths": jax.vmap(lambda own: uneven(own, BINS, TOK_DEV, SPAN, 2))(jax.random.split(arg_keys[5], BINS * TP_WAYS)).reshape((BINS, TP_WAYS, BINS)).astype(jnp.int32),
        "bins": jax.vmap(lambda own: jax.random.permutation(own, BINS))(jax.random.split(arg_keys[6], BINS * TP_WAYS)).reshape((BINS, TP_WAYS, BINS)).astype(jnp.int32),
        "advantage": scatter_about(arg_keys[7], (BINS, TP_WAYS, BINS), 1.0, 4.0, ((0, 8), (1, 4)), jnp.float32),
        "logprob_gap": jnp.clip(jax.random.uniform(arg_keys[8], (TOKENS,), jnp.float32, -1.0, 1.0) * block_levels(arg_keys[8], (TOKENS,), ((0, 32),), -0.4, 0.0), -1.0, 1.0),
        "cotangent": scatter_about(arg_keys[9], (BINS, TP_WAYS, SLOTS, VW), 1.0, 6.0, ((0, 8), (1, 4))),
    }


EPS = 1e-06
BETA = 1.0

def run_values(run_rows, ref_gain, ref_weight):
    accum = jnp.zeros((run_rows.shape[0], VW), jnp.float32)
    for index in range(D // BLOCK):
        lower = index * BLOCK
        scaled = (run_rows[:, lower:lower + BLOCK].astype(jnp.float32) * ref_gain[lower:lower + BLOCK][None, :]).astype(jnp.bfloat16)
        partial_value = jnp.dot(scaled, ref_weight[lower:lower + BLOCK], preferred_element_type=jnp.float32)
        accum = accum + lax.optimization_barrier(partial_value.astype(jnp.bfloat16)).astype(jnp.float32)
    power = lax.optimization_barrier(jnp.mean(jnp.square(run_rows.astype(jnp.float32)), axis=1))
    return (accum * lax.rsqrt(power + EPS)[:, None]).astype(jnp.bfloat16)

def reference(tokens, ref_gain, ref_weight, pol_gain, pol_weight, lengths, bins, advantage, logprob_gap, cotangent):
    run_rows = tokens.reshape(BINS * TP_WAYS, TOK_DEV, D)
    ref_values = lax.map(lambda stretch_rows: run_values(stretch_rows, ref_gain, ref_weight), run_rows)
    ref_flat = ref_values.reshape(TOKENS, VW)
    seq_start = (jnp.cumsum(lengths, axis=2).astype(jnp.int32) - lengths).astype(jnp.int32)
    chosen = bins[:, :, None, :] == jnp.arange(BINS, dtype=jnp.int32)[None, None, :, None]
    bin_len = lax.optimization_barrier(jnp.sum(jnp.where(chosen, lengths[:, :, None, :], 0), axis=3)).astype(jnp.int32)
    bin_start = lax.optimization_barrier(jnp.sum(jnp.where(chosen, seq_start[:, :, None, :], 0), axis=3)).astype(jnp.int32)
    bin_adv = lax.optimization_barrier(jnp.sum(jnp.where(chosen, advantage[:, :, None, :], jnp.float32(0.0)), axis=3))
    run_index = (jnp.arange(BINS, dtype=jnp.int32)[:, None] * TP_WAYS + jnp.arange(TP_WAYS, dtype=jnp.int32)[None, :]).astype(jnp.int32)
    offsets = jnp.arange(SPAN, dtype=jnp.int32)
    usable = offsets[None, None, None, :] < bin_len[..., None]
    local_row = jnp.clip(bin_start[..., None] + offsets[None, None, None, :], 0, TOK_DEV - 1).astype(jnp.int32)
    source = (run_index[:, :, None, None] * TOK_DEV + local_row).astype(jnp.int32)
    importance = jnp.minimum(jnp.exp(logprob_gap[source]), jnp.float32(2.0))
    len_float = bin_len[..., None].astype(jnp.float32)
    coef_adv = lax.optimization_barrier(jnp.where(usable, bin_adv[..., None] * importance / len_float, jnp.float32(0.0)).astype(jnp.bfloat16))
    coef_pull = lax.optimization_barrier(jnp.where(usable, BETA / len_float, jnp.float32(0.0)).astype(jnp.bfloat16))
    factor = 1.0 / math.sqrt(SEQS)

    def pick(array, bin_index):
        return jnp.transpose(array[:, :, bin_index], (1, 0, 2)).reshape(TP_WAYS * SLOTS)

    def per_bin(accum, bin_index):
        src_rows = pick(source, bin_index)
        use_rows = pick(usable, bin_index)
        adv_rows = pick(coef_adv, bin_index).astype(jnp.float32)[:, None]
        pull_rows = pick(coef_pull, bin_index).astype(jnp.float32)[:, None]
        packed_rows = jnp.where(use_rows[:, None], tokens[src_rows], jnp.zeros((), jnp.bfloat16))
        packed_ref = jnp.where(use_rows[:, None], ref_flat[src_rows], jnp.zeros((), jnp.bfloat16)).astype(jnp.float32)
        power = lax.optimization_barrier(jnp.mean(jnp.square(packed_rows.astype(jnp.float32)), axis=1))
        normed = (packed_rows.astype(jnp.float32) * lax.rsqrt(power + EPS)[:, None] * pol_gain[None, :]).astype(jnp.bfloat16)
        values = jnp.dot(normed, pol_weight, preferred_element_type=jnp.float32)
        upstream = cotangent[bin_index].reshape(TP_WAYS * SLOTS, VW).astype(jnp.float32)
        slope = (adv_rows * upstream + pull_rows * (values - packed_ref)).astype(jnp.bfloat16)
        term = lax.dot_general(normed, slope, (((0,), (0,)), ((), ())), preferred_element_type=jnp.float32)
        return (accum + term, values.astype(jnp.bfloat16).reshape(TP_WAYS, SLOTS, VW))
    grad_sum, policy_values = lax.scan(per_bin, jnp.zeros((D, VW), jnp.float32), jnp.arange(BINS, dtype=jnp.int32))
    return (policy_values, grad_sum * factor)
```

```python
import math

import jax
import jax.numpy as jnp
from jax import lax
from jax.sharding import PartitionSpec as P

EPS = 1e-06
BETA = 1.0
AXES = ("dp", "tensor")
BF16 = jnp.bfloat16
F32 = jnp.float32


def take_chunk(array, index, rows):
    return lax.dynamic_slice_in_dim(array, index * rows, rows, 0)


def sum_over_tensor(partial, rows, count):
    me = lax.axis_index("tensor")
    terms = [take_chunk(partial, me, rows)]
    for step in range(1, count):
        pairs = [(i, (i + step) % count) for i in range(count)]
        terms.append(
            lax.ppermute(take_chunk(partial, (me + step) % count, rows), "tensor", pairs)
        )
    return terms


def on_device(
    tokens,
    ref_gain,
    ref_weight,
    pol_gain,
    pol_weight,
    lengths,
    bins,
    advantage,
    logprob_gap,
    cotangent,
):
    tensor_count = lax.axis_size("tensor")
    dp_count = lax.axis_size("dp")
    t = lax.axis_index("tensor")
    d = lax.axis_index("dp")
    cores = dp_count // tensor_count
    assert cores == 2
    places = dp_count // cores
    levels = places.bit_length() - 1
    assert 1 << levels == places
    place = d // cores
    core = d % cores
    group_rows, block = tokens.shape
    own_rows = group_rows // tensor_count
    slot_count = cotangent.shape[2]
    span_rows = slot_count // dp_count
    value_width = ref_weight.shape[1]
    model_width = pol_gain.shape[0]
    shard = pol_weight.shape[0]
    factor = 1.0 / math.sqrt(dp_count * tensor_count * lengths.shape[2])

    def flat(p, c, z):
        return (p * cores + c) * tensor_count + z

    got_cot = lax.all_to_all(
        cotangent.reshape(slot_count, value_width), "dp", split_axis=0, concat_axis=0, tiled=True
    )

    relative = place ^ t
    piece_count = 2
    piece_rows = shard // piece_count
    pieces = []
    for piece in range(piece_count):
        held = pol_weight[piece * piece_rows : (piece + 1) * piece_rows]
        holders = [0]
        for stage in range(levels):
            bit = 1 << ((piece + stage) % levels)
            pairs = [
                (flat(q ^ z, c, z), flat(q ^ bit ^ z, c, z))
                for q in holders
                for c in range(cores)
                for z in range(tensor_count)
            ]
            got = lax.ppermute(held, AXES, pairs)
            getters = [q ^ bit for q in holders]
            is_getter = jnp.zeros((), jnp.bool_)
            for q in getters:
                is_getter = is_getter | (relative == q)
            held = jnp.where(is_getter, got, held)
            holders = holders + getters
        pieces.append(held)
    mine = jnp.concatenate(pieces, axis=0)
    swap = [(i, i ^ 1) for i in range(dp_count)]
    other = lax.ppermute(mine, "dp", swap)
    weight = jnp.where(
        core == 0,
        jnp.concatenate([mine, other], axis=0),
        jnp.concatenate([other, mine], axis=0),
    )

    tokens_f32 = tokens.astype(F32)
    scaled = (tokens_f32 * ref_gain[None, :]).astype(BF16)
    ref_part = jnp.dot(scaled, ref_weight, preferred_element_type=F32).astype(BF16)
    square = jnp.sum(jnp.square(tokens_f32), axis=1)
    square_sum = sum(sum_over_tensor(square, own_rows, tensor_count))
    row_scale = lax.rsqrt(square_sum / model_width + EPS)[:, None]
    ref_sum = sum(x.astype(F32) for x in sum_over_tensor(ref_part, own_rows, tensor_count))
    ref_values = (ref_sum * row_scale).astype(BF16).astype(F32)

    seq_lens = lengths.reshape(-1)
    seq_bins = bins.reshape(-1)
    seq_adv = advantage.reshape(-1)
    seq_starts = jnp.cumsum(seq_lens) - seq_lens
    row = jnp.arange(own_rows, dtype=jnp.int32)
    in_seq = (row[:, None] >= seq_starts[None, :]) & (
        row[:, None] < (seq_starts + seq_lens)[None, :]
    )
    row_slot = jnp.sum(
        jnp.where(in_seq, seq_bins * span_rows + row[:, None] - seq_starts[None, :], 0), axis=1
    )
    row_len = jnp.sum(jnp.where(in_seq, seq_lens[None, :], 0), axis=1).astype(F32)
    row_adv = jnp.sum(jnp.where(in_seq, seq_adv[None, :], 0.0), axis=1)
    importance = jnp.minimum(jnp.exp(logprob_gap), jnp.float32(2.0))
    coef_adv = (row_adv * importance / row_len).astype(BF16).astype(F32)[:, None]
    coef_pull = (BETA / row_len).astype(BF16).astype(F32)[:, None]
    slot = jnp.arange(slot_count, dtype=jnp.int32)
    row_at = (row_slot[:, None] == slot[None, :]).astype(BF16)
    slot_at = (slot[:, None] == row_slot[None, :]).astype(BF16)
    upstream = jnp.dot(row_at, got_cot, preferred_element_type=F32)

    pol_gain_block = lax.dynamic_slice_in_dim(pol_gain, t * block, block, 0)
    pol_scaled = (tokens_f32 * pol_gain_block[None, :]).astype(BF16)
    value_part = jnp.dot(pol_scaled, weight, preferred_element_type=F32).astype(BF16)
    value_sum = sum(x.astype(F32) for x in sum_over_tensor(value_part, own_rows, tensor_count))
    values = value_sum * row_scale
    sent = jnp.dot(slot_at, values.astype(BF16), preferred_element_type=F32).astype(BF16)
    policy_values = lax.all_to_all(sent, "dp", split_axis=0, concat_axis=0, tiled=True)

    slope = coef_adv * upstream + coef_pull * (values - ref_values)
    slope = (slope * row_scale).astype(BF16)
    slopes = jnp.zeros((group_rows, value_width), BF16)
    slopes = lax.dynamic_update_slice_in_dim(slopes, slope, t * own_rows, 0)
    for step in range(1, tensor_count):
        pairs = [(i, (i + step) % tensor_count) for i in range(tensor_count)]
        got = lax.ppermute(slope, "tensor", pairs)
        source = (t - step) % tensor_count
        slopes = lax.dynamic_update_slice_in_dim(slopes, got, source * own_rows, 0)

    grad = lax.dot_general(tokens, slopes, (((0,), (0,)), ((), ())), preferred_element_type=F32)
    grad = (grad * (pol_gain_block * factor)[:, None]).astype(BF16)
    kept = take_chunk(grad, core, shard)
    given = take_chunk(grad, 1 - core, shard)
    half = (kept.astype(F32) + lax.ppermute(given, "dp", swap).astype(F32)).astype(BF16)
    out_rows = shard // tensor_count
    total = take_chunk(half, place, out_rows).astype(F32)
    for step in range(1, places):
        pairs = [
            (p * cores + c, (p ^ step) * cores + c) for p in range(places) for c in range(cores)
        ]
        total = total + lax.ppermute(
            take_chunk(half, place ^ step, out_rows), "dp", pairs
        ).astype(F32)
    pairs = [
        (flat(p, c, z), flat(z, c, p))
        for p in range(places)
        for c in range(cores)
        for z in range(tensor_count)
    ]
    grad_weight = lax.ppermute(total.astype(BF16), AXES, pairs).astype(F32)
    return (policy_values.reshape(1, 1, slot_count, value_width), grad_weight)


def solution(mesh):
    in_specs = (
        P("dp", "tensor"),
        P("tensor"),
        P("tensor", None),
        P(),
        P("dp", None),
        P("dp", "tensor", None),
        P("dp", "tensor", None),
        P("dp", "tensor", None),
        P(("dp", "tensor")),
        P("dp", "tensor", None, None),
    )
    out_specs = (P("dp", "tensor", None, None), P(("dp", "tensor"), None))
    return jax.shard_map(
        on_device, mesh=mesh, in_specs=in_specs, out_specs=out_specs, check_vma=False
    )
```

```python
import math

import jax
import jax.numpy as jnp
from jax import lax
from jax.sharding import PartitionSpec as P

EPS = 1e-06
BETA = 1.0
AXES = ("dp", "tensor")
BF16 = jnp.bfloat16
F32 = jnp.float32


def take_chunk(array, index, rows):
    return lax.dynamic_slice_in_dim(array, index * rows, rows, 0)


def dot(a, b):
    return jnp.dot(a, b, preferred_element_type=F32)


def dot_rows(a, b):
    return lax.dot_general(a, b, (((0,), (0,)), ((), ())), preferred_element_type=F32)


def swapped(array, dp_count):
    return lax.ppermute(array, "dp", [(i, i ^ 1) for i in range(dp_count)])


def scatter_over_tensor(partial, rows, count):
    me = lax.axis_index("tensor")
    got = []
    for step in range(1, count):
        pairs = [(i, (i + step) % count) for i in range(count)]
        part = take_chunk(partial, (me + step) % count, rows).astype(BF16)
        got.append(lax.ppermute(part, "tensor", pairs))
    return got


def on_device(
    tokens,
    ref_gain,
    ref_weight,
    pol_gain,
    pol_weight,
    lengths,
    bins,
    advantage,
    logprob_gap,
    cotangent,
):
    tensor_count = lax.axis_size("tensor")
    dp_count = lax.axis_size("dp")
    t = lax.axis_index("tensor")
    d = lax.axis_index("dp")
    cores = dp_count // tensor_count
    assert cores == 2
    places = dp_count // cores
    levels = places.bit_length() - 1
    assert 1 << levels == places
    place = d // cores
    core = d % cores
    group_rows, block = tokens.shape
    own_rows = group_rows // tensor_count
    slot_count = cotangent.shape[2]
    span_rows = slot_count // dp_count
    value_width = ref_weight.shape[1]
    model_width = pol_gain.shape[0]
    shard = pol_weight.shape[0]
    factor = 1.0 / math.sqrt(dp_count * tensor_count * lengths.shape[2])

    def flat(p, c, z):
        return (p * cores + c) * tensor_count + z

    relative = place ^ t
    gain_shard = take_chunk(pol_gain, d, shard)
    sent_weight = (pol_weight.astype(F32) * gain_shard[:, None]).astype(BF16)
    halves = 2
    half_rows = shard // halves
    held = [sent_weight[i * half_rows : (i + 1) * half_rows] for i in range(halves)]
    holders = [[0] for _ in range(halves)]

    def stage(number):
        for i in range(halves):
            bit = 1 << ((i + number) % levels)
            pairs = [
                (flat(q ^ z, c, z), flat(q ^ bit ^ z, c, z))
                for q in holders[i]
                for c in range(cores)
                for z in range(tensor_count)
            ]
            got = lax.ppermute(held[i], AXES, pairs)
            getters = [q ^ bit for q in holders[i]]
            is_getter = jnp.zeros((), jnp.bool_)
            for q in getters:
                is_getter = is_getter | (relative == q)
            held[i] = jnp.where(is_getter, got, held[i])
            holders[i] = holders[i] + getters

    stage(0)

    kept_rows = lax.dynamic_slice_in_dim(tokens, core * shard, shard, 1)
    given_rows = lax.dynamic_slice_in_dim(tokens, (1 - core) * shard, shard, 1)
    tokens_f32 = tokens.astype(F32)
    scaled = (tokens_f32 * ref_gain[None, :]).astype(BF16)
    ref_part = dot(scaled, ref_weight).astype(BF16)
    square = jnp.sum(jnp.square(tokens_f32), axis=1)

    tied = lax.optimization_barrier((*held, kept_rows, given_rows, ref_part, square))
    held = list(tied[:halves])
    kept_rows, given_rows, ref_part, square = tied[halves:]

    got_rows = swapped(given_rows, dp_count)
    ref_got = scatter_over_tensor(ref_part, own_rows, tensor_count)
    square_sum = take_chunk(lax.psum(square, "tensor"), t, own_rows)
    got_cot = lax.all_to_all(
        cotangent.reshape(slot_count, value_width), "dp", split_axis=0, concat_axis=0, tiled=True
    )
    for number in range(1, levels):
        stage(number)

    row_scale = lax.rsqrt(square_sum / model_width + EPS)[:, None]
    ref_sum = sum(x.astype(F32) for x in ref_got) + take_chunk(ref_part, t, own_rows).astype(F32)
    ref_values = (ref_sum * row_scale).astype(BF16).astype(F32)

    seq_lens = lengths.reshape(-1)
    seq_bins = bins.reshape(-1)
    seq_adv = advantage.reshape(-1)
    seq_starts = jnp.cumsum(seq_lens) - seq_lens
    row = jnp.arange(own_rows, dtype=jnp.int32)
    in_seq = (row[:, None] >= seq_starts[None, :]) & (
        row[:, None] < (seq_starts + seq_lens)[None, :]
    )
    row_slot = jnp.sum(
        jnp.where(in_seq, seq_bins * span_rows + row[:, None] - seq_starts[None, :], 0), axis=1
    )
    row_len = jnp.sum(jnp.where(in_seq, seq_lens[None, :], 0), axis=1).astype(F32)
    row_adv = jnp.sum(jnp.where(in_seq, seq_adv[None, :], 0.0), axis=1)
    importance = jnp.minimum(jnp.exp(logprob_gap), jnp.float32(2.0))
    coef_adv = (row_adv * importance / row_len).astype(BF16).astype(F32)[:, None]
    coef_pull = (BETA / row_len).astype(BF16).astype(F32)[:, None]
    slot = jnp.arange(slot_count, dtype=jnp.int32)
    row_at = (row_slot[:, None] == slot[None, :]).astype(BF16)
    slot_at = (slot[:, None] == row_slot[None, :]).astype(BF16)
    upstream = dot(row_at, got_cot)
    fixed = coef_adv * upstream - coef_pull * ref_values

    tied = lax.optimization_barrier((*held, fixed, coef_pull, row_scale, slot_at, got_rows))
    weight = jnp.concatenate(tied[:halves], axis=0)
    fixed, coef_pull, row_scale, slot_at, got_rows = tied[halves:]

    value_given = dot(got_rows, weight).astype(BF16)
    value_got = swapped(value_given, dp_count)
    value_part = dot(kept_rows, weight) + value_got.astype(F32)
    value_sum = take_chunk(value_part, t, own_rows)
    for got in scatter_over_tensor(value_part, own_rows, tensor_count):
        value_sum = value_sum + got.astype(F32)
    values = value_sum * row_scale

    slope = ((fixed + coef_pull * values) * row_scale).astype(BF16)
    slopes = jnp.zeros((group_rows, value_width), BF16)
    slopes = lax.dynamic_update_slice_in_dim(slopes, slope, t * own_rows, 0)
    for step in range(1, tensor_count):
        pairs = [(i, (i + step) % tensor_count) for i in range(tensor_count)]
        got = lax.ppermute(slope, "tensor", pairs)
        source = (t - step) % tensor_count
        slopes = lax.dynamic_update_slice_in_dim(slopes, got, source * own_rows, 0)
    slopes_got = swapped(slopes, dp_count)

    sent = dot(slot_at, values.astype(BF16)).astype(BF16)
    policy_values = lax.all_to_all(sent, "dp", split_axis=0, concat_axis=0, tiled=True)

    grad = dot_rows(kept_rows, slopes) + dot_rows(got_rows, slopes_got)
    gain_block = lax.dynamic_slice_in_dim(pol_gain, t * block + core * shard, shard, 0)
    grad = (grad * (gain_block * factor)[:, None]).astype(BF16)
    grad, policy_values = lax.optimization_barrier((grad, policy_values))
    out_rows = shard // tensor_count
    total = take_chunk(grad, place, out_rows).astype(F32)
    for step in range(1, places):
        pairs = [
            (p * cores + c, (p ^ step) * cores + c) for p in range(places) for c in range(cores)
        ]
        total = total + lax.ppermute(
            take_chunk(grad, place ^ step, out_rows), "dp", pairs
        ).astype(F32)
    pairs = [
        (flat(p, c, z), flat(z, c, p))
        for p in range(places)
        for c in range(cores)
        for z in range(tensor_count)
    ]
    grad_weight = lax.ppermute(total.astype(BF16), AXES, pairs).astype(F32)
    return (policy_values.reshape(1, 1, slot_count, value_width), grad_weight)


def solution(mesh):
    in_specs = (
        P("dp", "tensor"),
        P("tensor"),
        P("tensor", None),
        P(),
        P("dp", None),
        P("dp", "tensor", None),
        P("dp", "tensor", None),
        P("dp", "tensor", None),
        P(("dp", "tensor")),
        P("dp", "tensor", None, None),
    )
    out_specs = (P("dp", "tensor", None, None), P(("dp", "tensor"), None))
    return jax.shard_map(
        on_device, mesh=mesh, in_specs=in_specs, out_specs=out_specs, check_vma=False
    )
```

```python
import math

import jax
import jax.numpy as jnp
from jax import lax
from jax.sharding import PartitionSpec as P

EPS = 1e-06
BETA = 1.0
AXES = ("dp", "tensor")
BF16 = jnp.bfloat16
F32 = jnp.float32


def take_chunk(array, index, rows):
    return lax.dynamic_slice_in_dim(array, index * rows, rows, 0)


def dot(a, b):
    return jnp.dot(a, b, preferred_element_type=F32)


def dot_rows(a, b):
    return lax.dot_general(a, b, (((0,), (0,)), ((), ())), preferred_element_type=F32)


def swapped(array, dp_count):
    return lax.ppermute(array, "dp", [(i, i ^ 1) for i in range(dp_count)])


def exchanged(array, axis):
    return lax.all_to_all(array, axis, split_axis=0, concat_axis=0, tiled=True)


def on_device(
    tokens,
    ref_gain,
    ref_weight,
    pol_gain,
    pol_weight,
    lengths,
    bins,
    advantage,
    logprob_gap,
    cotangent,
):
    tensor_count = lax.axis_size("tensor")
    dp_count = lax.axis_size("dp")
    t = lax.axis_index("tensor")
    d = lax.axis_index("dp")
    cores = dp_count // tensor_count
    assert cores == 2
    places = dp_count // cores
    levels = places.bit_length() - 1
    assert 1 << levels == places
    place = d // cores
    core = d % cores
    group_rows, block = tokens.shape
    own_rows = group_rows // tensor_count
    slot_count = cotangent.shape[2]
    span_rows = slot_count // dp_count
    value_width = ref_weight.shape[1]
    model_width = pol_gain.shape[0]
    shard = pol_weight.shape[0]
    factor = 1.0 / math.sqrt(dp_count * tensor_count * lengths.shape[2])

    def flat(p, c, z):
        return (p * cores + c) * tensor_count + z

    relative = place ^ t
    gain_shard = take_chunk(pol_gain, d, shard)
    halves = 2
    half_rows = shard // halves
    held = [
        (
            pol_weight[i * half_rows : (i + 1) * half_rows].astype(F32)
            * gain_shard[i * half_rows : (i + 1) * half_rows, None]
        ).astype(BF16)
        for i in range(halves)
    ]
    holders = [[0] for _ in range(halves)]

    def stage(number):
        for i in range(halves):
            bit = 1 << ((i + number) % levels)
            pairs = [
                (flat(q ^ z, c, z), flat(q ^ bit ^ z, c, z))
                for q in holders[i]
                for c in range(cores)
                for z in range(tensor_count)
            ]
            got = lax.ppermute(held[i], AXES, pairs)
            getters = [q ^ bit for q in holders[i]]
            is_getter = jnp.zeros((), jnp.bool_)
            for q in getters:
                is_getter = is_getter | (relative == q)
            held[i] = jnp.where(is_getter, got, held[i])
            holders[i] = holders[i] + getters

    stage(0)

    kept_rows = lax.dynamic_slice_in_dim(tokens, core * shard, shard, 1)
    got_rows = swapped(lax.dynamic_slice_in_dim(tokens, (1 - core) * shard, shard, 1), dp_count)
    got_cot = exchanged(cotangent.reshape(slot_count, value_width), "dp")

    tied = lax.optimization_barrier((*held, kept_rows, tokens))
    held = list(tied[:halves])
    kept_rows, ref_tokens = tied[halves:]
    for number in range(1, levels):
        stage(number)

    tokens_f32 = ref_tokens.astype(F32)
    scaled = (tokens_f32 * ref_gain[None, :]).astype(BF16)
    ref_part = dot(scaled, ref_weight).astype(BF16)
    square = jnp.sum(jnp.square(tokens_f32), axis=1)
    square_high = lax.optimization_barrier(square.astype(BF16))
    square_low = (square - square_high.astype(F32)).astype(BF16)
    power_rows = 16
    powers = jnp.stack([square_high, square_low]).reshape(2, tensor_count, own_rows)
    powers = jnp.pad(
        powers.transpose(1, 0, 2), ((0, 0), (0, power_rows - 2), (0, value_width - own_rows))
    )
    ref_sent = jnp.concatenate(
        [ref_part.reshape(tensor_count, own_rows, value_width), powers], axis=1
    )
    tied = lax.optimization_barrier((*held, ref_sent, got_rows))
    weight = jnp.concatenate(tied[:halves], axis=0)
    ref_sent, got_rows = tied[halves:]
    ref_got = exchanged(ref_sent, "tensor")

    seq_lens = lengths.reshape(-1)
    seq_bins = bins.reshape(-1)
    seq_adv = advantage.reshape(-1)
    seq_starts = jnp.cumsum(seq_lens) - seq_lens
    row = jnp.arange(own_rows, dtype=jnp.int32)
    in_seq = (row[:, None] >= seq_starts[None, :]) & (
        row[:, None] < (seq_starts + seq_lens)[None, :]
    )
    row_slot = jnp.sum(
        jnp.where(in_seq, seq_bins * span_rows + row[:, None] - seq_starts[None, :], 0), axis=1
    )
    row_len = jnp.sum(jnp.where(in_seq, seq_lens[None, :], 0), axis=1).astype(F32)
    row_adv = jnp.sum(jnp.where(in_seq, seq_adv[None, :], 0.0), axis=1)
    importance = jnp.minimum(jnp.exp(logprob_gap), jnp.float32(2.0))
    coef_adv = (row_adv * importance / row_len).astype(BF16).astype(F32)[:, None]
    coef_pull = (BETA / row_len).astype(BF16).astype(F32)[:, None]
    slot = jnp.arange(slot_count, dtype=jnp.int32)
    row_at = (row_slot[:, None] == slot[None, :]).astype(BF16)
    slot_at = (slot[:, None] == row_slot[None, :]).astype(BF16)
    upstream = dot(row_at, got_cot)
    value_given = dot(got_rows, weight).astype(BF16)
    value_got = swapped(value_given, dp_count)
    value_part = (dot(kept_rows, weight) + value_got.astype(F32)).astype(BF16)

    value_part, ref_got = lax.optimization_barrier((value_part, ref_got))
    value_got = exchanged(value_part, "tensor").reshape(tensor_count, own_rows, value_width)
    ref_got = ref_got.astype(F32)
    square_sum = jnp.sum(ref_got[:, own_rows : own_rows + 2, :own_rows], axis=(0, 1))
    row_scale = lax.rsqrt(square_sum / model_width + EPS)[:, None]
    ref_values = jnp.sum(ref_got[:, :own_rows], axis=0) * row_scale
    ref_values = ref_values.astype(BF16).astype(F32)
    fixed = coef_adv * upstream - coef_pull * ref_values
    fixed, row_scale, value_got = lax.optimization_barrier((fixed, row_scale, value_got))
    values = jnp.sum(value_got.astype(F32), axis=0) * row_scale

    slope = ((fixed + coef_pull * values) * row_scale).astype(BF16)
    slopes = exchanged(jnp.tile(slope, (tensor_count, 1)), "tensor")
    sent = dot(slot_at, values.astype(BF16)).astype(BF16)
    policy_values = exchanged(sent, "dp")
    slopes, policy_values = lax.optimization_barrier((slopes, policy_values))
    slopes_got = swapped(slopes, dp_count)

    grad = dot_rows(kept_rows, slopes) + dot_rows(got_rows, slopes_got)
    gain_block = lax.dynamic_slice_in_dim(pol_gain, t * block + core * shard, shard, 0)
    grad = (grad * (gain_block * factor)[:, None]).astype(BF16)

    def turned(z):
        return sum(((z >> i) & 1) << (levels - 1 - i) for i in range(levels))

    out_rows = shard // tensor_count
    total = take_chunk(grad, place ^ turned(t), out_rows).astype(F32)
    for step in range(1, places):
        pairs = [
            (p * cores + c, (p ^ step) * cores + c) for p in range(places) for c in range(cores)
        ]
        total = total + lax.ppermute(
            take_chunk(grad, place ^ step ^ turned(t), out_rows), "dp", pairs
        ).astype(F32)
    pairs = [
        (flat(p, c, z), flat(z, c, p ^ turned(z)))
        for p in range(places)
        for c in range(cores)
        for z in range(tensor_count)
    ]
    grad_weight = lax.ppermute(total.astype(BF16), AXES, pairs).astype(F32)
    return (policy_values.reshape(1, 1, slot_count, value_width), grad_weight)


def solution(mesh):
    in_specs = (
        P("dp", "tensor"),
        P("tensor"),
        P("tensor", None),
        P(),
        P("dp", None),
        P("dp", "tensor", None),
        P("dp", "tensor", None),
        P("dp", "tensor", None),
        P(("dp", "tensor")),
        P("dp", "tensor", None, None),
    )
    out_specs = (P("dp", "tensor", None, None), P(("dp", "tensor"), None))
    return jax.shard_map(
        on_device, mesh=mesh, in_specs=in_specs, out_specs=out_specs, check_vma=False
    )
```

```python
import functools
import math

import jax
import jax.numpy as jnp
from jax import lax
from jax.experimental import pallas as pl
from jax.experimental.pallas import tpu as pltpu
from jax.sharding import PartitionSpec as P

EPS = 1e-06
BETA = 1.0
AXES = ("dp", "tensor")
BF16 = jnp.bfloat16
F32 = jnp.float32
POWER_ROWS = 16
PARTS = 2


def dot(a, b):
    return jnp.dot(a, b, preferred_element_type=F32)


def dot_rows(a, b):
    return lax.dot_general(a, b, (((0,), (0,)), ((), ())), preferred_element_type=F32)


def swapped(array, dp_count):
    return lax.ppermute(array, "dp", [(i, i ^ 1) for i in range(dp_count)])


def shifted(array, count, step):
    return lax.ppermute(array, "tensor", [(i, (i + step) % count) for i in range(count)])


def prepare_kernel(count, steps, at, x_ref, gain_ref, weight_ref, given_ref, kept_ref, *refs):
    sent_refs, (rows_ref, total, square) = refs[:count], refs[count:]
    f = pl.program_id(0)
    own = x_ref.shape[0] // count
    for k in range(count):
        source = lax.rem(at[0] - k + count, count)
        rows_ref[k * own : (k + 1) * own, :] = x_ref[pl.ds(pl.multiple_of(source * own, own), own), :]
    rows = rows_ref[...]

    @pl.when(f < steps // 2)
    def _():
        given_ref[...] = rows

    @pl.when(f >= steps // 2)
    def _():
        kept_ref[...] = rows

    wide = rows.astype(F32)
    part = dot((wide * gain_ref[...]).astype(BF16), weight_ref[...])
    squares = jnp.sum(wide * wide, axis=1, keepdims=True)

    @pl.when(f == 0)
    def _():
        total[...] = part
        square[...] = squares

    @pl.when(f > 0)
    def _():
        total[...] += part
        square[...] += squares

    @pl.when(f == steps - 1)
    def _():
        for k in range(count):
            sent = sent_refs[k]
            sent[:own, :] = total[k * own : (k + 1) * own, :].astype(BF16)
            power = jnp.broadcast_to(square[k * own : (k + 1) * own, :], (own, 128)).T
            high = power[: POWER_ROWS // 2].astype(BF16).astype(F32)
            low = power[: POWER_ROWS // 2] - high
            sent[own:, :] = jnp.zeros((POWER_ROWS, sent.shape[1]), BF16)
            sent[own:, :own] = jnp.concatenate([high, low], axis=0).astype(BF16)


def grad_kernel(places, at, kept_ref, got_ref, slope_ref, slope_got_ref, gain_ref, *refs):
    out_refs, grad = refs[:places], refs[places]
    total = dot_rows(kept_ref[...], slope_ref[...]) + dot_rows(got_ref[...], slope_got_ref[...])
    grad[...] = total * gain_ref[...]
    rows = out_refs[0].shape[0]
    for s in range(places):
        chunk = grad[pl.ds(pl.multiple_of(at[s] * rows, rows), rows), :]
        out_refs[s][...] = chunk.astype(out_refs[s].dtype)


def on_device(
    tokens,
    ref_gain,
    ref_weight,
    pol_gain,
    pol_weight,
    lengths,
    bins,
    advantage,
    logprob_gap,
    cotangent,
):
    tensor_count = lax.axis_size("tensor")
    dp_count = lax.axis_size("dp")
    t = lax.axis_index("tensor")
    d = lax.axis_index("dp")
    cores = dp_count // tensor_count
    assert cores == 2
    places = dp_count // cores
    levels = places.bit_length() - 1
    assert 1 << levels == places
    place = d // cores
    core = d % cores
    group_rows, block = tokens.shape
    own_rows = group_rows // tensor_count
    slot_count = cotangent.shape[2]
    span_rows = slot_count // dp_count
    value_width = ref_weight.shape[1]
    model_width = pol_gain.shape[0]
    shard = pol_weight.shape[0]
    width = value_width // PARTS
    out_rows = shard // tensor_count
    factor = 1.0 / math.sqrt(dp_count * tensor_count * lengths.shape[2])
    relative = place ^ t

    def flat(p, c, z):
        return (p * cores + c) * tensor_count + z

    halves = 2
    half_rows = shard // halves
    gain_shard = lax.dynamic_slice_in_dim(pol_gain, d * shard, shard, 0)

    def first(j, i):
        rows = slice(i * half_rows, (i + 1) * half_rows)
        piece = pol_weight[rows, j * width : (j + 1) * width].astype(F32)
        return (piece * gain_shard[rows, None]).astype(BF16)

    def stage(number, held):
        result = []
        for i in range(halves):
            holders = [0]
            for before in range(number):
                bit = 1 << ((i + before) % levels)
                holders = holders + [q ^ bit for q in holders]
            bit = 1 << ((i + number) % levels)
            pairs = [
                (flat(q ^ z, c, z), flat(q ^ bit ^ z, c, z))
                for q in holders
                for c in range(cores)
                for z in range(tensor_count)
            ]
            got = lax.ppermute(held[i], AXES, pairs)
            is_getter = jnp.zeros((), jnp.bool_)
            for q in holders:
                is_getter = is_getter | (relative == (q ^ bit))
            result.append(jnp.where(is_getter, got, held[i]))
        return result

    held = [[first(j, i) for i in range(halves)] for j in range(PARTS)]
    held[0] = stage(0, held[0])

    steps = 4
    feature_step = block // steps
    at = jnp.stack([t, (1 - core) * (steps // 2)]).astype(jnp.int32)
    sent_shape = (own_rows + POWER_ROWS, value_width)

    def at_step(f, at):
        return lax.rem(f + at[1], steps)

    prepared = pl.pallas_call(
        functools.partial(prepare_kernel, tensor_count, steps),
        grid_spec=pltpu.PrefetchScalarGridSpec(
            num_scalar_prefetch=1,
            grid=(steps,),
            in_specs=[
                pl.BlockSpec((group_rows, feature_step), lambda f, at: (0, at_step(f, at))),
                pl.BlockSpec((1, feature_step), lambda f, at: (0, at_step(f, at))),
                pl.BlockSpec((feature_step, value_width), lambda f, at: (at_step(f, at), 0)),
            ],
            out_specs=[
                pl.BlockSpec(
                    (group_rows, feature_step), lambda f, at: (0, jnp.minimum(f, steps // 2 - 1))
                ),
                pl.BlockSpec(
                    (group_rows, feature_step), lambda f, at: (0, jnp.maximum(f - steps // 2, 0))
                ),
            ]
            + [pl.BlockSpec(sent_shape, lambda f, at: (0, 0))] * tensor_count,
            scratch_shapes=[
                pltpu.VMEM((group_rows, feature_step), BF16),
                pltpu.VMEM((group_rows, value_width), F32),
                pltpu.VMEM((group_rows, 1), F32),
            ],
        ),
        out_shape=[jax.ShapeDtypeStruct((group_rows, shard), BF16)] * 2
        + [jax.ShapeDtypeStruct(sent_shape, BF16)] * tensor_count,
        compiler_params=pltpu.CompilerParams(vmem_limit_bytes=32 * 2**20),
        cost_estimate=pl.CostEstimate(
            flops=2 * group_rows * block * value_width,
            bytes_accessed=8 * 2**20,
            transcendentals=0,
        ),
        name="prepare",
    )(at, tokens, ref_gain.reshape(1, block), ref_weight)
    given_rows, kept_rows, *ref_sent = prepared

    tied = lax.optimization_barrier((*held[0], *held[1], given_rows, kept_rows, *ref_sent))
    held[0], held[1] = list(tied[:halves]), list(tied[halves : 2 * halves])
    given_rows, kept_rows, *ref_sent = tied[2 * halves :]
    ref_got = [ref_sent[0]] + [
        shifted(ref_sent[k], tensor_count, -k) for k in range(1, tensor_count)
    ]
    for number in range(1, levels):
        held[0] = stage(number, held[0])
    for number in range(levels):
        held[1] = stage(number, held[1])
    got_rows = swapped(given_rows, dp_count)
    got_cot = lax.all_to_all(
        cotangent.reshape(slot_count, value_width), "dp", split_axis=0, concat_axis=0, tiled=True
    )

    seq_lens = lengths.reshape(-1)
    seq_bins = bins.reshape(-1)
    seq_adv = advantage.reshape(-1)
    seq_starts = jnp.cumsum(seq_lens) - seq_lens
    row = jnp.arange(own_rows, dtype=jnp.int32)
    in_seq = (row[:, None] >= seq_starts[None, :]) & (
        row[:, None] < (seq_starts + seq_lens)[None, :]
    )
    row_slot = jnp.sum(
        jnp.where(in_seq, seq_bins * span_rows + row[:, None] - seq_starts[None, :], 0), axis=1
    )
    row_len = jnp.sum(jnp.where(in_seq, seq_lens[None, :], 0), axis=1).astype(F32)
    row_adv = jnp.sum(jnp.where(in_seq, seq_adv[None, :], 0.0), axis=1)
    importance = jnp.minimum(jnp.exp(logprob_gap), jnp.float32(2.0))
    coef_adv = (row_adv * importance / row_len).astype(BF16).astype(F32)[:, None]
    coef_pull = (BETA / row_len).astype(BF16).astype(F32)[:, None]
    slot = jnp.arange(slot_count, dtype=jnp.int32)
    row_at = (row_slot[:, None] == slot[None, :]).astype(BF16)
    slot_at = (slot[:, None] == row_slot[None, :]).astype(BF16)
    upstream = dot(row_at, got_cot)

    ref_total = sum(x.astype(F32) for x in ref_got)
    half_power = POWER_ROWS // 2
    square_sum = ref_total[own_rows, :own_rows] + ref_total[own_rows + half_power, :own_rows]
    row_scale = lax.rsqrt(square_sum / model_width + EPS)[:, None]
    ref_values = (ref_total[:own_rows] * row_scale).astype(BF16).astype(F32)
    fixed = coef_adv * upstream - coef_pull * ref_values
    gain_block = lax.dynamic_slice_in_dim(pol_gain, t * block + core * shard, shard, 0)
    grad_gain = (gain_block * factor)[:, None]

    def turned(z):
        return sum(((z >> i) & 1) << (levels - 1 - i) for i in range(levels))

    chunk_at = jnp.stack([place ^ s ^ turned(t) for s in range(places)]).astype(jnp.int32)

    tied = lax.optimization_barrier(
        (*held[0], got_rows, kept_rows, row_scale, fixed, coef_pull, slot_at, grad_gain, chunk_at)
    )
    held[0] = list(tied[:halves])
    got_rows, kept_rows, row_scale, fixed, coef_pull, slot_at, grad_gain, chunk_at = tied[halves:]

    values, slopes = [], []
    for j in range(PARTS):
        weight = jnp.concatenate(held[j], axis=0)
        value_got = swapped(dot(got_rows, weight).astype(BF16), dp_count).astype(F32)
        value_part = dot(kept_rows, weight) + value_got
        total = value_part[:own_rows]
        for k in range(1, tensor_count):
            part = value_part[k * own_rows : (k + 1) * own_rows].astype(BF16)
            total = total + shifted(part, tensor_count, -k).astype(F32)
        values.append(total * row_scale)

        cols = slice(j * width, (j + 1) * width)
        slope = ((fixed[:, cols] + coef_pull * values[j]) * row_scale).astype(BF16)
        slopes.append(
            jnp.concatenate(
                [slope] + [shifted(slope, tensor_count, k) for k in range(1, tensor_count)], axis=0
            )
        )

    sent = dot(slot_at, jnp.concatenate(values, axis=1).astype(BF16)).astype(BF16)
    policy_values = lax.all_to_all(sent, "dp", split_axis=0, concat_axis=0, tiled=True)

    grads = []
    for j in range(PARTS):
        if j == PARTS - 1:
            slopes[j], policy_values = lax.optimization_barrier((slopes[j], policy_values))
        slopes_got = swapped(slopes[j], dp_count)
        chunks = pl.pallas_call(
            functools.partial(grad_kernel, places),
            grid_spec=pltpu.PrefetchScalarGridSpec(
                num_scalar_prefetch=1,
                grid=(1,),
                in_specs=[
                    pl.BlockSpec((group_rows, shard), lambda i, at: (0, 0)),
                    pl.BlockSpec((group_rows, shard), lambda i, at: (0, 0)),
                    pl.BlockSpec((group_rows, width), lambda i, at: (0, 0)),
                    pl.BlockSpec((group_rows, width), lambda i, at: (0, 0)),
                    pl.BlockSpec((shard, 1), lambda i, at: (0, 0)),
                ],
                out_specs=[pl.BlockSpec((out_rows, width), lambda i, at: (0, 0))] * places,
                scratch_shapes=[pltpu.VMEM((shard, width), F32)],
            ),
            out_shape=[
                jax.ShapeDtypeStruct((out_rows, width), F32 if s == 0 else BF16)
                for s in range(places)
            ],
            compiler_params=pltpu.CompilerParams(vmem_limit_bytes=32 * 2**20),
            cost_estimate=pl.CostEstimate(
                flops=4 * group_rows * shard * width,
                bytes_accessed=4 * 2**20,
                transcendentals=0,
            ),
            name="gradient",
        )(chunk_at, kept_rows, got_rows, slopes[j], slopes_got, grad_gain)
        total = chunks[0]
        for s in range(1, places):
            pairs = [
                (p * cores + c, (p ^ s) * cores + c) for p in range(places) for c in range(cores)
            ]
            total = total + lax.ppermute(chunks[s], "dp", pairs).astype(F32)
        pairs = [
            (flat(p, c, z), flat(z, c, p ^ turned(z)))
            for p in range(places)
            for c in range(cores)
            for z in range(tensor_count)
        ]
        grads.append(lax.ppermute(total.astype(BF16), AXES, pairs))
    grad_weight = jnp.concatenate(grads, axis=1).astype(F32)
    return (policy_values.reshape(1, 1, slot_count, value_width), grad_weight)


def solution(mesh):
    in_specs = (
        P("dp", "tensor"),
        P("tensor"),
        P("tensor", None),
        P(),
        P("dp", None),
        P("dp", "tensor", None),
        P("dp", "tensor", None),
        P("dp", "tensor", None),
        P(("dp", "tensor")),
        P("dp", "tensor", None, None),
    )
    out_specs = (P("dp", "tensor", None, None), P(("dp", "tensor"), None))
    return jax.shard_map(
        on_device, mesh=mesh, in_specs=in_specs, out_specs=out_specs, check_vma=False
    )
```

```python
import functools
import math

import jax
import jax.numpy as jnp
from jax import lax
from jax.experimental import pallas as pl
from jax.experimental.pallas import tpu as pltpu
from jax.sharding import PartitionSpec as P

EPS = 1e-06
BETA = 1.0
AXES = ("dp", "tensor")
BF16 = jnp.bfloat16
F32 = jnp.float32
POWER_ROWS = 16
PARTS = 2


def dot(a, b):
    return jnp.dot(a, b, preferred_element_type=F32)


def dot_rows(a, b):
    return lax.dot_general(a, b, (((0,), (0,)), ((), ())), preferred_element_type=F32)


def swapped(array, dp_count):
    return lax.ppermute(array, "dp", [(i, i ^ 1) for i in range(dp_count)])


def shifted(array, count, step):
    return lax.ppermute(array, "tensor", [(i, (i + step) % count) for i in range(count)])


def prepare_kernel(
    count, steps, at, x_ref, gain_ref, weight_ref, pol_ref, given_ref, kept_ref, *refs
):
    sent_refs, (rows_ref, total, square) = refs[:count], refs[count:]
    f = pl.program_id(0)
    own = x_ref.shape[0] // count
    for k in range(count):
        source = lax.rem(at[0] - k + count, count)
        rows_ref[k * own : (k + 1) * own, :] = x_ref[pl.ds(pl.multiple_of(source * own, own), own), :]
    wide = rows_ref[...].astype(F32)
    gained = (wide * pol_ref[...]).astype(BF16)

    @pl.when(f < steps // 2)
    def _():
        given_ref[...] = gained

    @pl.when(f >= steps // 2)
    def _():
        kept_ref[...] = gained

    part = dot((wide * gain_ref[...]).astype(BF16), weight_ref[...])
    squares = jnp.sum(wide * wide, axis=1, keepdims=True)

    @pl.when(f == 0)
    def _():
        total[...] = part
        square[...] = squares

    @pl.when(f > 0)
    def _():
        total[...] += part
        square[...] += squares

    @pl.when(f == steps - 1)
    def _():
        for k in range(count):
            sent = sent_refs[k]
            sent[:own, :] = total[k * own : (k + 1) * own, :].astype(BF16)
            power = jnp.broadcast_to(square[k * own : (k + 1) * own, :], (own, 128)).T
            high = power[: POWER_ROWS // 2].astype(BF16).astype(F32)
            low = power[: POWER_ROWS // 2] - high
            sent[own:, :] = jnp.zeros((POWER_ROWS, sent.shape[1]), BF16)
            sent[own:, :own] = jnp.concatenate([high, low], axis=0).astype(BF16)


def select_kernel(at, *refs):
    count = len(refs) // 3
    for i in range(count):
        held_ref, got_ref, out_ref = refs[i], refs[count + i], refs[2 * count + i]

        @pl.when(at[i] > 0)
        def _():
            out_ref[...] = got_ref[...]

        @pl.when(at[i] <= 0)
        def _():
            out_ref[...] = held_ref[...]


def value_kernel(at, got_rows_ref, kept_rows_ref, *refs):
    given_ref, kept_ref, weight = refs[-3:]
    count = (len(refs) - 3) // 2
    rows = weight.shape[0] // count
    for i in range(count):
        held_ref, got_ref = refs[i], refs[count + i]

        @pl.when(at[i] > 0)
        def _():
            weight[i * rows : (i + 1) * rows, :] = got_ref[...]

        @pl.when(at[i] <= 0)
        def _():
            weight[i * rows : (i + 1) * rows, :] = held_ref[...]

    given_ref[...] = dot(got_rows_ref[...], weight[...]).astype(BF16)
    kept_ref[...] = dot(kept_rows_ref[...], weight[...])


def grad_kernel(places, factor, at, kept_ref, got_ref, slope_ref, slope_got_ref, *refs):
    out_refs, grad = refs[:places], refs[places]
    total = dot_rows(kept_ref[...], slope_ref[...]) + dot_rows(got_ref[...], slope_got_ref[...])
    grad[...] = total * factor
    rows = out_refs[0].shape[0]
    for s in range(places):
        chunk = grad[pl.ds(pl.multiple_of(at[s] * rows, rows), rows), :]
        out_refs[s][...] = chunk.astype(out_refs[s].dtype)


def on_device(
    tokens,
    ref_gain,
    ref_weight,
    pol_gain,
    pol_weight,
    lengths,
    bins,
    advantage,
    logprob_gap,
    cotangent,
):
    tensor_count = lax.axis_size("tensor")
    dp_count = lax.axis_size("dp")
    t = lax.axis_index("tensor")
    d = lax.axis_index("dp")
    cores = dp_count // tensor_count
    assert cores == 2
    places = dp_count // cores
    levels = places.bit_length() - 1
    assert 1 << levels == places
    place = d // cores
    core = d % cores
    group_rows, block = tokens.shape
    own_rows = group_rows // tensor_count
    slot_count = cotangent.shape[2]
    span_rows = slot_count // dp_count
    value_width = ref_weight.shape[1]
    model_width = pol_gain.shape[0]
    shard = pol_weight.shape[0]
    width = value_width // PARTS
    out_rows = shard // tensor_count
    factor = 1.0 / math.sqrt(dp_count * tensor_count * lengths.shape[2])
    relative = place ^ t

    def flat(p, c, z):
        return (p * cores + c) * tensor_count + z

    halves = 2
    half_rows = shard // halves

    def stage(number, held):
        got, is_getter = [], []
        for i in range(halves):
            holders = [0]
            for before in range(number):
                bit = 1 << ((i + before) % levels)
                holders = holders + [q ^ bit for q in holders]
            bit = 1 << ((i + number) % levels)
            pairs = [
                (flat(q ^ z, c, z), flat(q ^ bit ^ z, c, z))
                for q in holders
                for c in range(cores)
                for z in range(tensor_count)
            ]
            got.append(lax.ppermute(held[i], AXES, pairs))
            is_getter.append(functools.reduce(jnp.logical_or, [relative == (q ^ bit) for q in holders]))
        return got, jnp.stack(is_getter).astype(jnp.int32)

    def whole(shape):
        return pl.BlockSpec(shape, lambda i, at: (0,) * len(shape))

    def select(held, got, is_getter):
        shape = (half_rows, width)
        return list(
            pl.pallas_call(
                select_kernel,
                grid_spec=pltpu.PrefetchScalarGridSpec(
                    num_scalar_prefetch=1,
                    grid=(1,),
                    in_specs=[whole(shape)] * (2 * halves),
                    out_specs=[whole(shape)] * halves,
                ),
                out_shape=[jax.ShapeDtypeStruct(shape, BF16)] * halves,
                cost_estimate=pl.CostEstimate(flops=0, bytes_accessed=2**20, transcendentals=0),
                name="select",
            )(is_getter, *held, *got)
        )

    held = [
        [
            pol_weight[i * half_rows : (i + 1) * half_rows, j * width : (j + 1) * width]
            for i in range(halves)
        ]
        for j in range(PARTS)
    ]
    got = [None] * PARTS
    flags = [None] * PARTS
    got[0], flags[0] = stage(0, held[0])

    steps = 4
    feature_step = block // steps
    at = jnp.stack([t, (1 - core) * (steps // 2)]).astype(jnp.int32)
    sent_shape = (own_rows + POWER_ROWS, value_width)

    def at_step(f, at):
        return lax.rem(f + at[1], steps)

    prepared = pl.pallas_call(
        functools.partial(prepare_kernel, tensor_count, steps),
        grid_spec=pltpu.PrefetchScalarGridSpec(
            num_scalar_prefetch=1,
            grid=(steps,),
            in_specs=[
                pl.BlockSpec((group_rows, feature_step), lambda f, at: (0, at_step(f, at))),
                pl.BlockSpec((1, feature_step), lambda f, at: (0, at_step(f, at))),
                pl.BlockSpec((feature_step, value_width), lambda f, at: (at_step(f, at), 0)),
                pl.BlockSpec(
                    (1, feature_step), lambda f, at: (0, at[0] * steps + at_step(f, at))
                ),
            ],
            out_specs=[
                pl.BlockSpec(
                    (group_rows, feature_step), lambda f, at: (0, jnp.minimum(f, steps // 2 - 1))
                ),
                pl.BlockSpec(
                    (group_rows, feature_step), lambda f, at: (0, jnp.maximum(f - steps // 2, 0))
                ),
            ]
            + [pl.BlockSpec(sent_shape, lambda f, at: (0, 0))] * tensor_count,
            scratch_shapes=[
                pltpu.VMEM((group_rows, feature_step), BF16),
                pltpu.VMEM((group_rows, value_width), F32),
                pltpu.VMEM((group_rows, 1), F32),
            ],
        ),
        out_shape=[jax.ShapeDtypeStruct((group_rows, shard), BF16)] * 2
        + [jax.ShapeDtypeStruct(sent_shape, BF16)] * tensor_count,
        compiler_params=pltpu.CompilerParams(vmem_limit_bytes=56 * 2**20),
        cost_estimate=pl.CostEstimate(
            flops=2 * group_rows * block * value_width,
            bytes_accessed=8 * 2**20,
            transcendentals=0,
        ),
        name="prepare",
    )(at, tokens, ref_gain.reshape(1, block), ref_weight, pol_gain.reshape(1, model_width))
    given_rows, kept_rows, *ref_sent = prepared

    ref_got = [ref_sent[0]] + [
        shifted(ref_sent[k], tensor_count, -k) for k in range(1, tensor_count)
    ]
    got_rows = swapped(given_rows, dp_count)

    cot = cotangent.reshape(slot_count, value_width)
    tied = lax.optimization_barrier((*got[0], *held[1], kept_rows, cot))
    got[0], held[1] = list(tied[:halves]), list(tied[halves : 2 * halves])
    kept_rows, cot = tied[2 * halves :]
    for number in range(1, levels):
        held[0] = select(held[0], got[0], flags[0])
        got[0], flags[0] = stage(number, held[0])
    got[1], flags[1] = stage(0, held[1])
    for number in range(1, levels):
        held[1] = select(held[1], got[1], flags[1])
        got[1], flags[1] = stage(number, held[1])
    got_cot = lax.all_to_all(cot, "dp", split_axis=0, concat_axis=0, tiled=True)

    seq_lens = lengths.reshape(-1)
    seq_bins = bins.reshape(-1)
    seq_adv = advantage.reshape(-1)
    seq_starts = jnp.cumsum(seq_lens) - seq_lens
    row = jnp.arange(own_rows, dtype=jnp.int32)
    in_seq = (row[:, None] >= seq_starts[None, :]) & (
        row[:, None] < (seq_starts + seq_lens)[None, :]
    )
    row_slot = jnp.sum(
        jnp.where(in_seq, seq_bins * span_rows + row[:, None] - seq_starts[None, :], 0), axis=1
    )
    row_len = jnp.sum(jnp.where(in_seq, seq_lens[None, :], 0), axis=1).astype(F32)
    row_adv = jnp.sum(jnp.where(in_seq, seq_adv[None, :], 0.0), axis=1)
    importance = jnp.minimum(jnp.exp(logprob_gap), jnp.float32(2.0))
    coef_adv = (row_adv * importance / row_len).astype(BF16).astype(F32)[:, None]
    coef_pull = (BETA / row_len).astype(BF16).astype(F32)[:, None]
    slot = jnp.arange(slot_count, dtype=jnp.int32)
    row_at = (row_slot[:, None] == slot[None, :]).astype(BF16)
    slot_at = (slot[:, None] == row_slot[None, :]).astype(BF16)
    upstream = dot(row_at, got_cot)

    ref_total = sum(x.astype(F32) for x in ref_got)
    half_power = POWER_ROWS // 2
    square_sum = ref_total[own_rows, :own_rows] + ref_total[own_rows + half_power, :own_rows]
    row_scale = lax.rsqrt(square_sum / model_width + EPS)[:, None]
    ref_values = (ref_total[:own_rows] * row_scale).astype(BF16).astype(F32)
    fixed = coef_adv * upstream - coef_pull * ref_values

    def turned(z):
        return sum(((z >> i) & 1) << (levels - 1 - i) for i in range(levels))

    chunk_at = jnp.stack([place ^ s ^ turned(t) for s in range(places)]).astype(jnp.int32)

    values, slopes = [], []
    for j in range(PARTS):
        value_given, value_kept = pl.pallas_call(
            value_kernel,
            grid_spec=pltpu.PrefetchScalarGridSpec(
                num_scalar_prefetch=1,
                grid=(1,),
                in_specs=[whole((group_rows, shard))] * 2 + [whole((half_rows, width))] * 2 * halves,
                out_specs=[whole((group_rows, width))] * 2,
                scratch_shapes=[pltpu.VMEM((shard, width), BF16)],
            ),
            out_shape=[
                jax.ShapeDtypeStruct((group_rows, width), BF16),
                jax.ShapeDtypeStruct((group_rows, width), F32),
            ],
            compiler_params=pltpu.CompilerParams(vmem_limit_bytes=32 * 2**20),
            cost_estimate=pl.CostEstimate(
                flops=4 * group_rows * shard * width,
                bytes_accessed=4 * 2**20,
                transcendentals=0,
            ),
            name="values",
        )(flags[j], got_rows, kept_rows, *held[j], *got[j])
        value_part = value_kept + swapped(value_given, dp_count).astype(F32)
        total = value_part[:own_rows]
        for k in range(1, tensor_count):
            part = value_part[k * own_rows : (k + 1) * own_rows].astype(BF16)
            total = total + shifted(part, tensor_count, -k).astype(F32)
        values.append(total * row_scale)

        cols = slice(j * width, (j + 1) * width)
        slope = ((fixed[:, cols] + coef_pull * values[j]) * row_scale).astype(BF16)
        slopes.append(
            jnp.concatenate(
                [slope] + [shifted(slope, tensor_count, k) for k in range(1, tensor_count)], axis=0
            )
        )

    sent = dot(slot_at, jnp.concatenate(values, axis=1).astype(BF16)).astype(BF16)

    grads = []
    for j in range(PARTS):
        slopes_got = swapped(slopes[j], dp_count)
        chunks = pl.pallas_call(
            functools.partial(grad_kernel, places, factor),
            grid_spec=pltpu.PrefetchScalarGridSpec(
                num_scalar_prefetch=1,
                grid=(1,),
                in_specs=[
                    pl.BlockSpec((group_rows, shard), lambda i, at: (0, 0)),
                    pl.BlockSpec((group_rows, shard), lambda i, at: (0, 0)),
                    pl.BlockSpec((group_rows, width), lambda i, at: (0, 0)),
                    pl.BlockSpec((group_rows, width), lambda i, at: (0, 0)),
                ],
                out_specs=[pl.BlockSpec((out_rows, width), lambda i, at: (0, 0))] * places,
                scratch_shapes=[pltpu.VMEM((shard, width), F32)],
            ),
            out_shape=[
                jax.ShapeDtypeStruct((out_rows, width), F32 if s == 0 else BF16)
                for s in range(places)
            ],
            compiler_params=pltpu.CompilerParams(vmem_limit_bytes=32 * 2**20),
            cost_estimate=pl.CostEstimate(
                flops=4 * group_rows * shard * width,
                bytes_accessed=4 * 2**20,
                transcendentals=0,
            ),
            name="gradient",
        )(chunk_at, kept_rows, got_rows, slopes[j], slopes_got)
        total = chunks[0]
        for s in range(1, places):
            pairs = [
                (p * cores + c, (p ^ s) * cores + c) for p in range(places) for c in range(cores)
            ]
            total = total + lax.ppermute(chunks[s], "dp", pairs).astype(F32)
        total = total.astype(BF16)
        if j == 0:
            total, sent = lax.optimization_barrier((total, sent))
            policy_values = lax.all_to_all(sent, "dp", split_axis=0, concat_axis=0, tiled=True)
        pairs = [
            (flat(p, c, z), flat(z, c, p ^ turned(z)))
            for p in range(places)
            for c in range(cores)
            for z in range(tensor_count)
        ]
        grads.append(lax.ppermute(total, AXES, pairs))
    grad_weight = jnp.concatenate(grads, axis=1).astype(F32)
    return (policy_values.reshape(1, 1, slot_count, value_width), grad_weight)


def solution(mesh):
    in_specs = (
        P("dp", "tensor"),
        P("tensor"),
        P("tensor", None),
        P(),
        P("dp", None),
        P("dp", "tensor", None),
        P("dp", "tensor", None),
        P("dp", "tensor", None),
        P(("dp", "tensor")),
        P("dp", "tensor", None, None),
    )
    out_specs = (P("dp", "tensor", None, None), P(("dp", "tensor"), None))
    return jax.shard_map(
        on_device, mesh=mesh, in_specs=in_specs, out_specs=out_specs, check_vma=False
    )
```

```python
import functools
import math

import jax
import jax.numpy as jnp
from jax import lax
from jax.experimental import pallas as pl
from jax.experimental.pallas import tpu as pltpu
from jax.sharding import PartitionSpec as P

EPS = 1e-06
BETA = 1.0
AXES = ("dp", "tensor")
BF16 = jnp.bfloat16
F32 = jnp.float32
POWER_ROWS = 16
PARTS = 2


def dot(a, b):
    return jnp.dot(a, b, preferred_element_type=F32)


def dot_rows(a, b):
    return lax.dot_general(a, b, (((0,), (0,)), ((), ())), preferred_element_type=F32)


def swapped(array, dp_count):
    return lax.ppermute(array, "dp", [(i, i ^ 1) for i in range(dp_count)])


def shifted(array, count, step):
    return lax.ppermute(array, "tensor", [(i, (i + step) % count) for i in range(count)])


def prepare_kernel(
    count, steps, at, x_ref, gain_ref, weight_ref, pol_ref, given_ref, kept_ref, *refs
):
    sent_refs, (rows_ref, total, square) = refs[:count], refs[count:]
    f = pl.program_id(0)
    own = x_ref.shape[0] // count
    for k in range(count):
        source = lax.rem(at[0] - k + count, count)
        rows_ref[k * own : (k + 1) * own, :] = x_ref[pl.ds(pl.multiple_of(source * own, own), own), :]
    wide = rows_ref[...].astype(F32)
    gained = (wide * pol_ref[...]).astype(BF16)

    @pl.when(f < steps // 2)
    def _():
        given_ref[...] = gained

    @pl.when(f >= steps // 2)
    def _():
        kept_ref[...] = gained

    part = dot((wide * gain_ref[...]).astype(BF16), weight_ref[...])
    squares = jnp.sum(wide * wide, axis=1, keepdims=True)

    @pl.when(f == 0)
    def _():
        total[...] = part
        square[...] = squares

    @pl.when(f > 0)
    def _():
        total[...] += part
        square[...] += squares

    @pl.when(f == steps - 1)
    def _():
        for k in range(count):
            sent = sent_refs[k]
            sent[:own, :] = total[k * own : (k + 1) * own, :].astype(BF16)
            power = jnp.broadcast_to(square[k * own : (k + 1) * own, :], (own, 128)).T
            high = power[: POWER_ROWS // 2].astype(BF16).astype(F32)
            low = power[: POWER_ROWS // 2] - high
            sent[own:, :] = jnp.zeros((POWER_ROWS, sent.shape[1]), BF16)
            sent[own:, :own] = jnp.concatenate([high, low], axis=0).astype(BF16)


def row_kernel(
    count, span, model_width, lengths, bins, advantage, gap_ref, cot_ref, *refs
):
    ref_refs, (fixed_ref, pull_ref, scale_ref, row_at_ref) = refs[:count], refs[count:]
    own = pull_ref.shape[0]
    slots = row_at_ref.shape[1]
    row = lax.broadcasted_iota(jnp.int32, (own, slots), 0)
    slot = lax.broadcasted_iota(jnp.int32, (own, slots), 1)
    chosen = jnp.zeros((own, slots), jnp.bool_)
    size = jnp.ones((own, 128), F32)
    weight = jnp.zeros((own, 128), F32)
    start = jnp.int32(0)
    for s in range(lengths.shape[0]):
        end = start + lengths[s]
        inside = (row >= start) & (row < end)
        chosen = chosen | (inside & (slot - bins[s] * span == row - start))
        size = jnp.where(inside[:, :128], lengths[s].astype(F32), size)
        weight = jnp.where(inside[:, :128], advantage[s], weight)
        start = end
    row_at = jnp.where(chosen, 1.0, 0.0).astype(BF16)
    row_at_ref[...] = row_at
    importance = jnp.minimum(jnp.exp(jnp.broadcast_to(gap_ref[...], (128, own)).T), 2.0)
    coef_adv = (weight * importance / size).astype(BF16).astype(F32)
    coef_pull = (BETA / size).astype(BF16).astype(F32)
    total = ref_refs[0][...].astype(F32)
    for ref in ref_refs[1:]:
        total = total + ref[...].astype(F32)
    half = POWER_ROWS // 2
    square = total[own : own + 1, :own] + total[own + half : own + half + 1, :own]
    scale = lax.rsqrt(jnp.broadcast_to(square, (128, own)).T / model_width + EPS)
    reference = (total[:own] * scale[:, :1]).astype(BF16).astype(F32)
    upstream = dot(row_at, cot_ref[...])
    fixed_ref[...] = (coef_adv[:, :1] * upstream - coef_pull[:, :1] * reference) * scale[:, :1]
    pull_ref[...] = coef_pull * scale * scale
    scale_ref[...] = scale


def grad_kernel(places, factor, at, kept_ref, got_ref, slope_ref, slope_got_ref, *refs):
    out_refs, grad = refs[:places], refs[places]
    total = dot_rows(kept_ref[...], slope_ref[...]) + dot_rows(got_ref[...], slope_got_ref[...])
    grad[...] = total * factor
    rows = out_refs[0].shape[0]
    for s in range(places):
        chunk = grad[pl.ds(pl.multiple_of(at[s] * rows, rows), rows), :]
        out_refs[s][...] = chunk.astype(out_refs[s].dtype)


def on_device(
    tokens,
    ref_gain,
    ref_weight,
    pol_gain,
    pol_weight,
    lengths,
    bins,
    advantage,
    logprob_gap,
    cotangent,
):
    tensor_count = lax.axis_size("tensor")
    dp_count = lax.axis_size("dp")
    t = lax.axis_index("tensor")
    d = lax.axis_index("dp")
    cores = dp_count // tensor_count
    assert cores == 2
    places = dp_count // cores
    levels = places.bit_length() - 1
    assert 1 << levels == places
    place = d // cores
    core = d % cores
    group_rows, block = tokens.shape
    own_rows = group_rows // tensor_count
    slot_count = cotangent.shape[2]
    span_rows = slot_count // dp_count
    value_width = ref_weight.shape[1]
    model_width = pol_gain.shape[0]
    shard = pol_weight.shape[0]
    width = value_width // PARTS
    out_rows = shard // tensor_count
    factor = 1.0 / math.sqrt(dp_count * tensor_count * lengths.shape[2])
    relative = place ^ t

    def flat(p, c, z):
        return (p * cores + c) * tensor_count + z

    halves = 2
    half_rows = shard // halves

    def stage(number, held):
        got, is_getter = [], []
        for i in range(halves):
            holders = [0]
            for before in range(number):
                bit = 1 << ((i + before) % levels)
                holders = holders + [q ^ bit for q in holders]
            bit = 1 << ((i + number) % levels)
            pairs = [
                (flat(q ^ z, c, z), flat(q ^ bit ^ z, c, z))
                for q in holders
                for c in range(cores)
                for z in range(tensor_count)
            ]
            got.append(lax.ppermute(held[i], AXES, pairs))
            is_getter.append(
                functools.reduce(jnp.logical_or, [relative == (q ^ bit) for q in holders])
            )
        return got, is_getter

    def select(held, got, is_getter):
        return [jnp.where(is_getter[i], got[i], held[i]) for i in range(halves)]

    held = [pol_weight[i * half_rows : (i + 1) * half_rows] for i in range(halves)]
    got, flags = stage(0, held)

    steps = 4
    feature_step = block // steps
    at = jnp.stack([t, (1 - core) * (steps // 2)]).astype(jnp.int32)
    sent_shape = (own_rows + POWER_ROWS, value_width)

    def at_step(f, at):
        return lax.rem(f + at[1], steps)

    prepared = pl.pallas_call(
        functools.partial(prepare_kernel, tensor_count, steps),
        grid_spec=pltpu.PrefetchScalarGridSpec(
            num_scalar_prefetch=1,
            grid=(steps,),
            in_specs=[
                pl.BlockSpec((group_rows, feature_step), lambda f, at: (0, at_step(f, at))),
                pl.BlockSpec((1, feature_step), lambda f, at: (0, at_step(f, at))),
                pl.BlockSpec((feature_step, value_width), lambda f, at: (at_step(f, at), 0)),
                pl.BlockSpec(
                    (1, feature_step), lambda f, at: (0, at[0] * steps + at_step(f, at))
                ),
            ],
            out_specs=[
                pl.BlockSpec(
                    (group_rows, feature_step), lambda f, at: (0, jnp.minimum(f, steps // 2 - 1))
                ),
                pl.BlockSpec(
                    (group_rows, feature_step), lambda f, at: (0, jnp.maximum(f - steps // 2, 0))
                ),
            ]
            + [pl.BlockSpec(sent_shape, lambda f, at: (0, 0))] * tensor_count,
            scratch_shapes=[
                pltpu.VMEM((group_rows, feature_step), BF16),
                pltpu.VMEM((group_rows, value_width), F32),
                pltpu.VMEM((group_rows, 1), F32),
            ],
        ),
        out_shape=[jax.ShapeDtypeStruct((group_rows, shard), BF16)] * 2
        + [jax.ShapeDtypeStruct(sent_shape, BF16)] * tensor_count,
        compiler_params=pltpu.CompilerParams(vmem_limit_bytes=56 * 2**20),
        cost_estimate=pl.CostEstimate(
            flops=2 * group_rows * block * value_width,
            bytes_accessed=8 * 2**20,
            transcendentals=0,
        ),
        name="prepare",
    )(at, tokens, ref_gain.reshape(1, block), ref_weight, pol_gain.reshape(1, model_width))
    given_rows, kept_rows, *ref_sent = prepared

    ref_got = [ref_sent[0]] + [
        shifted(ref_sent[k], tensor_count, -k) for k in range(1, tensor_count)
    ]
    got_rows = swapped(given_rows, dp_count)

    cot = cotangent.reshape(slot_count, value_width)
    *got, cot, kept_rows = lax.optimization_barrier((*got, cot, kept_rows))
    parts = []
    for j in range(PARTS):
        cols = slice(j * width, (j + 1) * width)
        held_part = select([x[:, cols] for x in held], [x[:, cols] for x in got], flags)
        for number in range(1, levels):
            got_part, flags_part = stage(number, held_part)
            if number < levels - 1:
                held_part = select(held_part, got_part, flags_part)
        parts.append((held_part, got_part, flags_part))
    got_cot = lax.all_to_all(cot, "dp", split_axis=0, concat_axis=0, tiled=True)

    def turned(z):
        return sum(((z >> i) & 1) << (levels - 1 - i) for i in range(levels))

    chunk_at = jnp.stack([place ^ s ^ turned(t) for s in range(places)]).astype(jnp.int32)

    values, slopes = [], []
    for j in range(PARTS):
        held_part, got_part, flags_part = parts[j]
        if j == 0:
            *got_part, got_cot = lax.optimization_barrier((*got_part, got_cot))
        weight = jnp.concatenate(select(held_part, got_part, flags_part), axis=0)
        value_given = dot(got_rows, weight).astype(BF16)
        if j == 0:
            tied = lax.optimization_barrier((value_given, lengths, bins, advantage, logprob_gap))
            value_given, lengths, bins, advantage, logprob_gap = tied
            smem = pl.BlockSpec(memory_space=pltpu.SMEM)
            vmem = pl.BlockSpec(memory_space=pltpu.VMEM)
            fixed, pull, row_scale, row_at = pl.pallas_call(
                functools.partial(row_kernel, tensor_count, span_rows, model_width),
                in_specs=[smem] * 3 + [vmem] * (2 + tensor_count),
                out_specs=[vmem] * 4,
                out_shape=[
                    jax.ShapeDtypeStruct((own_rows, value_width), F32),
                    jax.ShapeDtypeStruct((own_rows, 128), F32),
                    jax.ShapeDtypeStruct((own_rows, 128), F32),
                    jax.ShapeDtypeStruct((own_rows, slot_count), BF16),
                ],
                compiler_params=pltpu.CompilerParams(vmem_limit_bytes=16 * 2**20),
                cost_estimate=pl.CostEstimate(
                    flops=2 * own_rows * slot_count * value_width,
                    bytes_accessed=2**21,
                    transcendentals=0,
                ),
                name="rows",
            )(
                lengths.reshape(-1),
                bins.reshape(-1),
                advantage.reshape(-1),
                logprob_gap.reshape(1, own_rows),
                got_cot,
                *ref_got,
            )
        value_part = dot(kept_rows, weight) + swapped(value_given, dp_count).astype(F32)
        total = value_part[:own_rows]
        for k in range(1, tensor_count):
            part = value_part[k * own_rows : (k + 1) * own_rows].astype(BF16)
            total = total + shifted(part, tensor_count, -k).astype(F32)
        values.append(total * row_scale[:, :1])

        cols = slice(j * width, (j + 1) * width)
        slope = (fixed[:, cols] + pull[:, :1] * total).astype(BF16)
        slopes.append(
            jnp.concatenate(
                [slope] + [shifted(slope, tensor_count, k) for k in range(1, tensor_count)], axis=0
            )
        )

    sent = dot_rows(row_at, jnp.concatenate(values, axis=1).astype(BF16)).astype(BF16)

    grads = []
    for j in range(PARTS):
        slopes_got = swapped(slopes[j], dp_count)
        chunks = pl.pallas_call(
            functools.partial(grad_kernel, places, factor),
            grid_spec=pltpu.PrefetchScalarGridSpec(
                num_scalar_prefetch=1,
                grid=(1,),
                in_specs=[
                    pl.BlockSpec((group_rows, shard), lambda i, at: (0, 0)),
                    pl.BlockSpec((group_rows, shard), lambda i, at: (0, 0)),
                    pl.BlockSpec((group_rows, width), lambda i, at: (0, 0)),
                    pl.BlockSpec((group_rows, width), lambda i, at: (0, 0)),
                ],
                out_specs=[pl.BlockSpec((out_rows, width), lambda i, at: (0, 0))] * places,
                scratch_shapes=[pltpu.VMEM((shard, width), F32)],
            ),
            out_shape=[
                jax.ShapeDtypeStruct((out_rows, width), F32 if s == 0 else BF16)
                for s in range(places)
            ],
            compiler_params=pltpu.CompilerParams(vmem_limit_bytes=32 * 2**20),
            cost_estimate=pl.CostEstimate(
                flops=4 * group_rows * shard * width,
                bytes_accessed=4 * 2**20,
                transcendentals=0,
            ),
            name="gradient",
        )(chunk_at, kept_rows, got_rows, slopes[j], slopes_got)
        if j == PARTS - 1:
            *chunks, sent = lax.optimization_barrier((*chunks, sent))
            policy_values = lax.all_to_all(sent, "dp", split_axis=0, concat_axis=0, tiled=True)
        total = chunks[0]
        for s in range(1, places):
            pairs = [
                (p * cores + c, (p ^ s) * cores + c) for p in range(places) for c in range(cores)
            ]
            total = total + lax.ppermute(chunks[s], "dp", pairs).astype(F32)
        total = total.astype(BF16)
        pairs = [
            (flat(p, c, z), flat(z, c, p ^ turned(z)))
            for p in range(places)
            for c in range(cores)
            for z in range(tensor_count)
        ]
        grads.append(lax.ppermute(total, AXES, pairs))
    grad_weight = jnp.concatenate(grads, axis=1).astype(F32)
    return (policy_values.reshape(1, 1, slot_count, value_width), grad_weight)


def solution(mesh):
    in_specs = (
        P("dp", "tensor"),
        P("tensor"),
        P("tensor", None),
        P(),
        P("dp", None),
        P("dp", "tensor", None),
        P("dp", "tensor", None),
        P("dp", "tensor", None),
        P(("dp", "tensor")),
        P("dp", "tensor", None, None),
    )
    out_specs = (P("dp", "tensor", None, None), P(("dp", "tensor"), None))
    return jax.shard_map(
        on_device, mesh=mesh, in_specs=in_specs, out_specs=out_specs, check_vma=False
    )
```

```python
import functools
import math

import jax
import jax.numpy as jnp
from jax import lax
from jax.experimental import pallas as pl
from jax.experimental.pallas import tpu as pltpu
from jax.sharding import PartitionSpec as P

EPS = 1e-06
BETA = 1.0
AXES = ("dp", "tensor")
BF16 = jnp.bfloat16
F32 = jnp.float32
POWER_ROWS = 16
PARTS = 2


def dot(a, b):
    return jnp.dot(a, b, preferred_element_type=F32)


def dot_rows(a, b):
    return lax.dot_general(a, b, (((0,), (0,)), ((), ())), preferred_element_type=F32)


def swapped(array, dp_count):
    return lax.ppermute(array, "dp", [(i, i ^ 1) for i in range(dp_count)])


def turned(index, levels):
    return sum(((index >> i) & 1) << (levels - 1 - i) for i in range(levels))


def crossed(array, count, step):
    return lax.ppermute(array, "tensor", [(i, i ^ step) for i in range(count)])


def prepare_kernel(
    count, steps, at, x_ref, gain_ref, weight_ref, pol_ref, given_ref, kept_ref, *refs
):
    sent_refs, (rows_ref, total, square) = refs[:count], refs[count:]
    f = pl.program_id(0)
    own = x_ref.shape[0] // count
    levels = count.bit_length() - 1
    for i in range(count):
        source = jnp.bitwise_xor(at[0], turned(i, levels))
        rows_ref[i * own : (i + 1) * own, :] = x_ref[pl.ds(pl.multiple_of(source * own, own), own), :]
    wide = rows_ref[...].astype(F32)
    gained = (wide * pol_ref[...]).astype(BF16)

    @pl.when(f < steps // 2)
    def _():
        given_ref[...] = gained

    @pl.when(f >= steps // 2)
    def _():
        kept_ref[...] = gained

    part = dot((wide * gain_ref[...]).astype(BF16), weight_ref[...])
    squares = jnp.sum(wide * wide, axis=1, keepdims=True)

    @pl.when(f == 0)
    def _():
        total[...] = part
        square[...] = squares

    @pl.when(f > 0)
    def _():
        total[...] += part
        square[...] += squares

    @pl.when(f == steps - 1)
    def _():
        for i in range(count):
            sent = sent_refs[turned(i, levels)]
            sent[:own, :] = total[i * own : (i + 1) * own, :].astype(BF16)
            power = jnp.broadcast_to(square[i * own : (i + 1) * own, :], (own, 128)).T
            high = power[: POWER_ROWS // 2].astype(BF16).astype(F32)
            low = power[: POWER_ROWS // 2] - high
            sent[own:, :] = jnp.zeros((POWER_ROWS, sent.shape[1]), BF16)
            sent[own:, :own] = jnp.concatenate([high, low], axis=0).astype(BF16)


def row_kernel(
    count, span, model_width, lengths, bins, advantage, gap_ref, cot_ref, *refs
):
    ref_refs, (fixed_ref, pull_ref, scale_ref, row_at_ref) = refs[:count], refs[count:]
    own = pull_ref.shape[0]
    slots = row_at_ref.shape[1]
    row = lax.broadcasted_iota(jnp.int32, (own, slots), 0)
    slot = lax.broadcasted_iota(jnp.int32, (own, slots), 1)
    chosen = jnp.zeros((own, slots), jnp.bool_)
    size = jnp.ones((own, 128), F32)
    weight = jnp.zeros((own, 128), F32)
    start = jnp.int32(0)
    for s in range(lengths.shape[0]):
        end = start + lengths[s]
        inside = (row >= start) & (row < end)
        chosen = chosen | (inside & (slot - bins[s] * span == row - start))
        size = jnp.where(inside[:, :128], lengths[s].astype(F32), size)
        weight = jnp.where(inside[:, :128], advantage[s], weight)
        start = end
    row_at = jnp.where(chosen, 1.0, 0.0).astype(BF16)
    row_at_ref[...] = row_at
    importance = jnp.minimum(jnp.exp(jnp.broadcast_to(gap_ref[...], (128, own)).T), 2.0)
    coef_adv = (weight * importance / size).astype(BF16).astype(F32)
    coef_pull = (BETA / size).astype(BF16).astype(F32)
    total = ref_refs[0][...].astype(F32)
    for ref in ref_refs[1:]:
        total = total + ref[...].astype(F32)
    half = POWER_ROWS // 2
    square = total[own : own + 1, :own] + total[own + half : own + half + 1, :own]
    scale = lax.rsqrt(jnp.broadcast_to(square, (128, own)).T / model_width + EPS)
    reference = (total[:own] * scale[:, :1]).astype(BF16).astype(F32)
    upstream = dot(row_at, cot_ref[...])
    fixed_ref[...] = (coef_adv[:, :1] * upstream - coef_pull[:, :1] * reference) * scale[:, :1]
    pull_ref[...] = coef_pull * scale * scale
    scale_ref[...] = scale


def grad_kernel(places, factor, at, kept_ref, got_ref, slope_ref, slope_got_ref, *refs):
    out_refs, grad = refs[:places], refs[places]
    total = dot_rows(kept_ref[...], slope_ref[...]) + dot_rows(got_ref[...], slope_got_ref[...])
    grad[...] = total * factor
    rows = out_refs[0].shape[0]
    for s in range(places):
        chunk = grad[pl.ds(pl.multiple_of(at[s] * rows, rows), rows), :]
        out_refs[s][...] = chunk.astype(out_refs[s].dtype)


def on_device(
    tokens,
    ref_gain,
    ref_weight,
    pol_gain,
    pol_weight,
    lengths,
    bins,
    advantage,
    logprob_gap,
    cotangent,
):
    tensor_count = lax.axis_size("tensor")
    dp_count = lax.axis_size("dp")
    t = lax.axis_index("tensor")
    d = lax.axis_index("dp")
    cores = dp_count // tensor_count
    assert cores == 2
    places = dp_count // cores
    levels = places.bit_length() - 1
    assert 1 << levels == places == tensor_count
    place = d // cores
    core = d % cores
    group_rows, block = tokens.shape
    own_rows = group_rows // tensor_count
    slot_count = cotangent.shape[2]
    span_rows = slot_count // dp_count
    value_width = ref_weight.shape[1]
    model_width = pol_gain.shape[0]
    shard = pol_weight.shape[0]
    width = value_width // PARTS
    out_rows = shard // tensor_count
    factor = 1.0 / math.sqrt(dp_count * tensor_count * lengths.shape[2])
    relative = place ^ t

    def flat(p, c, z):
        return (p * cores + c) * tensor_count + z

    def stage(number, held):
        pairs, is_getter = [], jnp.zeros((), jnp.bool_)
        for c in range(cores):
            holders = [0]
            for before in range(number):
                bit = 1 << ((c + before) % levels)
                holders = holders + [q ^ bit for q in holders]
            bit = 1 << ((c + number) % levels)
            for q in holders:
                pairs += [
                    (flat(q ^ z, c, z), flat(q ^ bit ^ z, c, z)) for z in range(tensor_count)
                ]
                is_getter = is_getter | ((core == c) & (relative == (q ^ bit)))
        return lax.ppermute(held, AXES, pairs), is_getter

    got, is_getter = stage(0, pol_weight)

    steps = 4
    feature_step = block // steps
    at = jnp.stack([t, (1 - core) * (steps // 2)]).astype(jnp.int32)
    sent_shape = (own_rows + POWER_ROWS, value_width)

    def at_step(f, at):
        return lax.rem(f + at[1], steps)

    prepared = pl.pallas_call(
        functools.partial(prepare_kernel, tensor_count, steps),
        grid_spec=pltpu.PrefetchScalarGridSpec(
            num_scalar_prefetch=1,
            grid=(steps,),
            in_specs=[
                pl.BlockSpec((group_rows, feature_step), lambda f, at: (0, at_step(f, at))),
                pl.BlockSpec((1, feature_step), lambda f, at: (0, at_step(f, at))),
                pl.BlockSpec((feature_step, value_width), lambda f, at: (at_step(f, at), 0)),
                pl.BlockSpec(
                    (1, feature_step), lambda f, at: (0, at[0] * steps + at_step(f, at))
                ),
            ],
            out_specs=[
                pl.BlockSpec(
                    (group_rows, feature_step), lambda f, at: (0, jnp.minimum(f, steps // 2 - 1))
                ),
                pl.BlockSpec(
                    (group_rows, feature_step), lambda f, at: (0, jnp.maximum(f - steps // 2, 0))
                ),
            ]
            + [pl.BlockSpec(sent_shape, lambda f, at: (0, 0))] * tensor_count,
            scratch_shapes=[
                pltpu.VMEM((group_rows, feature_step), BF16),
                pltpu.VMEM((group_rows, value_width), F32),
                pltpu.VMEM((group_rows, 1), F32),
            ],
        ),
        out_shape=[jax.ShapeDtypeStruct((group_rows, shard), BF16)] * 2
        + [jax.ShapeDtypeStruct(sent_shape, BF16)] * tensor_count,
        compiler_params=pltpu.CompilerParams(vmem_limit_bytes=56 * 2**20),
        cost_estimate=pl.CostEstimate(
            flops=2 * group_rows * block * value_width,
            bytes_accessed=8 * 2**20,
            transcendentals=0,
        ),
        name="prepare",
    )(at, tokens, ref_gain.reshape(1, block), ref_weight, pol_gain.reshape(1, model_width))
    given_rows, kept_rows, *ref_sent = prepared

    ref_got = [ref_sent[0]] + [
        crossed(ref_sent[k], tensor_count, k) for k in range(1, tensor_count)
    ]
    got_rows = swapped(given_rows, dp_count)

    cot = cotangent.reshape(slot_count, value_width)
    got, cot, kept_rows = lax.optimization_barrier((got, cot, kept_rows))
    parts = []
    for j in range(PARTS):
        cols = slice(j * width, (j + 1) * width)
        held_part = jnp.where(is_getter, got[:, cols], pol_weight[:, cols])
        for number in range(1, levels):
            got_part, is_getter_part = stage(number, held_part)
            if number < levels - 1:
                held_part = jnp.where(is_getter_part, got_part, held_part)
        parts.append((held_part, got_part, is_getter_part))
    got_cot = lax.all_to_all(cot, "dp", split_axis=0, concat_axis=0, tiled=True)

    chunk_at = jnp.stack([place ^ s ^ turned(t, levels) for s in range(places)]).astype(jnp.int32)

    values, slopes = [], []
    for j in range(PARTS):
        held_part, got_part, is_getter_part = parts[j]
        if j == 0:
            got_part, got_cot, *ref_got = lax.optimization_barrier((got_part, got_cot, *ref_got))
        weight = jnp.where(is_getter_part, got_part, held_part)
        value_given = dot(got_rows, weight).astype(BF16)
        if j == 0:
            smem = pl.BlockSpec(memory_space=pltpu.SMEM)
            vmem = pl.BlockSpec(memory_space=pltpu.VMEM)
            fixed, pull, row_scale, row_at = pl.pallas_call(
                functools.partial(row_kernel, tensor_count, span_rows, model_width),
                in_specs=[smem] * 3 + [vmem] * (2 + tensor_count),
                out_specs=[vmem] * 4,
                out_shape=[
                    jax.ShapeDtypeStruct((own_rows, value_width), F32),
                    jax.ShapeDtypeStruct((own_rows, 128), F32),
                    jax.ShapeDtypeStruct((own_rows, 128), F32),
                    jax.ShapeDtypeStruct((own_rows, slot_count), BF16),
                ],
                compiler_params=pltpu.CompilerParams(vmem_limit_bytes=16 * 2**20),
                cost_estimate=pl.CostEstimate(
                    flops=2 * own_rows * slot_count * value_width,
                    bytes_accessed=2**21,
                    transcendentals=0,
                ),
                name="rows",
            )(
                lengths.reshape(-1),
                bins.reshape(-1),
                advantage.reshape(-1),
                logprob_gap.reshape(1, own_rows),
                got_cot,
                *ref_got,
            )
        value_part = dot(kept_rows, weight) + swapped(value_given, dp_count).astype(F32)
        total = value_part
        for level in range(levels):
            rows = total.shape[0] // 2
            sent = total[rows:].astype(BF16)
            total = total[:rows] + crossed(sent, tensor_count, 1 << level).astype(F32)
        values.append(total * row_scale[:, :1])

        cols = slice(j * width, (j + 1) * width)
        slope = (fixed[:, cols] + pull[:, :1] * total).astype(BF16)
        for level in reversed(range(levels)):
            got = crossed(slope, tensor_count, 1 << level)
            slope = jnp.concatenate([slope, got], axis=0)
        slopes.append(slope)

    sent = dot_rows(row_at, jnp.concatenate(values, axis=1).astype(BF16)).astype(BF16)

    grad_own, grad_got = [], []
    for j in range(PARTS):
        slopes_got = swapped(slopes[j], dp_count)
        if j > 0:
            slopes_got, grad_own[j - 1] = lax.optimization_barrier((slopes_got, grad_own[j - 1]))
        chunks = pl.pallas_call(
            functools.partial(grad_kernel, places, factor),
            grid_spec=pltpu.PrefetchScalarGridSpec(
                num_scalar_prefetch=1,
                grid=(1,),
                in_specs=[
                    pl.BlockSpec((group_rows, shard), lambda i, at: (0, 0)),
                    pl.BlockSpec((group_rows, shard), lambda i, at: (0, 0)),
                    pl.BlockSpec((group_rows, width), lambda i, at: (0, 0)),
                    pl.BlockSpec((group_rows, width), lambda i, at: (0, 0)),
                ],
                out_specs=[pl.BlockSpec((out_rows, width), lambda i, at: (0, 0))] * places,
                scratch_shapes=[pltpu.VMEM((shard, width), F32)],
            ),
            out_shape=[
                jax.ShapeDtypeStruct((out_rows, width), F32 if s == 0 else BF16)
                for s in range(places)
            ],
            compiler_params=pltpu.CompilerParams(vmem_limit_bytes=32 * 2**20),
            cost_estimate=pl.CostEstimate(
                flops=4 * group_rows * shard * width,
                bytes_accessed=4 * 2**20,
                transcendentals=0,
            ),
            name="gradient",
        )(chunk_at, kept_rows, got_rows, slopes[j], slopes_got)
        grad_own.append(chunks[0])
        grad_got.append([])
        if j == PARTS - 1:
            grad_own[j], sent = lax.optimization_barrier((grad_own[j], sent))
            policy_values = lax.all_to_all(sent, "dp", split_axis=0, concat_axis=0, tiled=True)
        for s in range(1, places):
            pairs = [
                (p * cores + c, (p ^ s) * cores + c) for p in range(places) for c in range(cores)
            ]
            grad_got[j].append(lax.ppermute(chunks[s], "dp", pairs))
    grads = []
    for j in range(PARTS):
        total = (grad_own[j] + sum(x.astype(F32) for x in grad_got[j])).astype(BF16)
        pairs = [
            (flat(p, c, z), flat(z, c, p ^ turned(z, levels)))
            for p in range(places)
            for c in range(cores)
            for z in range(tensor_count)
        ]
        grads.append(lax.ppermute(total, AXES, pairs))
    grad_weight = jnp.concatenate(grads, axis=1).astype(F32)
    return (policy_values.reshape(1, 1, slot_count, value_width), grad_weight)


def solution(mesh):
    in_specs = (
        P("dp", "tensor"),
        P("tensor"),
        P("tensor", None),
        P(),
        P("dp", None),
        P("dp", "tensor", None),
        P("dp", "tensor", None),
        P("dp", "tensor", None),
        P(("dp", "tensor")),
        P("dp", "tensor", None, None),
    )
    out_specs = (P("dp", "tensor", None, None), P(("dp", "tensor"), None))
    return jax.shard_map(
        on_device, mesh=mesh, in_specs=in_specs, out_specs=out_specs, check_vma=False
    )
```

```python
import functools
import math

import jax
import jax.numpy as jnp
from jax import lax
from jax.experimental import pallas as pl
from jax.experimental.pallas import tpu as pltpu
from jax.sharding import PartitionSpec as P

EPS = 1e-06
BETA = 1.0
AXES = ("dp", "tensor")
BF16 = jnp.bfloat16
F32 = jnp.float32
POWER_ROWS = 16
PARTS = 2


def dot(a, b):
    return jnp.dot(a, b, preferred_element_type=F32)


def dot_rows(a, b):
    return lax.dot_general(a, b, (((0,), (0,)), ((), ())), preferred_element_type=F32)


def swapped(array, dp_count):
    return lax.ppermute(array, "dp", [(i, i ^ 1) for i in range(dp_count)])


def turned(index, levels):
    return sum(((index >> i) & 1) << (levels - 1 - i) for i in range(levels))


def crossed(array, count, step):
    return lax.ppermute(array, "tensor", [(i, i ^ step) for i in range(count)])


def ordered(count, at, x_ref, rows_ref):
    levels = count.bit_length() - 1
    own = x_ref.shape[0] // count
    for i in range(count):
        source = jnp.bitwise_xor(at[0], turned(i, levels))
        rows_ref[i * own : (i + 1) * own, :] = x_ref[pl.ds(pl.multiple_of(source * own, own), own), :]
    return rows_ref[...].astype(F32)


def split_kernel(count, steps, at, x_ref, gain_ref, given_ref, kept_ref, rows_ref):
    f = pl.program_id(0)
    gained = (ordered(count, at, x_ref, rows_ref) * gain_ref[...]).astype(BF16)

    @pl.when(f < steps // 2)
    def _():
        given_ref[...] = gained

    @pl.when(f >= steps // 2)
    def _():
        kept_ref[...] = gained


def reference_kernel(
    count, steps, at, x_ref, gain_ref, weight_ref, kept_ref, sent_ref, rows_ref, total, square
):
    f = pl.program_id(0)
    own = x_ref.shape[0] // count
    wide = ordered(count, at, x_ref, rows_ref)
    part = dot((wide * gain_ref[...]).astype(BF16), weight_ref[...])
    squares = jnp.sum(wide * wide, axis=1, keepdims=True)

    @pl.when(f == 0)
    def _():
        total[...] = part
        square[...] = squares

    @pl.when(f > 0)
    def _():
        total[...] += part
        square[...] += squares

    @pl.when(f == steps - 1)
    def _():
        for i in range(count):
            out = (kept_ref, sent_ref)[i // (count // 2)].at[i % (count // 2)]
            out[:own, :] = total[i * own : (i + 1) * own, :].astype(BF16)
            power = jnp.broadcast_to(square[i * own : (i + 1) * own, :], (own, 128)).T
            high = power[: POWER_ROWS // 2].astype(BF16).astype(F32)
            low = power[: POWER_ROWS // 2] - high
            out[own:, :] = jnp.zeros((POWER_ROWS, out.shape[1]), BF16)
            out[own:, :own] = jnp.concatenate([high, low], axis=0).astype(BF16)


def row_kernel(
    span, model_width, lengths, bins, advantage, gap_ref, cot_ref, kept_ref, got_ref, *refs
):
    fixed_ref, pull_ref, scale_ref, row_at_ref = refs
    own = pull_ref.shape[0]
    slots = row_at_ref.shape[1]
    row = lax.broadcasted_iota(jnp.int32, (own, slots), 0)
    slot = lax.broadcasted_iota(jnp.int32, (own, slots), 1)
    chosen = jnp.zeros((own, slots), jnp.bool_)
    size = jnp.ones((own, 128), F32)
    weight = jnp.zeros((own, 128), F32)
    start = jnp.int32(0)
    for s in range(lengths.shape[0]):
        end = start + lengths[s]
        inside = (row >= start) & (row < end)
        chosen = chosen | (inside & (slot - bins[s] * span == row - start))
        size = jnp.where(inside[:, :128], lengths[s].astype(F32), size)
        weight = jnp.where(inside[:, :128], advantage[s], weight)
        start = end
    row_at = jnp.where(chosen, 1.0, 0.0).astype(BF16)
    row_at_ref[...] = row_at
    importance = jnp.minimum(jnp.exp(jnp.broadcast_to(gap_ref[...], (128, own)).T), 2.0)
    coef_adv = (weight * importance / size).astype(BF16).astype(F32)
    coef_pull = (BETA / size).astype(BF16).astype(F32)
    total = kept_ref[...].astype(F32) + got_ref[...].astype(F32)
    square = jnp.zeros((1, own), F32)
    for power_row in range(own, total.shape[0], POWER_ROWS // 2):
        square = square + total[power_row : power_row + 1, :own]
    scale = lax.rsqrt(jnp.broadcast_to(square, (128, own)).T / model_width + EPS)
    reference = (total[:own] * scale[:, :1]).astype(BF16).astype(F32)
    upstream = dot(row_at, cot_ref[...])
    fixed_ref[...] = (coef_adv[:, :1] * upstream - coef_pull[:, :1] * reference) * scale[:, :1]
    pull_ref[...] = coef_pull * scale * scale
    scale_ref[...] = scale


def grad_kernel(places, factor, at, kept_ref, got_ref, slope_ref, slope_got_ref, *refs):
    out_refs, grad = refs[:places], refs[places]
    total = dot_rows(kept_ref[...], slope_ref[...]) + dot_rows(got_ref[...], slope_got_ref[...])
    grad[...] = total * factor
    rows = out_refs[0].shape[0]
    for s in range(places):
        chunk = grad[pl.ds(pl.multiple_of(at[s] * rows, rows), rows), :]
        out_refs[s][...] = chunk.astype(out_refs[s].dtype)


def on_device(
    tokens,
    ref_gain,
    ref_weight,
    pol_gain,
    pol_weight,
    lengths,
    bins,
    advantage,
    logprob_gap,
    cotangent,
):
    tensor_count = lax.axis_size("tensor")
    dp_count = lax.axis_size("dp")
    t = lax.axis_index("tensor")
    d = lax.axis_index("dp")
    cores = dp_count // tensor_count
    assert cores == 2
    places = dp_count // cores
    levels = places.bit_length() - 1
    assert 1 << levels == places == tensor_count
    place = d // cores
    core = d % cores
    group_rows, block = tokens.shape
    own_rows = group_rows // tensor_count
    slot_count = cotangent.shape[2]
    span_rows = slot_count // dp_count
    value_width = ref_weight.shape[1]
    model_width = pol_gain.shape[0]
    shard = pol_weight.shape[0]
    width = value_width // PARTS
    out_rows = shard // tensor_count
    factor = 1.0 / math.sqrt(dp_count * tensor_count * lengths.shape[2])
    relative = place ^ t

    def flat(p, c, z):
        return (p * cores + c) * tensor_count + z

    def stage(number, held):
        pairs, is_getter = [], jnp.zeros((), jnp.bool_)
        for c in range(cores):
            holders = [0]
            for before in range(number):
                bit = 1 << ((c + before) % levels)
                holders = holders + [q ^ bit for q in holders]
            bit = 1 << ((c + number) % levels)
            for q in holders:
                pairs += [
                    (flat(q ^ z, c, z), flat(q ^ bit ^ z, c, z)) for z in range(tensor_count)
                ]
                is_getter = is_getter | ((core == c) & (relative == (q ^ bit)))
        return lax.ppermute(held, AXES, pairs), is_getter

    cot = cotangent.reshape(slot_count, value_width)
    got_cot = lax.all_to_all(cot, "dp", split_axis=0, concat_axis=0, tiled=True)
    held, got, is_getter = [], [], [None] * PARTS
    rest = pol_weight
    for j in range(PARTS):
        held.append(rest[:, j * width : (j + 1) * width])
        if j < PARTS - 1:
            held[j], rest = lax.optimization_barrier((held[j], rest))
        part, is_getter[j] = stage(0, held[j])
        got.append(part)

    def later_stages(j):
        for number in range(1, levels):
            held[j] = jnp.where(is_getter[j], got[j], held[j])
            got[j], is_getter[j] = stage(number, held[j])

    steps = 4
    feature_step = block // steps
    at = jnp.stack([t, (1 - core) * (steps // 2)]).astype(jnp.int32)

    def at_step(f, at):
        return lax.rem(f + at[1], steps)

    rows_spec = pl.BlockSpec((group_rows, feature_step), lambda f, at: (0, at_step(f, at)))
    rows_scratch = pltpu.VMEM((group_rows, feature_step), BF16)
    got[0], tokens, pol_gain = lax.optimization_barrier((got[0], tokens, pol_gain))
    later_stages(0)
    given_rows, kept_rows = pl.pallas_call(
        functools.partial(split_kernel, tensor_count, steps),
        grid_spec=pltpu.PrefetchScalarGridSpec(
            num_scalar_prefetch=1,
            grid=(steps,),
            in_specs=[
                rows_spec,
                pl.BlockSpec(
                    (1, feature_step), lambda f, at: (0, at[0] * steps + at_step(f, at))
                ),
            ],
            out_specs=[
                pl.BlockSpec(
                    (group_rows, feature_step), lambda f, at: (0, jnp.minimum(f, steps // 2 - 1))
                ),
                pl.BlockSpec(
                    (group_rows, feature_step), lambda f, at: (0, jnp.maximum(f - steps // 2, 0))
                ),
            ],
            scratch_shapes=[rows_scratch],
        ),
        out_shape=[jax.ShapeDtypeStruct((group_rows, shard), BF16)] * 2,
        compiler_params=pltpu.CompilerParams(vmem_limit_bytes=56 * 2**20),
        cost_estimate=pl.CostEstimate(
            flops=group_rows * block, bytes_accessed=4 * 2**20, transcendentals=0
        ),
        name="split",
    )(at, tokens, pol_gain.reshape(1, model_width))
    got_rows = swapped(given_rows, dp_count)

    got[1:], tokens = lax.optimization_barrier((got[1:], tokens))
    for j in range(1, PARTS):
        later_stages(j)
    ref_shape = (tensor_count // 2, own_rows + POWER_ROWS, value_width)
    ref_kept, ref_sent = pl.pallas_call(
        functools.partial(reference_kernel, tensor_count, steps),
        grid_spec=pltpu.PrefetchScalarGridSpec(
            num_scalar_prefetch=1,
            grid=(steps,),
            in_specs=[
                rows_spec,
                pl.BlockSpec((1, feature_step), lambda f, at: (0, at_step(f, at))),
                pl.BlockSpec((feature_step, value_width), lambda f, at: (at_step(f, at), 0)),
            ],
            out_specs=[pl.BlockSpec(ref_shape, lambda f, at: (0, 0, 0))] * 2,
            scratch_shapes=[
                rows_scratch,
                pltpu.VMEM((group_rows, value_width), F32),
                pltpu.VMEM((group_rows, 1), F32),
            ],
        ),
        out_shape=[jax.ShapeDtypeStruct(ref_shape, BF16)] * 2,
        compiler_params=pltpu.CompilerParams(vmem_limit_bytes=56 * 2**20),
        cost_estimate=pl.CostEstimate(
            flops=2 * group_rows * block * value_width,
            bytes_accessed=5 * 2**20,
            transcendentals=0,
        ),
        name="reference",
    )(at, tokens, ref_gain.reshape(1, block), ref_weight)
    ref_got = crossed(ref_sent, tensor_count, 1)
    for level in range(1, levels):
        ref_sum = (ref_kept[:, :own_rows].astype(F32) + ref_got[:, :own_rows].astype(F32)).astype(BF16)
        ref_all = jnp.concatenate([ref_sum, ref_kept[:, own_rows:], ref_got[:, own_rows:]], axis=1)
        half_count = ref_all.shape[0] // 2
        ref_kept = ref_all[:half_count]
        ref_got = crossed(ref_all[half_count:], tensor_count, 1 << level)

    chunk_at = jnp.stack([place ^ s ^ turned(t, levels) for s in range(places)]).astype(jnp.int32)

    values, slopes = [], []
    for j in range(PARTS):
        weight = jnp.where(is_getter[j], got[j], held[j])
        value_given = dot(got_rows, weight).astype(BF16)
        if j == 0:
            smem = pl.BlockSpec(memory_space=pltpu.SMEM)
            vmem = pl.BlockSpec(memory_space=pltpu.VMEM)
            fixed, pull, row_scale, row_at = pl.pallas_call(
                functools.partial(row_kernel, span_rows, model_width),
                in_specs=[smem] * 3 + [vmem] * 4,
                out_specs=[vmem] * 4,
                out_shape=[
                    jax.ShapeDtypeStruct((own_rows, value_width), F32),
                    jax.ShapeDtypeStruct((own_rows, 128), F32),
                    jax.ShapeDtypeStruct((own_rows, 128), F32),
                    jax.ShapeDtypeStruct((own_rows, slot_count), BF16),
                ],
                compiler_params=pltpu.CompilerParams(vmem_limit_bytes=16 * 2**20),
                cost_estimate=pl.CostEstimate(
                    flops=2 * own_rows * slot_count * value_width,
                    bytes_accessed=2**21,
                    transcendentals=0,
                ),
                name="rows",
            )(
                lengths.reshape(-1),
                bins.reshape(-1),
                advantage.reshape(-1),
                logprob_gap.reshape(1, own_rows),
                got_cot,
                ref_kept[0],
                ref_got[0],
            )
        value_part = dot(kept_rows, weight) + swapped(value_given, dp_count).astype(F32)
        total = value_part
        for level in range(levels):
            rows = total.shape[0] // 2
            sent = total[rows:].astype(BF16)
            total = total[:rows] + crossed(sent, tensor_count, 1 << level).astype(F32)
        values.append(total * row_scale[:, :1])

        cols = slice(j * width, (j + 1) * width)
        slope = (fixed[:, cols] + pull[:, :1] * total).astype(BF16)
        for level in reversed(range(levels)):
            slope = jnp.concatenate([slope, crossed(slope, tensor_count, 1 << level)], axis=0)
        slopes.append(slope)

    sent = dot_rows(row_at, jnp.concatenate(values, axis=1).astype(BF16)).astype(BF16)

    grad_own, grad_got = [], []
    for j in range(PARTS):
        slopes_got = swapped(slopes[j], dp_count)
        if j > 0:
            slopes_got, grad_own[j - 1] = lax.optimization_barrier((slopes_got, grad_own[j - 1]))
        chunks = pl.pallas_call(
            functools.partial(grad_kernel, places, factor),
            grid_spec=pltpu.PrefetchScalarGridSpec(
                num_scalar_prefetch=1,
                grid=(1,),
                in_specs=[
                    pl.BlockSpec((group_rows, shard), lambda i, at: (0, 0)),
                    pl.BlockSpec((group_rows, shard), lambda i, at: (0, 0)),
                    pl.BlockSpec((group_rows, width), lambda i, at: (0, 0)),
                    pl.BlockSpec((group_rows, width), lambda i, at: (0, 0)),
                ],
                out_specs=[pl.BlockSpec((out_rows, width), lambda i, at: (0, 0))] * places,
                scratch_shapes=[pltpu.VMEM((shard, width), F32)],
            ),
            out_shape=[
                jax.ShapeDtypeStruct((out_rows, width), F32 if s == 0 else BF16)
                for s in range(places)
            ],
            compiler_params=pltpu.CompilerParams(vmem_limit_bytes=32 * 2**20),
            cost_estimate=pl.CostEstimate(
                flops=4 * group_rows * shard * width,
                bytes_accessed=4 * 2**20,
                transcendentals=0,
            ),
            name="gradient",
        )(chunk_at, kept_rows, got_rows, slopes[j], slopes_got)
        grad_own.append(chunks[0])
        grad_got.append([])
        for s in range(1, places):
            pairs = [
                (p * cores + c, (p ^ s) * cores + c) for p in range(places) for c in range(cores)
            ]
            grad_got[j].append(lax.ppermute(chunks[s], "dp", pairs))
    grad_got[0][-1], sent = lax.optimization_barrier((grad_got[0][-1], sent))
    policy_values = lax.all_to_all(sent, "dp", split_axis=0, concat_axis=0, tiled=True)
    grads = []
    for j in range(PARTS):
        total = (grad_own[j] + sum(x.astype(F32) for x in grad_got[j])).astype(BF16)
        pairs = [
            (flat(p, c, z), flat(z, c, p ^ turned(z, levels)))
            for p in range(places)
            for c in range(cores)
            for z in range(tensor_count)
        ]
        grads.append(lax.ppermute(total, AXES, pairs))
    grad_weight = jnp.concatenate(grads, axis=1).astype(F32)
    return (policy_values.reshape(1, 1, slot_count, value_width), grad_weight)


def solution(mesh):
    in_specs = (
        P("dp", "tensor"),
        P("tensor"),
        P("tensor", None),
        P(),
        P("dp", None),
        P("dp", "tensor", None),
        P("dp", "tensor", None),
        P("dp", "tensor", None),
        P(("dp", "tensor")),
        P("dp", "tensor", None, None),
    )
    out_specs = (P("dp", "tensor", None, None), P(("dp", "tensor"), None))
    return jax.shard_map(
        on_device, mesh=mesh, in_specs=in_specs, out_specs=out_specs, check_vma=False
    )
```

```python
import functools
import math

import jax
import jax.numpy as jnp
from jax import lax
from jax.experimental import pallas as pl
from jax.experimental.pallas import tpu as pltpu
from jax.sharding import PartitionSpec as P

EPS = 1e-06
BETA = 1.0
AXES = ("dp", "tensor")
BF16 = jnp.bfloat16
F32 = jnp.float32
POWER_ROWS = 16
PARTS = 2


def dot(a, b):
    return jnp.dot(a, b, preferred_element_type=F32)


def dot_rows(a, b):
    return lax.dot_general(a, b, (((0,), (0,)), ((), ())), preferred_element_type=F32)


def swapped(array, dp_count):
    return lax.ppermute(array, "dp", [(i, i ^ 1) for i in range(dp_count)])


def turned(index, levels):
    return sum(((index >> i) & 1) << (levels - 1 - i) for i in range(levels))


def crossed(array, count, step):
    return lax.ppermute(array, "tensor", [(i, i ^ step) for i in range(count)])


def chunk_start(count, at, own, i):
    source = jnp.bitwise_xor(at[0], turned(i, count.bit_length() - 1))
    return pl.multiple_of(source * own, own)


def split_kernel(count, steps, at, x_ref, gain_ref, given_ref, kept_ref):
    f = pl.program_id(0)
    own = x_ref.shape[0] // count

    def fill(out_ref):
        for i in range(count):
            rows = x_ref[pl.ds(chunk_start(count, at, own, i), own), :].astype(F32)
            out_ref[i * own : (i + 1) * own, :] = (rows * gain_ref[...]).astype(BF16)

    @pl.when(f < steps // 2)
    def _():
        fill(given_ref)

    @pl.when(f >= steps // 2)
    def _():
        fill(kept_ref)


def reference_kernel(
    count, steps, at, x_ref, gain_ref, weight_ref, kept_ref, sent_ref, rows_ref, total, square
):
    f = pl.program_id(0)
    own = x_ref.shape[0] // count

    @pl.when(f == 0)
    def _():
        square[...] = jnp.zeros_like(square)

    for i in range(count):
        wide = x_ref[pl.ds(chunk_start(count, at, own, i), own), :].astype(F32)
        rows_ref[i * own : (i + 1) * own, :] = (wide * gain_ref[...]).astype(BF16)
        square[i * own : (i + 1) * own, :] += jnp.sum(wide * wide, axis=1, keepdims=True)
    part = dot(rows_ref[...], weight_ref[...])

    @pl.when(f == 0)
    def _():
        total[...] = part

    @pl.when(f > 0)
    def _():
        total[...] += part

    @pl.when(f == steps - 1)
    def _():
        for i in range(count):
            out = (kept_ref, sent_ref)[i // (count // 2)].at[i % (count // 2)]
            out[:own, :] = total[i * own : (i + 1) * own, :].astype(BF16)
            power = jnp.broadcast_to(square[i * own : (i + 1) * own, :], (own, 128)).T
            high = power[: POWER_ROWS // 2].astype(BF16).astype(F32)
            low = power[: POWER_ROWS // 2] - high
            out[own:, :] = jnp.zeros((POWER_ROWS, out.shape[1]), BF16)
            out[own:, :own] = jnp.concatenate([high, low], axis=0).astype(BF16)


def row_kernel(
    span, model_width, lengths, bins, advantage, gap_ref, cot_ref, kept_ref, got_ref, *refs
):
    fixed_ref, pull_ref, scale_ref, row_at_ref = refs
    own = pull_ref.shape[0]
    slots = row_at_ref.shape[1]
    row = lax.broadcasted_iota(jnp.int32, (own, slots), 0)
    slot = lax.broadcasted_iota(jnp.int32, (own, slots), 1)
    chosen = jnp.zeros((own, slots), jnp.bool_)
    size = jnp.ones((own, 128), F32)
    weight = jnp.zeros((own, 128), F32)
    start = jnp.int32(0)
    for s in range(lengths.shape[0]):
        end = start + lengths[s]
        inside = (row >= start) & (row < end)
        chosen = chosen | (inside & (slot - bins[s] * span == row - start))
        size = jnp.where(inside[:, :128], lengths[s].astype(F32), size)
        weight = jnp.where(inside[:, :128], advantage[s], weight)
        start = end
    row_at = jnp.where(chosen, 1.0, 0.0).astype(BF16)
    row_at_ref[...] = row_at
    importance = jnp.minimum(jnp.exp(jnp.broadcast_to(gap_ref[...], (128, own)).T), 2.0)
    coef_adv = (weight * importance / size).astype(BF16).astype(F32)
    coef_pull = (BETA / size).astype(BF16).astype(F32)
    total = kept_ref[...].astype(F32) + got_ref[...].astype(F32)
    square = jnp.zeros((1, own), F32)
    for power_row in range(own, total.shape[0], POWER_ROWS // 2):
        square = square + total[power_row : power_row + 1, :own]
    scale = lax.rsqrt(jnp.broadcast_to(square, (128, own)).T / model_width + EPS)
    reference = (total[:own] * scale[:, :1]).astype(BF16).astype(F32)
    upstream = dot(row_at, cot_ref[...])
    fixed_ref[...] = (coef_adv[:, :1] * upstream - coef_pull[:, :1] * reference) * scale[:, :1]
    pull_ref[...] = coef_pull * scale * scale
    scale_ref[...] = scale


def grad_kernel(places, factor, at, kept_ref, got_ref, slope_ref, slope_got_ref, *refs):
    out_refs, grad = refs[:places], refs[places]
    total = dot_rows(kept_ref[...], slope_ref[...]) + dot_rows(got_ref[...], slope_got_ref[...])
    grad[...] = total * factor
    rows = out_refs[0].shape[0]
    for s in range(places):
        chunk = grad[pl.ds(pl.multiple_of(at[s] * rows, rows), rows), :]
        out_refs[s][...] = chunk.astype(out_refs[s].dtype)


def on_device(
    tokens,
    ref_gain,
    ref_weight,
    pol_gain,
    pol_weight,
    lengths,
    bins,
    advantage,
    logprob_gap,
    cotangent,
):
    tensor_count = lax.axis_size("tensor")
    dp_count = lax.axis_size("dp")
    t = lax.axis_index("tensor")
    d = lax.axis_index("dp")
    cores = dp_count // tensor_count
    assert cores == 2
    places = dp_count // cores
    levels = places.bit_length() - 1
    assert 1 << levels == places == tensor_count
    place = d // cores
    core = d % cores
    group_rows, block = tokens.shape
    own_rows = group_rows // tensor_count
    slot_count = cotangent.shape[2]
    span_rows = slot_count // dp_count
    value_width = ref_weight.shape[1]
    model_width = pol_gain.shape[0]
    shard = pol_weight.shape[0]
    width = value_width // PARTS
    out_rows = shard // tensor_count
    factor = 1.0 / math.sqrt(dp_count * tensor_count * lengths.shape[2])
    relative = place ^ t

    def flat(p, c, z):
        return (p * cores + c) * tensor_count + z

    def stage(number, held):
        pairs, is_getter = [], jnp.zeros((), jnp.bool_)
        for c in range(cores):
            holders = [0]
            for before in range(number):
                bit = 1 << ((c + before) % levels)
                holders = holders + [q ^ bit for q in holders]
            bit = 1 << ((c + number) % levels)
            for q in holders:
                pairs += [
                    (flat(q ^ z, c, z), flat(q ^ bit ^ z, c, z)) for z in range(tensor_count)
                ]
                is_getter = is_getter | ((core == c) & (relative == (q ^ bit)))
        return lax.ppermute(held, AXES, pairs), is_getter

    def exchanged(slots):
        every = lax.all_gather(slots, "dp", axis=0)
        own = lax.dynamic_slice_in_dim(every, d * span_rows, span_rows, 1)
        return own.reshape(slot_count, value_width)

    held, got, is_getter = [], [], [None] * PARTS
    rest = pol_weight
    for j in range(PARTS):
        held.append(rest[:, j * width : (j + 1) * width])
        if j < PARTS - 1:
            held[j], rest = lax.optimization_barrier((held[j], rest))
        part, is_getter[j] = stage(0, held[j])
        got.append(part)

    def later_stages(j):
        for number in range(1, levels):
            held[j] = jnp.where(is_getter[j], got[j], held[j])
            got[j], is_getter[j] = stage(number, held[j])

    steps = 4
    feature_step = block // steps
    at = jnp.stack([t, (1 - core) * (steps // 2)]).astype(jnp.int32)

    def at_step(f, at):
        return lax.rem(f + at[1], steps)

    rows_spec = pl.BlockSpec((group_rows, feature_step), lambda f, at: (0, at_step(f, at)))
    rows_scratch = pltpu.VMEM((group_rows, feature_step), BF16)
    given_rows, kept_rows = pl.pallas_call(
        functools.partial(split_kernel, tensor_count, steps),
        grid_spec=pltpu.PrefetchScalarGridSpec(
            num_scalar_prefetch=1,
            grid=(steps,),
            in_specs=[
                rows_spec,
                pl.BlockSpec(
                    (1, feature_step), lambda f, at: (0, at[0] * steps + at_step(f, at))
                ),
            ],
            out_specs=[
                pl.BlockSpec(
                    (group_rows, feature_step), lambda f, at: (0, jnp.minimum(f, steps // 2 - 1))
                ),
                pl.BlockSpec(
                    (group_rows, feature_step), lambda f, at: (0, jnp.maximum(f - steps // 2, 0))
                ),
            ],
        ),
        out_shape=[jax.ShapeDtypeStruct((group_rows, shard), BF16)] * 2,
        compiler_params=pltpu.CompilerParams(vmem_limit_bytes=56 * 2**20),
        cost_estimate=pl.CostEstimate(
            flops=group_rows * block, bytes_accessed=4 * 2**20, transcendentals=0
        ),
        name="split",
    )(at, tokens, pol_gain.reshape(1, model_width))
    got_rows = swapped(given_rows, dp_count)

    for j in range(PARTS):
        later_stages(j)
    held[1:], tokens = lax.optimization_barrier((held[1:], tokens))
    got[0], cot = lax.optimization_barrier((got[0], cotangent.reshape(slot_count, value_width)))
    got_cot = exchanged(cot)
    ref_shape = (tensor_count // 2, own_rows + POWER_ROWS, value_width)
    ref_kept, ref_sent = pl.pallas_call(
        functools.partial(reference_kernel, tensor_count, steps),
        grid_spec=pltpu.PrefetchScalarGridSpec(
            num_scalar_prefetch=1,
            grid=(steps,),
            in_specs=[
                rows_spec,
                pl.BlockSpec((1, feature_step), lambda f, at: (0, at_step(f, at))),
                pl.BlockSpec((feature_step, value_width), lambda f, at: (at_step(f, at), 0)),
            ],
            out_specs=[pl.BlockSpec(ref_shape, lambda f, at: (0, 0, 0))] * 2,
            scratch_shapes=[
                rows_scratch,
                pltpu.VMEM((group_rows, value_width), F32),
                pltpu.VMEM((group_rows, 1), F32),
            ],
        ),
        out_shape=[jax.ShapeDtypeStruct(ref_shape, BF16)] * 2,
        compiler_params=pltpu.CompilerParams(vmem_limit_bytes=56 * 2**20),
        cost_estimate=pl.CostEstimate(
            flops=2 * group_rows * block * value_width,
            bytes_accessed=5 * 2**20,
            transcendentals=0,
        ),
        name="reference",
    )(at, tokens, ref_gain.reshape(1, block), ref_weight)
    ref_got = crossed(ref_sent, tensor_count, 1)
    for level in range(1, levels):
        ref_sum = (ref_kept[:, :own_rows].astype(F32) + ref_got[:, :own_rows].astype(F32)).astype(BF16)
        ref_all = jnp.concatenate([ref_sum, ref_kept[:, own_rows:], ref_got[:, own_rows:]], axis=1)
        half_count = ref_all.shape[0] // 2
        ref_kept = ref_all[:half_count]
        ref_got = crossed(ref_all[half_count:], tensor_count, 1 << level)

    chunk_at = jnp.stack([place ^ s ^ turned(t, levels) for s in range(places)]).astype(jnp.int32)

    values, slopes = [], []
    for j in range(PARTS):
        weight = jnp.where(is_getter[j], got[j], held[j])
        value_given = dot(got_rows, weight).astype(BF16)
        if j == 0:
            smem = pl.BlockSpec(memory_space=pltpu.SMEM)
            vmem = pl.BlockSpec(memory_space=pltpu.VMEM)
            fixed, pull, row_scale, row_at = pl.pallas_call(
                functools.partial(row_kernel, span_rows, model_width),
                in_specs=[smem] * 3 + [vmem] * 4,
                out_specs=[vmem] * 4,
                out_shape=[
                    jax.ShapeDtypeStruct((own_rows, value_width), F32),
                    jax.ShapeDtypeStruct((own_rows, 128), F32),
                    jax.ShapeDtypeStruct((own_rows, 128), F32),
                    jax.ShapeDtypeStruct((own_rows, slot_count), BF16),
                ],
                compiler_params=pltpu.CompilerParams(vmem_limit_bytes=16 * 2**20),
                cost_estimate=pl.CostEstimate(
                    flops=2 * own_rows * slot_count * value_width,
                    bytes_accessed=2**21,
                    transcendentals=0,
                ),
                name="rows",
            )(
                lengths.reshape(-1),
                bins.reshape(-1),
                advantage.reshape(-1),
                logprob_gap.reshape(1, own_rows),
                got_cot,
                ref_kept[0],
                ref_got[0],
            )
        value_part = dot(kept_rows, weight) + swapped(value_given, dp_count).astype(F32)
        total = value_part
        for level in range(levels):
            rows = total.shape[0] // 2
            sent = total[rows:].astype(BF16)
            total = total[:rows] + crossed(sent, tensor_count, 1 << level).astype(F32)
        values.append(total * row_scale[:, :1])

        cols = slice(j * width, (j + 1) * width)
        slope = (fixed[:, cols] + pull[:, :1] * total).astype(BF16)
        for level in reversed(range(levels)):
            slope = jnp.concatenate([slope, crossed(slope, tensor_count, 1 << level)], axis=0)
        slopes.append(slope)

    sent = dot_rows(row_at, jnp.concatenate(values, axis=1).astype(BF16)).astype(BF16)

    grad_own, grad_got = [], []
    for j in range(PARTS):
        slopes_got = swapped(slopes[j], dp_count)
        chunks = pl.pallas_call(
            functools.partial(grad_kernel, places, factor),
            grid_spec=pltpu.PrefetchScalarGridSpec(
                num_scalar_prefetch=1,
                grid=(1,),
                in_specs=[
                    pl.BlockSpec((group_rows, shard), lambda i, at: (0, 0)),
                    pl.BlockSpec((group_rows, shard), lambda i, at: (0, 0)),
                    pl.BlockSpec((group_rows, width), lambda i, at: (0, 0)),
                    pl.BlockSpec((group_rows, width), lambda i, at: (0, 0)),
                ],
                out_specs=[pl.BlockSpec((out_rows, width), lambda i, at: (0, 0))] * places,
                scratch_shapes=[pltpu.VMEM((shard, width), F32)],
            ),
            out_shape=[
                jax.ShapeDtypeStruct((out_rows, width), F32 if s == 0 else BF16)
                for s in range(places)
            ],
            compiler_params=pltpu.CompilerParams(vmem_limit_bytes=32 * 2**20),
            cost_estimate=pl.CostEstimate(
                flops=4 * group_rows * shard * width,
                bytes_accessed=4 * 2**20,
                transcendentals=0,
            ),
            name="gradient",
        )(chunk_at, kept_rows, got_rows, slopes[j], slopes_got)
        grad_own.append(chunks[0])
        grad_got.append([])
        for s in range(1, places):
            pairs = [
                (p * cores + c, (p ^ s) * cores + c) for p in range(places) for c in range(cores)
            ]
            grad_got[j].append(lax.ppermute(chunks[s], "dp", pairs))
    policy_values = exchanged(sent)
    grads = []
    for j in range(PARTS):
        total = (grad_own[j] + sum(x.astype(F32) for x in grad_got[j])).astype(BF16)
        pairs = [
            (flat(p, c, z), flat(z, c, p ^ turned(z, levels)))
            for p in range(places)
            for c in range(cores)
            for z in range(tensor_count)
        ]
        grads.append(lax.ppermute(total, AXES, pairs))
    grad_weight = jnp.concatenate(grads, axis=1).astype(F32)
    return (policy_values.reshape(1, 1, slot_count, value_width), grad_weight)


def solution(mesh):
    in_specs = (
        P("dp", "tensor"),
        P("tensor"),
        P("tensor", None),
        P(),
        P("dp", None),
        P("dp", "tensor", None),
        P("dp", "tensor", None),
        P("dp", "tensor", None),
        P(("dp", "tensor")),
        P("dp", "tensor", None, None),
    )
    out_specs = (P("dp", "tensor", None, None), P(("dp", "tensor"), None))
    return jax.shard_map(
        on_device, mesh=mesh, in_specs=in_specs, out_specs=out_specs, check_vma=False
    )
```

```python
import functools
import math

import jax
import jax.numpy as jnp
from jax import lax
from jax.experimental import pallas as pl
from jax.experimental.pallas import tpu as pltpu
from jax.sharding import PartitionSpec as P

EPS = 1e-06
BETA = 1.0
AXES = ("dp", "tensor")
BF16 = jnp.bfloat16
F32 = jnp.float32
POWER_ROWS = 16
PARTS = 2


def dot(a, b):
    return jnp.dot(a, b, preferred_element_type=F32)


def dot_rows(a, b):
    return lax.dot_general(a, b, (((0,), (0,)), ((), ())), preferred_element_type=F32)


def swapped(array, dp_count):
    return lax.ppermute(array, "dp", [(i, i ^ 1) for i in range(dp_count)])


def turned(index, levels):
    return sum(((index >> i) & 1) << (levels - 1 - i) for i in range(levels))


def crossed(array, count, step):
    return lax.ppermute(array, "tensor", [(i, i ^ step) for i in range(count)])


def prepare_kernel(
    count, steps, at, x_ref, gain_ref, weight_ref, pol_ref, given_ref, kept_ref, *refs
):
    sent_refs, (rows_ref, total, square) = refs[:2], refs[2:]
    f = pl.program_id(0)
    own = x_ref.shape[0] // count
    levels = count.bit_length() - 1
    for i in range(count):
        source = jnp.bitwise_xor(at[0], turned(i, levels))
        rows_ref[i * own : (i + 1) * own, :] = x_ref[pl.ds(pl.multiple_of(source * own, own), own), :]
    wide = rows_ref[...].astype(F32)
    gained = (wide * pol_ref[...]).astype(BF16)

    @pl.when(f < steps // 2)
    def _():
        given_ref[...] = gained

    @pl.when(f >= steps // 2)
    def _():
        kept_ref[...] = gained

    part = dot((wide * gain_ref[...]).astype(BF16), weight_ref[...])
    squares = jnp.sum(wide * wide, axis=1, keepdims=True)

    @pl.when(f == 0)
    def _():
        total[...] = part
        square[...] = squares

    @pl.when(f > 0)
    def _():
        total[...] += part
        square[...] += squares

    @pl.when(f == steps - 1)
    def _():
        for i in range(count):
            sent = sent_refs[i // (count // 2)].at[i % (count // 2)]
            sent[:own, :] = total[i * own : (i + 1) * own, :].astype(BF16)
            power = jnp.broadcast_to(square[i * own : (i + 1) * own, :], (own, 128)).T
            high = power[: POWER_ROWS // 2].astype(BF16).astype(F32)
            low = power[: POWER_ROWS // 2] - high
            sent[own:, :] = jnp.zeros((POWER_ROWS, sent.shape[1]), BF16)
            sent[own:, :own] = jnp.concatenate([high, low], axis=0).astype(BF16)


def row_kernel(
    span, model_width, lengths, bins, advantage, gap_ref, cot_ref, kept_ref, got_ref, *refs
):
    fixed_ref, pull_ref, scale_ref, row_at_ref = refs
    own = pull_ref.shape[0]
    slots = row_at_ref.shape[1]
    row = lax.broadcasted_iota(jnp.int32, (own, slots), 0)
    slot = lax.broadcasted_iota(jnp.int32, (own, slots), 1)
    chosen = jnp.zeros((own, slots), jnp.bool_)
    size = jnp.ones((own, 128), F32)
    weight = jnp.zeros((own, 128), F32)
    start = jnp.int32(0)
    for s in range(lengths.shape[0]):
        end = start + lengths[s]
        inside = (row >= start) & (row < end)
        chosen = chosen | (inside & (slot - bins[s] * span == row - start))
        size = jnp.where(inside[:, :128], lengths[s].astype(F32), size)
        weight = jnp.where(inside[:, :128], advantage[s], weight)
        start = end
    row_at = jnp.where(chosen, 1.0, 0.0).astype(BF16)
    row_at_ref[...] = row_at
    importance = jnp.minimum(jnp.exp(jnp.broadcast_to(gap_ref[...], (128, own)).T), 2.0)
    coef_adv = (weight * importance / size).astype(BF16).astype(F32)
    coef_pull = (BETA / size).astype(BF16).astype(F32)
    total = kept_ref[...].astype(F32) + got_ref[...].astype(F32)
    square = jnp.zeros((1, own), F32)
    for power_row in range(own, total.shape[0], POWER_ROWS // 2):
        square = square + total[power_row : power_row + 1, :own]
    scale = lax.rsqrt(jnp.broadcast_to(square, (128, own)).T / model_width + EPS)
    reference = (total[:own] * scale[:, :1]).astype(BF16).astype(F32)
    upstream = dot(row_at, cot_ref[...])
    fixed_ref[...] = (coef_adv[:, :1] * upstream - coef_pull[:, :1] * reference) * scale[:, :1]
    pull_ref[...] = coef_pull * scale * scale
    scale_ref[...] = scale


def grad_kernel(factor, at, kept_ref, got_ref, slope_ref, slope_got_ref, *refs):
    *out_refs, grad = refs
    total = dot_rows(kept_ref[...], slope_ref[...]) + dot_rows(got_ref[...], slope_got_ref[...])
    grad[...] = total * factor
    rows = grad.shape[0] // at.shape[0]
    count = at.shape[0] // 2
    for s in range(2 * count):
        chunk = grad[pl.ds(pl.multiple_of(at[s] * rows, rows), rows), :]
        out_ref = out_refs[s // count]
        place = s % count
        out_ref[place * rows : (place + 1) * rows, :] = chunk.astype(out_ref.dtype)


def on_device(
    tokens,
    ref_gain,
    ref_weight,
    pol_gain,
    pol_weight,
    lengths,
    bins,
    advantage,
    logprob_gap,
    cotangent,
):
    tensor_count = lax.axis_size("tensor")
    dp_count = lax.axis_size("dp")
    t = lax.axis_index("tensor")
    d = lax.axis_index("dp")
    cores = dp_count // tensor_count
    assert cores == 2
    places = dp_count // cores
    levels = places.bit_length() - 1
    assert 1 << levels == places == tensor_count
    place = d // cores
    core = d % cores
    group_rows, block = tokens.shape
    own_rows = group_rows // tensor_count
    slot_count = cotangent.shape[2]
    span_rows = slot_count // dp_count
    value_width = ref_weight.shape[1]
    model_width = pol_gain.shape[0]
    shard = pol_weight.shape[0]
    width = value_width // PARTS
    factor = 1.0 / math.sqrt(dp_count * tensor_count * lengths.shape[2])
    relative = place ^ t

    def flat(p, c, z):
        return (p * cores + c) * tensor_count + z

    def stage(number, held):
        pairs, is_getter = [], jnp.zeros((), jnp.bool_)
        for c in range(cores):
            holders = [0]
            for before in range(number):
                bit = 1 << ((c + before) % levels)
                holders = holders + [q ^ bit for q in holders]
            bit = 1 << ((c + number) % levels)
            for q in holders:
                pairs += [
                    (flat(q ^ z, c, z), flat(q ^ bit ^ z, c, z)) for z in range(tensor_count)
                ]
                is_getter = is_getter | ((core == c) & (relative == (q ^ bit)))
        return lax.ppermute(held, AXES, pairs), is_getter

    held, got, is_getter = [], [], [None] * PARTS
    rest = pol_weight
    for j in range(PARTS):
        held.append(rest[:, j * width : (j + 1) * width])
        if j < PARTS - 1:
            held[j], rest = lax.optimization_barrier((held[j], rest))
        part, is_getter[j] = stage(0, held[j])
        got.append(part)

    steps = 4
    feature_step = block // steps
    at = jnp.stack([t, (1 - core) * (steps // 2)]).astype(jnp.int32)
    ref_shape = (tensor_count // 2, own_rows + POWER_ROWS, value_width)

    def at_step(f, at):
        return lax.rem(f + at[1], steps)

    prepared = pl.pallas_call(
        functools.partial(prepare_kernel, tensor_count, steps),
        grid_spec=pltpu.PrefetchScalarGridSpec(
            num_scalar_prefetch=1,
            grid=(steps,),
            in_specs=[
                pl.BlockSpec((group_rows, feature_step), lambda f, at: (0, at_step(f, at))),
                pl.BlockSpec((1, feature_step), lambda f, at: (0, at_step(f, at))),
                pl.BlockSpec((feature_step, value_width), lambda f, at: (at_step(f, at), 0)),
                pl.BlockSpec(
                    (1, feature_step), lambda f, at: (0, at[0] * steps + at_step(f, at))
                ),
            ],
            out_specs=[
                pl.BlockSpec(
                    (group_rows, feature_step), lambda f, at: (0, jnp.minimum(f, steps // 2 - 1))
                ),
                pl.BlockSpec(
                    (group_rows, feature_step), lambda f, at: (0, jnp.maximum(f - steps // 2, 0))
                ),
            ]
            + [pl.BlockSpec(ref_shape, lambda f, at: (0, 0, 0))] * 2,
            scratch_shapes=[
                pltpu.VMEM((group_rows, feature_step), BF16),
                pltpu.VMEM((group_rows, value_width), F32),
                pltpu.VMEM((group_rows, 1), F32),
            ],
        ),
        out_shape=[jax.ShapeDtypeStruct((group_rows, shard), BF16)] * 2
        + [jax.ShapeDtypeStruct(ref_shape, BF16)] * 2,
        compiler_params=pltpu.CompilerParams(vmem_limit_bytes=56 * 2**20),
        cost_estimate=pl.CostEstimate(
            flops=2 * group_rows * block * value_width,
            bytes_accessed=8 * 2**20,
            transcendentals=0,
        ),
        name="prepare",
    )(at, tokens, ref_gain.reshape(1, block), ref_weight, pol_gain.reshape(1, model_width))
    given_rows, kept_rows, ref_kept, ref_sent = prepared
    ref_got = crossed(ref_sent, tensor_count, 1)
    got_rows = swapped(given_rows, dp_count)

    cot = cotangent.reshape(slot_count, value_width)
    got[-1], cot, kept_rows, ref_got = lax.optimization_barrier((got[-1], cot, kept_rows, ref_got))
    for j in range(PARTS):
        for number in range(1, levels):
            held[j] = jnp.where(is_getter[j], got[j], held[j])
            got[j], is_getter[j] = stage(number, held[j])
    for level in range(1, levels):
        ref_sum = ref_kept[:, :own_rows].astype(F32) + ref_got[:, :own_rows].astype(F32)
        ref_all = jnp.concatenate(
            [ref_sum.astype(BF16), ref_kept[:, own_rows:], ref_got[:, own_rows:]], axis=1
        )
        half_count = ref_all.shape[0] // 2
        ref_kept = ref_all[:half_count]
        ref_got = crossed(ref_all[half_count:], tensor_count, 1 << level)
    got_cot = lax.all_to_all(cot, "dp", split_axis=0, concat_axis=0, tiled=True)

    def plane_bit(level):
        return jnp.where(core == 0, 1 << (level % levels), 1 << ((1 + level) % levels))

    chunk_at = []
    for i in range(places):
        away = sum(plane_bit(level) * ((i >> (levels - 1 - level)) & 1) for level in range(levels))
        chunk_at.append(place ^ away ^ turned(t, levels))
    chunk_at = jnp.stack(chunk_at).astype(jnp.int32)

    values, slopes = [], []
    for j in range(PARTS):
        if j == 0:
            got[0], got_cot = lax.optimization_barrier((got[0], got_cot))
        weight = jnp.where(is_getter[j], got[j], held[j])
        value_given = dot(got_rows, weight).astype(BF16)
        if j == 0:
            smem = pl.BlockSpec(memory_space=pltpu.SMEM)
            vmem = pl.BlockSpec(memory_space=pltpu.VMEM)
            fixed, pull, row_scale, row_at = pl.pallas_call(
                functools.partial(row_kernel, span_rows, model_width),
                in_specs=[smem] * 3 + [vmem] * 4,
                out_specs=[vmem] * 4,
                out_shape=[
                    jax.ShapeDtypeStruct((own_rows, value_width), F32),
                    jax.ShapeDtypeStruct((own_rows, 128), F32),
                    jax.ShapeDtypeStruct((own_rows, 128), F32),
                    jax.ShapeDtypeStruct((own_rows, slot_count), BF16),
                ],
                compiler_params=pltpu.CompilerParams(vmem_limit_bytes=16 * 2**20),
                cost_estimate=pl.CostEstimate(
                    flops=2 * own_rows * slot_count * value_width,
                    bytes_accessed=2**21,
                    transcendentals=0,
                ),
                name="rows",
            )(
                lengths.reshape(-1),
                bins.reshape(-1),
                advantage.reshape(-1),
                logprob_gap.reshape(1, own_rows),
                got_cot,
                ref_kept[0],
                ref_got[0],
            )
        value_part = dot(kept_rows, weight) + swapped(value_given, dp_count).astype(F32)
        total = value_part
        for level in range(levels):
            rows = total.shape[0] // 2
            sent = total[rows:].astype(BF16)
            total = total[:rows] + crossed(sent, tensor_count, 1 << level).astype(F32)
        values.append(total * row_scale[:, :1])

        cols = slice(j * width, (j + 1) * width)
        slope = (fixed[:, cols] + pull[:, :1] * total).astype(BF16)
        for level in reversed(range(levels)):
            slope = jnp.concatenate([slope, crossed(slope, tensor_count, 1 << level)], axis=0)
        slopes.append(slope)

    sent = dot_rows(row_at, jnp.concatenate(values, axis=1).astype(BF16)).astype(BF16)

    grad_kept, grad_sent = [], []
    for j in range(PARTS):
        slopes_got = swapped(slopes[j], dp_count)
        chunks = pl.pallas_call(
            functools.partial(grad_kernel, factor),
            grid_spec=pltpu.PrefetchScalarGridSpec(
                num_scalar_prefetch=1,
                grid=(1,),
                in_specs=[
                    pl.BlockSpec((group_rows, shard), lambda i, at: (0, 0)),
                    pl.BlockSpec((group_rows, shard), lambda i, at: (0, 0)),
                    pl.BlockSpec((group_rows, width), lambda i, at: (0, 0)),
                    pl.BlockSpec((group_rows, width), lambda i, at: (0, 0)),
                ],
                out_specs=[pl.BlockSpec((shard // 2, width), lambda i, at: (0, 0))] * 2,
                scratch_shapes=[pltpu.VMEM((shard, width), F32)],
            ),
            out_shape=[
                jax.ShapeDtypeStruct((shard // 2, width), F32),
                jax.ShapeDtypeStruct((shard // 2, width), BF16),
            ],
            compiler_params=pltpu.CompilerParams(vmem_limit_bytes=32 * 2**20),
            cost_estimate=pl.CostEstimate(
                flops=4 * group_rows * shard * width,
                bytes_accessed=4 * 2**20,
                transcendentals=0,
            ),
            name="gradient",
        )(chunk_at, kept_rows, got_rows, slopes[j], slopes_got)
        grad_kept.append(chunks[0])
        grad_sent.append(chunks[1])
    *grad_kept, sent = lax.optimization_barrier((*grad_kept, sent))
    policy_values = lax.all_to_all(sent, "dp", split_axis=0, concat_axis=0, tiled=True)
    grads = []
    for j in range(PARTS):
        total, given = grad_kept[j], grad_sent[j]
        for level in range(levels):
            pairs = [
                (p * cores + c, (p ^ (1 << ((c + level) % levels))) * cores + c)
                for p in range(places)
                for c in range(cores)
            ]
            total = total + lax.ppermute(given, "dp", pairs).astype(F32)
            half_rows = total.shape[0] // 2
            if level < levels - 1:
                total, given = total[:half_rows], total[half_rows:].astype(BF16)
        total = total.astype(BF16)
        pairs = [
            (flat(p, c, z), flat(z, c, p ^ turned(z, levels)))
            for p in range(places)
            for c in range(cores)
            for z in range(tensor_count)
        ]
        grads.append(lax.ppermute(total, AXES, pairs))
    grad_weight = jnp.concatenate(grads, axis=1).astype(F32)
    return (policy_values.reshape(1, 1, slot_count, value_width), grad_weight)


def solution(mesh):
    in_specs = (
        P("dp", "tensor"),
        P("tensor"),
        P("tensor", None),
        P(),
        P("dp", None),
        P("dp", "tensor", None),
        P("dp", "tensor", None),
        P("dp", "tensor", None),
        P(("dp", "tensor")),
        P("dp", "tensor", None, None),
    )
    out_specs = (P("dp", "tensor", None, None), P(("dp", "tensor"), None))
    return jax.shard_map(
        on_device, mesh=mesh, in_specs=in_specs, out_specs=out_specs, check_vma=False
    )
```

```python
import functools
import math

import jax
import jax.numpy as jnp
from jax import lax
from jax.experimental import pallas as pl
from jax.experimental.pallas import tpu as pltpu
from jax.sharding import PartitionSpec as P

EPS = 1e-06
BETA = 1.0
AXES = ("dp", "tensor")
BF16 = jnp.bfloat16
F32 = jnp.float32
POWER_ROWS = 16
PARTS = 2


def dot(a, b):
    return jnp.dot(a, b, preferred_element_type=F32)


def dot_rows(a, b):
    return lax.dot_general(a, b, (((0,), (0,)), ((), ())), preferred_element_type=F32)


def swapped(array, dp_count):
    return lax.ppermute(array, "dp", [(i, i ^ 1) for i in range(dp_count)])


def turned(index, levels):
    return sum(((index >> i) & 1) << (levels - 1 - i) for i in range(levels))


def crossed(array, count, step):
    return lax.ppermute(array, "tensor", [(i, i ^ step) for i in range(count)])


def prepare_kernel(
    count, steps, at, x_ref, gain_ref, weight_ref, pol_ref, given_ref, kept_ref, *refs
):
    sent_refs, (rows_ref, total, square) = refs[:2], refs[2:]
    f = pl.program_id(0)
    own = x_ref.shape[0] // count
    levels = count.bit_length() - 1
    for i in range(count):
        source = jnp.bitwise_xor(at[0], turned(i, levels))
        rows_ref[i * own : (i + 1) * own, :] = x_ref[pl.ds(pl.multiple_of(source * own, own), own), :]
    wide = rows_ref[...].astype(F32)
    gained = (wide * pol_ref[...]).astype(BF16)

    @pl.when(f < steps // 2)
    def _():
        given_ref[...] = gained

    @pl.when(f >= steps // 2)
    def _():
        kept_ref[...] = gained

    part = dot((wide * gain_ref[...]).astype(BF16), weight_ref[...])
    squares = jnp.sum(wide * wide, axis=1, keepdims=True)

    @pl.when(f == 0)
    def _():
        total[...] = part
        square[...] = squares

    @pl.when(f > 0)
    def _():
        total[...] += part
        square[...] += squares

    @pl.when(f == steps - 1)
    def _():
        for i in range(count):
            sent = sent_refs[i // (count // 2)].at[i % (count // 2)]
            sent[:own, :] = total[i * own : (i + 1) * own, :].astype(BF16)
            power = jnp.broadcast_to(square[i * own : (i + 1) * own, :], (own, 128)).T
            high = power[: POWER_ROWS // 2].astype(BF16).astype(F32)
            low = power[: POWER_ROWS // 2] - high
            sent[own:, :] = jnp.zeros((POWER_ROWS, sent.shape[1]), BF16)
            sent[own:, :own] = jnp.concatenate([high, low], axis=0).astype(BF16)


def row_kernel(
    span, model_width, lengths, bins, advantage, gap_ref, cot_ref, kept_ref, got_ref, *refs
):
    fixed_ref, pull_ref, scale_ref, row_at_ref, sent_ref = refs
    own = pull_ref.shape[0]
    slots = row_at_ref.shape[1]
    row = lax.broadcasted_iota(jnp.int32, (own, slots), 0)
    slot = lax.broadcasted_iota(jnp.int32, (own, slots), 1)
    chosen = jnp.zeros((own, slots), jnp.bool_)
    size = jnp.ones((own, 128), F32)
    weight = jnp.zeros((own, 128), F32)
    start = jnp.int32(0)
    for s in range(lengths.shape[0]):
        end = start + lengths[s]
        inside = (row >= start) & (row < end)
        chosen = chosen | (inside & (slot - bins[s] * span == row - start))
        size = jnp.where(inside[:, :128], lengths[s].astype(F32), size)
        weight = jnp.where(inside[:, :128], advantage[s], weight)
        start = end
    row_at = jnp.where(chosen, 1.0, 0.0).astype(BF16)
    row_at_ref[...] = row_at
    importance = jnp.minimum(jnp.exp(jnp.broadcast_to(gap_ref[...], (128, own)).T), 2.0)
    coef_adv = (weight * importance / size).astype(BF16).astype(F32)
    coef_pull = (BETA / size).astype(BF16).astype(F32)
    total = kept_ref[...].astype(F32) + got_ref[...].astype(F32)
    square = jnp.zeros((1, own), F32)
    for power_row in range(own, total.shape[0], POWER_ROWS // 2):
        square = square + total[power_row : power_row + 1, :own]
    scale = lax.rsqrt(jnp.broadcast_to(square, (128, own)).T / model_width + EPS)
    reference = (total[:own] * scale[:, :1]).astype(BF16).astype(F32)
    upstream = dot(row_at, cot_ref[...])
    fixed = (coef_adv[:, :1] * upstream - coef_pull[:, :1] * reference) * scale[:, :1]
    pull = coef_pull * scale * scale
    high = pull.astype(BF16).astype(F32)
    width = fixed.shape[1]
    fixed_ref[...] = fixed
    pull_ref[...] = pull
    scale_ref[...] = scale
    sent_ref[:, :width] = fixed.astype(BF16)
    lane = lax.broadcasted_iota(jnp.int32, pull.shape, 1)
    sent_ref[:, width:] = jnp.where(lane < 64, high, pull - high).astype(BF16)


def grad_kernel(factor, at, kept_ref, got_ref, slope_ref, slope_got_ref, *refs):
    *out_refs, grad = refs
    total = dot_rows(kept_ref[...], slope_ref[...]) + dot_rows(got_ref[...], slope_got_ref[...])
    grad[...] = total * factor
    rows = grad.shape[0] // at.shape[0]
    count = at.shape[0] // 2
    for s in range(2 * count):
        chunk = grad[pl.ds(pl.multiple_of(at[s] * rows, rows), rows), :]
        out_ref = out_refs[s // count]
        place = s % count
        out_ref[place * rows : (place + 1) * rows, :] = chunk.astype(out_ref.dtype)


def on_device(
    tokens,
    ref_gain,
    ref_weight,
    pol_gain,
    pol_weight,
    lengths,
    bins,
    advantage,
    logprob_gap,
    cotangent,
):
    tensor_count = lax.axis_size("tensor")
    dp_count = lax.axis_size("dp")
    t = lax.axis_index("tensor")
    d = lax.axis_index("dp")
    cores = dp_count // tensor_count
    assert cores == 2
    places = dp_count // cores
    levels = places.bit_length() - 1
    assert 1 << levels == places == tensor_count
    place = d // cores
    core = d % cores
    group_rows, block = tokens.shape
    own_rows = group_rows // tensor_count
    slot_count = cotangent.shape[2]
    span_rows = slot_count // dp_count
    value_width = ref_weight.shape[1]
    model_width = pol_gain.shape[0]
    shard = pol_weight.shape[0]
    width = value_width // PARTS
    factor = 1.0 / math.sqrt(dp_count * tensor_count * lengths.shape[2])
    relative = place ^ t

    def flat(p, c, z):
        return (p * cores + c) * tensor_count + z

    def stage(number, held):
        pairs, is_getter = [], jnp.zeros((), jnp.bool_)
        for c in range(cores):
            holders = [0]
            for before in range(number):
                bit = 1 << ((c + before) % levels)
                holders = holders + [q ^ bit for q in holders]
            bit = 1 << ((c + number) % levels)
            for q in holders:
                pairs += [
                    (flat(q ^ z, c, z), flat(q ^ bit ^ z, c, z)) for z in range(tensor_count)
                ]
                is_getter = is_getter | ((core == c) & (relative == (q ^ bit)))
        return lax.ppermute(held, AXES, pairs), is_getter

    first_got, first_getter = stage(0, pol_weight)

    steps = 4
    feature_step = block // steps
    at = jnp.stack([t, (1 - core) * (steps // 2)]).astype(jnp.int32)
    ref_shape = (tensor_count // 2, own_rows + POWER_ROWS, value_width)

    def at_step(f, at):
        return lax.rem(f + at[1], steps)

    prepared = pl.pallas_call(
        functools.partial(prepare_kernel, tensor_count, steps),
        grid_spec=pltpu.PrefetchScalarGridSpec(
            num_scalar_prefetch=1,
            grid=(steps,),
            in_specs=[
                pl.BlockSpec((group_rows, feature_step), lambda f, at: (0, at_step(f, at))),
                pl.BlockSpec((1, feature_step), lambda f, at: (0, at_step(f, at))),
                pl.BlockSpec((feature_step, value_width), lambda f, at: (at_step(f, at), 0)),
                pl.BlockSpec(
                    (1, feature_step), lambda f, at: (0, at[0] * steps + at_step(f, at))
                ),
            ],
            out_specs=[
                pl.BlockSpec(
                    (group_rows, feature_step), lambda f, at: (0, jnp.minimum(f, steps // 2 - 1))
                ),
                pl.BlockSpec(
                    (group_rows, feature_step), lambda f, at: (0, jnp.maximum(f - steps // 2, 0))
                ),
            ]
            + [pl.BlockSpec(ref_shape, lambda f, at: (0, 0, 0))] * 2,
            scratch_shapes=[
                pltpu.VMEM((group_rows, feature_step), BF16),
                pltpu.VMEM((group_rows, value_width), F32),
                pltpu.VMEM((group_rows, 1), F32),
            ],
        ),
        out_shape=[jax.ShapeDtypeStruct((group_rows, shard), BF16)] * 2
        + [jax.ShapeDtypeStruct(ref_shape, BF16)] * 2,
        compiler_params=pltpu.CompilerParams(vmem_limit_bytes=56 * 2**20),
        cost_estimate=pl.CostEstimate(
            flops=2 * group_rows * block * value_width,
            bytes_accessed=8 * 2**20,
            transcendentals=0,
        ),
        name="prepare",
    )(at, tokens, ref_gain.reshape(1, block), ref_weight, pol_gain.reshape(1, model_width))
    given_rows, kept_rows, ref_kept, ref_sent = prepared
    ref_got = crossed(ref_sent, tensor_count, 1)
    got_rows = swapped(given_rows, dp_count)

    cot = cotangent.reshape(slot_count, value_width)
    held, got, is_getter = [], [], []
    for j in range(PARTS):
        cols = slice(j * width, (j + 1) * width)
        part = jnp.where(first_getter, first_got[:, cols], pol_weight[:, cols])
        if j < PARTS - 1:
            part, first_got = lax.optimization_barrier((part, first_got))
        else:
            part, cot, kept_rows = lax.optimization_barrier((part, cot, kept_rows))
        for number in range(1, levels):
            part_got, part_getter = stage(number, part)
            if number < levels - 1:
                part = jnp.where(part_getter, part_got, part)
        held.append(part)
        got.append(part_got)
        is_getter.append(part_getter)
    for level in range(1, levels):
        ref_sum = ref_kept[:, :own_rows].astype(F32) + ref_got[:, :own_rows].astype(F32)
        ref_all = jnp.concatenate(
            [ref_sum.astype(BF16), ref_kept[:, own_rows:], ref_got[:, own_rows:]], axis=1
        )
        half_count = ref_all.shape[0] // 2
        ref_kept = ref_all[:half_count]
        ref_got = crossed(ref_all[half_count:], tensor_count, 1 << level)
    got_cot = lax.all_to_all(cot, "dp", split_axis=0, concat_axis=0, tiled=True)

    def plane_bit(level):
        return jnp.where(core == 0, 1 << (level % levels), 1 << ((1 + level) % levels))

    chunk_at = []
    for i in range(places):
        away = sum(plane_bit(level) * ((i >> (levels - 1 - level)) & 1) for level in range(levels))
        chunk_at.append(place ^ away ^ turned(t, levels))
    chunk_at = jnp.stack(chunk_at).astype(jnp.int32)

    smem = pl.BlockSpec(memory_space=pltpu.SMEM)
    vmem = pl.BlockSpec(memory_space=pltpu.VMEM)
    got[-1], got_cot = lax.optimization_barrier((got[-1], got_cot))
    fixed, pull, row_scale, row_at, terms_sent = pl.pallas_call(
        functools.partial(row_kernel, span_rows, model_width),
        in_specs=[smem] * 3 + [vmem] * 4,
        out_specs=[vmem] * 5,
        out_shape=[
            jax.ShapeDtypeStruct((own_rows, value_width), F32),
            jax.ShapeDtypeStruct((own_rows, 128), F32),
            jax.ShapeDtypeStruct((own_rows, 128), F32),
            jax.ShapeDtypeStruct((own_rows, slot_count), BF16),
            jax.ShapeDtypeStruct((own_rows, value_width + 128), BF16),
        ],
        compiler_params=pltpu.CompilerParams(vmem_limit_bytes=16 * 2**20),
        cost_estimate=pl.CostEstimate(
            flops=2 * own_rows * slot_count * value_width,
            bytes_accessed=2**21,
            transcendentals=0,
        ),
        name="rows",
    )(
        lengths.reshape(-1),
        bins.reshape(-1),
        advantage.reshape(-1),
        logprob_gap.reshape(1, own_rows),
        got_cot,
        ref_kept[0],
        ref_got[0],
    )
    far = 1 << (levels - 1)
    terms_got = crossed(terms_sent, tensor_count, far).astype(F32)
    pull_got = terms_got[:, value_width : value_width + 1] + terms_got[:, -1:]
    fixed = jnp.concatenate([fixed, terms_got[:, :value_width]], axis=0)
    pull = jnp.concatenate([pull[:, :1], pull_got], axis=0)

    values, slopes = [], []
    for j in range(PARTS):
        weight = jnp.where(is_getter[j], got[j], held[j])
        value_given = dot(got_rows, weight).astype(BF16)
        total = dot(kept_rows, weight) + swapped(value_given, dp_count).astype(F32)
        for level in range(levels - 1):
            rows = total.shape[0] // 2
            total = total[:rows] + crossed(
                total[rows:].astype(BF16), tensor_count, 1 << level
            ).astype(F32)
        other = jnp.concatenate([total[own_rows:], total[:own_rows]], axis=0).astype(BF16)
        total = total + crossed(other, tensor_count, far).astype(F32)
        values.append(total[:own_rows] * row_scale[:, :1])

        cols = slice(j * width, (j + 1) * width)
        slope = (fixed[:, cols] + pull * total).astype(BF16)
        if j < PARTS - 1:
            slope, fixed, pull = lax.optimization_barrier((slope, fixed, pull))
        for level in reversed(range(levels - 1)):
            slope = jnp.concatenate([slope, crossed(slope, tensor_count, 1 << level)], axis=0)
        slopes.append(slope)

    sent = dot_rows(row_at, jnp.concatenate(values, axis=1).astype(BF16)).astype(BF16)
    policy_values = lax.all_to_all(sent, "dp", split_axis=0, concat_axis=0, tiled=True)

    grad_kept, grad_sent = [], []
    for j in range(PARTS):
        slopes_got = swapped(slopes[j], dp_count)
        if j == PARTS - 1:
            slopes_got, policy_values = lax.optimization_barrier((slopes_got, policy_values))
        chunks = pl.pallas_call(
            functools.partial(grad_kernel, factor),
            grid_spec=pltpu.PrefetchScalarGridSpec(
                num_scalar_prefetch=1,
                grid=(1,),
                in_specs=[
                    pl.BlockSpec((group_rows, shard), lambda i, at: (0, 0)),
                    pl.BlockSpec((group_rows, shard), lambda i, at: (0, 0)),
                    pl.BlockSpec((group_rows, width), lambda i, at: (0, 0)),
                    pl.BlockSpec((group_rows, width), lambda i, at: (0, 0)),
                ],
                out_specs=[pl.BlockSpec((shard // 2, width), lambda i, at: (0, 0))] * 2,
                scratch_shapes=[pltpu.VMEM((shard, width), F32)],
            ),
            out_shape=[
                jax.ShapeDtypeStruct((shard // 2, width), F32),
                jax.ShapeDtypeStruct((shard // 2, width), BF16),
            ],
            compiler_params=pltpu.CompilerParams(vmem_limit_bytes=32 * 2**20),
            cost_estimate=pl.CostEstimate(
                flops=4 * group_rows * shard * width,
                bytes_accessed=4 * 2**20,
                transcendentals=0,
            ),
            name="gradient",
        )(chunk_at, kept_rows, got_rows, slopes[j], slopes_got)
        grad_kept.append(chunks[0])
        grad_sent.append(chunks[1])
    grads = []
    for j in range(PARTS):
        total, given = grad_kept[j], grad_sent[j]
        for level in range(levels):
            pairs = [
                (p * cores + c, (p ^ (1 << ((c + level) % levels))) * cores + c)
                for p in range(places)
                for c in range(cores)
            ]
            total = total + lax.ppermute(given, "dp", pairs).astype(F32)
            half_rows = total.shape[0] // 2
            if level < levels - 1:
                total, given = total[:half_rows], total[half_rows:].astype(BF16)
        grads.append(total.astype(BF16))
    pairs = [
        (flat(p, c, z), flat(z, c, p ^ turned(z, levels)))
        for p in range(places)
        for c in range(cores)
        for z in range(tensor_count)
    ]
    grad_weight = lax.ppermute(jnp.concatenate(grads, axis=1), AXES, pairs).astype(F32)
    return (policy_values.reshape(1, 1, slot_count, value_width), grad_weight)


def solution(mesh):
    in_specs = (
        P("dp", "tensor"),
        P("tensor"),
        P("tensor", None),
        P(),
        P("dp", None),
        P("dp", "tensor", None),
        P("dp", "tensor", None),
        P("dp", "tensor", None),
        P(("dp", "tensor")),
        P("dp", "tensor", None, None),
    )
    out_specs = (P("dp", "tensor", None, None), P(("dp", "tensor"), None))
    return jax.shard_map(
        on_device, mesh=mesh, in_specs=in_specs, out_specs=out_specs, check_vma=False
    )
```

```python
import functools
import math

import jax
import jax.numpy as jnp
from jax import lax
from jax.experimental import pallas as pl
from jax.experimental.pallas import tpu as pltpu
from jax.sharding import PartitionSpec as P

EPS = 1e-06
BETA = 1.0
AXES = ("dp", "tensor")
BF16 = jnp.bfloat16
F32 = jnp.float32
POWER_ROWS = 16
PARTS = 2


def dot(a, b):
    return jnp.dot(a, b, preferred_element_type=F32)


def dot_rows(a, b):
    return lax.dot_general(a, b, (((0,), (0,)), ((), ())), preferred_element_type=F32)


def swapped(array, dp_count):
    return lax.ppermute(array, "dp", [(i, i ^ 1) for i in range(dp_count)])


def turned(index, levels):
    return sum(((index >> i) & 1) << (levels - 1 - i) for i in range(levels))


def crossed(array, count, step):
    return lax.ppermute(array, "tensor", [(i, i ^ step) for i in range(count)])


def prepare_kernel(
    count, steps, at, x_ref, gain_ref, weight_ref, pol_ref, given_ref, kept_ref, *refs
):
    sent_refs, (rows_ref, total, square) = refs[:2], refs[2:]
    f = pl.program_id(0)
    own = x_ref.shape[0] // count
    levels = count.bit_length() - 1
    for i in range(count):
        source = jnp.bitwise_xor(at[0], turned(i, levels))
        rows_ref[i * own : (i + 1) * own, :] = x_ref[pl.ds(pl.multiple_of(source * own, own), own), :]
    wide = rows_ref[...].astype(F32)
    gained = (wide * pol_ref[...]).astype(BF16)

    @pl.when(f < steps // 2)
    def _():
        given_ref[...] = gained

    @pl.when(f >= steps // 2)
    def _():
        kept_ref[...] = gained

    part = dot((wide * gain_ref[...]).astype(BF16), weight_ref[...])
    squares = jnp.sum(wide * wide, axis=1, keepdims=True)

    @pl.when(f == 0)
    def _():
        total[...] = part
        square[...] = squares

    @pl.when(f > 0)
    def _():
        total[...] += part
        square[...] += squares

    @pl.when(f == steps - 1)
    def _():
        for i in range(count):
            sent = sent_refs[i // (count // 2)].at[i % (count // 2)]
            sent[:own, :] = total[i * own : (i + 1) * own, :].astype(BF16)
            power = jnp.broadcast_to(square[i * own : (i + 1) * own, :], (own, 128)).T
            high = power[: POWER_ROWS // 2].astype(BF16).astype(F32)
            low = power[: POWER_ROWS // 2] - high
            sent[own:, :] = jnp.zeros((POWER_ROWS, sent.shape[1]), BF16)
            sent[own:, :own] = jnp.concatenate([high, low], axis=0).astype(BF16)


def row_kernel(
    span, model_width, lengths, bins, advantage, gap_ref, cot_ref, kept_ref, got_ref, *refs
):
    fixed_ref, pull_ref, scale_ref, row_at_ref, sent_ref = refs
    own = pull_ref.shape[0]
    slots = row_at_ref.shape[1]
    row = lax.broadcasted_iota(jnp.int32, (own, slots), 0)
    slot = lax.broadcasted_iota(jnp.int32, (own, slots), 1)
    chosen = jnp.zeros((own, slots), jnp.bool_)
    size = jnp.ones((own, 128), F32)
    weight = jnp.zeros((own, 128), F32)
    start = jnp.int32(0)
    for s in range(lengths.shape[0]):
        end = start + lengths[s]
        inside = (row >= start) & (row < end)
        chosen = chosen | (inside & (slot - bins[s] * span == row - start))
        size = jnp.where(inside[:, :128], lengths[s].astype(F32), size)
        weight = jnp.where(inside[:, :128], advantage[s], weight)
        start = end
    row_at = jnp.where(chosen, 1.0, 0.0).astype(BF16)
    row_at_ref[...] = row_at
    importance = jnp.minimum(jnp.exp(jnp.broadcast_to(gap_ref[...], (128, own)).T), 2.0)
    coef_adv = (weight * importance / size).astype(BF16).astype(F32)
    coef_pull = (BETA / size).astype(BF16).astype(F32)
    total = kept_ref[...].astype(F32) + got_ref[...].astype(F32)
    square = jnp.zeros((1, own), F32)
    for power_row in range(own, total.shape[0], POWER_ROWS // 2):
        square = square + total[power_row : power_row + 1, :own]
    scale = lax.rsqrt(jnp.broadcast_to(square, (128, own)).T / model_width + EPS)
    reference = (total[:own] * scale[:, :1]).astype(BF16).astype(F32)
    upstream = dot(row_at, cot_ref[...])
    fixed = (coef_adv[:, :1] * upstream - coef_pull[:, :1] * reference) * scale[:, :1]
    pull = coef_pull * scale * scale
    high = pull.astype(BF16).astype(F32)
    width = fixed.shape[1]
    fixed_ref[...] = fixed
    pull_ref[...] = pull
    scale_ref[...] = scale
    sent_ref[:, :width] = fixed.astype(BF16)
    lane = lax.broadcasted_iota(jnp.int32, pull.shape, 1)
    sent_ref[:, width:] = jnp.where(lane < 64, high, pull - high).astype(BF16)


def grad_kernel(factor, at, kept_ref, got_ref, slope_ref, slope_got_ref, *refs):
    *out_refs, grad = refs
    total = dot_rows(kept_ref[...], slope_ref[...]) + dot_rows(got_ref[...], slope_got_ref[...])
    grad[...] = total * factor
    rows = grad.shape[0] // at.shape[0]
    count = at.shape[0] // 2
    for s in range(2 * count):
        chunk = grad[pl.ds(pl.multiple_of(at[s] * rows, rows), rows), :]
        out_ref = out_refs[s // count]
        place = s % count
        out_ref[place * rows : (place + 1) * rows, :] = chunk.astype(out_ref.dtype)


def on_device(
    tokens,
    ref_gain,
    ref_weight,
    pol_gain,
    pol_weight,
    lengths,
    bins,
    advantage,
    logprob_gap,
    cotangent,
):
    tensor_count = lax.axis_size("tensor")
    dp_count = lax.axis_size("dp")
    t = lax.axis_index("tensor")
    d = lax.axis_index("dp")
    cores = dp_count // tensor_count
    assert cores == 2
    places = dp_count // cores
    levels = places.bit_length() - 1
    assert 1 << levels == places == tensor_count
    place = d // cores
    core = d % cores
    group_rows, block = tokens.shape
    own_rows = group_rows // tensor_count
    slot_count = cotangent.shape[2]
    span_rows = slot_count // dp_count
    value_width = ref_weight.shape[1]
    model_width = pol_gain.shape[0]
    shard = pol_weight.shape[0]
    width = value_width // PARTS
    factor = 1.0 / math.sqrt(dp_count * tensor_count * lengths.shape[2])
    relative = place ^ t

    def flat(p, c, z):
        return (p * cores + c) * tensor_count + z

    def stage(number, held):
        pairs, is_getter = [], jnp.zeros((), jnp.bool_)
        for c in range(cores):
            holders = [0]
            for before in range(number):
                bit = 1 << ((c + before) % levels)
                holders = holders + [q ^ bit for q in holders]
            bit = 1 << ((c + number) % levels)
            for q in holders:
                pairs += [
                    (flat(q ^ z, c, z), flat(q ^ bit ^ z, c, z)) for z in range(tensor_count)
                ]
                is_getter = is_getter | ((core == c) & (relative == (q ^ bit)))
        return lax.ppermute(held, AXES, pairs), is_getter

    held, got, is_getter = [], [], []
    rest = pol_weight
    for j in range(PARTS):
        part = rest[:, j * width : (j + 1) * width]
        if j < PARTS - 1:
            part, rest = lax.optimization_barrier((part, rest))
        part_got, part_getter = stage(0, part)
        held.append(part)
        got.append(part_got)
        is_getter.append(part_getter)

    steps = 4
    feature_step = block // steps
    at = jnp.stack([t, (1 - core) * (steps // 2)]).astype(jnp.int32)
    ref_shape = (tensor_count // 2, own_rows + POWER_ROWS, value_width)

    def at_step(f, at):
        return lax.rem(f + at[1], steps)

    prepared = pl.pallas_call(
        functools.partial(prepare_kernel, tensor_count, steps),
        grid_spec=pltpu.PrefetchScalarGridSpec(
            num_scalar_prefetch=1,
            grid=(steps,),
            in_specs=[
                pl.BlockSpec((group_rows, feature_step), lambda f, at: (0, at_step(f, at))),
                pl.BlockSpec((1, feature_step), lambda f, at: (0, at_step(f, at))),
                pl.BlockSpec((feature_step, value_width), lambda f, at: (at_step(f, at), 0)),
                pl.BlockSpec(
                    (1, feature_step), lambda f, at: (0, at[0] * steps + at_step(f, at))
                ),
            ],
            out_specs=[
                pl.BlockSpec(
                    (group_rows, feature_step), lambda f, at: (0, jnp.minimum(f, steps // 2 - 1))
                ),
                pl.BlockSpec(
                    (group_rows, feature_step), lambda f, at: (0, jnp.maximum(f - steps // 2, 0))
                ),
            ]
            + [pl.BlockSpec(ref_shape, lambda f, at: (0, 0, 0))] * 2,
            scratch_shapes=[
                pltpu.VMEM((group_rows, feature_step), BF16),
                pltpu.VMEM((group_rows, value_width), F32),
                pltpu.VMEM((group_rows, 1), F32),
            ],
        ),
        out_shape=[jax.ShapeDtypeStruct((group_rows, shard), BF16)] * 2
        + [jax.ShapeDtypeStruct(ref_shape, BF16)] * 2,
        compiler_params=pltpu.CompilerParams(vmem_limit_bytes=56 * 2**20),
        cost_estimate=pl.CostEstimate(
            flops=2 * group_rows * block * value_width,
            bytes_accessed=8 * 2**20,
            transcendentals=0,
        ),
        name="prepare",
    )(at, tokens, ref_gain.reshape(1, block), ref_weight, pol_gain.reshape(1, model_width))
    given_rows, kept_rows, ref_kept, ref_sent = prepared
    got[-1], ref_sent = lax.optimization_barrier((got[-1], ref_sent))
    ref_got = crossed(ref_sent, tensor_count, 1)
    got_rows = swapped(given_rows, dp_count)

    cot = cotangent.reshape(slot_count, value_width)
    for j in range(PARTS):
        for number in range(1, levels):
            held[j] = jnp.where(is_getter[j], got[j], held[j])
            if j == PARTS - 1 and number == 1:
                held[j], cot, kept_rows = lax.optimization_barrier((held[j], cot, kept_rows))
            got[j], is_getter[j] = stage(number, held[j])
    for level in range(1, levels):
        ref_sum = ref_kept[:, :own_rows].astype(F32) + ref_got[:, :own_rows].astype(F32)
        ref_all = jnp.concatenate(
            [ref_sum.astype(BF16), ref_kept[:, own_rows:], ref_got[:, own_rows:]], axis=1
        )
        half_count = ref_all.shape[0] // 2
        ref_kept = ref_all[:half_count]
        ref_got = crossed(ref_all[half_count:], tensor_count, 1 << level)
    got_cot = lax.all_to_all(cot, "dp", split_axis=0, concat_axis=0, tiled=True)

    def plane_bit(level):
        return jnp.where(core == 0, 1 << (level % levels), 1 << ((1 + level) % levels))

    chunk_at = []
    for i in range(places):
        away = sum(plane_bit(level) * ((i >> (levels - 1 - level)) & 1) for level in range(levels))
        chunk_at.append(place ^ away ^ turned(t, levels))
    chunk_at = jnp.stack(chunk_at).astype(jnp.int32)

    smem = pl.BlockSpec(memory_space=pltpu.SMEM)
    vmem = pl.BlockSpec(memory_space=pltpu.VMEM)
    fixed, pull, row_scale, row_at, terms_sent = pl.pallas_call(
        functools.partial(row_kernel, span_rows, model_width),
        in_specs=[smem] * 3 + [vmem] * 4,
        out_specs=[vmem] * 5,
        out_shape=[
            jax.ShapeDtypeStruct((own_rows, value_width), F32),
            jax.ShapeDtypeStruct((own_rows, 128), F32),
            jax.ShapeDtypeStruct((own_rows, 128), F32),
            jax.ShapeDtypeStruct((own_rows, slot_count), BF16),
            jax.ShapeDtypeStruct((own_rows, value_width + 128), BF16),
        ],
        compiler_params=pltpu.CompilerParams(vmem_limit_bytes=16 * 2**20),
        cost_estimate=pl.CostEstimate(
            flops=2 * own_rows * slot_count * value_width,
            bytes_accessed=2**21,
            transcendentals=0,
        ),
        name="rows",
    )(
        lengths.reshape(-1),
        bins.reshape(-1),
        advantage.reshape(-1),
        logprob_gap.reshape(1, own_rows),
        got_cot,
        ref_kept[0],
        ref_got[0],
    )
    far = 1 << (levels - 1)
    terms_got = crossed(terms_sent, tensor_count, far).astype(F32)
    pull_got = terms_got[:, value_width : value_width + 1] + terms_got[:, -1:]
    fixed = jnp.concatenate([fixed, terms_got[:, :value_width]], axis=0)
    pull = jnp.concatenate([pull[:, :1], pull_got], axis=0)

    values, slopes = [], []
    for j in range(PARTS):
        weight = jnp.where(is_getter[j], got[j], held[j])
        value_given = dot(got_rows, weight).astype(BF16)
        total = dot(kept_rows, weight) + swapped(value_given, dp_count).astype(F32)
        for level in range(levels - 1):
            rows = total.shape[0] // 2
            total = total[:rows] + crossed(
                total[rows:].astype(BF16), tensor_count, 1 << level
            ).astype(F32)
        other = jnp.concatenate([total[own_rows:], total[:own_rows]], axis=0).astype(BF16)
        total = total + crossed(other, tensor_count, far).astype(F32)
        values.append(total[:own_rows] * row_scale[:, :1])

        cols = slice(j * width, (j + 1) * width)
        slope = (fixed[:, cols] + pull * total).astype(BF16)
        if j < PARTS - 1:
            slope, fixed, pull = lax.optimization_barrier((slope, fixed, pull))
        for level in reversed(range(levels - 1)):
            slope = jnp.concatenate([slope, crossed(slope, tensor_count, 1 << level)], axis=0)
        slopes.append(slope)

    sent = dot_rows(row_at, jnp.concatenate(values, axis=1).astype(BF16)).astype(BF16)
    slopes[0], sent = lax.optimization_barrier((slopes[0], sent))
    policy_values = lax.all_to_all(sent, "dp", split_axis=0, concat_axis=0, tiled=True)

    grad_kept, grad_sent = [], []
    for j in range(PARTS):
        slopes_got = swapped(slopes[j], dp_count)
        chunks = pl.pallas_call(
            functools.partial(grad_kernel, factor),
            grid_spec=pltpu.PrefetchScalarGridSpec(
                num_scalar_prefetch=1,
                grid=(1,),
                in_specs=[
                    pl.BlockSpec((group_rows, shard), lambda i, at: (0, 0)),
                    pl.BlockSpec((group_rows, shard), lambda i, at: (0, 0)),
                    pl.BlockSpec((group_rows, width), lambda i, at: (0, 0)),
                    pl.BlockSpec((group_rows, width), lambda i, at: (0, 0)),
                ],
                out_specs=[pl.BlockSpec((shard // 2, width), lambda i, at: (0, 0))] * 2,
                scratch_shapes=[pltpu.VMEM((shard, width), F32)],
            ),
            out_shape=[
                jax.ShapeDtypeStruct((shard // 2, width), F32),
                jax.ShapeDtypeStruct((shard // 2, width), BF16),
            ],
            compiler_params=pltpu.CompilerParams(vmem_limit_bytes=32 * 2**20),
            cost_estimate=pl.CostEstimate(
                flops=4 * group_rows * shard * width,
                bytes_accessed=4 * 2**20,
                transcendentals=0,
            ),
            name="gradient",
        )(chunk_at, kept_rows, got_rows, slopes[j], slopes_got)
        grad_kept.append(chunks[0])
        grad_sent.append(chunks[1])
    grads = []
    for j in range(PARTS):
        total, given = grad_kept[j], grad_sent[j]
        for level in range(levels):
            pairs = [
                (p * cores + c, (p ^ (1 << ((c + level) % levels))) * cores + c)
                for p in range(places)
                for c in range(cores)
            ]
            total = total + lax.ppermute(given, "dp", pairs).astype(F32)
            half_rows = total.shape[0] // 2
            if level < levels - 1:
                total, given = total[:half_rows], total[half_rows:].astype(BF16)
        grads.append(total.astype(BF16))
    pairs = [
        (flat(p, c, z), flat(z, c, p ^ turned(z, levels)))
        for p in range(places)
        for c in range(cores)
        for z in range(tensor_count)
    ]
    grad_weight = lax.ppermute(jnp.concatenate(grads, axis=1), AXES, pairs).astype(F32)
    return (policy_values.reshape(1, 1, slot_count, value_width), grad_weight)


def solution(mesh):
    in_specs = (
        P("dp", "tensor"),
        P("tensor"),
        P("tensor", None),
        P(),
        P("dp", None),
        P("dp", "tensor", None),
        P("dp", "tensor", None),
        P("dp", "tensor", None),
        P(("dp", "tensor")),
        P("dp", "tensor", None, None),
    )
    out_specs = (P("dp", "tensor", None, None), P(("dp", "tensor"), None))
    return jax.shard_map(
        on_device, mesh=mesh, in_specs=in_specs, out_specs=out_specs, check_vma=False
    )
```

```python
import functools
import math

import jax
import jax.numpy as jnp
from jax import lax
from jax.experimental import pallas as pl
from jax.experimental.pallas import tpu as pltpu
from jax.sharding import PartitionSpec as P

EPS = 1e-06
BETA = 1.0
AXES = ("dp", "tensor")
BF16 = jnp.bfloat16
F32 = jnp.float32
POWER_ROWS = 16
PARTS = 2


def dot(a, b):
    return jnp.dot(a, b, preferred_element_type=F32)


def dot_rows(a, b):
    return lax.dot_general(a, b, (((0,), (0,)), ((), ())), preferred_element_type=F32)


def swapped(array, dp_count):
    return lax.ppermute(array, "dp", [(i, i ^ 1) for i in range(dp_count)])


def turned(index, levels):
    return sum(((index >> i) & 1) << (levels - 1 - i) for i in range(levels))


def crossed(array, count, step):
    return lax.ppermute(array, "tensor", [(i, i ^ step) for i in range(count)])


def prepare_kernel(
    count, steps, at, x_ref, gain_ref, weight_ref, pol_ref, given_ref, kept_ref, *refs
):
    sent_refs, (rows_ref, total, square) = refs[:2], refs[2:]
    f = pl.program_id(0)
    own = x_ref.shape[0] // count
    levels = count.bit_length() - 1
    for i in range(count):
        source = jnp.bitwise_xor(at[0], turned(i, levels))
        rows_ref[i * own : (i + 1) * own, :] = x_ref[pl.ds(pl.multiple_of(source * own, own), own), :]
    wide = rows_ref[...].astype(F32)
    gained = (wide * pol_ref[...]).astype(BF16)

    @pl.when(f < steps // 2)
    def _():
        given_ref[...] = gained

    @pl.when(f >= steps // 2)
    def _():
        kept_ref[...] = gained

    part = dot((wide * gain_ref[...]).astype(BF16), weight_ref[...])
    squares = jnp.sum(wide * wide, axis=1, keepdims=True)

    @pl.when(f == 0)
    def _():
        total[...] = part
        square[...] = squares

    @pl.when(f > 0)
    def _():
        total[...] += part
        square[...] += squares

    @pl.when(f == steps - 1)
    def _():
        for i in range(count):
            sent = sent_refs[i // (count // 2)].at[i % (count // 2)]
            sent[:own, :] = total[i * own : (i + 1) * own, :].astype(BF16)
            power = jnp.broadcast_to(square[i * own : (i + 1) * own, :], (own, 128)).T
            high = power[: POWER_ROWS // 2].astype(BF16).astype(F32)
            low = power[: POWER_ROWS // 2] - high
            sent[own:, :] = jnp.zeros((POWER_ROWS, sent.shape[1]), BF16)
            sent[own:, :own] = jnp.concatenate([high, low], axis=0).astype(BF16)


def row_kernel(
    span, model_width, lengths, bins, advantage, gap_ref, cot_ref, kept_ref, got_ref, *refs
):
    fixed_ref, pull_ref, scale_ref, row_at_ref, sent_ref = refs
    own = pull_ref.shape[0]
    slots = row_at_ref.shape[1]
    row = lax.broadcasted_iota(jnp.int32, (own, slots), 0)
    slot = lax.broadcasted_iota(jnp.int32, (own, slots), 1)
    chosen = jnp.zeros((own, slots), jnp.bool_)
    size = jnp.ones((own, 128), F32)
    weight = jnp.zeros((own, 128), F32)
    start = jnp.int32(0)
    for s in range(lengths.shape[0]):
        end = start + lengths[s]
        inside = (row >= start) & (row < end)
        chosen = chosen | (inside & (slot - bins[s] * span == row - start))
        size = jnp.where(inside[:, :128], lengths[s].astype(F32), size)
        weight = jnp.where(inside[:, :128], advantage[s], weight)
        start = end
    row_at = jnp.where(chosen, 1.0, 0.0).astype(BF16)
    row_at_ref[...] = row_at
    importance = jnp.minimum(jnp.exp(jnp.broadcast_to(gap_ref[...], (128, own)).T), 2.0)
    coef_adv = (weight * importance / size).astype(BF16).astype(F32)
    coef_pull = (BETA / size).astype(BF16).astype(F32)
    total = kept_ref[...].astype(F32) + got_ref[...].astype(F32)
    square = jnp.zeros((1, own), F32)
    for power_row in range(own, total.shape[0], POWER_ROWS // 2):
        square = square + total[power_row : power_row + 1, :own]
    scale = lax.rsqrt(jnp.broadcast_to(square, (128, own)).T / model_width + EPS)
    reference = (total[:own] * scale[:, :1]).astype(BF16).astype(F32)
    upstream = dot(row_at, cot_ref[...])
    fixed = (coef_adv[:, :1] * upstream - coef_pull[:, :1] * reference) * scale[:, :1]
    pull = coef_pull * scale * scale
    high = pull.astype(BF16).astype(F32)
    width = fixed.shape[1]
    fixed_ref[...] = fixed
    pull_ref[...] = pull
    scale_ref[...] = scale
    sent_ref[:, :width] = fixed.astype(BF16)
    lane = lax.broadcasted_iota(jnp.int32, pull.shape, 1)
    sent_ref[:, width:] = jnp.where(lane < 64, high, pull - high).astype(BF16)


def grad_kernel(factor, at, kept_ref, got_ref, slope_ref, slope_got_ref, *refs):
    *out_refs, grad = refs
    total = dot_rows(kept_ref[...], slope_ref[...]) + dot_rows(got_ref[...], slope_got_ref[...])
    grad[...] = total * factor
    rows = grad.shape[0] // at.shape[0]
    count = at.shape[0] // 2
    for s in range(2 * count):
        chunk = grad[pl.ds(pl.multiple_of(at[s] * rows, rows), rows), :]
        out_ref = out_refs[s // count]
        place = s % count
        out_ref[place * rows : (place + 1) * rows, :] = chunk.astype(out_ref.dtype)


def on_device(
    tokens,
    ref_gain,
    ref_weight,
    pol_gain,
    pol_weight,
    lengths,
    bins,
    advantage,
    logprob_gap,
    cotangent,
):
    tensor_count = lax.axis_size("tensor")
    dp_count = lax.axis_size("dp")
    t = lax.axis_index("tensor")
    d = lax.axis_index("dp")
    cores = dp_count // tensor_count
    assert cores == 2
    places = dp_count // cores
    levels = places.bit_length() - 1
    assert 1 << levels == places == tensor_count
    place = d // cores
    core = d % cores
    group_rows, block = tokens.shape
    own_rows = group_rows // tensor_count
    slot_count = cotangent.shape[2]
    span_rows = slot_count // dp_count
    value_width = ref_weight.shape[1]
    model_width = pol_gain.shape[0]
    shard = pol_weight.shape[0]
    width = value_width // PARTS
    factor = 1.0 / math.sqrt(dp_count * tensor_count * lengths.shape[2])
    relative = place ^ t

    def flat(p, c, z):
        return (p * cores + c) * tensor_count + z

    def stage(number, held):
        pairs, is_getter = [], jnp.zeros((), jnp.bool_)
        for c in range(cores):
            holders = [0]
            for before in range(number):
                bit = 1 << ((c + before) % levels)
                holders = holders + [q ^ bit for q in holders]
            bit = 1 << ((c + number) % levels)
            for q in holders:
                pairs += [
                    (flat(q ^ z, c, z), flat(q ^ bit ^ z, c, z)) for z in range(tensor_count)
                ]
                is_getter = is_getter | ((core == c) & (relative == (q ^ bit)))
        return lax.ppermute(held, AXES, pairs), is_getter

    first_got, first_getter = stage(0, pol_weight)

    steps = 4
    feature_step = block // steps
    at = jnp.stack([t, (1 - core) * (steps // 2)]).astype(jnp.int32)
    ref_shape = (tensor_count // 2, own_rows + POWER_ROWS, value_width)

    def at_step(f, at):
        return lax.rem(f + at[1], steps)

    prepared = pl.pallas_call(
        functools.partial(prepare_kernel, tensor_count, steps),
        grid_spec=pltpu.PrefetchScalarGridSpec(
            num_scalar_prefetch=1,
            grid=(steps,),
            in_specs=[
                pl.BlockSpec((group_rows, feature_step), lambda f, at: (0, at_step(f, at))),
                pl.BlockSpec((1, feature_step), lambda f, at: (0, at_step(f, at))),
                pl.BlockSpec((feature_step, value_width), lambda f, at: (at_step(f, at), 0)),
                pl.BlockSpec(
                    (1, feature_step), lambda f, at: (0, at[0] * steps + at_step(f, at))
                ),
            ],
            out_specs=[
                pl.BlockSpec(
                    (group_rows, feature_step), lambda f, at: (0, jnp.minimum(f, steps // 2 - 1))
                ),
                pl.BlockSpec(
                    (group_rows, feature_step), lambda f, at: (0, jnp.maximum(f - steps // 2, 0))
                ),
            ]
            + [pl.BlockSpec(ref_shape, lambda f, at: (0, 0, 0))] * 2,
            scratch_shapes=[
                pltpu.VMEM((group_rows, feature_step), BF16),
                pltpu.VMEM((group_rows, value_width), F32),
                pltpu.VMEM((group_rows, 1), F32),
            ],
        ),
        out_shape=[jax.ShapeDtypeStruct((group_rows, shard), BF16)] * 2
        + [jax.ShapeDtypeStruct(ref_shape, BF16)] * 2,
        compiler_params=pltpu.CompilerParams(vmem_limit_bytes=56 * 2**20),
        cost_estimate=pl.CostEstimate(
            flops=2 * group_rows * block * value_width,
            bytes_accessed=8 * 2**20,
            transcendentals=0,
        ),
        name="prepare",
    )(at, tokens, ref_gain.reshape(1, block), ref_weight, pol_gain.reshape(1, model_width))
    given_rows, kept_rows, ref_kept, ref_sent = prepared
    ref_got = crossed(ref_sent, tensor_count, 1)
    got_rows = swapped(given_rows, dp_count)

    held, got, is_getter = pol_weight, first_got, first_getter
    cot = cotangent.reshape(slot_count, value_width)
    for number in range(1, levels):
        held = jnp.where(is_getter, got, held)
        if number == 1:
            held, cot, kept_rows = lax.optimization_barrier((held, cot, kept_rows))
        got, is_getter = stage(number, held)
    for level in range(1, levels):
        ref_sum = ref_kept[:, :own_rows].astype(F32) + ref_got[:, :own_rows].astype(F32)
        ref_all = jnp.concatenate(
            [ref_sum.astype(BF16), ref_kept[:, own_rows:], ref_got[:, own_rows:]], axis=1
        )
        half_count = ref_all.shape[0] // 2
        ref_kept = ref_all[:half_count]
        ref_got = crossed(ref_all[half_count:], tensor_count, 1 << level)
    got_cot = lax.all_to_all(cot, "dp", split_axis=0, concat_axis=0, tiled=True)

    def plane_bit(level):
        return jnp.where(core == 0, 1 << (level % levels), 1 << ((1 + level) % levels))

    chunk_at = []
    for i in range(places):
        away = sum(plane_bit(level) * ((i >> (levels - 1 - level)) & 1) for level in range(levels))
        chunk_at.append(place ^ away ^ turned(t, levels))
    chunk_at = jnp.stack(chunk_at).astype(jnp.int32)

    smem = pl.BlockSpec(memory_space=pltpu.SMEM)
    vmem = pl.BlockSpec(memory_space=pltpu.VMEM)
    weight = jnp.where(is_getter, got, held)
    value_given = dot(got_rows, weight).astype(BF16)
    value_kept = dot(kept_rows, weight)
    tied = lax.optimization_barrier((value_given, lengths, bins, advantage, logprob_gap))
    value_given, lengths, bins, advantage, logprob_gap = tied
    fixed, pull, row_scale, row_at, terms_sent = pl.pallas_call(
        functools.partial(row_kernel, span_rows, model_width),
        in_specs=[smem] * 3 + [vmem] * 4,
        out_specs=[vmem] * 5,
        out_shape=[
            jax.ShapeDtypeStruct((own_rows, value_width), F32),
            jax.ShapeDtypeStruct((own_rows, 128), F32),
            jax.ShapeDtypeStruct((own_rows, 128), F32),
            jax.ShapeDtypeStruct((own_rows, slot_count), BF16),
            jax.ShapeDtypeStruct((own_rows, value_width + 128), BF16),
        ],
        compiler_params=pltpu.CompilerParams(vmem_limit_bytes=16 * 2**20),
        cost_estimate=pl.CostEstimate(
            flops=2 * own_rows * slot_count * value_width,
            bytes_accessed=2**21,
            transcendentals=0,
        ),
        name="rows",
    )(
        lengths.reshape(-1),
        bins.reshape(-1),
        advantage.reshape(-1),
        logprob_gap.reshape(1, own_rows),
        got_cot,
        ref_kept[0],
        ref_got[0],
    )
    far = 1 << (levels - 1)
    terms_got = crossed(terms_sent, tensor_count, far).astype(F32)
    pull_got = terms_got[:, value_width : value_width + 1] + terms_got[:, -1:]
    fixed = jnp.concatenate([fixed, terms_got[:, :value_width]], axis=0)
    pull = jnp.concatenate([pull[:, :1], pull_got], axis=0)

    values, slopes = [], []
    for j in range(PARTS):
        cols = slice(j * width, (j + 1) * width)
        total = value_kept[:, cols] + swapped(value_given[:, cols], dp_count).astype(F32)
        for level in range(levels - 1):
            rows = total.shape[0] // 2
            total = total[:rows] + crossed(
                total[rows:].astype(BF16), tensor_count, 1 << level
            ).astype(F32)
        other = jnp.concatenate([total[own_rows:], total[:own_rows]], axis=0).astype(BF16)
        total = total + crossed(other, tensor_count, far).astype(F32)
        values.append(total[:own_rows] * row_scale[:, :1])

        slope = (fixed[:, cols] + pull * total).astype(BF16)
        if j < PARTS - 1:
            slope, fixed, pull = lax.optimization_barrier((slope, fixed, pull))
        else:
            slope, *values = lax.optimization_barrier((slope, *values))
        for level in reversed(range(levels - 1)):
            slope = jnp.concatenate([slope, crossed(slope, tensor_count, 1 << level)], axis=0)
        slopes.append(slope)

    sent = dot_rows(row_at, jnp.concatenate(values, axis=1).astype(BF16)).astype(BF16)
    policy_values = lax.all_to_all(sent, "dp", split_axis=0, concat_axis=0, tiled=True)

    grad_kept, grad_sent = [], []
    for j in range(PARTS):
        slopes_got = swapped(slopes[j], dp_count)
        if j == PARTS - 1:
            slopes_got, policy_values = lax.optimization_barrier((slopes_got, policy_values))
        chunks = pl.pallas_call(
            functools.partial(grad_kernel, factor),
            grid_spec=pltpu.PrefetchScalarGridSpec(
                num_scalar_prefetch=1,
                grid=(1,),
                in_specs=[
                    pl.BlockSpec((group_rows, shard), lambda i, at: (0, 0)),
                    pl.BlockSpec((group_rows, shard), lambda i, at: (0, 0)),
                    pl.BlockSpec((group_rows, width), lambda i, at: (0, 0)),
                    pl.BlockSpec((group_rows, width), lambda i, at: (0, 0)),
                ],
                out_specs=[pl.BlockSpec((shard // 2, width), lambda i, at: (0, 0))] * 2,
                scratch_shapes=[pltpu.VMEM((shard, width), F32)],
            ),
            out_shape=[
                jax.ShapeDtypeStruct((shard // 2, width), F32),
                jax.ShapeDtypeStruct((shard // 2, width), BF16),
            ],
            compiler_params=pltpu.CompilerParams(vmem_limit_bytes=32 * 2**20),
            cost_estimate=pl.CostEstimate(
                flops=4 * group_rows * shard * width,
                bytes_accessed=4 * 2**20,
                transcendentals=0,
            ),
            name="gradient",
        )(chunk_at, kept_rows, got_rows, slopes[j], slopes_got)
        grad_kept.append(chunks[0])
        grad_sent.append(chunks[1])
    grads = []
    for j in range(PARTS):
        total, given = grad_kept[j], grad_sent[j]
        for level in range(levels):
            pairs = [
                (p * cores + c, (p ^ (1 << ((c + level) % levels))) * cores + c)
                for p in range(places)
                for c in range(cores)
            ]
            total = total + lax.ppermute(given, "dp", pairs).astype(F32)
            half_rows = total.shape[0] // 2
            if level < levels - 1:
                total, given = total[:half_rows], total[half_rows:].astype(BF16)
        grads.append(total.astype(BF16))
    pairs = [
        (flat(p, c, z), flat(z, c, p ^ turned(z, levels)))
        for p in range(places)
        for c in range(cores)
        for z in range(tensor_count)
    ]
    grad_weight = lax.ppermute(jnp.concatenate(grads, axis=1), AXES, pairs).astype(F32)
    return (policy_values.reshape(1, 1, slot_count, value_width), grad_weight)


def solution(mesh):
    in_specs = (
        P("dp", "tensor"),
        P("tensor"),
        P("tensor", None),
        P(),
        P("dp", None),
        P("dp", "tensor", None),
        P("dp", "tensor", None),
        P("dp", "tensor", None),
        P(("dp", "tensor")),
        P("dp", "tensor", None, None),
    )
    out_specs = (P("dp", "tensor", None, None), P(("dp", "tensor"), None))
    return jax.shard_map(
        on_device, mesh=mesh, in_specs=in_specs, out_specs=out_specs, check_vma=False
    )
```

```python
import functools
import math

import jax
import jax.numpy as jnp
from jax import lax
from jax.experimental import pallas as pl
from jax.experimental.pallas import tpu as pltpu
from jax.sharding import PartitionSpec as P

EPS = 1e-06
BETA = 1.0
AXES = ("dp", "tensor")
BF16 = jnp.bfloat16
F32 = jnp.float32
POWER_ROWS = 16
PARTS = 2


def dot(a, b):
    return jnp.dot(a, b, preferred_element_type=F32)


def dot_rows(a, b):
    return lax.dot_general(a, b, (((0,), (0,)), ((), ())), preferred_element_type=F32)


def swapped(array, dp_count):
    return lax.ppermute(array, "dp", [(i, i ^ 1) for i in range(dp_count)])


def turned(index, levels):
    return sum(((index >> i) & 1) << (levels - 1 - i) for i in range(levels))


def crossed(array, count, step):
    return lax.ppermute(array, "tensor", [(i, i ^ step) for i in range(count)])


def prepare_kernel(
    count, steps, at, x_ref, gain_ref, weight_ref, pol_ref, given_ref, kept_ref, *refs
):
    sent_refs, (rows_ref, total, square) = refs[:2], refs[2:]
    f = pl.program_id(0)
    own = x_ref.shape[0] // count
    levels = count.bit_length() - 1
    for i in range(count):
        source = jnp.bitwise_xor(at[0], turned(i, levels))
        rows_ref[i * own : (i + 1) * own, :] = x_ref[pl.ds(pl.multiple_of(source * own, own), own), :]
    wide = rows_ref[...].astype(F32)
    gained = (wide * pol_ref[...]).astype(BF16)

    @pl.when(f < steps // 2)
    def _():
        given_ref[...] = gained

    @pl.when(f >= steps // 2)
    def _():
        kept_ref[...] = gained

    part = dot((wide * gain_ref[...]).astype(BF16), weight_ref[...])
    squares = jnp.sum(wide * wide, axis=1, keepdims=True)

    @pl.when(f == 0)
    def _():
        total[...] = part
        square[...] = squares

    @pl.when(f > 0)
    def _():
        total[...] += part
        square[...] += squares

    @pl.when(f == steps - 1)
    def _():
        for i in range(count):
            sent = sent_refs[i // (count // 2)].at[i % (count // 2)]
            sent[:own, :] = total[i * own : (i + 1) * own, :].astype(BF16)
            power = jnp.broadcast_to(square[i * own : (i + 1) * own, :], (own, 128)).T
            high = power[: POWER_ROWS // 2].astype(BF16).astype(F32)
            low = power[: POWER_ROWS // 2] - high
            sent[own:, :] = jnp.zeros((POWER_ROWS, sent.shape[1]), BF16)
            sent[own:, :own] = jnp.concatenate([high, low], axis=0).astype(BF16)


def row_kernel(
    span, model_width, lengths, bins, advantage, gap_ref, cot_ref, kept_ref, got_ref, *refs
):
    fixed_ref, pull_ref, scale_ref, row_at_ref, sent_ref = refs
    own = pull_ref.shape[0]
    slots = row_at_ref.shape[1]
    row = lax.broadcasted_iota(jnp.int32, (own, slots), 0)
    slot = lax.broadcasted_iota(jnp.int32, (own, slots), 1)
    chosen = jnp.zeros((own, slots), jnp.bool_)
    size = jnp.ones((own, 128), F32)
    weight = jnp.zeros((own, 128), F32)
    start = jnp.int32(0)
    for s in range(lengths.shape[0]):
        end = start + lengths[s]
        inside = (row >= start) & (row < end)
        chosen = chosen | (inside & (slot - bins[s] * span == row - start))
        size = jnp.where(inside[:, :128], lengths[s].astype(F32), size)
        weight = jnp.where(inside[:, :128], advantage[s], weight)
        start = end
    row_at = jnp.where(chosen, 1.0, 0.0).astype(BF16)
    row_at_ref[...] = row_at
    importance = jnp.minimum(jnp.exp(jnp.broadcast_to(gap_ref[...], (128, own)).T), 2.0)
    coef_adv = (weight * importance / size).astype(BF16).astype(F32)
    coef_pull = (BETA / size).astype(BF16).astype(F32)
    total = kept_ref[...].astype(F32) + got_ref[...].astype(F32)
    square = jnp.zeros((1, own), F32)
    for power_row in range(own, total.shape[0], POWER_ROWS // 2):
        square = square + total[power_row : power_row + 1, :own]
    scale = lax.rsqrt(jnp.broadcast_to(square, (128, own)).T / model_width + EPS)
    reference = (total[:own] * scale[:, :1]).astype(BF16).astype(F32)
    upstream = dot(row_at, cot_ref[...])
    fixed = (coef_adv[:, :1] * upstream - coef_pull[:, :1] * reference) * scale[:, :1]
    pull = coef_pull * scale * scale
    high = pull.astype(BF16).astype(F32)
    width = fixed.shape[1]
    fixed_ref[...] = fixed
    pull_ref[...] = pull
    scale_ref[...] = scale
    sent_ref[:, :width] = fixed.astype(BF16)
    lane = lax.broadcasted_iota(jnp.int32, pull.shape, 1)
    sent_ref[:, width:] = jnp.where(lane < 64, high, pull - high).astype(BF16)


def grad_kernel(factor, at, kept_ref, got_ref, slope_ref, slope_got_ref, *refs):
    *out_refs, grad = refs
    total = dot_rows(kept_ref[...], slope_ref[...]) + dot_rows(got_ref[...], slope_got_ref[...])
    grad[...] = total * factor
    rows = grad.shape[0] // at.shape[0]
    count = at.shape[0] // 2
    for s in range(2 * count):
        chunk = grad[pl.ds(pl.multiple_of(at[s] * rows, rows), rows), :]
        out_ref = out_refs[s // count]
        place = s % count
        out_ref[place * rows : (place + 1) * rows, :] = chunk.astype(out_ref.dtype)


def on_device(
    tokens,
    ref_gain,
    ref_weight,
    pol_gain,
    pol_weight,
    lengths,
    bins,
    advantage,
    logprob_gap,
    cotangent,
):
    tensor_count = lax.axis_size("tensor")
    dp_count = lax.axis_size("dp")
    t = lax.axis_index("tensor")
    d = lax.axis_index("dp")
    cores = dp_count // tensor_count
    assert cores == 2
    places = dp_count // cores
    levels = places.bit_length() - 1
    assert 1 << levels == places == tensor_count
    place = d // cores
    core = d % cores
    group_rows, block = tokens.shape
    own_rows = group_rows // tensor_count
    slot_count = cotangent.shape[2]
    span_rows = slot_count // dp_count
    value_width = ref_weight.shape[1]
    model_width = pol_gain.shape[0]
    shard = pol_weight.shape[0]
    width = value_width // PARTS
    factor = 1.0 / math.sqrt(dp_count * tensor_count * lengths.shape[2])
    relative = place ^ t

    def flat(p, c, z):
        return (p * cores + c) * tensor_count + z

    def stage(number, held):
        pairs, is_getter = [], jnp.zeros((), jnp.bool_)
        for c in range(cores):
            holders = [0]
            for before in range(number):
                bit = 1 << ((c + before) % levels)
                holders = holders + [q ^ bit for q in holders]
            bit = 1 << ((c + number) % levels)
            for q in holders:
                pairs += [
                    (flat(q ^ z, c, z), flat(q ^ bit ^ z, c, z)) for z in range(tensor_count)
                ]
                is_getter = is_getter | ((core == c) & (relative == (q ^ bit)))
        return lax.ppermute(held, AXES, pairs), is_getter

    first_got, first_getter = stage(0, pol_weight)

    steps = 4
    feature_step = block // steps
    at = jnp.stack([t, (1 - core) * (steps // 2)]).astype(jnp.int32)
    ref_shape = (tensor_count // 2, own_rows + POWER_ROWS, value_width)

    def at_step(f, at):
        return lax.rem(f + at[1], steps)

    prepared = pl.pallas_call(
        functools.partial(prepare_kernel, tensor_count, steps),
        grid_spec=pltpu.PrefetchScalarGridSpec(
            num_scalar_prefetch=1,
            grid=(steps,),
            in_specs=[
                pl.BlockSpec((group_rows, feature_step), lambda f, at: (0, at_step(f, at))),
                pl.BlockSpec((1, feature_step), lambda f, at: (0, at_step(f, at))),
                pl.BlockSpec((feature_step, value_width), lambda f, at: (at_step(f, at), 0)),
                pl.BlockSpec(
                    (1, feature_step), lambda f, at: (0, at[0] * steps + at_step(f, at))
                ),
            ],
            out_specs=[
                pl.BlockSpec(
                    (group_rows, feature_step), lambda f, at: (0, jnp.minimum(f, steps // 2 - 1))
                ),
                pl.BlockSpec(
                    (group_rows, feature_step), lambda f, at: (0, jnp.maximum(f - steps // 2, 0))
                ),
            ]
            + [pl.BlockSpec(ref_shape, lambda f, at: (0, 0, 0))] * 2,
            scratch_shapes=[
                pltpu.VMEM((group_rows, feature_step), BF16),
                pltpu.VMEM((group_rows, value_width), F32),
                pltpu.VMEM((group_rows, 1), F32),
            ],
        ),
        out_shape=[jax.ShapeDtypeStruct((group_rows, shard), BF16)] * 2
        + [jax.ShapeDtypeStruct(ref_shape, BF16)] * 2,
        compiler_params=pltpu.CompilerParams(vmem_limit_bytes=56 * 2**20),
        cost_estimate=pl.CostEstimate(
            flops=2 * group_rows * block * value_width,
            bytes_accessed=8 * 2**20,
            transcendentals=0,
        ),
        name="prepare",
    )(at, tokens, ref_gain.reshape(1, block), ref_weight, pol_gain.reshape(1, model_width))
    given_rows, kept_rows, ref_kept, ref_sent = prepared
    ref_got = crossed(ref_sent, tensor_count, 1)
    got_rows = swapped(given_rows, dp_count)

    held, got, is_getter = pol_weight, first_got, first_getter
    cot = cotangent.reshape(slot_count, value_width)
    ref_got, cot = lax.optimization_barrier((ref_got, cot))
    for number in range(1, levels):
        held = jnp.where(is_getter, got, held)
        if number == 1:
            held, kept_rows = lax.optimization_barrier((held, kept_rows))
        got, is_getter = stage(number, held)
    for level in range(1, levels):
        ref_sum = ref_kept[:, :own_rows].astype(F32) + ref_got[:, :own_rows].astype(F32)
        ref_all = jnp.concatenate(
            [ref_sum.astype(BF16), ref_kept[:, own_rows:], ref_got[:, own_rows:]], axis=1
        )
        half_count = ref_all.shape[0] // 2
        ref_kept = ref_all[:half_count]
        ref_got = crossed(ref_all[half_count:], tensor_count, 1 << level)
    got_cot = lax.all_to_all(cot, "dp", split_axis=0, concat_axis=0, tiled=True)

    def plane_bit(level):
        return jnp.where(core == 0, 1 << (level % levels), 1 << ((1 + level) % levels))

    chunk_at = []
    for i in range(places):
        away = sum(plane_bit(level) * ((i >> (levels - 1 - level)) & 1) for level in range(levels))
        chunk_at.append(place ^ away ^ turned(t, levels))
    chunk_at = jnp.stack(chunk_at).astype(jnp.int32)

    smem = pl.BlockSpec(memory_space=pltpu.SMEM)
    vmem = pl.BlockSpec(memory_space=pltpu.VMEM)
    value_kept, value_got = [], []
    for j in range(PARTS):
        cols = slice(j * width, (j + 1) * width)
        weight = lax.optimization_barrier(jnp.where(is_getter, got[:, cols], held[:, cols]))
        value_got.append(swapped(dot(got_rows, weight).astype(BF16), dp_count))
        value_kept.append(dot(kept_rows, weight))
    tied = lax.optimization_barrier((value_got[0], lengths, bins, advantage, logprob_gap))
    value_got[0], lengths, bins, advantage, logprob_gap = tied
    fixed, pull, row_scale, row_at, terms_sent = pl.pallas_call(
        functools.partial(row_kernel, span_rows, model_width),
        in_specs=[smem] * 3 + [vmem] * 4,
        out_specs=[vmem] * 5,
        out_shape=[
            jax.ShapeDtypeStruct((own_rows, value_width), F32),
            jax.ShapeDtypeStruct((own_rows, 128), F32),
            jax.ShapeDtypeStruct((own_rows, 128), F32),
            jax.ShapeDtypeStruct((own_rows, slot_count), BF16),
            jax.ShapeDtypeStruct((own_rows, value_width + 128), BF16),
        ],
        compiler_params=pltpu.CompilerParams(vmem_limit_bytes=16 * 2**20),
        cost_estimate=pl.CostEstimate(
            flops=2 * own_rows * slot_count * value_width,
            bytes_accessed=2**21,
            transcendentals=0,
        ),
        name="rows",
    )(
        lengths.reshape(-1),
        bins.reshape(-1),
        advantage.reshape(-1),
        logprob_gap.reshape(1, own_rows),
        got_cot,
        ref_kept[0],
        ref_got[0],
    )
    far = 1 << (levels - 1)
    terms_got = crossed(terms_sent, tensor_count, far)

    values, slopes = [], []
    for j in range(PARTS):
        cols = slice(j * width, (j + 1) * width)
        total = value_kept[j] + value_got[j].astype(F32)
        for level in range(levels - 1):
            rows = total.shape[0] // 2
            total = total[:rows] + crossed(
                total[rows:].astype(BF16), tensor_count, 1 << level
            ).astype(F32)
        if j == 0:
            total, terms_got = lax.optimization_barrier((total, terms_got))
            terms_got = terms_got.astype(F32)
            pull_got = terms_got[:, value_width : value_width + 1] + terms_got[:, -1:]
            fixed = jnp.concatenate([fixed, terms_got[:, :value_width]], axis=0)
            pull = jnp.concatenate([pull[:, :1], pull_got], axis=0)
        other = jnp.concatenate([total[own_rows:], total[:own_rows]], axis=0).astype(BF16)
        total = total + crossed(other, tensor_count, far).astype(F32)
        values.append(total[:own_rows] * row_scale[:, :1])

        slope = (fixed[:, cols] + pull * total).astype(BF16)
        if j < PARTS - 1:
            slope, fixed, pull = lax.optimization_barrier((slope, fixed, pull))
        else:
            slope, *values = lax.optimization_barrier((slope, *values))
        for level in reversed(range(levels - 1)):
            slope = jnp.concatenate([slope, crossed(slope, tensor_count, 1 << level)], axis=0)
        slopes.append(slope)

    sent = dot_rows(row_at, jnp.concatenate(values, axis=1).astype(BF16)).astype(BF16)
    slopes[0], sent = lax.optimization_barrier((slopes[0], sent))
    policy_values = lax.all_to_all(sent, "dp", split_axis=0, concat_axis=0, tiled=True)

    grad_kept, grad_sent = [], []
    for j in range(PARTS):
        slopes_got = swapped(slopes[j], dp_count)
        chunks = pl.pallas_call(
            functools.partial(grad_kernel, factor),
            grid_spec=pltpu.PrefetchScalarGridSpec(
                num_scalar_prefetch=1,
                grid=(1,),
                in_specs=[
                    pl.BlockSpec((group_rows, shard), lambda i, at: (0, 0)),
                    pl.BlockSpec((group_rows, shard), lambda i, at: (0, 0)),
                    pl.BlockSpec((group_rows, width), lambda i, at: (0, 0)),
                    pl.BlockSpec((group_rows, width), lambda i, at: (0, 0)),
                ],
                out_specs=[pl.BlockSpec((shard // 2, width), lambda i, at: (0, 0))] * 2,
                scratch_shapes=[pltpu.VMEM((shard, width), F32)],
            ),
            out_shape=[
                jax.ShapeDtypeStruct((shard // 2, width), F32),
                jax.ShapeDtypeStruct((shard // 2, width), BF16),
            ],
            compiler_params=pltpu.CompilerParams(vmem_limit_bytes=32 * 2**20),
            cost_estimate=pl.CostEstimate(
                flops=4 * group_rows * shard * width,
                bytes_accessed=4 * 2**20,
                transcendentals=0,
            ),
            name="gradient",
        )(chunk_at, kept_rows, got_rows, slopes[j], slopes_got)
        grad_kept.append(chunks[0])
        grad_sent.append(chunks[1])
    grads = []
    for j in range(PARTS):
        total, given = grad_kept[j], grad_sent[j]
        for level in range(levels):
            pairs = [
                (p * cores + c, (p ^ (1 << ((c + level) % levels))) * cores + c)
                for p in range(places)
                for c in range(cores)
            ]
            total = total + lax.ppermute(given, "dp", pairs).astype(F32)
            half_rows = total.shape[0] // 2
            if j == PARTS - 1 and level == 0:
                total, policy_values = lax.optimization_barrier((total, policy_values))
            if level < levels - 1:
                total, given = total[:half_rows], total[half_rows:].astype(BF16)
        grads.append(total.astype(BF16))
    pairs = [
        (flat(p, c, z), flat(z, c, p ^ turned(z, levels)))
        for p in range(places)
        for c in range(cores)
        for z in range(tensor_count)
    ]
    grad_weight = lax.ppermute(jnp.concatenate(grads, axis=1), AXES, pairs).astype(F32)
    return (policy_values.reshape(1, 1, slot_count, value_width), grad_weight)


def solution(mesh):
    in_specs = (
        P("dp", "tensor"),
        P("tensor"),
        P("tensor", None),
        P(),
        P("dp", None),
        P("dp", "tensor", None),
        P("dp", "tensor", None),
        P("dp", "tensor", None),
        P(("dp", "tensor")),
        P("dp", "tensor", None, None),
    )
    out_specs = (P("dp", "tensor", None, None), P(("dp", "tensor"), None))
    return jax.shard_map(
        on_device, mesh=mesh, in_specs=in_specs, out_specs=out_specs, check_vma=False
    )
```

```python
import functools
import math

import jax
import jax.numpy as jnp
from jax import lax
from jax.experimental import pallas as pl
from jax.experimental.pallas import tpu as pltpu
from jax.sharding import PartitionSpec as P

EPS = 1e-06
BETA = 1.0
AXES = ("dp", "tensor")
BF16 = jnp.bfloat16
F32 = jnp.float32
POWER_ROWS = 16
PARTS = 2


def dot(a, b):
    return jnp.dot(a, b, preferred_element_type=F32)


def dot_rows(a, b):
    return lax.dot_general(a, b, (((0,), (0,)), ((), ())), preferred_element_type=F32)


def swapped(array, dp_count):
    return lax.ppermute(array, "dp", [(i, i ^ 1) for i in range(dp_count)])


def turned(index, levels):
    return sum(((index >> i) & 1) << (levels - 1 - i) for i in range(levels))


def crossed(array, count, step):
    return lax.ppermute(array, "tensor", [(i, i ^ step) for i in range(count)])


def chunk_start(count, at, own, i):
    source = jnp.bitwise_xor(at[0], turned(i, count.bit_length() - 1))
    return pl.multiple_of(source * own, own)


def split_kernel(count, steps, at, x_ref, gain_ref, given_ref, kept_ref):
    f = pl.program_id(0)
    own = x_ref.shape[0] // count

    def fill(out_ref):
        for i in range(count):
            rows = x_ref[pl.ds(chunk_start(count, at, own, i), own), :].astype(F32)
            out_ref[i * own : (i + 1) * own, :] = (rows * gain_ref[...]).astype(BF16)

    @pl.when(f < steps // 2)
    def _():
        fill(given_ref)

    @pl.when(f >= steps // 2)
    def _():
        fill(kept_ref)


def reference_kernel(
    count, steps, at, x_ref, gain_ref, weight_ref, kept_ref, sent_ref, rows_ref, total, square
):
    f = pl.program_id(0)
    own = x_ref.shape[0] // count

    @pl.when(f == 0)
    def _():
        square[...] = jnp.zeros_like(square)

    for i in range(count):
        wide = x_ref[pl.ds(chunk_start(count, at, own, i), own), :].astype(F32)
        rows_ref[i * own : (i + 1) * own, :] = (wide * gain_ref[...]).astype(BF16)
        square[i * own : (i + 1) * own, :] += jnp.sum(wide * wide, axis=1, keepdims=True)
    part = dot(rows_ref[...], weight_ref[...])

    @pl.when(f == 0)
    def _():
        total[...] = part

    @pl.when(f > 0)
    def _():
        total[...] += part

    @pl.when(f == steps - 1)
    def _():
        for i in range(count):
            out = (kept_ref, sent_ref)[i // (count // 2)].at[i % (count // 2)]
            out[:own, :] = total[i * own : (i + 1) * own, :].astype(BF16)
            power = jnp.broadcast_to(square[i * own : (i + 1) * own, :], (own, 128)).T
            high = power[: POWER_ROWS // 2].astype(BF16).astype(F32)
            low = power[: POWER_ROWS // 2] - high
            out[own:, :] = jnp.zeros((POWER_ROWS, out.shape[1]), BF16)
            out[own:, :own] = jnp.concatenate([high, low], axis=0).astype(BF16)


def row_kernel(
    span, model_width, lengths, bins, advantage, gap_ref, cot_ref, kept_ref, got_ref, *refs
):
    fixed_ref, pull_ref, scale_ref, row_at_ref, sent_ref = refs
    own = pull_ref.shape[0]
    slots = row_at_ref.shape[1]
    row = lax.broadcasted_iota(jnp.int32, (own, slots), 0)
    slot = lax.broadcasted_iota(jnp.int32, (own, slots), 1)
    chosen = jnp.zeros((own, slots), jnp.bool_)
    size = jnp.ones((own, 128), F32)
    weight = jnp.zeros((own, 128), F32)
    start = jnp.int32(0)
    for s in range(lengths.shape[0]):
        end = start + lengths[s]
        inside = (row >= start) & (row < end)
        chosen = chosen | (inside & (slot - bins[s] * span == row - start))
        size = jnp.where(inside[:, :128], lengths[s].astype(F32), size)
        weight = jnp.where(inside[:, :128], advantage[s], weight)
        start = end
    row_at = jnp.where(chosen, 1.0, 0.0).astype(BF16)
    row_at_ref[...] = row_at
    importance = jnp.minimum(jnp.exp(jnp.broadcast_to(gap_ref[...], (128, own)).T), 2.0)
    coef_adv = (weight * importance / size).astype(BF16).astype(F32)
    coef_pull = (BETA / size).astype(BF16).astype(F32)
    total = kept_ref[...].astype(F32) + got_ref[...].astype(F32)
    square = jnp.zeros((1, own), F32)
    for power_row in range(own, total.shape[0], POWER_ROWS // 2):
        square = square + total[power_row : power_row + 1, :own]
    scale = lax.rsqrt(jnp.broadcast_to(square, (128, own)).T / model_width + EPS)
    reference = (total[:own] * scale[:, :1]).astype(BF16).astype(F32)
    upstream = dot(row_at, cot_ref[...])
    fixed = (coef_adv[:, :1] * upstream - coef_pull[:, :1] * reference) * scale[:, :1]
    pull = coef_pull * scale * scale
    high = pull.astype(BF16).astype(F32)
    width = fixed.shape[1]
    fixed_ref[...] = fixed
    pull_ref[...] = pull
    scale_ref[...] = scale
    sent_ref[:, :width] = fixed.astype(BF16)
    lane = lax.broadcasted_iota(jnp.int32, pull.shape, 1)
    sent_ref[:, width:] = jnp.where(lane < 64, high, pull - high).astype(BF16)


def grad_kernel(factor, at, kept_ref, got_ref, slope_ref, slope_got_ref, *refs):
    *out_refs, grad = refs
    total = dot_rows(kept_ref[...], slope_ref[...]) + dot_rows(got_ref[...], slope_got_ref[...])
    grad[...] = total * factor
    rows = grad.shape[0] // at.shape[0]
    count = at.shape[0] // 2
    for s in range(2 * count):
        chunk = grad[pl.ds(pl.multiple_of(at[s] * rows, rows), rows), :]
        out_ref = out_refs[s // count]
        place = s % count
        out_ref[place * rows : (place + 1) * rows, :] = chunk.astype(out_ref.dtype)


def on_device(
    tokens,
    ref_gain,
    ref_weight,
    pol_gain,
    pol_weight,
    lengths,
    bins,
    advantage,
    logprob_gap,
    cotangent,
):
    tensor_count = lax.axis_size("tensor")
    dp_count = lax.axis_size("dp")
    t = lax.axis_index("tensor")
    d = lax.axis_index("dp")
    cores = dp_count // tensor_count
    assert cores == 2
    places = dp_count // cores
    levels = places.bit_length() - 1
    assert 1 << levels == places == tensor_count
    place = d // cores
    core = d % cores
    group_rows, block = tokens.shape
    own_rows = group_rows // tensor_count
    slot_count = cotangent.shape[2]
    span_rows = slot_count // dp_count
    value_width = ref_weight.shape[1]
    model_width = pol_gain.shape[0]
    shard = pol_weight.shape[0]
    width = value_width // PARTS
    factor = 1.0 / math.sqrt(dp_count * tensor_count * lengths.shape[2])
    relative = place ^ t

    def flat(p, c, z):
        return (p * cores + c) * tensor_count + z

    def stage(number, held):
        pairs, is_getter = [], jnp.zeros((), jnp.bool_)
        for c in range(cores):
            holders = [0]
            for before in range(number):
                bit = 1 << ((c + before) % levels)
                holders = holders + [q ^ bit for q in holders]
            bit = 1 << ((c + number) % levels)
            for q in holders:
                pairs += [
                    (flat(q ^ z, c, z), flat(q ^ bit ^ z, c, z)) for z in range(tensor_count)
                ]
                is_getter = is_getter | ((core == c) & (relative == (q ^ bit)))
        return lax.ppermute(held, AXES, pairs), is_getter

    first_got, first_getter = stage(0, pol_weight)

    steps = 4
    feature_step = block // steps
    at = jnp.stack([t, (1 - core) * (steps // 2)]).astype(jnp.int32)
    ref_shape = (tensor_count // 2, own_rows + POWER_ROWS, value_width)

    def at_step(f, at):
        return lax.rem(f + at[1], steps)

    rows_spec = pl.BlockSpec((group_rows, feature_step), lambda f, at: (0, at_step(f, at)))
    ref_kept, ref_sent = pl.pallas_call(
        functools.partial(reference_kernel, tensor_count, steps),
        grid_spec=pltpu.PrefetchScalarGridSpec(
            num_scalar_prefetch=1,
            grid=(steps,),
            in_specs=[
                rows_spec,
                pl.BlockSpec((1, feature_step), lambda f, at: (0, at_step(f, at))),
                pl.BlockSpec((feature_step, value_width), lambda f, at: (at_step(f, at), 0)),
            ],
            out_specs=[pl.BlockSpec(ref_shape, lambda f, at: (0, 0, 0))] * 2,
            scratch_shapes=[
                pltpu.VMEM((group_rows, feature_step), BF16),
                pltpu.VMEM((group_rows, value_width), F32),
                pltpu.VMEM((group_rows, 1), F32),
            ],
        ),
        out_shape=[jax.ShapeDtypeStruct(ref_shape, BF16)] * 2,
        compiler_params=pltpu.CompilerParams(vmem_limit_bytes=56 * 2**20),
        cost_estimate=pl.CostEstimate(
            flops=2 * group_rows * block * value_width,
            bytes_accessed=5 * 2**20,
            transcendentals=0,
        ),
        name="reference",
    )(at, tokens, ref_gain.reshape(1, block), ref_weight)
    ref_sent, tokens = lax.optimization_barrier((ref_sent, tokens))
    ref_got = crossed(ref_sent, tensor_count, 1)
    given_rows, kept_rows = pl.pallas_call(
        functools.partial(split_kernel, tensor_count, steps),
        grid_spec=pltpu.PrefetchScalarGridSpec(
            num_scalar_prefetch=1,
            grid=(steps,),
            in_specs=[
                rows_spec,
                pl.BlockSpec(
                    (1, feature_step), lambda f, at: (0, at[0] * steps + at_step(f, at))
                ),
            ],
            out_specs=[
                pl.BlockSpec(
                    (group_rows, feature_step), lambda f, at: (0, jnp.minimum(f, steps // 2 - 1))
                ),
                pl.BlockSpec(
                    (group_rows, feature_step), lambda f, at: (0, jnp.maximum(f - steps // 2, 0))
                ),
            ],
        ),
        out_shape=[jax.ShapeDtypeStruct((group_rows, shard), BF16)] * 2,
        compiler_params=pltpu.CompilerParams(vmem_limit_bytes=56 * 2**20),
        cost_estimate=pl.CostEstimate(
            flops=group_rows * block, bytes_accessed=4 * 2**20, transcendentals=0
        ),
        name="split",
    )(at, tokens, pol_gain.reshape(1, model_width))
    got_rows = swapped(given_rows, dp_count)

    held, got, is_getter = pol_weight, first_got, first_getter
    cot = cotangent.reshape(slot_count, value_width)
    for number in range(1, levels):
        held = jnp.where(is_getter, got, held)
        if number == 1:
            tied = lax.optimization_barrier((held, kept_rows, ref_got, cot))
            held, kept_rows, ref_got, cot = tied
        got, is_getter = stage(number, held)
    for level in range(1, levels):
        ref_sum = ref_kept[:, :own_rows].astype(F32) + ref_got[:, :own_rows].astype(F32)
        ref_all = jnp.concatenate(
            [ref_sum.astype(BF16), ref_kept[:, own_rows:], ref_got[:, own_rows:]], axis=1
        )
        half_count = ref_all.shape[0] // 2
        ref_kept = ref_all[:half_count]
        ref_got = crossed(ref_all[half_count:], tensor_count, 1 << level)
    got_cot = lax.all_to_all(cot, "dp", split_axis=0, concat_axis=0, tiled=True)

    def plane_bit(level):
        return jnp.where(core == 0, 1 << (level % levels), 1 << ((1 + level) % levels))

    chunk_at = []
    for i in range(places):
        away = sum(plane_bit(level) * ((i >> (levels - 1 - level)) & 1) for level in range(levels))
        chunk_at.append(place ^ away ^ turned(t, levels))
    chunk_at = jnp.stack(chunk_at).astype(jnp.int32)

    smem = pl.BlockSpec(memory_space=pltpu.SMEM)
    vmem = pl.BlockSpec(memory_space=pltpu.VMEM)
    value_kept, value_got = [], []
    for j in range(PARTS):
        cols = slice(j * width, (j + 1) * width)
        weight = lax.optimization_barrier(jnp.where(is_getter, got[:, cols], held[:, cols]))
        value_got.append(swapped(dot(got_rows, weight).astype(BF16), dp_count))
        value_kept.append(dot(kept_rows, weight))
    fixed, pull, row_scale, row_at, terms_sent = pl.pallas_call(
        functools.partial(row_kernel, span_rows, model_width),
        in_specs=[smem] * 3 + [vmem] * 4,
        out_specs=[vmem] * 5,
        out_shape=[
            jax.ShapeDtypeStruct((own_rows, value_width), F32),
            jax.ShapeDtypeStruct((own_rows, 128), F32),
            jax.ShapeDtypeStruct((own_rows, 128), F32),
            jax.ShapeDtypeStruct((own_rows, slot_count), BF16),
            jax.ShapeDtypeStruct((own_rows, value_width + 128), BF16),
        ],
        compiler_params=pltpu.CompilerParams(vmem_limit_bytes=16 * 2**20),
        cost_estimate=pl.CostEstimate(
            flops=2 * own_rows * slot_count * value_width,
            bytes_accessed=2**21,
            transcendentals=0,
        ),
        name="rows",
    )(
        lengths.reshape(-1),
        bins.reshape(-1),
        advantage.reshape(-1),
        logprob_gap.reshape(1, own_rows),
        got_cot,
        ref_kept[0],
        ref_got[0],
    )
    far = 1 << (levels - 1)
    terms_got = crossed(terms_sent, tensor_count, far)

    values, slopes = [], []
    for j in range(PARTS):
        cols = slice(j * width, (j + 1) * width)
        total = value_kept[j] + value_got[j].astype(F32)
        for level in range(levels - 1):
            rows = total.shape[0] // 2
            total = total[:rows] + crossed(
                total[rows:].astype(BF16), tensor_count, 1 << level
            ).astype(F32)
        if j == 0:
            total, terms_got = lax.optimization_barrier((total, terms_got))
            terms_got = terms_got.astype(F32)
            pull_got = terms_got[:, value_width : value_width + 1] + terms_got[:, -1:]
            fixed = jnp.concatenate([fixed, terms_got[:, :value_width]], axis=0)
            pull = jnp.concatenate([pull[:, :1], pull_got], axis=0)
        other = jnp.concatenate([total[own_rows:], total[:own_rows]], axis=0).astype(BF16)
        total = total + crossed(other, tensor_count, far).astype(F32)
        values.append(total[:own_rows] * row_scale[:, :1])

        slope = (fixed[:, cols] + pull * total).astype(BF16)
        if j < PARTS - 1:
            slope, fixed, pull = lax.optimization_barrier((slope, fixed, pull))
        else:
            slope, *values = lax.optimization_barrier((slope, *values))
        for level in reversed(range(levels - 1)):
            slope = jnp.concatenate([slope, crossed(slope, tensor_count, 1 << level)], axis=0)
        slopes.append(slope)

    sent = dot_rows(row_at, jnp.concatenate(values, axis=1).astype(BF16)).astype(BF16)
    policy_values = lax.all_to_all(sent, "dp", split_axis=0, concat_axis=0, tiled=True)

    grad_kept, grad_sent = [], []
    for j in range(PARTS):
        slopes_got = swapped(slopes[j], dp_count)
        chunks = pl.pallas_call(
            functools.partial(grad_kernel, factor),
            grid_spec=pltpu.PrefetchScalarGridSpec(
                num_scalar_prefetch=1,
                grid=(1,),
                in_specs=[
                    pl.BlockSpec((group_rows, shard), lambda i, at: (0, 0)),
                    pl.BlockSpec((group_rows, shard), lambda i, at: (0, 0)),
                    pl.BlockSpec((group_rows, width), lambda i, at: (0, 0)),
                    pl.BlockSpec((group_rows, width), lambda i, at: (0, 0)),
                ],
                out_specs=[pl.BlockSpec((shard // 2, width), lambda i, at: (0, 0))] * 2,
                scratch_shapes=[pltpu.VMEM((shard, width), F32)],
            ),
            out_shape=[
                jax.ShapeDtypeStruct((shard // 2, width), F32),
                jax.ShapeDtypeStruct((shard // 2, width), BF16),
            ],
            compiler_params=pltpu.CompilerParams(vmem_limit_bytes=32 * 2**20),
            cost_estimate=pl.CostEstimate(
                flops=4 * group_rows * shard * width,
                bytes_accessed=4 * 2**20,
                transcendentals=0,
            ),
            name="gradient",
        )(chunk_at, kept_rows, got_rows, slopes[j], slopes_got)
        grad_kept.append(chunks[0])
        grad_sent.append(chunks[1])
    grad_sent[-1], policy_values = lax.optimization_barrier((grad_sent[-1], policy_values))
    grads = []
    for j in range(PARTS):
        total, given = grad_kept[j], grad_sent[j]
        for level in range(levels):
            pairs = [
                (p * cores + c, (p ^ (1 << ((c + level) % levels))) * cores + c)
                for p in range(places)
                for c in range(cores)
            ]
            total = total + lax.ppermute(given, "dp", pairs).astype(F32)
            half_rows = total.shape[0] // 2
            if level < levels - 1:
                total, given = total[:half_rows], total[half_rows:].astype(BF16)
        grads.append(total.astype(BF16))
    pairs = [
        (flat(p, c, z), flat(z, c, p ^ turned(z, levels)))
        for p in range(places)
        for c in range(cores)
        for z in range(tensor_count)
    ]
    grad_weight = lax.ppermute(jnp.concatenate(grads, axis=1), AXES, pairs).astype(F32)
    return (policy_values.reshape(1, 1, slot_count, value_width), grad_weight)


def solution(mesh):
    in_specs = (
        P("dp", "tensor"),
        P("tensor"),
        P("tensor", None),
        P(),
        P("dp", None),
        P("dp", "tensor", None),
        P("dp", "tensor", None),
        P("dp", "tensor", None),
        P(("dp", "tensor")),
        P("dp", "tensor", None, None),
    )
    out_specs = (P("dp", "tensor", None, None), P(("dp", "tensor"), None))
    return jax.shard_map(
        on_device, mesh=mesh, in_specs=in_specs, out_specs=out_specs, check_vma=False
    )
```

```python
import functools
import math

import jax
import jax.numpy as jnp
from jax import lax
from jax.experimental import pallas as pl
from jax.experimental.pallas import tpu as pltpu
from jax.sharding import PartitionSpec as P

EPS = 1e-06
BETA = 1.0
AXES = ("dp", "tensor")
BF16 = jnp.bfloat16
F32 = jnp.float32
POWER_ROWS = 16
PARTS = 2


def dot(a, b):
    return jnp.dot(a, b, preferred_element_type=F32)


def dot_rows(a, b):
    return lax.dot_general(a, b, (((0,), (0,)), ((), ())), preferred_element_type=F32)


def swapped(array, dp_count):
    return lax.ppermute(array, "dp", [(i, i ^ 1) for i in range(dp_count)])


def turned(index, levels):
    return sum(((index >> i) & 1) << (levels - 1 - i) for i in range(levels))


def crossed(array, count, step):
    return lax.ppermute(array, "tensor", [(i, i ^ step) for i in range(count)])


def chunk_start(count, at, own, i):
    source = jnp.bitwise_xor(at[0], turned(i, count.bit_length() - 1))
    return pl.multiple_of(source * own, own)


def split_kernel(count, steps, at, x_ref, gain_ref, given_ref, kept_ref):
    f = pl.program_id(0)
    own = x_ref.shape[0] // count

    def fill(out_ref):
        for i in range(count):
            rows = x_ref[pl.ds(chunk_start(count, at, own, i), own), :].astype(F32)
            out_ref[i * own : (i + 1) * own, :] = (rows * gain_ref[...]).astype(BF16)

    @pl.when(f < steps // 2)
    def _():
        fill(given_ref)

    @pl.when(f >= steps // 2)
    def _():
        fill(kept_ref)


def reference_kernel(
    count, steps, at, x_ref, gain_ref, weight_ref, kept_ref, sent_ref, rows_ref, total, square
):
    f = pl.program_id(0)
    own = x_ref.shape[0] // count

    @pl.when(f == 0)
    def _():
        square[...] = jnp.zeros_like(square)

    for i in range(count):
        wide = x_ref[pl.ds(chunk_start(count, at, own, i), own), :].astype(F32)
        rows_ref[i * own : (i + 1) * own, :] = (wide * gain_ref[...]).astype(BF16)
        square[i * own : (i + 1) * own, :] += jnp.sum(wide * wide, axis=1, keepdims=True)
    part = dot(rows_ref[...], weight_ref[...])

    @pl.when(f == 0)
    def _():
        total[...] = part

    @pl.when(f > 0)
    def _():
        total[...] += part

    @pl.when(f == steps - 1)
    def _():
        for i in range(count):
            out = (kept_ref, sent_ref)[i // (count // 2)].at[i % (count // 2)]
            out[:own, :] = total[i * own : (i + 1) * own, :].astype(BF16)
            power = jnp.broadcast_to(square[i * own : (i + 1) * own, :], (own, 128)).T
            high = power[: POWER_ROWS // 2].astype(BF16).astype(F32)
            low = power[: POWER_ROWS // 2] - high
            out[own:, :] = jnp.zeros((POWER_ROWS, out.shape[1]), BF16)
            out[own:, :own] = jnp.concatenate([high, low], axis=0).astype(BF16)


def row_kernel(
    span, model_width, lengths, bins, advantage, gap_ref, cot_ref, kept_ref, got_ref, *refs
):
    fixed_ref, pull_ref, scale_ref, row_at_ref, sent_ref = refs
    own = pull_ref.shape[0]
    slots = row_at_ref.shape[1]
    row = lax.broadcasted_iota(jnp.int32, (own, slots), 0)
    slot = lax.broadcasted_iota(jnp.int32, (own, slots), 1)
    chosen = jnp.zeros((own, slots), jnp.bool_)
    size = jnp.ones((own, 128), F32)
    weight = jnp.zeros((own, 128), F32)
    start = jnp.int32(0)
    for s in range(lengths.shape[0]):
        end = start + lengths[s]
        inside = (row >= start) & (row < end)
        chosen = chosen | (inside & (slot - bins[s] * span == row - start))
        size = jnp.where(inside[:, :128], lengths[s].astype(F32), size)
        weight = jnp.where(inside[:, :128], advantage[s], weight)
        start = end
    row_at = jnp.where(chosen, 1.0, 0.0).astype(BF16)
    row_at_ref[...] = row_at
    importance = jnp.minimum(jnp.exp(jnp.broadcast_to(gap_ref[...], (128, own)).T), 2.0)
    coef_adv = (weight * importance / size).astype(BF16).astype(F32)
    coef_pull = (BETA / size).astype(BF16).astype(F32)
    total = kept_ref[...].astype(F32) + got_ref[...].astype(F32)
    square = jnp.zeros((1, own), F32)
    for power_row in range(own, total.shape[0], POWER_ROWS // 2):
        square = square + total[power_row : power_row + 1, :own]
    scale = lax.rsqrt(jnp.broadcast_to(square, (128, own)).T / model_width + EPS)
    reference = (total[:own] * scale[:, :1]).astype(BF16).astype(F32)
    upstream = dot(row_at, cot_ref[...])
    fixed = (coef_adv[:, :1] * upstream - coef_pull[:, :1] * reference) * scale[:, :1]
    pull = coef_pull * scale * scale
    high = pull.astype(BF16).astype(F32)
    width = fixed.shape[1]
    fixed_ref[...] = fixed
    pull_ref[...] = pull
    scale_ref[...] = scale
    sent_ref[:, :width] = fixed.astype(BF16)
    lane = lax.broadcasted_iota(jnp.int32, pull.shape, 1)
    sent_ref[:, width:] = jnp.where(lane < 64, high, pull - high).astype(BF16)


def grad_kernel(factor, at, kept_ref, got_ref, slope_ref, slope_got_ref, *refs):
    *out_refs, grad = refs
    total = dot_rows(kept_ref[...], slope_ref[...]) + dot_rows(got_ref[...], slope_got_ref[...])
    grad[...] = total * factor
    rows = grad.shape[0] // at.shape[0]
    count = at.shape[0] // 2
    for s in range(2 * count):
        chunk = grad[pl.ds(pl.multiple_of(at[s] * rows, rows), rows), :]
        out_ref = out_refs[s // count]
        place = s % count
        out_ref[place * rows : (place + 1) * rows, :] = chunk.astype(out_ref.dtype)


def on_device(
    tokens,
    ref_gain,
    ref_weight,
    pol_gain,
    pol_weight,
    lengths,
    bins,
    advantage,
    logprob_gap,
    cotangent,
):
    tensor_count = lax.axis_size("tensor")
    dp_count = lax.axis_size("dp")
    t = lax.axis_index("tensor")
    d = lax.axis_index("dp")
    cores = dp_count // tensor_count
    assert cores == 2
    places = dp_count // cores
    levels = places.bit_length() - 1
    assert 1 << levels == places == tensor_count
    place = d // cores
    core = d % cores
    group_rows, block = tokens.shape
    own_rows = group_rows // tensor_count
    slot_count = cotangent.shape[2]
    span_rows = slot_count // dp_count
    value_width = ref_weight.shape[1]
    model_width = pol_gain.shape[0]
    shard = pol_weight.shape[0]
    width = value_width // PARTS
    factor = 1.0 / math.sqrt(dp_count * tensor_count * lengths.shape[2])
    relative = place ^ t

    def flat(p, c, z):
        return (p * cores + c) * tensor_count + z

    def stage(number, held):
        pairs, is_getter = [], jnp.zeros((), jnp.bool_)
        for c in range(cores):
            holders = [0]
            for before in range(number):
                bit = 1 << ((c + before) % levels)
                holders = holders + [q ^ bit for q in holders]
            bit = 1 << ((c + number) % levels)
            for q in holders:
                pairs += [
                    (flat(q ^ z, c, z), flat(q ^ bit ^ z, c, z)) for z in range(tensor_count)
                ]
                is_getter = is_getter | ((core == c) & (relative == (q ^ bit)))
        return lax.ppermute(held, AXES, pairs), is_getter

    first_got, first_getter = stage(0, pol_weight)

    steps = 4
    feature_step = block // steps
    at = jnp.stack([t, (1 - core) * (steps // 2)]).astype(jnp.int32)
    ref_shape = (tensor_count // 2, own_rows + POWER_ROWS, value_width)

    def at_step(f, at):
        return lax.rem(f + at[1], steps)

    rows_spec = pl.BlockSpec((group_rows, feature_step), lambda f, at: (0, at_step(f, at)))
    ref_kept, ref_sent = pl.pallas_call(
        functools.partial(reference_kernel, tensor_count, steps),
        grid_spec=pltpu.PrefetchScalarGridSpec(
            num_scalar_prefetch=1,
            grid=(steps,),
            in_specs=[
                rows_spec,
                pl.BlockSpec((1, feature_step), lambda f, at: (0, at_step(f, at))),
                pl.BlockSpec((feature_step, value_width), lambda f, at: (at_step(f, at), 0)),
            ],
            out_specs=[pl.BlockSpec(ref_shape, lambda f, at: (0, 0, 0))] * 2,
            scratch_shapes=[
                pltpu.VMEM((group_rows, feature_step), BF16),
                pltpu.VMEM((group_rows, value_width), F32),
                pltpu.VMEM((group_rows, 1), F32),
            ],
        ),
        out_shape=[jax.ShapeDtypeStruct(ref_shape, BF16)] * 2,
        compiler_params=pltpu.CompilerParams(vmem_limit_bytes=56 * 2**20),
        cost_estimate=pl.CostEstimate(
            flops=2 * group_rows * block * value_width,
            bytes_accessed=5 * 2**20,
            transcendentals=0,
        ),
        name="reference",
    )(at, tokens, ref_gain.reshape(1, block), ref_weight)
    ref_sent, tokens = lax.optimization_barrier((ref_sent, tokens))
    ref_got = crossed(ref_sent, tensor_count, 1)
    given_rows, kept_rows = pl.pallas_call(
        functools.partial(split_kernel, tensor_count, steps),
        grid_spec=pltpu.PrefetchScalarGridSpec(
            num_scalar_prefetch=1,
            grid=(steps,),
            in_specs=[
                rows_spec,
                pl.BlockSpec(
                    (1, feature_step), lambda f, at: (0, at[0] * steps + at_step(f, at))
                ),
            ],
            out_specs=[
                pl.BlockSpec(
                    (group_rows, feature_step), lambda f, at: (0, jnp.minimum(f, steps // 2 - 1))
                ),
                pl.BlockSpec(
                    (group_rows, feature_step), lambda f, at: (0, jnp.maximum(f - steps // 2, 0))
                ),
            ],
        ),
        out_shape=[jax.ShapeDtypeStruct((group_rows, shard), BF16)] * 2,
        compiler_params=pltpu.CompilerParams(vmem_limit_bytes=56 * 2**20),
        cost_estimate=pl.CostEstimate(
            flops=group_rows * block, bytes_accessed=4 * 2**20, transcendentals=0
        ),
        name="split",
    )(at, tokens, pol_gain.reshape(1, model_width))
    got_rows = swapped(given_rows, dp_count)

    held, got, is_getter = pol_weight, first_got, first_getter
    cot = cotangent.reshape(slot_count, value_width)
    for number in range(1, levels):
        held = jnp.where(is_getter, got, held)
        if number == 1:
            held, kept_rows, ref_got = lax.optimization_barrier((held, kept_rows, ref_got))
        got, is_getter = stage(number, held)
    for level in range(1, levels):
        ref_sum = ref_kept[:, :own_rows].astype(F32) + ref_got[:, :own_rows].astype(F32)
        ref_all = jnp.concatenate(
            [ref_sum.astype(BF16), ref_kept[:, own_rows:], ref_got[:, own_rows:]], axis=1
        )
        ref_all, cot = lax.optimization_barrier((ref_all, cot))
        half_count = ref_all.shape[0] // 2
        ref_kept = ref_all[:half_count]
        ref_got = crossed(ref_all[half_count:], tensor_count, 1 << level)
    got_cot = lax.all_to_all(cot, "dp", split_axis=0, concat_axis=0, tiled=True)

    def plane_bit(level):
        return jnp.where(core == 0, 1 << (level % levels), 1 << ((1 + level) % levels))

    chunk_at = []
    for i in range(places):
        away = sum(plane_bit(level) * ((i >> (levels - 1 - level)) & 1) for level in range(levels))
        chunk_at.append(place ^ away ^ turned(t, levels))
    chunk_at = jnp.stack(chunk_at).astype(jnp.int32)

    smem = pl.BlockSpec(memory_space=pltpu.SMEM)
    vmem = pl.BlockSpec(memory_space=pltpu.VMEM)
    value_kept, value_got = [], []
    for j in range(PARTS):
        cols = slice(j * width, (j + 1) * width)
        weight = lax.optimization_barrier(jnp.where(is_getter, got[:, cols], held[:, cols]))
        value_given = dot(got_rows, weight).astype(BF16)
        if j == PARTS - 1:
            tied = lax.optimization_barrier((value_given, lengths, bins, advantage, logprob_gap))
            value_given, lengths, bins, advantage, logprob_gap = tied
        value_got.append(swapped(value_given, dp_count))
        value_kept.append(dot(kept_rows, weight))
    fixed, pull, row_scale, row_at, terms_sent = pl.pallas_call(
        functools.partial(row_kernel, span_rows, model_width),
        in_specs=[smem] * 3 + [vmem] * 4,
        out_specs=[vmem] * 5,
        out_shape=[
            jax.ShapeDtypeStruct((own_rows, value_width), F32),
            jax.ShapeDtypeStruct((own_rows, 128), F32),
            jax.ShapeDtypeStruct((own_rows, 128), F32),
            jax.ShapeDtypeStruct((own_rows, slot_count), BF16),
            jax.ShapeDtypeStruct((own_rows, value_width + 128), BF16),
        ],
        compiler_params=pltpu.CompilerParams(vmem_limit_bytes=16 * 2**20),
        cost_estimate=pl.CostEstimate(
            flops=2 * own_rows * slot_count * value_width,
            bytes_accessed=2**21,
            transcendentals=0,
        ),
        name="rows",
    )(
        lengths.reshape(-1),
        bins.reshape(-1),
        advantage.reshape(-1),
        logprob_gap.reshape(1, own_rows),
        got_cot,
        ref_kept[0],
        ref_got[0],
    )
    far = 1 << (levels - 1)
    terms_got = crossed(terms_sent, tensor_count, far)

    values, slopes = [], []
    for j in range(PARTS):
        cols = slice(j * width, (j + 1) * width)
        total = value_kept[j] + value_got[j].astype(F32)
        for level in range(levels - 1):
            rows = total.shape[0] // 2
            total = total[:rows] + crossed(
                total[rows:].astype(BF16), tensor_count, 1 << level
            ).astype(F32)
        if j == 0:
            total, terms_got = lax.optimization_barrier((total, terms_got))
            terms_got = terms_got.astype(F32)
            pull_got = terms_got[:, value_width : value_width + 1] + terms_got[:, -1:]
            fixed = jnp.concatenate([fixed, terms_got[:, :value_width]], axis=0)
            pull = jnp.concatenate([pull[:, :1], pull_got], axis=0)
        other = jnp.concatenate([total[own_rows:], total[:own_rows]], axis=0).astype(BF16)
        total = total + crossed(other, tensor_count, far).astype(F32)
        values.append(total[:own_rows] * row_scale[:, :1])

        slope = (fixed[:, cols] + pull * total).astype(BF16)
        if j < PARTS - 1:
            slope, fixed, pull = lax.optimization_barrier((slope, fixed, pull))
        else:
            slope, *values = lax.optimization_barrier((slope, *values))
        for level in reversed(range(levels - 1)):
            slope = jnp.concatenate([slope, crossed(slope, tensor_count, 1 << level)], axis=0)
        slopes.append(slope)

    sent = dot_rows(row_at, jnp.concatenate(values, axis=1).astype(BF16)).astype(BF16)
    policy_values = lax.all_to_all(sent, "dp", split_axis=0, concat_axis=0, tiled=True)

    grad_kept, grad_sent = [], []
    for j in range(PARTS):
        slopes_got = swapped(slopes[j], dp_count)
        if j == PARTS - 1:
            slopes_got, policy_values = lax.optimization_barrier((slopes_got, policy_values))
        chunks = pl.pallas_call(
            functools.partial(grad_kernel, factor),
            grid_spec=pltpu.PrefetchScalarGridSpec(
                num_scalar_prefetch=1,
                grid=(1,),
                in_specs=[
                    pl.BlockSpec((group_rows, shard), lambda i, at: (0, 0)),
                    pl.BlockSpec((group_rows, shard), lambda i, at: (0, 0)),
                    pl.BlockSpec((group_rows, width), lambda i, at: (0, 0)),
                    pl.BlockSpec((group_rows, width), lambda i, at: (0, 0)),
                ],
                out_specs=[pl.BlockSpec((shard // 2, width), lambda i, at: (0, 0))] * 2,
                scratch_shapes=[pltpu.VMEM((shard, width), F32)],
            ),
            out_shape=[
                jax.ShapeDtypeStruct((shard // 2, width), F32),
                jax.ShapeDtypeStruct((shard // 2, width), BF16),
            ],
            compiler_params=pltpu.CompilerParams(vmem_limit_bytes=32 * 2**20),
            cost_estimate=pl.CostEstimate(
                flops=4 * group_rows * shard * width,
                bytes_accessed=4 * 2**20,
                transcendentals=0,
            ),
            name="gradient",
        )(chunk_at, kept_rows, got_rows, slopes[j], slopes_got)
        grad_kept.append(chunks[0])
        grad_sent.append(chunks[1])
    grads = []
    for j in range(PARTS):
        total, given = grad_kept[j], grad_sent[j]
        for level in range(levels):
            pairs = [
                (p * cores + c, (p ^ (1 << ((c + level) % levels))) * cores + c)
                for p in range(places)
                for c in range(cores)
            ]
            total = total + lax.ppermute(given, "dp", pairs).astype(F32)
            half_rows = total.shape[0] // 2
            if level < levels - 1:
                total, given = total[:half_rows], total[half_rows:].astype(BF16)
        grads.append(total.astype(BF16))
    pairs = [
        (flat(p, c, z), flat(z, c, p ^ turned(z, levels)))
        for p in range(places)
        for c in range(cores)
        for z in range(tensor_count)
    ]
    grad_weight = lax.ppermute(jnp.concatenate(grads, axis=1), AXES, pairs).astype(F32)
    return (policy_values.reshape(1, 1, slot_count, value_width), grad_weight)


def solution(mesh):
    in_specs = (
        P("dp", "tensor"),
        P("tensor"),
        P("tensor", None),
        P(),
        P("dp", None),
        P("dp", "tensor", None),
        P("dp", "tensor", None),
        P("dp", "tensor", None),
        P(("dp", "tensor")),
        P("dp", "tensor", None, None),
    )
    out_specs = (P("dp", "tensor", None, None), P(("dp", "tensor"), None))
    return jax.shard_map(
        on_device, mesh=mesh, in_specs=in_specs, out_specs=out_specs, check_vma=False
    )
```

```python
import functools
import math

import jax
import jax.numpy as jnp
from jax import lax
from jax.experimental import pallas as pl
from jax.experimental.pallas import tpu as pltpu
from jax.sharding import PartitionSpec as P

EPS = 1e-06
BETA = 1.0
AXES = ("dp", "tensor")
BF16 = jnp.bfloat16
F32 = jnp.float32
POWER_ROWS = 16
PARTS = 2


def dot(a, b):
    return jnp.dot(a, b, preferred_element_type=F32)


def dot_rows(a, b):
    return lax.dot_general(a, b, (((0,), (0,)), ((), ())), preferred_element_type=F32)


def swapped(array, dp_count):
    return lax.ppermute(array, "dp", [(i, i ^ 1) for i in range(dp_count)])


def turned(index, levels):
    return sum(((index >> i) & 1) << (levels - 1 - i) for i in range(levels))


def crossed(array, count, step):
    return lax.ppermute(array, "tensor", [(i, i ^ step) for i in range(count)])


def prepare_kernel(
    count, steps, at, x_ref, gain_ref, weight_ref, pol_ref, given_ref, kept_ref, *refs
):
    sent_refs, (rows_ref, total, square) = refs[:count], refs[count:]
    f = pl.program_id(0)
    own = x_ref.shape[0] // count
    levels = count.bit_length() - 1
    for i in range(count):
        source = jnp.bitwise_xor(at[0], turned(i, levels))
        rows_ref[i * own : (i + 1) * own, :] = x_ref[pl.ds(pl.multiple_of(source * own, own), own), :]
    wide = rows_ref[...].astype(F32)
    gained = (wide * pol_ref[...]).astype(BF16)

    @pl.when(f < steps // 2)
    def _():
        given_ref[...] = gained

    @pl.when(f >= steps // 2)
    def _():
        kept_ref[...] = gained

    part = dot((wide * gain_ref[...]).astype(BF16), weight_ref[...])
    squares = jnp.sum(wide * wide, axis=1, keepdims=True)

    @pl.when(f == 0)
    def _():
        total[...] = part
        square[...] = squares

    @pl.when(f > 0)
    def _():
        total[...] += part
        square[...] += squares

    @pl.when(f == steps - 1)
    def _():
        for i in range(count):
            sent = sent_refs[turned(i, levels)]
            sent[:own, :] = total[i * own : (i + 1) * own, :].astype(BF16)
            power = jnp.broadcast_to(square[i * own : (i + 1) * own, :], (own, 128)).T
            high = power[: POWER_ROWS // 2].astype(BF16).astype(F32)
            low = power[: POWER_ROWS // 2] - high
            sent[own:, :] = jnp.zeros((POWER_ROWS, sent.shape[1]), BF16)
            sent[own:, :own] = jnp.concatenate([high, low], axis=0).astype(BF16)


def row_kernel(
    count, span, model_width, lengths, bins, advantage, gap_ref, cot_ref, *refs
):
    ref_refs, (fixed_ref, pull_ref, scale_ref, row_at_ref) = refs[:count], refs[count:]
    own = pull_ref.shape[0]
    slots = row_at_ref.shape[1]
    row = lax.broadcasted_iota(jnp.int32, (own, slots), 0)
    slot = lax.broadcasted_iota(jnp.int32, (own, slots), 1)
    chosen = jnp.zeros((own, slots), jnp.bool_)
    size = jnp.ones((own, 128), F32)
    weight = jnp.zeros((own, 128), F32)
    start = jnp.int32(0)
    for s in range(lengths.shape[0]):
        end = start + lengths[s]
        inside = (row >= start) & (row < end)
        chosen = chosen | (inside & (slot - bins[s] * span == row - start))
        size = jnp.where(inside[:, :128], lengths[s].astype(F32), size)
        weight = jnp.where(inside[:, :128], advantage[s], weight)
        start = end
    row_at = jnp.where(chosen, 1.0, 0.0).astype(BF16)
    row_at_ref[...] = row_at
    importance = jnp.minimum(jnp.exp(jnp.broadcast_to(gap_ref[...], (128, own)).T), 2.0)
    coef_adv = (weight * importance / size).astype(BF16).astype(F32)
    coef_pull = (BETA / size).astype(BF16).astype(F32)
    total = ref_refs[0][...].astype(F32)
    for ref in ref_refs[1:]:
        total = total + ref[...].astype(F32)
    half = POWER_ROWS // 2
    square = total[own : own + 1, :own] + total[own + half : own + half + 1, :own]
    scale = lax.rsqrt(jnp.broadcast_to(square, (128, own)).T / model_width + EPS)
    reference = (total[:own] * scale[:, :1]).astype(BF16).astype(F32)
    upstream = dot(row_at, cot_ref[...])
    fixed_ref[...] = (coef_adv[:, :1] * upstream - coef_pull[:, :1] * reference) * scale[:, :1]
    pull_ref[...] = coef_pull * scale * scale
    scale_ref[...] = scale


def grad_kernel(factor, at, kept_ref, got_ref, slope_ref, slope_got_ref, *refs):
    *out_refs, grad = refs
    total = dot_rows(kept_ref[...], slope_ref[...]) + dot_rows(got_ref[...], slope_got_ref[...])
    grad[...] = total * factor
    rows = grad.shape[0] // at.shape[0]
    count = at.shape[0] // 2
    for s in range(2 * count):
        chunk = grad[pl.ds(pl.multiple_of(at[s] * rows, rows), rows), :]
        out_ref = out_refs[s // count]
        place = s % count
        out_ref[place * rows : (place + 1) * rows, :] = chunk.astype(out_ref.dtype)


def on_device(
    tokens,
    ref_gain,
    ref_weight,
    pol_gain,
    pol_weight,
    lengths,
    bins,
    advantage,
    logprob_gap,
    cotangent,
):
    tensor_count = lax.axis_size("tensor")
    dp_count = lax.axis_size("dp")
    t = lax.axis_index("tensor")
    d = lax.axis_index("dp")
    cores = dp_count // tensor_count
    assert cores == 2
    places = dp_count // cores
    levels = places.bit_length() - 1
    assert 1 << levels == places == tensor_count
    place = d // cores
    core = d % cores
    group_rows, block = tokens.shape
    own_rows = group_rows // tensor_count
    slot_count = cotangent.shape[2]
    span_rows = slot_count // dp_count
    value_width = ref_weight.shape[1]
    model_width = pol_gain.shape[0]
    shard = pol_weight.shape[0]
    width = value_width // PARTS
    factor = 1.0 / math.sqrt(dp_count * tensor_count * lengths.shape[2])
    relative = place ^ t

    def flat(p, c, z):
        return (p * cores + c) * tensor_count + z

    def stage(number, held):
        pairs, is_getter = [], jnp.zeros((), jnp.bool_)
        for c in range(cores):
            holders = [0]
            for before in range(number):
                bit = 1 << ((c + before) % levels)
                holders = holders + [q ^ bit for q in holders]
            bit = 1 << ((c + number) % levels)
            for q in holders:
                pairs += [
                    (flat(q ^ z, c, z), flat(q ^ bit ^ z, c, z)) for z in range(tensor_count)
                ]
                is_getter = is_getter | ((core == c) & (relative == (q ^ bit)))
        return lax.ppermute(held, AXES, pairs), is_getter

    got, is_getter = stage(0, pol_weight)

    steps = 4
    feature_step = block // steps
    at = jnp.stack([t, (1 - core) * (steps // 2)]).astype(jnp.int32)
    sent_shape = (own_rows + POWER_ROWS, value_width)

    def at_step(f, at):
        return lax.rem(f + at[1], steps)

    prepared = pl.pallas_call(
        functools.partial(prepare_kernel, tensor_count, steps),
        grid_spec=pltpu.PrefetchScalarGridSpec(
            num_scalar_prefetch=1,
            grid=(steps,),
            in_specs=[
                pl.BlockSpec((group_rows, feature_step), lambda f, at: (0, at_step(f, at))),
                pl.BlockSpec((1, feature_step), lambda f, at: (0, at_step(f, at))),
                pl.BlockSpec((feature_step, value_width), lambda f, at: (at_step(f, at), 0)),
                pl.BlockSpec(
                    (1, feature_step), lambda f, at: (0, at[0] * steps + at_step(f, at))
                ),
            ],
            out_specs=[
                pl.BlockSpec(
                    (group_rows, feature_step), lambda f, at: (0, jnp.minimum(f, steps // 2 - 1))
                ),
                pl.BlockSpec(
                    (group_rows, feature_step), lambda f, at: (0, jnp.maximum(f - steps // 2, 0))
                ),
            ]
            + [pl.BlockSpec(sent_shape, lambda f, at: (0, 0))] * tensor_count,
            scratch_shapes=[
                pltpu.VMEM((group_rows, feature_step), BF16),
                pltpu.VMEM((group_rows, value_width), F32),
                pltpu.VMEM((group_rows, 1), F32),
            ],
        ),
        out_shape=[jax.ShapeDtypeStruct((group_rows, shard), BF16)] * 2
        + [jax.ShapeDtypeStruct(sent_shape, BF16)] * tensor_count,
        compiler_params=pltpu.CompilerParams(vmem_limit_bytes=56 * 2**20),
        cost_estimate=pl.CostEstimate(
            flops=2 * group_rows * block * value_width,
            bytes_accessed=8 * 2**20,
            transcendentals=0,
        ),
        name="prepare",
    )(at, tokens, ref_gain.reshape(1, block), ref_weight, pol_gain.reshape(1, model_width))
    given_rows, kept_rows, *ref_sent = prepared

    ref_got = [ref_sent[0]] + [
        crossed(ref_sent[k], tensor_count, k) for k in range(1, tensor_count)
    ]
    got_rows = swapped(given_rows, dp_count)

    cot = cotangent.reshape(slot_count, value_width)
    got, cot, kept_rows = lax.optimization_barrier((got, cot, kept_rows))
    parts = []
    for j in range(PARTS):
        cols = slice(j * width, (j + 1) * width)
        held_part = jnp.where(is_getter, got[:, cols], pol_weight[:, cols])
        for number in range(1, levels):
            got_part, is_getter_part = stage(number, held_part)
            if number < levels - 1:
                held_part = jnp.where(is_getter_part, got_part, held_part)
        parts.append((held_part, got_part, is_getter_part))
    got_cot = lax.all_to_all(cot, "dp", split_axis=0, concat_axis=0, tiled=True)

    def plane_bit(level):
        return jnp.where(core == 0, 1 << (level % levels), 1 << ((1 + level) % levels))

    chunk_at = []
    for i in range(places):
        away = sum(plane_bit(level) * ((i >> (levels - 1 - level)) & 1) for level in range(levels))
        chunk_at.append(place ^ away ^ turned(t, levels))
    chunk_at = jnp.stack(chunk_at).astype(jnp.int32)

    values, slopes = [], []
    for j in range(PARTS):
        held_part, got_part, is_getter_part = parts[j]
        if j == 0:
            got_part, got_cot, *ref_got = lax.optimization_barrier((got_part, got_cot, *ref_got))
        weight = jnp.where(is_getter_part, got_part, held_part)
        value_given = dot(got_rows, weight).astype(BF16)
        if j == 0:
            smem = pl.BlockSpec(memory_space=pltpu.SMEM)
            vmem = pl.BlockSpec(memory_space=pltpu.VMEM)
            fixed, pull, row_scale, row_at = pl.pallas_call(
                functools.partial(row_kernel, tensor_count, span_rows, model_width),
                in_specs=[smem] * 3 + [vmem] * (2 + tensor_count),
                out_specs=[vmem] * 4,
                out_shape=[
                    jax.ShapeDtypeStruct((own_rows, value_width), F32),
                    jax.ShapeDtypeStruct((own_rows, 128), F32),
                    jax.ShapeDtypeStruct((own_rows, 128), F32),
                    jax.ShapeDtypeStruct((own_rows, slot_count), BF16),
                ],
                compiler_params=pltpu.CompilerParams(vmem_limit_bytes=16 * 2**20),
                cost_estimate=pl.CostEstimate(
                    flops=2 * own_rows * slot_count * value_width,
                    bytes_accessed=2**21,
                    transcendentals=0,
                ),
                name="rows",
            )(
                lengths.reshape(-1),
                bins.reshape(-1),
                advantage.reshape(-1),
                logprob_gap.reshape(1, own_rows),
                got_cot,
                *ref_got,
            )
        value_part = dot(kept_rows, weight) + swapped(value_given, dp_count).astype(F32)
        total = value_part
        for level in range(levels):
            rows = total.shape[0] // 2
            sent = total[rows:].astype(BF16)
            total = total[:rows] + crossed(sent, tensor_count, 1 << level).astype(F32)
        values.append(total * row_scale[:, :1])

        cols = slice(j * width, (j + 1) * width)
        slope = (fixed[:, cols] + pull[:, :1] * total).astype(BF16)
        for level in reversed(range(levels)):
            slope = jnp.concatenate([slope, crossed(slope, tensor_count, 1 << level)], axis=0)
        slopes.append(slope)

    sent = dot_rows(row_at, jnp.concatenate(values, axis=1).astype(BF16)).astype(BF16)

    slopes[0], sent = lax.optimization_barrier((slopes[0], sent))
    policy_values = lax.all_to_all(sent, "dp", split_axis=0, concat_axis=0, tiled=True)

    grad_kept, grad_sent = [], []
    for j in range(PARTS):
        slopes_got = swapped(slopes[j], dp_count)
        chunks = pl.pallas_call(
            functools.partial(grad_kernel, factor),
            grid_spec=pltpu.PrefetchScalarGridSpec(
                num_scalar_prefetch=1,
                grid=(1,),
                in_specs=[
                    pl.BlockSpec((group_rows, shard), lambda i, at: (0, 0)),
                    pl.BlockSpec((group_rows, shard), lambda i, at: (0, 0)),
                    pl.BlockSpec((group_rows, width), lambda i, at: (0, 0)),
                    pl.BlockSpec((group_rows, width), lambda i, at: (0, 0)),
                ],
                out_specs=[pl.BlockSpec((shard // 2, width), lambda i, at: (0, 0))] * 2,
                scratch_shapes=[pltpu.VMEM((shard, width), F32)],
            ),
            out_shape=[
                jax.ShapeDtypeStruct((shard // 2, width), F32),
                jax.ShapeDtypeStruct((shard // 2, width), BF16),
            ],
            compiler_params=pltpu.CompilerParams(vmem_limit_bytes=32 * 2**20),
            cost_estimate=pl.CostEstimate(
                flops=4 * group_rows * shard * width,
                bytes_accessed=4 * 2**20,
                transcendentals=0,
            ),
            name="gradient",
        )(chunk_at, kept_rows, got_rows, slopes[j], slopes_got)
        grad_kept.append(chunks[0])
        grad_sent.append(chunks[1])
    grads = []
    for j in range(PARTS):
        total, given = grad_kept[j], grad_sent[j]
        for level in range(levels):
            pairs = [
                (p * cores + c, (p ^ (1 << ((c + level) % levels))) * cores + c)
                for p in range(places)
                for c in range(cores)
            ]
            total = total + lax.ppermute(given, "dp", pairs).astype(F32)
            half_rows = total.shape[0] // 2
            if level < levels - 1:
                total, given = total[:half_rows], total[half_rows:].astype(BF16)
        grads.append(total.astype(BF16))
    pairs = [
        (flat(p, c, z), flat(z, c, p ^ turned(z, levels)))
        for p in range(places)
        for c in range(cores)
        for z in range(tensor_count)
    ]
    grad_weight = lax.ppermute(jnp.concatenate(grads, axis=1), AXES, pairs).astype(F32)
    return (policy_values.reshape(1, 1, slot_count, value_width), grad_weight)


def solution(mesh):
    in_specs = (
        P("dp", "tensor"),
        P("tensor"),
        P("tensor", None),
        P(),
        P("dp", None),
        P("dp", "tensor", None),
        P("dp", "tensor", None),
        P("dp", "tensor", None),
        P(("dp", "tensor")),
        P("dp", "tensor", None, None),
    )
    out_specs = (P("dp", "tensor", None, None), P(("dp", "tensor"), None))
    return jax.shard_map(
        on_device, mesh=mesh, in_specs=in_specs, out_specs=out_specs, check_vma=False
    )
```

```python
import functools
import math

import jax
import jax.numpy as jnp
from jax import lax
from jax.experimental import pallas as pl
from jax.experimental.pallas import tpu as pltpu
from jax.sharding import PartitionSpec as P

EPS = 1e-06
BETA = 1.0
AXES = ("dp", "tensor")
BF16 = jnp.bfloat16
F32 = jnp.float32
POWER_ROWS = 16
PARTS = 2


def dot(a, b):
    return jnp.dot(a, b, preferred_element_type=F32)


def dot_rows(a, b):
    return lax.dot_general(a, b, (((0,), (0,)), ((), ())), preferred_element_type=F32)


def swapped(array, dp_count):
    return lax.ppermute(array, "dp", [(i, i ^ 1) for i in range(dp_count)])


def turned(index, levels):
    return sum(((index >> i) & 1) << (levels - 1 - i) for i in range(levels))


def crossed(array, count, step):
    return lax.ppermute(array, "tensor", [(i, i ^ step) for i in range(count)])


def prepare_kernel(
    count, steps, at, x_ref, gain_ref, weight_ref, pol_ref, given_ref, kept_ref, *refs
):
    sent_refs, (rows_ref, total, square) = refs[:count], refs[count:]
    f = pl.program_id(0)
    own = x_ref.shape[0] // count
    levels = count.bit_length() - 1
    for i in range(count):
        source = jnp.bitwise_xor(at[0], turned(i, levels))
        rows_ref[i * own : (i + 1) * own, :] = x_ref[pl.ds(pl.multiple_of(source * own, own), own), :]
    wide = rows_ref[...].astype(F32)
    gained = (wide * pol_ref[...]).astype(BF16)

    @pl.when(f < steps // 2)
    def _():
        given_ref[...] = gained

    @pl.when(f >= steps // 2)
    def _():
        kept_ref[...] = gained

    part = dot((wide * gain_ref[...]).astype(BF16), weight_ref[...])
    squares = jnp.sum(wide * wide, axis=1, keepdims=True)

    @pl.when(f == 0)
    def _():
        total[...] = part
        square[...] = squares

    @pl.when(f > 0)
    def _():
        total[...] += part
        square[...] += squares

    @pl.when(f == steps - 1)
    def _():
        for i in range(count):
            sent = sent_refs[turned(i, levels)]
            sent[:own, :] = total[i * own : (i + 1) * own, :].astype(BF16)
            power = jnp.broadcast_to(square[i * own : (i + 1) * own, :], (own, 128)).T
            high = power[: POWER_ROWS // 2].astype(BF16).astype(F32)
            low = power[: POWER_ROWS // 2] - high
            sent[own:, :] = jnp.zeros((POWER_ROWS, sent.shape[1]), BF16)
            sent[own:, :own] = jnp.concatenate([high, low], axis=0).astype(BF16)


def row_kernel(
    count, span, model_width, lengths, bins, advantage, gap_ref, cot_ref, *refs
):
    ref_refs, (fixed_ref, pull_ref, scale_ref, row_at_ref) = refs[:count], refs[count:]
    own = pull_ref.shape[0]
    slots = row_at_ref.shape[1]
    row = lax.broadcasted_iota(jnp.int32, (own, slots), 0)
    slot = lax.broadcasted_iota(jnp.int32, (own, slots), 1)
    chosen = jnp.zeros((own, slots), jnp.bool_)
    size = jnp.ones((own, 128), F32)
    weight = jnp.zeros((own, 128), F32)
    start = jnp.int32(0)
    for s in range(lengths.shape[0]):
        end = start + lengths[s]
        inside = (row >= start) & (row < end)
        chosen = chosen | (inside & (slot - bins[s] * span == row - start))
        size = jnp.where(inside[:, :128], lengths[s].astype(F32), size)
        weight = jnp.where(inside[:, :128], advantage[s], weight)
        start = end
    row_at = jnp.where(chosen, 1.0, 0.0).astype(BF16)
    row_at_ref[...] = row_at
    importance = jnp.minimum(jnp.exp(jnp.broadcast_to(gap_ref[...], (128, own)).T), 2.0)
    coef_adv = (weight * importance / size).astype(BF16).astype(F32)
    coef_pull = (BETA / size).astype(BF16).astype(F32)
    total = ref_refs[0][...].astype(F32)
    for ref in ref_refs[1:]:
        total = total + ref[...].astype(F32)
    half = POWER_ROWS // 2
    square = total[own : own + 1, :own] + total[own + half : own + half + 1, :own]
    scale = lax.rsqrt(jnp.broadcast_to(square, (128, own)).T / model_width + EPS)
    reference = (total[:own] * scale[:, :1]).astype(BF16).astype(F32)
    upstream = dot(row_at, cot_ref[...])
    fixed_ref[...] = (coef_adv[:, :1] * upstream - coef_pull[:, :1] * reference) * scale[:, :1]
    pull_ref[...] = coef_pull * scale * scale
    scale_ref[...] = scale


def grad_kernel(factor, at, kept_ref, got_ref, slope_ref, slope_got_ref, *refs):
    *out_refs, grad = refs
    total = dot_rows(kept_ref[...], slope_ref[...]) + dot_rows(got_ref[...], slope_got_ref[...])
    grad[...] = total * factor
    rows = grad.shape[0] // at.shape[0]
    count = at.shape[0] // 2
    for s in range(2 * count):
        chunk = grad[pl.ds(pl.multiple_of(at[s] * rows, rows), rows), :]
        out_ref = out_refs[s // count]
        place = s % count
        out_ref[place * rows : (place + 1) * rows, :] = chunk.astype(out_ref.dtype)


def on_device(
    tokens,
    ref_gain,
    ref_weight,
    pol_gain,
    pol_weight,
    lengths,
    bins,
    advantage,
    logprob_gap,
    cotangent,
):
    tensor_count = lax.axis_size("tensor")
    dp_count = lax.axis_size("dp")
    t = lax.axis_index("tensor")
    d = lax.axis_index("dp")
    cores = dp_count // tensor_count
    assert cores == 2
    places = dp_count // cores
    levels = places.bit_length() - 1
    assert 1 << levels == places == tensor_count
    place = d // cores
    core = d % cores
    group_rows, block = tokens.shape
    own_rows = group_rows // tensor_count
    slot_count = cotangent.shape[2]
    span_rows = slot_count // dp_count
    value_width = ref_weight.shape[1]
    model_width = pol_gain.shape[0]
    shard = pol_weight.shape[0]
    width = value_width // PARTS
    factor = 1.0 / math.sqrt(dp_count * tensor_count * lengths.shape[2])
    relative = place ^ t

    def flat(p, c, z):
        return (p * cores + c) * tensor_count + z

    def stage(number, held):
        pairs, is_getter = [], jnp.zeros((), jnp.bool_)
        for c in range(cores):
            holders = [0]
            for before in range(number):
                bit = 1 << ((c + before) % levels)
                holders = holders + [q ^ bit for q in holders]
            bit = 1 << ((c + number) % levels)
            for q in holders:
                pairs += [
                    (flat(q ^ z, c, z), flat(q ^ bit ^ z, c, z)) for z in range(tensor_count)
                ]
                is_getter = is_getter | ((core == c) & (relative == (q ^ bit)))
        return lax.ppermute(held, AXES, pairs), is_getter

    got, is_getter = stage(0, pol_weight)

    steps = 4
    feature_step = block // steps
    at = jnp.stack([t, (1 - core) * (steps // 2)]).astype(jnp.int32)
    sent_shape = (own_rows + POWER_ROWS, value_width)

    def at_step(f, at):
        return lax.rem(f + at[1], steps)

    prepared = pl.pallas_call(
        functools.partial(prepare_kernel, tensor_count, steps),
        grid_spec=pltpu.PrefetchScalarGridSpec(
            num_scalar_prefetch=1,
            grid=(steps,),
            in_specs=[
                pl.BlockSpec((group_rows, feature_step), lambda f, at: (0, at_step(f, at))),
                pl.BlockSpec((1, feature_step), lambda f, at: (0, at_step(f, at))),
                pl.BlockSpec((feature_step, value_width), lambda f, at: (at_step(f, at), 0)),
                pl.BlockSpec(
                    (1, feature_step), lambda f, at: (0, at[0] * steps + at_step(f, at))
                ),
            ],
            out_specs=[
                pl.BlockSpec(
                    (group_rows, feature_step), lambda f, at: (0, jnp.minimum(f, steps // 2 - 1))
                ),
                pl.BlockSpec(
                    (group_rows, feature_step), lambda f, at: (0, jnp.maximum(f - steps // 2, 0))
                ),
            ]
            + [pl.BlockSpec(sent_shape, lambda f, at: (0, 0))] * tensor_count,
            scratch_shapes=[
                pltpu.VMEM((group_rows, feature_step), BF16),
                pltpu.VMEM((group_rows, value_width), F32),
                pltpu.VMEM((group_rows, 1), F32),
            ],
        ),
        out_shape=[jax.ShapeDtypeStruct((group_rows, shard), BF16)] * 2
        + [jax.ShapeDtypeStruct(sent_shape, BF16)] * tensor_count,
        compiler_params=pltpu.CompilerParams(vmem_limit_bytes=56 * 2**20),
        cost_estimate=pl.CostEstimate(
            flops=2 * group_rows * block * value_width,
            bytes_accessed=8 * 2**20,
            transcendentals=0,
        ),
        name="prepare",
    )(at, tokens, ref_gain.reshape(1, block), ref_weight, pol_gain.reshape(1, model_width))
    given_rows, kept_rows, *ref_sent = prepared

    ref_got = [ref_sent[0]] + [
        crossed(ref_sent[k], tensor_count, k) for k in range(1, tensor_count)
    ]
    got_rows = swapped(given_rows, dp_count)

    cot = cotangent.reshape(slot_count, value_width)
    got, cot, kept_rows = lax.optimization_barrier((got, cot, kept_rows))
    parts = []
    for j in range(PARTS):
        cols = slice(j * width, (j + 1) * width)
        held_part = jnp.where(is_getter, got[:, cols], pol_weight[:, cols])
        for number in range(1, levels):
            got_part, is_getter_part = stage(number, held_part)
            if number < levels - 1:
                held_part = jnp.where(is_getter_part, got_part, held_part)
        parts.append((held_part, got_part, is_getter_part))
    got_cot = lax.all_to_all(cot, "dp", split_axis=0, concat_axis=0, tiled=True)

    def plane_bit(level):
        return jnp.where(core == 0, 1 << (level % levels), 1 << ((1 + level) % levels))

    chunk_at = []
    for i in range(places):
        away = sum(plane_bit(level) * ((i >> (levels - 1 - level)) & 1) for level in range(levels))
        chunk_at.append(place ^ away ^ turned(t, levels))
    chunk_at = jnp.stack(chunk_at).astype(jnp.int32)

    value_parts = []
    for j in range(PARTS):
        held_part, got_part, is_getter_part = parts[j]
        if j == PARTS - 1:
            got_part, got_cot = lax.optimization_barrier((got_part, got_cot))
        weight = jnp.where(is_getter_part, got_part, held_part)
        value_given = dot(got_rows, weight).astype(BF16)
        value_got = swapped(value_given, dp_count).astype(F32)
        value_parts.append(dot(kept_rows, weight) + value_got)

    smem = pl.BlockSpec(memory_space=pltpu.SMEM)
    vmem = pl.BlockSpec(memory_space=pltpu.VMEM)
    fixed, pull, row_scale, row_at = pl.pallas_call(
        functools.partial(row_kernel, tensor_count, span_rows, model_width),
        in_specs=[smem] * 3 + [vmem] * (2 + tensor_count),
        out_specs=[vmem] * 4,
        out_shape=[
            jax.ShapeDtypeStruct((own_rows, value_width), F32),
            jax.ShapeDtypeStruct((own_rows, 128), F32),
            jax.ShapeDtypeStruct((own_rows, 128), F32),
            jax.ShapeDtypeStruct((own_rows, slot_count), BF16),
        ],
        compiler_params=pltpu.CompilerParams(vmem_limit_bytes=16 * 2**20),
        cost_estimate=pl.CostEstimate(
            flops=2 * own_rows * slot_count * value_width,
            bytes_accessed=2**21,
            transcendentals=0,
        ),
        name="rows",
    )(
        lengths.reshape(-1),
        bins.reshape(-1),
        advantage.reshape(-1),
        logprob_gap.reshape(1, own_rows),
        got_cot,
        *ref_got,
    )

    values, slopes = [], []
    for j in range(PARTS):
        total = value_parts[j]
        for level in range(levels):
            rows = total.shape[0] // 2
            sent = total[rows:].astype(BF16)
            total = total[:rows] + crossed(sent, tensor_count, 1 << level).astype(F32)
        values.append(total * row_scale[:, :1])

        cols = slice(j * width, (j + 1) * width)
        slope = (fixed[:, cols] + pull[:, :1] * total).astype(BF16)
        for level in reversed(range(levels)):
            slope = jnp.concatenate([slope, crossed(slope, tensor_count, 1 << level)], axis=0)
        slopes.append(slope)

    sent = dot_rows(row_at, jnp.concatenate(values, axis=1).astype(BF16)).astype(BF16)

    slopes[0], sent = lax.optimization_barrier((slopes[0], sent))
    policy_values = lax.all_to_all(sent, "dp", split_axis=0, concat_axis=0, tiled=True)

    grad_kept, grad_sent = [], []
    for j in range(PARTS):
        slopes_got = swapped(slopes[j], dp_count)
        chunks = pl.pallas_call(
            functools.partial(grad_kernel, factor),
            grid_spec=pltpu.PrefetchScalarGridSpec(
                num_scalar_prefetch=1,
                grid=(1,),
                in_specs=[
                    pl.BlockSpec((group_rows, shard), lambda i, at: (0, 0)),
                    pl.BlockSpec((group_rows, shard), lambda i, at: (0, 0)),
                    pl.BlockSpec((group_rows, width), lambda i, at: (0, 0)),
                    pl.BlockSpec((group_rows, width), lambda i, at: (0, 0)),
                ],
                out_specs=[pl.BlockSpec((shard // 2, width), lambda i, at: (0, 0))] * 2,
                scratch_shapes=[pltpu.VMEM((shard, width), F32)],
            ),
            out_shape=[
                jax.ShapeDtypeStruct((shard // 2, width), F32),
                jax.ShapeDtypeStruct((shard // 2, width), BF16),
            ],
            compiler_params=pltpu.CompilerParams(vmem_limit_bytes=32 * 2**20),
            cost_estimate=pl.CostEstimate(
                flops=4 * group_rows * shard * width,
                bytes_accessed=4 * 2**20,
                transcendentals=0,
            ),
            name="gradient",
        )(chunk_at, kept_rows, got_rows, slopes[j], slopes_got)
        grad_kept.append(chunks[0])
        grad_sent.append(chunks[1])
    grads = []
    for j in range(PARTS):
        total, given = grad_kept[j], grad_sent[j]
        for level in range(levels):
            pairs = [
                (p * cores + c, (p ^ (1 << ((c + level) % levels))) * cores + c)
                for p in range(places)
                for c in range(cores)
            ]
            total = total + lax.ppermute(given, "dp", pairs).astype(F32)
            half_rows = total.shape[0] // 2
            if level < levels - 1:
                total, given = total[:half_rows], total[half_rows:].astype(BF16)
        grads.append(total.astype(BF16))
    pairs = [
        (flat(p, c, z), flat(z, c, p ^ turned(z, levels)))
        for p in range(places)
        for c in range(cores)
        for z in range(tensor_count)
    ]
    grad_weight = lax.ppermute(jnp.concatenate(grads, axis=1), AXES, pairs).astype(F32)
    return (policy_values.reshape(1, 1, slot_count, value_width), grad_weight)


def solution(mesh):
    in_specs = (
        P("dp", "tensor"),
        P("tensor"),
        P("tensor", None),
        P(),
        P("dp", None),
        P("dp", "tensor", None),
        P("dp", "tensor", None),
        P("dp", "tensor", None),
        P(("dp", "tensor")),
        P("dp", "tensor", None, None),
    )
    out_specs = (P("dp", "tensor", None, None), P(("dp", "tensor"), None))
    return jax.shard_map(
        on_device, mesh=mesh, in_specs=in_specs, out_specs=out_specs, check_vma=False
    )
```

```python
import functools
import math

import jax
import jax.numpy as jnp
from jax import lax
from jax.experimental import pallas as pl
from jax.experimental.pallas import tpu as pltpu
from jax.sharding import PartitionSpec as P

EPS = 1e-06
BETA = 1.0
AXES = ("dp", "tensor")
BF16 = jnp.bfloat16
F32 = jnp.float32
POWER_ROWS = 16
PARTS = 2


def dot(a, b):
    return jnp.dot(a, b, preferred_element_type=F32)


def dot_rows(a, b):
    return lax.dot_general(a, b, (((0,), (0,)), ((), ())), preferred_element_type=F32)


def swapped(array, dp_count):
    return lax.ppermute(array, "dp", [(i, i ^ 1) for i in range(dp_count)])


def turned(index, levels):
    return sum(((index >> i) & 1) << (levels - 1 - i) for i in range(levels))


def crossed(array, count, step):
    return lax.ppermute(array, "tensor", [(i, i ^ step) for i in range(count)])


def prepare_kernel(
    count, steps, at, x_ref, gain_ref, weight_ref, pol_ref, given_ref, kept_ref, *refs
):
    sent_refs, (rows_ref, total, square) = refs[:count], refs[count:]
    f = pl.program_id(0)
    own = x_ref.shape[0] // count
    levels = count.bit_length() - 1
    for i in range(count):
        source = jnp.bitwise_xor(at[0], turned(i, levels))
        rows_ref[i * own : (i + 1) * own, :] = x_ref[pl.ds(pl.multiple_of(source * own, own), own), :]
    wide = rows_ref[...].astype(F32)
    gained = (wide * pol_ref[...]).astype(BF16)

    @pl.when(f < steps // 2)
    def _():
        given_ref[...] = gained

    @pl.when(f >= steps // 2)
    def _():
        kept_ref[...] = gained

    part = dot((wide * gain_ref[...]).astype(BF16), weight_ref[...])
    squares = jnp.sum(wide * wide, axis=1, keepdims=True)

    @pl.when(f == 0)
    def _():
        total[...] = part
        square[...] = squares

    @pl.when(f > 0)
    def _():
        total[...] += part
        square[...] += squares

    @pl.when(f == steps - 1)
    def _():
        for i in range(count):
            sent = sent_refs[turned(i, levels)]
            sent[:own, :] = total[i * own : (i + 1) * own, :].astype(BF16)
            power = jnp.broadcast_to(square[i * own : (i + 1) * own, :], (own, 128)).T
            high = power[: POWER_ROWS // 2].astype(BF16).astype(F32)
            low = power[: POWER_ROWS // 2] - high
            sent[own:, :] = jnp.zeros((POWER_ROWS, sent.shape[1]), BF16)
            sent[own:, :own] = jnp.concatenate([high, low], axis=0).astype(BF16)


def row_kernel(
    count, span, model_width, lengths, bins, advantage, gap_ref, cot_ref, *refs
):
    ref_refs, (fixed_ref, pull_ref, scale_ref, row_at_ref) = refs[:count], refs[count:]
    own = pull_ref.shape[0]
    slots = row_at_ref.shape[1]
    row = lax.broadcasted_iota(jnp.int32, (own, slots), 0)
    slot = lax.broadcasted_iota(jnp.int32, (own, slots), 1)
    chosen = jnp.zeros((own, slots), jnp.bool_)
    size = jnp.ones((own, 128), F32)
    weight = jnp.zeros((own, 128), F32)
    start = jnp.int32(0)
    for s in range(lengths.shape[0]):
        end = start + lengths[s]
        inside = (row >= start) & (row < end)
        chosen = chosen | (inside & (slot - bins[s] * span == row - start))
        size = jnp.where(inside[:, :128], lengths[s].astype(F32), size)
        weight = jnp.where(inside[:, :128], advantage[s], weight)
        start = end
    row_at = jnp.where(chosen, 1.0, 0.0).astype(BF16)
    row_at_ref[...] = row_at
    importance = jnp.minimum(jnp.exp(jnp.broadcast_to(gap_ref[...], (128, own)).T), 2.0)
    coef_adv = (weight * importance / size).astype(BF16).astype(F32)
    coef_pull = (BETA / size).astype(BF16).astype(F32)
    total = ref_refs[0][...].astype(F32)
    for ref in ref_refs[1:]:
        total = total + ref[...].astype(F32)
    half = POWER_ROWS // 2
    square = total[own : own + 1, :own] + total[own + half : own + half + 1, :own]
    scale = lax.rsqrt(jnp.broadcast_to(square, (128, own)).T / model_width + EPS)
    reference = (total[:own] * scale[:, :1]).astype(BF16).astype(F32)
    upstream = dot(row_at, cot_ref[...])
    fixed_ref[...] = (coef_adv[:, :1] * upstream - coef_pull[:, :1] * reference) * scale[:, :1]
    pull_ref[...] = coef_pull * scale * scale
    scale_ref[...] = scale


def grad_kernel(factor, at, kept_ref, got_ref, slope_ref, slope_got_ref, *refs):
    *out_refs, grad = refs
    total = dot_rows(kept_ref[...], slope_ref[...]) + dot_rows(got_ref[...], slope_got_ref[...])
    grad[...] = total * factor
    rows = grad.shape[0] // at.shape[0]
    count = at.shape[0] // 2
    for s in range(2 * count):
        chunk = grad[pl.ds(pl.multiple_of(at[s] * rows, rows), rows), :]
        out_ref = out_refs[s // count]
        place = s % count
        out_ref[place * rows : (place + 1) * rows, :] = chunk.astype(out_ref.dtype)


def on_device(
    tokens,
    ref_gain,
    ref_weight,
    pol_gain,
    pol_weight,
    lengths,
    bins,
    advantage,
    logprob_gap,
    cotangent,
):
    tensor_count = lax.axis_size("tensor")
    dp_count = lax.axis_size("dp")
    t = lax.axis_index("tensor")
    d = lax.axis_index("dp")
    cores = dp_count // tensor_count
    assert cores == 2
    places = dp_count // cores
    levels = places.bit_length() - 1
    assert 1 << levels == places == tensor_count
    place = d // cores
    core = d % cores
    group_rows, block = tokens.shape
    own_rows = group_rows // tensor_count
    slot_count = cotangent.shape[2]
    span_rows = slot_count // dp_count
    value_width = ref_weight.shape[1]
    model_width = pol_gain.shape[0]
    shard = pol_weight.shape[0]
    width = value_width // PARTS
    factor = 1.0 / math.sqrt(dp_count * tensor_count * lengths.shape[2])
    relative = place ^ t

    def flat(p, c, z):
        return (p * cores + c) * tensor_count + z

    def stage(number, held):
        pairs, is_getter = [], jnp.zeros((), jnp.bool_)
        for c in range(cores):
            holders = [0]
            for before in range(number):
                bit = 1 << ((c + before) % levels)
                holders = holders + [q ^ bit for q in holders]
            bit = 1 << ((c + number) % levels)
            for q in holders:
                pairs += [
                    (flat(q ^ z, c, z), flat(q ^ bit ^ z, c, z)) for z in range(tensor_count)
                ]
                is_getter = is_getter | ((core == c) & (relative == (q ^ bit)))
        return lax.ppermute(held, AXES, pairs), is_getter

    got, is_getter = stage(0, pol_weight)

    steps = 4
    feature_step = block // steps
    at = jnp.stack([t, (1 - core) * (steps // 2)]).astype(jnp.int32)
    sent_shape = (own_rows + POWER_ROWS, value_width)

    def at_step(f, at):
        return lax.rem(f + at[1], steps)

    prepared = pl.pallas_call(
        functools.partial(prepare_kernel, tensor_count, steps),
        grid_spec=pltpu.PrefetchScalarGridSpec(
            num_scalar_prefetch=1,
            grid=(steps,),
            in_specs=[
                pl.BlockSpec((group_rows, feature_step), lambda f, at: (0, at_step(f, at))),
                pl.BlockSpec((1, feature_step), lambda f, at: (0, at_step(f, at))),
                pl.BlockSpec((feature_step, value_width), lambda f, at: (at_step(f, at), 0)),
                pl.BlockSpec(
                    (1, feature_step), lambda f, at: (0, at[0] * steps + at_step(f, at))
                ),
            ],
            out_specs=[
                pl.BlockSpec(
                    (group_rows, feature_step), lambda f, at: (0, jnp.minimum(f, steps // 2 - 1))
                ),
                pl.BlockSpec(
                    (group_rows, feature_step), lambda f, at: (0, jnp.maximum(f - steps // 2, 0))
                ),
            ]
            + [pl.BlockSpec(sent_shape, lambda f, at: (0, 0))] * tensor_count,
            scratch_shapes=[
                pltpu.VMEM((group_rows, feature_step), BF16),
                pltpu.VMEM((group_rows, value_width), F32),
                pltpu.VMEM((group_rows, 1), F32),
            ],
        ),
        out_shape=[jax.ShapeDtypeStruct((group_rows, shard), BF16)] * 2
        + [jax.ShapeDtypeStruct(sent_shape, BF16)] * tensor_count,
        compiler_params=pltpu.CompilerParams(vmem_limit_bytes=56 * 2**20),
        cost_estimate=pl.CostEstimate(
            flops=2 * group_rows * block * value_width,
            bytes_accessed=8 * 2**20,
            transcendentals=0,
        ),
        name="prepare",
    )(at, tokens, ref_gain.reshape(1, block), ref_weight, pol_gain.reshape(1, model_width))
    given_rows, kept_rows, *ref_sent = prepared

    ref_got = [ref_sent[0]] + [
        crossed(ref_sent[k], tensor_count, k) for k in range(1, tensor_count)
    ]
    got_rows = swapped(given_rows, dp_count)

    cot = cotangent.reshape(slot_count, value_width)
    got, cot, kept_rows = lax.optimization_barrier((got, cot, kept_rows))
    parts = []
    for j in range(PARTS):
        cols = slice(j * width, (j + 1) * width)
        held_part = jnp.where(is_getter, got[:, cols], pol_weight[:, cols])
        for number in range(1, levels):
            got_part, is_getter_part = stage(number, held_part)
            if number < levels - 1:
                held_part = jnp.where(is_getter_part, got_part, held_part)
        parts.append((held_part, got_part, is_getter_part))
    got_cot = lax.all_to_all(cot, "dp", split_axis=0, concat_axis=0, tiled=True)

    def plane_bit(level):
        return jnp.where(core == 0, 1 << (level % levels), 1 << ((1 + level) % levels))

    chunk_at = []
    for i in range(places):
        away = sum(plane_bit(level) * ((i >> (levels - 1 - level)) & 1) for level in range(levels))
        chunk_at.append(place ^ away ^ turned(t, levels))
    chunk_at = jnp.stack(chunk_at).astype(jnp.int32)

    value_parts = []
    for j in range(PARTS):
        held_part, got_part, is_getter_part = parts[j]
        if j == PARTS - 1:
            got_part, got_cot = lax.optimization_barrier((got_part, got_cot))
        weight = jnp.where(is_getter_part, got_part, held_part)
        value_given = dot(got_rows, weight).astype(BF16)
        value_got = swapped(value_given, dp_count).astype(F32)
        value_parts.append(dot(kept_rows, weight) + value_got)

    smem = pl.BlockSpec(memory_space=pltpu.SMEM)
    vmem = pl.BlockSpec(memory_space=pltpu.VMEM)
    fixed, pull, row_scale, row_at = pl.pallas_call(
        functools.partial(row_kernel, tensor_count, span_rows, model_width),
        in_specs=[smem] * 3 + [vmem] * (2 + tensor_count),
        out_specs=[vmem] * 4,
        out_shape=[
            jax.ShapeDtypeStruct((own_rows, value_width), F32),
            jax.ShapeDtypeStruct((own_rows, 128), F32),
            jax.ShapeDtypeStruct((own_rows, 128), F32),
            jax.ShapeDtypeStruct((own_rows, slot_count), BF16),
        ],
        compiler_params=pltpu.CompilerParams(vmem_limit_bytes=16 * 2**20),
        cost_estimate=pl.CostEstimate(
            flops=2 * own_rows * slot_count * value_width,
            bytes_accessed=2**21,
            transcendentals=0,
        ),
        name="rows",
    )(
        lengths.reshape(-1),
        bins.reshape(-1),
        advantage.reshape(-1),
        logprob_gap.reshape(1, own_rows),
        got_cot,
        *ref_got,
    )

    values, slopes = [], []
    for j in range(PARTS):
        total = value_parts[j]
        for level in range(levels):
            rows = total.shape[0] // 2
            sent = total[rows:].astype(BF16)
            total = total[:rows] + crossed(sent, tensor_count, 1 << level).astype(F32)
        values.append(total * row_scale[:, :1])

        cols = slice(j * width, (j + 1) * width)
        slope = (fixed[:, cols] + pull[:, :1] * total).astype(BF16)
        for level in reversed(range(levels)):
            slope = jnp.concatenate([slope, crossed(slope, tensor_count, 1 << level)], axis=0)
        slopes.append(slope)

    sent = dot_rows(row_at, jnp.concatenate(values, axis=1).astype(BF16)).astype(BF16)

    grad_kept, grad_sent = [], []
    for j in range(PARTS):
        slopes_got = swapped(slopes[j], dp_count)
        chunks = pl.pallas_call(
            functools.partial(grad_kernel, factor),
            grid_spec=pltpu.PrefetchScalarGridSpec(
                num_scalar_prefetch=1,
                grid=(1,),
                in_specs=[
                    pl.BlockSpec((group_rows, shard), lambda i, at: (0, 0)),
                    pl.BlockSpec((group_rows, shard), lambda i, at: (0, 0)),
                    pl.BlockSpec((group_rows, width), lambda i, at: (0, 0)),
                    pl.BlockSpec((group_rows, width), lambda i, at: (0, 0)),
                ],
                out_specs=[pl.BlockSpec((shard // 2, width), lambda i, at: (0, 0))] * 2,
                scratch_shapes=[pltpu.VMEM((shard, width), F32)],
            ),
            out_shape=[
                jax.ShapeDtypeStruct((shard // 2, width), F32),
                jax.ShapeDtypeStruct((shard // 2, width), BF16),
            ],
            compiler_params=pltpu.CompilerParams(vmem_limit_bytes=32 * 2**20),
            cost_estimate=pl.CostEstimate(
                flops=4 * group_rows * shard * width,
                bytes_accessed=4 * 2**20,
                transcendentals=0,
            ),
            name="gradient",
        )(chunk_at, kept_rows, got_rows, slopes[j], slopes_got)
        grad_kept.append(chunks[0])
        grad_sent.append(chunks[1])
    *grad_kept, sent = lax.optimization_barrier((*grad_kept, sent))
    policy_values = lax.all_to_all(sent, "dp", split_axis=0, concat_axis=0, tiled=True)
    grads = []
    for j in range(PARTS):
        total, given = grad_kept[j], grad_sent[j]
        for level in range(levels):
            pairs = [
                (p * cores + c, (p ^ (1 << ((c + level) % levels))) * cores + c)
                for p in range(places)
                for c in range(cores)
            ]
            total = total + lax.ppermute(given, "dp", pairs).astype(F32)
            half_rows = total.shape[0] // 2
            if level < levels - 1:
                total, given = total[:half_rows], total[half_rows:].astype(BF16)
        grads.append(total.astype(BF16))
    pairs = [
        (flat(p, c, z), flat(z, c, p ^ turned(z, levels)))
        for p in range(places)
        for c in range(cores)
        for z in range(tensor_count)
    ]
    grad_weight = lax.ppermute(jnp.concatenate(grads, axis=1), AXES, pairs).astype(F32)
    return (policy_values.reshape(1, 1, slot_count, value_width), grad_weight)


def solution(mesh):
    in_specs = (
        P("dp", "tensor"),
        P("tensor"),
        P("tensor", None),
        P(),
        P("dp", None),
        P("dp", "tensor", None),
        P("dp", "tensor", None),
        P("dp", "tensor", None),
        P(("dp", "tensor")),
        P("dp", "tensor", None, None),
    )
    out_specs = (P("dp", "tensor", None, None), P(("dp", "tensor"), None))
    return jax.shard_map(
        on_device, mesh=mesh, in_specs=in_specs, out_specs=out_specs, check_vma=False
    )
```

```python
import functools
import math

import jax
import jax.numpy as jnp
from jax import lax
from jax.experimental import pallas as pl
from jax.experimental.pallas import tpu as pltpu
from jax.sharding import PartitionSpec as P

EPS = 1e-06
BETA = 1.0
AXES = ("dp", "tensor")
BF16 = jnp.bfloat16
F32 = jnp.float32
POWER_ROWS = 16
PARTS = 2


def dot(a, b):
    return jnp.dot(a, b, preferred_element_type=F32)


def dot_rows(a, b):
    return lax.dot_general(a, b, (((0,), (0,)), ((), ())), preferred_element_type=F32)


def swapped(array, dp_count):
    return lax.ppermute(array, "dp", [(i, i ^ 1) for i in range(dp_count)])


def turned(index, levels):
    return sum(((index >> i) & 1) << (levels - 1 - i) for i in range(levels))


def crossed(array, count, step):
    return lax.ppermute(array, "tensor", [(i, i ^ step) for i in range(count)])


def prepare_kernel(
    count, steps, at, x_ref, gain_ref, weight_ref, pol_ref, given_ref, kept_ref, *refs
):
    sent_refs, (rows_ref, total, square) = refs[:count], refs[count:]
    f = pl.program_id(0)
    own = x_ref.shape[0] // count
    levels = count.bit_length() - 1
    for i in range(count):
        source = jnp.bitwise_xor(at[0], turned(i, levels))
        rows_ref[i * own : (i + 1) * own, :] = x_ref[pl.ds(pl.multiple_of(source * own, own), own), :]
    wide = rows_ref[...].astype(F32)
    gained = (wide * pol_ref[...]).astype(BF16)

    @pl.when(f < steps // 2)
    def _():
        given_ref[...] = gained

    @pl.when(f >= steps // 2)
    def _():
        kept_ref[...] = gained

    part = dot((wide * gain_ref[...]).astype(BF16), weight_ref[...])
    squares = jnp.sum(wide * wide, axis=1, keepdims=True)

    @pl.when(f == 0)
    def _():
        total[...] = part
        square[...] = squares

    @pl.when(f > 0)
    def _():
        total[...] += part
        square[...] += squares

    @pl.when(f == steps - 1)
    def _():
        for i in range(count):
            sent = sent_refs[turned(i, levels)]
            sent[:own, :] = total[i * own : (i + 1) * own, :].astype(BF16)
            power = jnp.broadcast_to(square[i * own : (i + 1) * own, :], (own, 128)).T
            high = power[: POWER_ROWS // 2].astype(BF16).astype(F32)
            low = power[: POWER_ROWS // 2] - high
            sent[own:, :] = jnp.zeros((POWER_ROWS, sent.shape[1]), BF16)
            sent[own:, :own] = jnp.concatenate([high, low], axis=0).astype(BF16)


def row_kernel(
    count, span, model_width, lengths, bins, advantage, gap_ref, cot_ref, *refs
):
    ref_refs, (fixed_ref, pull_ref, scale_ref, row_at_ref) = refs[:count], refs[count:]
    own = pull_ref.shape[0]
    slots = row_at_ref.shape[1]
    row = lax.broadcasted_iota(jnp.int32, (own, slots), 0)
    slot = lax.broadcasted_iota(jnp.int32, (own, slots), 1)
    chosen = jnp.zeros((own, slots), jnp.bool_)
    size = jnp.ones((own, 128), F32)
    weight = jnp.zeros((own, 128), F32)
    start = jnp.int32(0)
    for s in range(lengths.shape[0]):
        end = start + lengths[s]
        inside = (row >= start) & (row < end)
        chosen = chosen | (inside & (slot - bins[s] * span == row - start))
        size = jnp.where(inside[:, :128], lengths[s].astype(F32), size)
        weight = jnp.where(inside[:, :128], advantage[s], weight)
        start = end
    row_at = jnp.where(chosen, 1.0, 0.0).astype(BF16)
    row_at_ref[...] = row_at
    importance = jnp.minimum(jnp.exp(jnp.broadcast_to(gap_ref[...], (128, own)).T), 2.0)
    coef_adv = (weight * importance / size).astype(BF16).astype(F32)
    coef_pull = (BETA / size).astype(BF16).astype(F32)
    total = ref_refs[0][...].astype(F32)
    for ref in ref_refs[1:]:
        total = total + ref[...].astype(F32)
    half = POWER_ROWS // 2
    square = total[own : own + 1, :own] + total[own + half : own + half + 1, :own]
    scale = lax.rsqrt(jnp.broadcast_to(square, (128, own)).T / model_width + EPS)
    reference = (total[:own] * scale[:, :1]).astype(BF16).astype(F32)
    upstream = dot(row_at, cot_ref[...])
    fixed_ref[...] = (coef_adv[:, :1] * upstream - coef_pull[:, :1] * reference) * scale[:, :1]
    pull_ref[...] = coef_pull * scale * scale
    scale_ref[...] = scale


def grad_kernel(factor, at, kept_ref, got_ref, slope_ref, slope_got_ref, *refs):
    *out_refs, grad = refs
    total = dot_rows(kept_ref[...], slope_ref[...]) + dot_rows(got_ref[...], slope_got_ref[...])
    grad[...] = total * factor
    rows = grad.shape[0] // at.shape[0]
    count = at.shape[0] // 2
    for s in range(2 * count):
        chunk = grad[pl.ds(pl.multiple_of(at[s] * rows, rows), rows), :]
        out_ref = out_refs[s // count]
        place = s % count
        out_ref[place * rows : (place + 1) * rows, :] = chunk.astype(out_ref.dtype)


def on_device(
    tokens,
    ref_gain,
    ref_weight,
    pol_gain,
    pol_weight,
    lengths,
    bins,
    advantage,
    logprob_gap,
    cotangent,
):
    tensor_count = lax.axis_size("tensor")
    dp_count = lax.axis_size("dp")
    t = lax.axis_index("tensor")
    d = lax.axis_index("dp")
    cores = dp_count // tensor_count
    assert cores == 2
    places = dp_count // cores
    levels = places.bit_length() - 1
    assert 1 << levels == places == tensor_count
    place = d // cores
    core = d % cores
    group_rows, block = tokens.shape
    own_rows = group_rows // tensor_count
    slot_count = cotangent.shape[2]
    span_rows = slot_count // dp_count
    value_width = ref_weight.shape[1]
    model_width = pol_gain.shape[0]
    shard = pol_weight.shape[0]
    width = value_width // PARTS
    factor = 1.0 / math.sqrt(dp_count * tensor_count * lengths.shape[2])
    relative = place ^ t

    def flat(p, c, z):
        return (p * cores + c) * tensor_count + z

    def stage(number, held):
        pairs, is_getter = [], jnp.zeros((), jnp.bool_)
        for c in range(cores):
            holders = [0]
            for before in range(number):
                bit = 1 << ((c + before) % levels)
                holders = holders + [q ^ bit for q in holders]
            bit = 1 << ((c + number) % levels)
            for q in holders:
                pairs += [
                    (flat(q ^ z, c, z), flat(q ^ bit ^ z, c, z)) for z in range(tensor_count)
                ]
                is_getter = is_getter | ((core == c) & (relative == (q ^ bit)))
        return lax.ppermute(held, AXES, pairs), is_getter

    got, is_getter = stage(0, pol_weight)

    steps = 4
    feature_step = block // steps
    at = jnp.stack([t, (1 - core) * (steps // 2)]).astype(jnp.int32)
    sent_shape = (own_rows + POWER_ROWS, value_width)

    def at_step(f, at):
        return lax.rem(f + at[1], steps)

    prepared = pl.pallas_call(
        functools.partial(prepare_kernel, tensor_count, steps),
        grid_spec=pltpu.PrefetchScalarGridSpec(
            num_scalar_prefetch=1,
            grid=(steps,),
            in_specs=[
                pl.BlockSpec((group_rows, feature_step), lambda f, at: (0, at_step(f, at))),
                pl.BlockSpec((1, feature_step), lambda f, at: (0, at_step(f, at))),
                pl.BlockSpec((feature_step, value_width), lambda f, at: (at_step(f, at), 0)),
                pl.BlockSpec(
                    (1, feature_step), lambda f, at: (0, at[0] * steps + at_step(f, at))
                ),
            ],
            out_specs=[
                pl.BlockSpec(
                    (group_rows, feature_step), lambda f, at: (0, jnp.minimum(f, steps // 2 - 1))
                ),
                pl.BlockSpec(
                    (group_rows, feature_step), lambda f, at: (0, jnp.maximum(f - steps // 2, 0))
                ),
            ]
            + [pl.BlockSpec(sent_shape, lambda f, at: (0, 0))] * tensor_count,
            scratch_shapes=[
                pltpu.VMEM((group_rows, feature_step), BF16),
                pltpu.VMEM((group_rows, value_width), F32),
                pltpu.VMEM((group_rows, 1), F32),
            ],
        ),
        out_shape=[jax.ShapeDtypeStruct((group_rows, shard), BF16)] * 2
        + [jax.ShapeDtypeStruct(sent_shape, BF16)] * tensor_count,
        compiler_params=pltpu.CompilerParams(vmem_limit_bytes=56 * 2**20),
        cost_estimate=pl.CostEstimate(
            flops=2 * group_rows * block * value_width,
            bytes_accessed=8 * 2**20,
            transcendentals=0,
        ),
        name="prepare",
    )(at, tokens, ref_gain.reshape(1, block), ref_weight, pol_gain.reshape(1, model_width))
    given_rows, kept_rows, *ref_sent = prepared

    ref_got = [ref_sent[0]] + [
        crossed(ref_sent[k], tensor_count, k) for k in range(1, tensor_count)
    ]
    got_rows = swapped(given_rows, dp_count)

    cot = cotangent.reshape(slot_count, value_width)
    got, cot, kept_rows = lax.optimization_barrier((got, cot, kept_rows))
    parts = []
    for j in range(PARTS):
        cols = slice(j * width, (j + 1) * width)
        held_part = jnp.where(is_getter, got[:, cols], pol_weight[:, cols])
        for number in range(1, levels):
            got_part, is_getter_part = stage(number, held_part)
            if number < levels - 1:
                held_part = jnp.where(is_getter_part, got_part, held_part)
        parts.append((held_part, got_part, is_getter_part))
    got_cot = lax.all_to_all(cot, "dp", split_axis=0, concat_axis=0, tiled=True)

    def plane_bit(level):
        return jnp.where(core == 0, 1 << (level % levels), 1 << ((1 + level) % levels))

    chunk_at = []
    for i in range(places):
        away = sum(plane_bit(level) * ((i >> (levels - 1 - level)) & 1) for level in range(levels))
        chunk_at.append(place ^ away ^ turned(t, levels))
    chunk_at = jnp.stack(chunk_at).astype(jnp.int32)

    value_parts = []
    for j in range(PARTS):
        held_part, got_part, is_getter_part = parts[j]
        if j == PARTS - 1:
            got_part, got_cot = lax.optimization_barrier((got_part, got_cot))
        weight = jnp.where(is_getter_part, got_part, held_part)
        value_given = dot(got_rows, weight).astype(BF16)
        value_got = swapped(value_given, dp_count).astype(F32)
        value_parts.append(dot(kept_rows, weight) + value_got)

    smem = pl.BlockSpec(memory_space=pltpu.SMEM)
    vmem = pl.BlockSpec(memory_space=pltpu.VMEM)
    fixed, pull, row_scale, row_at = pl.pallas_call(
        functools.partial(row_kernel, tensor_count, span_rows, model_width),
        in_specs=[smem] * 3 + [vmem] * (2 + tensor_count),
        out_specs=[vmem] * 4,
        out_shape=[
            jax.ShapeDtypeStruct((own_rows, value_width), F32),
            jax.ShapeDtypeStruct((own_rows, 128), F32),
            jax.ShapeDtypeStruct((own_rows, 128), F32),
            jax.ShapeDtypeStruct((own_rows, slot_count), BF16),
        ],
        compiler_params=pltpu.CompilerParams(vmem_limit_bytes=16 * 2**20),
        cost_estimate=pl.CostEstimate(
            flops=2 * own_rows * slot_count * value_width,
            bytes_accessed=2**21,
            transcendentals=0,
        ),
        name="rows",
    )(
        lengths.reshape(-1),
        bins.reshape(-1),
        advantage.reshape(-1),
        logprob_gap.reshape(1, own_rows),
        got_cot,
        *ref_got,
    )

    values, slopes = [], []
    for j in range(PARTS):
        total = value_parts[j]
        for level in range(levels):
            rows = total.shape[0] // 2
            sent = total[rows:].astype(BF16)
            total = total[:rows] + crossed(sent, tensor_count, 1 << level).astype(F32)
        values.append(total * row_scale[:, :1])

        cols = slice(j * width, (j + 1) * width)
        slope = (fixed[:, cols] + pull[:, :1] * total).astype(BF16)
        for level in reversed(range(levels)):
            slope = jnp.concatenate([slope, crossed(slope, tensor_count, 1 << level)], axis=0)
        slopes.append(slope)

    sent = dot_rows(row_at, jnp.concatenate(values, axis=1).astype(BF16)).astype(BF16)

    slopes[0], sent = lax.optimization_barrier((slopes[0], sent))
    policy_values = lax.all_to_all(sent, "dp", split_axis=0, concat_axis=0, tiled=True)

    grad_kept, grad_sent = [], []
    for j in range(PARTS):
        slopes_got = swapped(slopes[j], dp_count)
        chunks = pl.pallas_call(
            functools.partial(grad_kernel, factor),
            grid_spec=pltpu.PrefetchScalarGridSpec(
                num_scalar_prefetch=1,
                grid=(1,),
                in_specs=[
                    pl.BlockSpec((group_rows, shard), lambda i, at: (0, 0)),
                    pl.BlockSpec((group_rows, shard), lambda i, at: (0, 0)),
                    pl.BlockSpec((group_rows, width), lambda i, at: (0, 0)),
                    pl.BlockSpec((group_rows, width), lambda i, at: (0, 0)),
                ],
                out_specs=[pl.BlockSpec((shard // 2, width), lambda i, at: (0, 0))] * 2,
                scratch_shapes=[pltpu.VMEM((shard, width), F32)],
            ),
            out_shape=[
                jax.ShapeDtypeStruct((shard // 2, width), F32),
                jax.ShapeDtypeStruct((shard // 2, width), BF16),
            ],
            compiler_params=pltpu.CompilerParams(vmem_limit_bytes=32 * 2**20),
            cost_estimate=pl.CostEstimate(
                flops=4 * group_rows * shard * width,
                bytes_accessed=4 * 2**20,
                transcendentals=0,
            ),
            name="gradient",
        )(chunk_at, kept_rows, got_rows, slopes[j], slopes_got)
        grad_kept.append(chunks[0])
        grad_sent.append(chunks[1])
    grads = []
    for j in range(PARTS):
        total, given = grad_kept[j], grad_sent[j]
        for level in range(levels):
            pairs = [
                (p * cores + c, (p ^ (1 << ((c + level) % levels))) * cores + c)
                for p in range(places)
                for c in range(cores)
            ]
            total = total + lax.ppermute(given, "dp", pairs).astype(F32)
            half_rows = total.shape[0] // 2
            if level < levels - 1:
                total, given = total[:half_rows], total[half_rows:].astype(BF16)
        grads.append(total.astype(BF16))
    pairs = [
        (flat(p, c, z), flat(z, c, p ^ turned(z, levels)))
        for p in range(places)
        for c in range(cores)
        for z in range(tensor_count)
    ]
    grad, policy_values = lax.optimization_barrier((jnp.concatenate(grads, axis=1), policy_values))
    grad_weight = lax.ppermute(grad, AXES, pairs).astype(F32)
    return (policy_values.reshape(1, 1, slot_count, value_width), grad_weight)


def solution(mesh):
    in_specs = (
        P("dp", "tensor"),
        P("tensor"),
        P("tensor", None),
        P(),
        P("dp", None),
        P("dp", "tensor", None),
        P("dp", "tensor", None),
        P("dp", "tensor", None),
        P(("dp", "tensor")),
        P("dp", "tensor", None, None),
    )
    out_specs = (P("dp", "tensor", None, None), P(("dp", "tensor"), None))
    return jax.shard_map(
        on_device, mesh=mesh, in_specs=in_specs, out_specs=out_specs, check_vma=False
    )
```

```python
import functools
import math

import jax
import jax.numpy as jnp
from jax import lax
from jax.experimental import pallas as pl
from jax.experimental.pallas import tpu as pltpu
from jax.sharding import PartitionSpec as P

EPS = 1e-06
BETA = 1.0
AXES = ("dp", "tensor")
BF16 = jnp.bfloat16
F32 = jnp.float32
POWER_ROWS = 16
PARTS = 2


def dot(a, b):
    return jnp.dot(a, b, preferred_element_type=F32)


def dot_rows(a, b):
    return lax.dot_general(a, b, (((0,), (0,)), ((), ())), preferred_element_type=F32)


def swapped(array, dp_count):
    return lax.ppermute(array, "dp", [(i, i ^ 1) for i in range(dp_count)])


def turned(index, levels):
    return sum(((index >> i) & 1) << (levels - 1 - i) for i in range(levels))


def crossed(array, count, step):
    return lax.ppermute(array, "tensor", [(i, i ^ step) for i in range(count)])


def prepare_kernel(
    count, steps, at, x_ref, gain_ref, weight_ref, pol_ref, given_ref, kept_ref, *refs
):
    sent_refs, (rows_ref, total, square) = refs[:count], refs[count:]
    f = pl.program_id(0)
    own = x_ref.shape[0] // count
    levels = count.bit_length() - 1
    for i in range(count):
        source = jnp.bitwise_xor(at[0], turned(i, levels))
        rows_ref[i * own : (i + 1) * own, :] = x_ref[pl.ds(pl.multiple_of(source * own, own), own), :]
    wide = rows_ref[...].astype(F32)
    gained = (wide * pol_ref[...]).astype(BF16)

    @pl.when(f < steps // 2)
    def _():
        given_ref[...] = gained

    @pl.when(f >= steps // 2)
    def _():
        kept_ref[...] = gained

    part = dot((wide * gain_ref[...]).astype(BF16), weight_ref[...])
    squares = jnp.sum(wide * wide, axis=1, keepdims=True)

    @pl.when(f == 0)
    def _():
        total[...] = part
        square[...] = squares

    @pl.when(f > 0)
    def _():
        total[...] += part
        square[...] += squares

    @pl.when(f == steps - 1)
    def _():
        for i in range(count):
            sent = sent_refs[turned(i, levels)]
            sent[:own, :] = total[i * own : (i + 1) * own, :].astype(BF16)
            power = jnp.broadcast_to(square[i * own : (i + 1) * own, :], (own, 128)).T
            high = power[: POWER_ROWS // 2].astype(BF16).astype(F32)
            low = power[: POWER_ROWS // 2] - high
            sent[own:, :] = jnp.zeros((POWER_ROWS, sent.shape[1]), BF16)
            sent[own:, :own] = jnp.concatenate([high, low], axis=0).astype(BF16)


def row_kernel(
    count, span, model_width, lengths, bins, advantage, gap_ref, cot_ref, *refs
):
    ref_refs, (fixed_ref, pull_ref, scale_ref, row_at_ref) = refs[:count], refs[count:]
    own = pull_ref.shape[0]
    slots = row_at_ref.shape[1]
    row = lax.broadcasted_iota(jnp.int32, (own, slots), 0)
    slot = lax.broadcasted_iota(jnp.int32, (own, slots), 1)
    chosen = jnp.zeros((own, slots), jnp.bool_)
    size = jnp.ones((own, 128), F32)
    weight = jnp.zeros((own, 128), F32)
    start = jnp.int32(0)
    for s in range(lengths.shape[0]):
        end = start + lengths[s]
        inside = (row >= start) & (row < end)
        chosen = chosen | (inside & (slot - bins[s] * span == row - start))
        size = jnp.where(inside[:, :128], lengths[s].astype(F32), size)
        weight = jnp.where(inside[:, :128], advantage[s], weight)
        start = end
    row_at = jnp.where(chosen, 1.0, 0.0).astype(BF16)
    row_at_ref[...] = row_at
    importance = jnp.minimum(jnp.exp(jnp.broadcast_to(gap_ref[...], (128, own)).T), 2.0)
    coef_adv = (weight * importance / size).astype(BF16).astype(F32)
    coef_pull = (BETA / size).astype(BF16).astype(F32)
    total = ref_refs[0][...].astype(F32)
    for ref in ref_refs[1:]:
        total = total + ref[...].astype(F32)
    half = POWER_ROWS // 2
    square = total[own : own + 1, :own] + total[own + half : own + half + 1, :own]
    scale = lax.rsqrt(jnp.broadcast_to(square, (128, own)).T / model_width + EPS)
    reference = (total[:own] * scale[:, :1]).astype(BF16).astype(F32)
    upstream = dot(row_at, cot_ref[...])
    fixed_ref[...] = (coef_adv[:, :1] * upstream - coef_pull[:, :1] * reference) * scale[:, :1]
    pull_ref[...] = coef_pull * scale * scale
    scale_ref[...] = scale


def grad_kernel(factor, at, kept_ref, got_ref, slope_ref, slope_got_ref, *refs):
    *out_refs, grad = refs
    total = dot_rows(kept_ref[...], slope_ref[...]) + dot_rows(got_ref[...], slope_got_ref[...])
    grad[...] = total * factor
    rows = grad.shape[0] // at.shape[0]
    count = at.shape[0] // 2
    for s in range(2 * count):
        chunk = grad[pl.ds(pl.multiple_of(at[s] * rows, rows), rows), :]
        out_ref = out_refs[s // count]
        place = s % count
        out_ref[place * rows : (place + 1) * rows, :] = chunk.astype(out_ref.dtype)


def on_device(
    tokens,
    ref_gain,
    ref_weight,
    pol_gain,
    pol_weight,
    lengths,
    bins,
    advantage,
    logprob_gap,
    cotangent,
):
    tensor_count = lax.axis_size("tensor")
    dp_count = lax.axis_size("dp")
    t = lax.axis_index("tensor")
    d = lax.axis_index("dp")
    cores = dp_count // tensor_count
    assert cores == 2
    places = dp_count // cores
    levels = places.bit_length() - 1
    assert 1 << levels == places == tensor_count
    place = d // cores
    core = d % cores
    group_rows, block = tokens.shape
    own_rows = group_rows // tensor_count
    slot_count = cotangent.shape[2]
    span_rows = slot_count // dp_count
    value_width = ref_weight.shape[1]
    model_width = pol_gain.shape[0]
    shard = pol_weight.shape[0]
    width = value_width // PARTS
    factor = 1.0 / math.sqrt(dp_count * tensor_count * lengths.shape[2])
    relative = place ^ t

    def flat(p, c, z):
        return (p * cores + c) * tensor_count + z

    def stage(number, held):
        pairs, is_getter = [], jnp.zeros((), jnp.bool_)
        for c in range(cores):
            holders = [0]
            for before in range(number):
                bit = 1 << ((c + before) % levels)
                holders = holders + [q ^ bit for q in holders]
            bit = 1 << ((c + number) % levels)
            for q in holders:
                pairs += [
                    (flat(q ^ z, c, z), flat(q ^ bit ^ z, c, z)) for z in range(tensor_count)
                ]
                is_getter = is_getter | ((core == c) & (relative == (q ^ bit)))
        return lax.ppermute(held, AXES, pairs), is_getter

    got, is_getter = stage(0, pol_weight)

    steps = 4
    feature_step = block // steps
    at = jnp.stack([t, (1 - core) * (steps // 2)]).astype(jnp.int32)
    sent_shape = (own_rows + POWER_ROWS, value_width)

    def at_step(f, at):
        return lax.rem(f + at[1], steps)

    prepared = pl.pallas_call(
        functools.partial(prepare_kernel, tensor_count, steps),
        grid_spec=pltpu.PrefetchScalarGridSpec(
            num_scalar_prefetch=1,
            grid=(steps,),
            in_specs=[
                pl.BlockSpec((group_rows, feature_step), lambda f, at: (0, at_step(f, at))),
                pl.BlockSpec((1, feature_step), lambda f, at: (0, at_step(f, at))),
                pl.BlockSpec((feature_step, value_width), lambda f, at: (at_step(f, at), 0)),
                pl.BlockSpec(
                    (1, feature_step), lambda f, at: (0, at[0] * steps + at_step(f, at))
                ),
            ],
            out_specs=[
                pl.BlockSpec(
                    (group_rows, feature_step), lambda f, at: (0, jnp.minimum(f, steps // 2 - 1))
                ),
                pl.BlockSpec(
                    (group_rows, feature_step), lambda f, at: (0, jnp.maximum(f - steps // 2, 0))
                ),
            ]
            + [pl.BlockSpec(sent_shape, lambda f, at: (0, 0))] * tensor_count,
            scratch_shapes=[
                pltpu.VMEM((group_rows, feature_step), BF16),
                pltpu.VMEM((group_rows, value_width), F32),
                pltpu.VMEM((group_rows, 1), F32),
            ],
        ),
        out_shape=[jax.ShapeDtypeStruct((group_rows, shard), BF16)] * 2
        + [jax.ShapeDtypeStruct(sent_shape, BF16)] * tensor_count,
        compiler_params=pltpu.CompilerParams(vmem_limit_bytes=56 * 2**20),
        cost_estimate=pl.CostEstimate(
            flops=2 * group_rows * block * value_width,
            bytes_accessed=8 * 2**20,
            transcendentals=0,
        ),
        name="prepare",
    )(at, tokens, ref_gain.reshape(1, block), ref_weight, pol_gain.reshape(1, model_width))
    given_rows, kept_rows, *ref_sent = prepared

    ref_got = [ref_sent[0]] + [
        crossed(ref_sent[k], tensor_count, k) for k in range(1, tensor_count)
    ]
    got_rows = swapped(given_rows, dp_count)

    cot = cotangent.reshape(slot_count, value_width)
    got, cot, kept_rows = lax.optimization_barrier((got, cot, kept_rows))
    parts = []
    for j in range(PARTS):
        cols = slice(j * width, (j + 1) * width)
        held_part = jnp.where(is_getter, got[:, cols], pol_weight[:, cols])
        for number in range(1, levels):
            got_part, is_getter_part = stage(number, held_part)
            if number < levels - 1:
                held_part = jnp.where(is_getter_part, got_part, held_part)
        parts.append((held_part, got_part, is_getter_part))
    got_cot = lax.all_to_all(cot, "dp", split_axis=0, concat_axis=0, tiled=True)

    def plane_bit(level):
        return jnp.where(core == 0, 1 << (level % levels), 1 << ((1 + level) % levels))

    chunk_at = []
    for i in range(places):
        away = sum(plane_bit(level) * ((i >> (levels - 1 - level)) & 1) for level in range(levels))
        chunk_at.append(place ^ away ^ turned(t, levels))
    chunk_at = jnp.stack(chunk_at).astype(jnp.int32)

    value_got, value_kept = [], []
    for j in range(PARTS):
        held_part, got_part, is_getter_part = parts[j]
        if j == PARTS - 1:
            tied = lax.optimization_barrier((got_part, got_cot, *value_kept))
            got_part, got_cot, *value_kept = tied
        weight = jnp.where(is_getter_part, got_part, held_part)
        value_got.append(swapped(dot(got_rows, weight).astype(BF16), dp_count))
        value_kept.append(dot(kept_rows, weight))

    smem = pl.BlockSpec(memory_space=pltpu.SMEM)
    vmem = pl.BlockSpec(memory_space=pltpu.VMEM)
    fixed, pull, row_scale, row_at = pl.pallas_call(
        functools.partial(row_kernel, tensor_count, span_rows, model_width),
        in_specs=[smem] * 3 + [vmem] * (2 + tensor_count),
        out_specs=[vmem] * 4,
        out_shape=[
            jax.ShapeDtypeStruct((own_rows, value_width), F32),
            jax.ShapeDtypeStruct((own_rows, 128), F32),
            jax.ShapeDtypeStruct((own_rows, 128), F32),
            jax.ShapeDtypeStruct((own_rows, slot_count), BF16),
        ],
        compiler_params=pltpu.CompilerParams(vmem_limit_bytes=16 * 2**20),
        cost_estimate=pl.CostEstimate(
            flops=2 * own_rows * slot_count * value_width,
            bytes_accessed=2**21,
            transcendentals=0,
        ),
        name="rows",
    )(
        lengths.reshape(-1),
        bins.reshape(-1),
        advantage.reshape(-1),
        logprob_gap.reshape(1, own_rows),
        got_cot,
        *ref_got,
    )

    values, slopes = [], []
    for j in range(PARTS):
        total = value_kept[j] + value_got[j].astype(F32)
        for level in range(levels):
            rows = total.shape[0] // 2
            sent = total[rows:].astype(BF16)
            total = total[:rows] + crossed(sent, tensor_count, 1 << level).astype(F32)
        values.append(total * row_scale[:, :1])

        cols = slice(j * width, (j + 1) * width)
        slope = (fixed[:, cols] + pull[:, :1] * total).astype(BF16)
        for level in reversed(range(levels)):
            slope = jnp.concatenate([slope, crossed(slope, tensor_count, 1 << level)], axis=0)
        slopes.append(slope)

    sent = dot_rows(row_at, jnp.concatenate(values, axis=1).astype(BF16)).astype(BF16)

    slopes[0], sent = lax.optimization_barrier((slopes[0], sent))
    policy_values = lax.all_to_all(sent, "dp", split_axis=0, concat_axis=0, tiled=True)

    grad_kept, grad_sent = [], []
    for j in range(PARTS):
        slopes_got = swapped(slopes[j], dp_count)
        chunks = pl.pallas_call(
            functools.partial(grad_kernel, factor),
            grid_spec=pltpu.PrefetchScalarGridSpec(
                num_scalar_prefetch=1,
                grid=(1,),
                in_specs=[
                    pl.BlockSpec((group_rows, shard), lambda i, at: (0, 0)),
                    pl.BlockSpec((group_rows, shard), lambda i, at: (0, 0)),
                    pl.BlockSpec((group_rows, width), lambda i, at: (0, 0)),
                    pl.BlockSpec((group_rows, width), lambda i, at: (0, 0)),
                ],
                out_specs=[pl.BlockSpec((shard // 2, width), lambda i, at: (0, 0))] * 2,
                scratch_shapes=[pltpu.VMEM((shard, width), F32)],
            ),
            out_shape=[
                jax.ShapeDtypeStruct((shard // 2, width), F32),
                jax.ShapeDtypeStruct((shard // 2, width), BF16),
            ],
            compiler_params=pltpu.CompilerParams(vmem_limit_bytes=32 * 2**20),
            cost_estimate=pl.CostEstimate(
                flops=4 * group_rows * shard * width,
                bytes_accessed=4 * 2**20,
                transcendentals=0,
            ),
            name="gradient",
        )(chunk_at, kept_rows, got_rows, slopes[j], slopes_got)
        grad_kept.append(chunks[0])
        grad_sent.append(chunks[1])
    grads = []
    for j in range(PARTS):
        total, given = grad_kept[j], grad_sent[j]
        for level in range(levels):
            pairs = [
                (p * cores + c, (p ^ (1 << ((c + level) % levels))) * cores + c)
                for p in range(places)
                for c in range(cores)
            ]
            total = total + lax.ppermute(given, "dp", pairs).astype(F32)
            half_rows = total.shape[0] // 2
            if level < levels - 1:
                total, given = total[:half_rows], total[half_rows:].astype(BF16)
        total = total.astype(BF16)
        if j == PARTS - 1:
            total, policy_values = lax.optimization_barrier((total, policy_values))
        pairs = [
            (flat(p, c, z), flat(z, c, p ^ turned(z, levels)))
            for p in range(places)
            for c in range(cores)
            for z in range(tensor_count)
        ]
        grads.append(lax.ppermute(total, AXES, pairs))
    grad_weight = jnp.concatenate(grads, axis=1).astype(F32)
    return (policy_values.reshape(1, 1, slot_count, value_width), grad_weight)


def solution(mesh):
    in_specs = (
        P("dp", "tensor"),
        P("tensor"),
        P("tensor", None),
        P(),
        P("dp", None),
        P("dp", "tensor", None),
        P("dp", "tensor", None),
        P("dp", "tensor", None),
        P(("dp", "tensor")),
        P("dp", "tensor", None, None),
    )
    out_specs = (P("dp", "tensor", None, None), P(("dp", "tensor"), None))
    return jax.shard_map(
        on_device, mesh=mesh, in_specs=in_specs, out_specs=out_specs, check_vma=False
    )
```

```python
import functools
import math

import jax
import jax.numpy as jnp
from jax import lax
from jax.experimental import pallas as pl
from jax.experimental.pallas import tpu as pltpu
from jax.sharding import PartitionSpec as P

EPS = 1e-06
BETA = 1.0
AXES = ("dp", "tensor")
BF16 = jnp.bfloat16
F32 = jnp.float32
POWER_ROWS = 16
PARTS = 2


def dot(a, b):
    return jnp.dot(a, b, preferred_element_type=F32)


def dot_rows(a, b):
    return lax.dot_general(a, b, (((0,), (0,)), ((), ())), preferred_element_type=F32)


def swapped(array, dp_count):
    return lax.ppermute(array, "dp", [(i, i ^ 1) for i in range(dp_count)])


def turned(index, levels):
    return sum(((index >> i) & 1) << (levels - 1 - i) for i in range(levels))


def crossed(array, count, step):
    return lax.ppermute(array, "tensor", [(i, i ^ step) for i in range(count)])


def prepare_kernel(
    count, steps, at, x_ref, gain_ref, weight_ref, pol_ref, given_ref, kept_ref, *refs
):
    sent_refs, (rows_ref, total, square) = refs[:count], refs[count:]
    f = pl.program_id(0)
    own = x_ref.shape[0] // count
    levels = count.bit_length() - 1
    for i in range(count):
        source = jnp.bitwise_xor(at[0], turned(i, levels))
        rows_ref[i * own : (i + 1) * own, :] = x_ref[pl.ds(pl.multiple_of(source * own, own), own), :]
    wide = rows_ref[...].astype(F32)
    gained = (wide * pol_ref[...]).astype(BF16)

    @pl.when(f < steps // 2)
    def _():
        given_ref[...] = gained

    @pl.when(f >= steps // 2)
    def _():
        kept_ref[...] = gained

    part = dot((wide * gain_ref[...]).astype(BF16), weight_ref[...])
    squares = jnp.sum(wide * wide, axis=1, keepdims=True)

    @pl.when(f == 0)
    def _():
        total[...] = part
        square[...] = squares

    @pl.when(f > 0)
    def _():
        total[...] += part
        square[...] += squares

    @pl.when(f == steps - 1)
    def _():
        for i in range(count):
            sent = sent_refs[turned(i, levels)]
            sent[:own, :] = total[i * own : (i + 1) * own, :].astype(BF16)
            power = jnp.broadcast_to(square[i * own : (i + 1) * own, :], (own, 128)).T
            high = power[: POWER_ROWS // 2].astype(BF16).astype(F32)
            low = power[: POWER_ROWS // 2] - high
            sent[own:, :] = jnp.zeros((POWER_ROWS, sent.shape[1]), BF16)
            sent[own:, :own] = jnp.concatenate([high, low], axis=0).astype(BF16)


def row_kernel(
    count, span, model_width, lengths, bins, advantage, gap_ref, cot_ref, *refs
):
    ref_refs, (fixed_ref, pull_ref, scale_ref, row_at_ref) = refs[:count], refs[count:]
    own = pull_ref.shape[0]
    slots = row_at_ref.shape[1]
    row = lax.broadcasted_iota(jnp.int32, (own, slots), 0)
    slot = lax.broadcasted_iota(jnp.int32, (own, slots), 1)
    chosen = jnp.zeros((own, slots), jnp.bool_)
    size = jnp.ones((own, 128), F32)
    weight = jnp.zeros((own, 128), F32)
    start = jnp.int32(0)
    for s in range(lengths.shape[0]):
        end = start + lengths[s]
        inside = (row >= start) & (row < end)
        chosen = chosen | (inside & (slot - bins[s] * span == row - start))
        size = jnp.where(inside[:, :128], lengths[s].astype(F32), size)
        weight = jnp.where(inside[:, :128], advantage[s], weight)
        start = end
    row_at = jnp.where(chosen, 1.0, 0.0).astype(BF16)
    row_at_ref[...] = row_at
    importance = jnp.minimum(jnp.exp(jnp.broadcast_to(gap_ref[...], (128, own)).T), 2.0)
    coef_adv = (weight * importance / size).astype(BF16).astype(F32)
    coef_pull = (BETA / size).astype(BF16).astype(F32)
    total = ref_refs[0][...].astype(F32)
    for ref in ref_refs[1:]:
        total = total + ref[...].astype(F32)
    half = POWER_ROWS // 2
    square = total[own : own + 1, :own] + total[own + half : own + half + 1, :own]
    scale = lax.rsqrt(jnp.broadcast_to(square, (128, own)).T / model_width + EPS)
    reference = (total[:own] * scale[:, :1]).astype(BF16).astype(F32)
    upstream = dot(row_at, cot_ref[...])
    fixed_ref[...] = (coef_adv[:, :1] * upstream - coef_pull[:, :1] * reference) * scale[:, :1]
    pull_ref[...] = coef_pull * scale * scale
    scale_ref[...] = scale


def grad_kernel(factor, at, kept_ref, got_ref, slope_ref, slope_got_ref, *refs):
    *out_refs, grad = refs
    total = dot_rows(kept_ref[...], slope_ref[...]) + dot_rows(got_ref[...], slope_got_ref[...])
    grad[...] = total * factor
    rows = grad.shape[0] // at.shape[0]
    count = at.shape[0] // 2
    for s in range(2 * count):
        chunk = grad[pl.ds(pl.multiple_of(at[s] * rows, rows), rows), :]
        out_ref = out_refs[s // count]
        place = s % count
        out_ref[place * rows : (place + 1) * rows, :] = chunk.astype(out_ref.dtype)


def on_device(
    tokens,
    ref_gain,
    ref_weight,
    pol_gain,
    pol_weight,
    lengths,
    bins,
    advantage,
    logprob_gap,
    cotangent,
):
    tensor_count = lax.axis_size("tensor")
    dp_count = lax.axis_size("dp")
    t = lax.axis_index("tensor")
    d = lax.axis_index("dp")
    cores = dp_count // tensor_count
    assert cores == 2
    places = dp_count // cores
    levels = places.bit_length() - 1
    assert 1 << levels == places == tensor_count
    place = d // cores
    core = d % cores
    group_rows, block = tokens.shape
    own_rows = group_rows // tensor_count
    slot_count = cotangent.shape[2]
    span_rows = slot_count // dp_count
    value_width = ref_weight.shape[1]
    model_width = pol_gain.shape[0]
    shard = pol_weight.shape[0]
    width = value_width // PARTS
    factor = 1.0 / math.sqrt(dp_count * tensor_count * lengths.shape[2])
    relative = place ^ t

    def flat(p, c, z):
        return (p * cores + c) * tensor_count + z

    def stage(number, held):
        pairs, is_getter = [], jnp.zeros((), jnp.bool_)
        for c in range(cores):
            holders = [0]
            for before in range(number):
                bit = 1 << ((c + before) % levels)
                holders = holders + [q ^ bit for q in holders]
            bit = 1 << ((c + number) % levels)
            for q in holders:
                pairs += [
                    (flat(q ^ z, c, z), flat(q ^ bit ^ z, c, z)) for z in range(tensor_count)
                ]
                is_getter = is_getter | ((core == c) & (relative == (q ^ bit)))
        return lax.ppermute(held, AXES, pairs), is_getter

    got, is_getter = stage(0, pol_weight)

    steps = 4
    feature_step = block // steps
    at = jnp.stack([t, (1 - core) * (steps // 2)]).astype(jnp.int32)
    sent_shape = (own_rows + POWER_ROWS, value_width)

    def at_step(f, at):
        return lax.rem(f + at[1], steps)

    prepared = pl.pallas_call(
        functools.partial(prepare_kernel, tensor_count, steps),
        grid_spec=pltpu.PrefetchScalarGridSpec(
            num_scalar_prefetch=1,
            grid=(steps,),
            in_specs=[
                pl.BlockSpec((group_rows, feature_step), lambda f, at: (0, at_step(f, at))),
                pl.BlockSpec((1, feature_step), lambda f, at: (0, at_step(f, at))),
                pl.BlockSpec((feature_step, value_width), lambda f, at: (at_step(f, at), 0)),
                pl.BlockSpec(
                    (1, feature_step), lambda f, at: (0, at[0] * steps + at_step(f, at))
                ),
            ],
            out_specs=[
                pl.BlockSpec(
                    (group_rows, feature_step), lambda f, at: (0, jnp.minimum(f, steps // 2 - 1))
                ),
                pl.BlockSpec(
                    (group_rows, feature_step), lambda f, at: (0, jnp.maximum(f - steps // 2, 0))
                ),
            ]
            + [pl.BlockSpec(sent_shape, lambda f, at: (0, 0))] * tensor_count,
            scratch_shapes=[
                pltpu.VMEM((group_rows, feature_step), BF16),
                pltpu.VMEM((group_rows, value_width), F32),
                pltpu.VMEM((group_rows, 1), F32),
            ],
        ),
        out_shape=[jax.ShapeDtypeStruct((group_rows, shard), BF16)] * 2
        + [jax.ShapeDtypeStruct(sent_shape, BF16)] * tensor_count,
        compiler_params=pltpu.CompilerParams(vmem_limit_bytes=56 * 2**20),
        cost_estimate=pl.CostEstimate(
            flops=2 * group_rows * block * value_width,
            bytes_accessed=8 * 2**20,
            transcendentals=0,
        ),
        name="prepare",
    )(at, tokens, ref_gain.reshape(1, block), ref_weight, pol_gain.reshape(1, model_width))
    given_rows, kept_rows, *ref_sent = prepared

    ref_got = [ref_sent[0]] + [
        crossed(ref_sent[k], tensor_count, k) for k in range(1, tensor_count)
    ]
    got_rows = swapped(given_rows, dp_count)

    cot = cotangent.reshape(slot_count, value_width)
    got, cot, kept_rows = lax.optimization_barrier((got, cot, kept_rows))
    parts = []
    for j in range(PARTS):
        cols = slice(j * width, (j + 1) * width)
        held_part = jnp.where(is_getter, got[:, cols], pol_weight[:, cols])
        for number in range(1, levels):
            got_part, is_getter_part = stage(number, held_part)
            if number < levels - 1:
                held_part = jnp.where(is_getter_part, got_part, held_part)
        parts.append((held_part, got_part, is_getter_part))
    got_cot = lax.all_to_all(cot, "dp", split_axis=0, concat_axis=0, tiled=True)

    def plane_bit(level):
        return jnp.where(core == 0, 1 << (level % levels), 1 << ((1 + level) % levels))

    chunk_at = []
    for i in range(places):
        away = sum(plane_bit(level) * ((i >> (levels - 1 - level)) & 1) for level in range(levels))
        chunk_at.append(place ^ away ^ turned(t, levels))
    chunk_at = jnp.stack(chunk_at).astype(jnp.int32)

    value_parts = []
    for j in range(PARTS):
        held_part, got_part, is_getter_part = parts[j]
        if j == 0:
            got_part, got_cot = lax.optimization_barrier((got_part, got_cot))
        weight = jnp.where(is_getter_part, got_part, held_part)
        value_given = dot(got_rows, weight).astype(BF16)
        value_got = swapped(value_given, dp_count).astype(F32)
        value_parts.append(dot(kept_rows, weight) + value_got)

    smem = pl.BlockSpec(memory_space=pltpu.SMEM)
    vmem = pl.BlockSpec(memory_space=pltpu.VMEM)
    fixed, pull, row_scale, row_at = pl.pallas_call(
        functools.partial(row_kernel, tensor_count, span_rows, model_width),
        in_specs=[smem] * 3 + [vmem] * (2 + tensor_count),
        out_specs=[vmem] * 4,
        out_shape=[
            jax.ShapeDtypeStruct((own_rows, value_width), F32),
            jax.ShapeDtypeStruct((own_rows, 128), F32),
            jax.ShapeDtypeStruct((own_rows, 128), F32),
            jax.ShapeDtypeStruct((own_rows, slot_count), BF16),
        ],
        compiler_params=pltpu.CompilerParams(vmem_limit_bytes=16 * 2**20),
        cost_estimate=pl.CostEstimate(
            flops=2 * own_rows * slot_count * value_width,
            bytes_accessed=2**21,
            transcendentals=0,
        ),
        name="rows",
    )(
        lengths.reshape(-1),
        bins.reshape(-1),
        advantage.reshape(-1),
        logprob_gap.reshape(1, own_rows),
        got_cot,
        *ref_got,
    )

    values, slopes = [], []
    for j in range(PARTS):
        total = value_parts[j]
        for level in range(levels):
            rows = total.shape[0] // 2
            sent = total[rows:].astype(BF16)
            total = total[:rows] + crossed(sent, tensor_count, 1 << level).astype(F32)
        values.append(total * row_scale[:, :1])

        cols = slice(j * width, (j + 1) * width)
        slope = (fixed[:, cols] + pull[:, :1] * total).astype(BF16)
        for level in reversed(range(levels)):
            slope = jnp.concatenate([slope, crossed(slope, tensor_count, 1 << level)], axis=0)
        slopes.append(slope)

    sent = dot_rows(row_at, jnp.concatenate(values, axis=1).astype(BF16)).astype(BF16)

    slopes[0], sent = lax.optimization_barrier((slopes[0], sent))
    policy_values = lax.all_to_all(sent, "dp", split_axis=0, concat_axis=0, tiled=True)

    grad_kept, grad_sent = [], []
    for j in range(PARTS):
        slopes_got = swapped(slopes[j], dp_count)
        chunks = pl.pallas_call(
            functools.partial(grad_kernel, factor),
            grid_spec=pltpu.PrefetchScalarGridSpec(
                num_scalar_prefetch=1,
                grid=(1,),
                in_specs=[
                    pl.BlockSpec((group_rows, shard), lambda i, at: (0, 0)),
                    pl.BlockSpec((group_rows, shard), lambda i, at: (0, 0)),
                    pl.BlockSpec((group_rows, width), lambda i, at: (0, 0)),
                    pl.BlockSpec((group_rows, width), lambda i, at: (0, 0)),
                ],
                out_specs=[pl.BlockSpec((shard // 2, width), lambda i, at: (0, 0))] * 2,
                scratch_shapes=[pltpu.VMEM((shard, width), F32)],
            ),
            out_shape=[
                jax.ShapeDtypeStruct((shard // 2, width), F32),
                jax.ShapeDtypeStruct((shard // 2, width), BF16),
            ],
            compiler_params=pltpu.CompilerParams(vmem_limit_bytes=32 * 2**20),
            cost_estimate=pl.CostEstimate(
                flops=4 * group_rows * shard * width,
                bytes_accessed=4 * 2**20,
                transcendentals=0,
            ),
            name="gradient",
        )(chunk_at, kept_rows, got_rows, slopes[j], slopes_got)
        grad_kept.append(chunks[0])
        grad_sent.append(chunks[1])
    grads = []
    for j in range(PARTS):
        total, given = grad_kept[j], grad_sent[j]
        for level in range(levels):
            pairs = [
                (p * cores + c, (p ^ (1 << ((c + level) % levels))) * cores + c)
                for p in range(places)
                for c in range(cores)
            ]
            total = total + lax.ppermute(given, "dp", pairs).astype(F32)
            half_rows = total.shape[0] // 2
            if level < levels - 1:
                total, given = total[:half_rows], total[half_rows:].astype(BF16)
        grads.append(total.astype(BF16))
    pairs = [
        (flat(p, c, z), flat(z, c, p ^ turned(z, levels)))
        for p in range(places)
        for c in range(cores)
        for z in range(tensor_count)
    ]
    grad, policy_values = lax.optimization_barrier((jnp.concatenate(grads, axis=1), policy_values))
    grad_weight = lax.ppermute(grad, AXES, pairs).astype(F32)
    return (policy_values.reshape(1, 1, slot_count, value_width), grad_weight)


def solution(mesh):
    in_specs = (
        P("dp", "tensor"),
        P("tensor"),
        P("tensor", None),
        P(),
        P("dp", None),
        P("dp", "tensor", None),
        P("dp", "tensor", None),
        P("dp", "tensor", None),
        P(("dp", "tensor")),
        P("dp", "tensor", None, None),
    )
    out_specs = (P("dp", "tensor", None, None), P(("dp", "tensor"), None))
    return jax.shard_map(
        on_device, mesh=mesh, in_specs=in_specs, out_specs=out_specs, check_vma=False
    )
```

```python
import functools
import math

import jax
import jax.numpy as jnp
from jax import lax
from jax.experimental import pallas as pl
from jax.experimental.pallas import tpu as pltpu
from jax.sharding import PartitionSpec as P

EPS = 1e-06
BETA = 1.0
AXES = ("dp", "tensor")
BF16 = jnp.bfloat16
F32 = jnp.float32
POWER_ROWS = 16
PARTS = 2


def dot(a, b):
    return jnp.dot(a, b, preferred_element_type=F32)


def dot_rows(a, b):
    return lax.dot_general(a, b, (((0,), (0,)), ((), ())), preferred_element_type=F32)


def swapped(array, dp_count):
    return lax.ppermute(array, "dp", [(i, i ^ 1) for i in range(dp_count)])


def turned(index, levels):
    return sum(((index >> i) & 1) << (levels - 1 - i) for i in range(levels))


def crossed(array, count, step):
    return lax.ppermute(array, "tensor", [(i, i ^ step) for i in range(count)])


def prepare_kernel(
    count, steps, at, x_ref, gain_ref, weight_ref, pol_ref, given_ref, kept_ref, *refs
):
    sent_refs, (rows_ref, total, square) = refs[:count], refs[count:]
    f = pl.program_id(0)
    own = x_ref.shape[0] // count
    levels = count.bit_length() - 1
    for i in range(count):
        source = jnp.bitwise_xor(at[0], turned(i, levels))
        rows_ref[i * own : (i + 1) * own, :] = x_ref[pl.ds(pl.multiple_of(source * own, own), own), :]
    wide = rows_ref[...].astype(F32)
    gained = (wide * pol_ref[...]).astype(BF16)

    @pl.when(f < steps // 2)
    def _():
        given_ref[...] = gained

    @pl.when(f >= steps // 2)
    def _():
        kept_ref[...] = gained

    part = dot((wide * gain_ref[...]).astype(BF16), weight_ref[...])
    squares = jnp.sum(wide * wide, axis=1, keepdims=True)

    @pl.when(f == 0)
    def _():
        total[...] = part
        square[...] = squares

    @pl.when(f > 0)
    def _():
        total[...] += part
        square[...] += squares

    @pl.when(f == steps - 1)
    def _():
        for i in range(count):
            sent = sent_refs[turned(i, levels)]
            sent[:own, :] = total[i * own : (i + 1) * own, :].astype(BF16)
            power = jnp.broadcast_to(square[i * own : (i + 1) * own, :], (own, 128)).T
            high = power[: POWER_ROWS // 2].astype(BF16).astype(F32)
            low = power[: POWER_ROWS // 2] - high
            sent[own:, :] = jnp.zeros((POWER_ROWS, sent.shape[1]), BF16)
            sent[own:, :own] = jnp.concatenate([high, low], axis=0).astype(BF16)


def row_kernel(
    count, span, model_width, lengths, bins, advantage, gap_ref, cot_ref, *refs
):
    ref_refs, (fixed_ref, pull_ref, scale_ref, row_at_ref) = refs[:count], refs[count:]
    own = pull_ref.shape[0]
    slots = row_at_ref.shape[1]
    row = lax.broadcasted_iota(jnp.int32, (own, slots), 0)
    slot = lax.broadcasted_iota(jnp.int32, (own, slots), 1)
    chosen = jnp.zeros((own, slots), jnp.bool_)
    size = jnp.ones((own, 128), F32)
    weight = jnp.zeros((own, 128), F32)
    start = jnp.int32(0)
    for s in range(lengths.shape[0]):
        end = start + lengths[s]
        inside = (row >= start) & (row < end)
        chosen = chosen | (inside & (slot - bins[s] * span == row - start))
        size = jnp.where(inside[:, :128], lengths[s].astype(F32), size)
        weight = jnp.where(inside[:, :128], advantage[s], weight)
        start = end
    row_at = jnp.where(chosen, 1.0, 0.0).astype(BF16)
    row_at_ref[...] = row_at
    importance = jnp.minimum(jnp.exp(jnp.broadcast_to(gap_ref[...], (128, own)).T), 2.0)
    coef_adv = (weight * importance / size).astype(BF16).astype(F32)
    coef_pull = (BETA / size).astype(BF16).astype(F32)
    total = ref_refs[0][...].astype(F32)
    for ref in ref_refs[1:]:
        total = total + ref[...].astype(F32)
    half = POWER_ROWS // 2
    square = total[own : own + 1, :own] + total[own + half : own + half + 1, :own]
    scale = lax.rsqrt(jnp.broadcast_to(square, (128, own)).T / model_width + EPS)
    reference = (total[:own] * scale[:, :1]).astype(BF16).astype(F32)
    upstream = dot(row_at, cot_ref[...])
    fixed_ref[...] = (coef_adv[:, :1] * upstream - coef_pull[:, :1] * reference) * scale[:, :1]
    pull_ref[...] = coef_pull * scale * scale
    scale_ref[...] = scale


def grad_kernel(factor, at, kept_ref, got_ref, slope_ref, slope_got_ref, *refs):
    *out_refs, grad = refs
    total = dot_rows(kept_ref[...], slope_ref[...]) + dot_rows(got_ref[...], slope_got_ref[...])
    grad[...] = total * factor
    rows = grad.shape[0] // at.shape[0]
    count = at.shape[0] // 2
    for s in range(2 * count):
        chunk = grad[pl.ds(pl.multiple_of(at[s] * rows, rows), rows), :]
        out_ref = out_refs[s // count]
        place = s % count
        out_ref[place * rows : (place + 1) * rows, :] = chunk.astype(out_ref.dtype)


def write_kernel(in_ref, out_ref):
    out_ref[...] = in_ref[...]


def on_device(
    tokens,
    ref_gain,
    ref_weight,
    pol_gain,
    pol_weight,
    lengths,
    bins,
    advantage,
    logprob_gap,
    cotangent,
):
    tensor_count = lax.axis_size("tensor")
    dp_count = lax.axis_size("dp")
    t = lax.axis_index("tensor")
    d = lax.axis_index("dp")
    cores = dp_count // tensor_count
    assert cores == 2
    places = dp_count // cores
    levels = places.bit_length() - 1
    assert 1 << levels == places == tensor_count
    place = d // cores
    core = d % cores
    group_rows, block = tokens.shape
    own_rows = group_rows // tensor_count
    slot_count = cotangent.shape[2]
    span_rows = slot_count // dp_count
    value_width = ref_weight.shape[1]
    model_width = pol_gain.shape[0]
    shard = pol_weight.shape[0]
    width = value_width // PARTS
    factor = 1.0 / math.sqrt(dp_count * tensor_count * lengths.shape[2])
    relative = place ^ t

    def flat(p, c, z):
        return (p * cores + c) * tensor_count + z

    def stage(number, held):
        pairs, is_getter = [], jnp.zeros((), jnp.bool_)
        for c in range(cores):
            holders = [0]
            for before in range(number):
                bit = 1 << ((c + before) % levels)
                holders = holders + [q ^ bit for q in holders]
            bit = 1 << ((c + number) % levels)
            for q in holders:
                pairs += [
                    (flat(q ^ z, c, z), flat(q ^ bit ^ z, c, z)) for z in range(tensor_count)
                ]
                is_getter = is_getter | ((core == c) & (relative == (q ^ bit)))
        return lax.ppermute(held, AXES, pairs), is_getter

    got, is_getter = stage(0, pol_weight)

    steps = 4
    feature_step = block // steps
    at = jnp.stack([t, (1 - core) * (steps // 2)]).astype(jnp.int32)
    sent_shape = (own_rows + POWER_ROWS, value_width)

    def at_step(f, at):
        return lax.rem(f + at[1], steps)

    prepared = pl.pallas_call(
        functools.partial(prepare_kernel, tensor_count, steps),
        grid_spec=pltpu.PrefetchScalarGridSpec(
            num_scalar_prefetch=1,
            grid=(steps,),
            in_specs=[
                pl.BlockSpec((group_rows, feature_step), lambda f, at: (0, at_step(f, at))),
                pl.BlockSpec((1, feature_step), lambda f, at: (0, at_step(f, at))),
                pl.BlockSpec((feature_step, value_width), lambda f, at: (at_step(f, at), 0)),
                pl.BlockSpec(
                    (1, feature_step), lambda f, at: (0, at[0] * steps + at_step(f, at))
                ),
            ],
            out_specs=[
                pl.BlockSpec(
                    (group_rows, feature_step), lambda f, at: (0, jnp.minimum(f, steps // 2 - 1))
                ),
                pl.BlockSpec(
                    (group_rows, feature_step), lambda f, at: (0, jnp.maximum(f - steps // 2, 0))
                ),
            ]
            + [pl.BlockSpec(sent_shape, lambda f, at: (0, 0))] * tensor_count,
            scratch_shapes=[
                pltpu.VMEM((group_rows, feature_step), BF16),
                pltpu.VMEM((group_rows, value_width), F32),
                pltpu.VMEM((group_rows, 1), F32),
            ],
        ),
        out_shape=[jax.ShapeDtypeStruct((group_rows, shard), BF16)] * 2
        + [jax.ShapeDtypeStruct(sent_shape, BF16)] * tensor_count,
        compiler_params=pltpu.CompilerParams(vmem_limit_bytes=56 * 2**20),
        cost_estimate=pl.CostEstimate(
            flops=2 * group_rows * block * value_width,
            bytes_accessed=8 * 2**20,
            transcendentals=0,
        ),
        name="prepare",
    )(at, tokens, ref_gain.reshape(1, block), ref_weight, pol_gain.reshape(1, model_width))
    given_rows, kept_rows, *ref_sent = prepared

    ref_got = [ref_sent[0]] + [
        crossed(ref_sent[k], tensor_count, k) for k in range(1, tensor_count)
    ]
    got_rows = swapped(given_rows, dp_count)

    cot = cotangent.reshape(slot_count, value_width)
    got, cot, kept_rows = lax.optimization_barrier((got, cot, kept_rows))
    parts = []
    for j in range(PARTS):
        cols = slice(j * width, (j + 1) * width)
        held_part = jnp.where(is_getter, got[:, cols], pol_weight[:, cols])
        for number in range(1, levels):
            got_part, is_getter_part = stage(number, held_part)
            if number < levels - 1:
                held_part = jnp.where(is_getter_part, got_part, held_part)
        parts.append((held_part, got_part, is_getter_part))
    got_cot = lax.all_to_all(cot, "dp", split_axis=0, concat_axis=0, tiled=True)

    def plane_bit(level):
        return jnp.where(core == 0, 1 << (level % levels), 1 << ((1 + level) % levels))

    chunk_at = []
    for i in range(places):
        away = sum(plane_bit(level) * ((i >> (levels - 1 - level)) & 1) for level in range(levels))
        chunk_at.append(place ^ away ^ turned(t, levels))
    chunk_at = jnp.stack(chunk_at).astype(jnp.int32)

    value_parts = []
    for j in range(PARTS):
        held_part, got_part, is_getter_part = parts[j]
        if j == 0:
            got_part, got_cot = lax.optimization_barrier((got_part, got_cot))
        weight = lax.optimization_barrier(jnp.where(is_getter_part, got_part, held_part))
        value_given = dot(got_rows, weight).astype(BF16)
        value_got = swapped(value_given, dp_count).astype(F32)
        value_parts.append(dot(kept_rows, weight) + value_got)

    smem = pl.BlockSpec(memory_space=pltpu.SMEM)
    vmem = pl.BlockSpec(memory_space=pltpu.VMEM)
    fixed, pull, row_scale, row_at = pl.pallas_call(
        functools.partial(row_kernel, tensor_count, span_rows, model_width),
        in_specs=[smem] * 3 + [vmem] * (2 + tensor_count),
        out_specs=[vmem] * 4,
        out_shape=[
            jax.ShapeDtypeStruct((own_rows, value_width), F32),
            jax.ShapeDtypeStruct((own_rows, 128), F32),
            jax.ShapeDtypeStruct((own_rows, 128), F32),
            jax.ShapeDtypeStruct((own_rows, slot_count), BF16),
        ],
        compiler_params=pltpu.CompilerParams(vmem_limit_bytes=16 * 2**20),
        cost_estimate=pl.CostEstimate(
            flops=2 * own_rows * slot_count * value_width,
            bytes_accessed=2**21,
            transcendentals=0,
        ),
        name="rows",
    )(
        lengths.reshape(-1),
        bins.reshape(-1),
        advantage.reshape(-1),
        logprob_gap.reshape(1, own_rows),
        got_cot,
        *ref_got,
    )

    values, slopes = [], []
    for j in range(PARTS):
        total = value_parts[j]
        for level in range(levels):
            rows = total.shape[0] // 2
            sent = total[rows:].astype(BF16)
            total = total[:rows] + crossed(sent, tensor_count, 1 << level).astype(F32)
        values.append(total * row_scale[:, :1])

        cols = slice(j * width, (j + 1) * width)
        slope = (fixed[:, cols] + pull[:, :1] * total).astype(BF16)
        for level in reversed(range(levels)):
            slope = jnp.concatenate([slope, crossed(slope, tensor_count, 1 << level)], axis=0)
        slopes.append(slope)

    sent = dot_rows(row_at, jnp.concatenate(values, axis=1).astype(BF16)).astype(BF16)

    slopes[0], sent = lax.optimization_barrier((slopes[0], sent))
    policy_values = lax.all_to_all(sent, "dp", split_axis=0, concat_axis=0, tiled=True)

    grad_kept, grad_sent = [], []
    for j in range(PARTS):
        slopes_got = swapped(slopes[j], dp_count)
        chunks = pl.pallas_call(
            functools.partial(grad_kernel, factor),
            grid_spec=pltpu.PrefetchScalarGridSpec(
                num_scalar_prefetch=1,
                grid=(1,),
                in_specs=[
                    pl.BlockSpec((group_rows, shard), lambda i, at: (0, 0)),
                    pl.BlockSpec((group_rows, shard), lambda i, at: (0, 0)),
                    pl.BlockSpec((group_rows, width), lambda i, at: (0, 0)),
                    pl.BlockSpec((group_rows, width), lambda i, at: (0, 0)),
                ],
                out_specs=[pl.BlockSpec((shard // 2, width), lambda i, at: (0, 0))] * 2,
                scratch_shapes=[pltpu.VMEM((shard, width), F32)],
            ),
            out_shape=[
                jax.ShapeDtypeStruct((shard // 2, width), F32),
                jax.ShapeDtypeStruct((shard // 2, width), BF16),
            ],
            compiler_params=pltpu.CompilerParams(vmem_limit_bytes=32 * 2**20),
            cost_estimate=pl.CostEstimate(
                flops=4 * group_rows * shard * width,
                bytes_accessed=4 * 2**20,
                transcendentals=0,
            ),
            name="gradient",
        )(chunk_at, kept_rows, got_rows, slopes[j], slopes_got)
        grad_kept.append(chunks[0])
        grad_sent.append(chunks[1])
    grads = []
    for j in range(PARTS):
        total, given = grad_kept[j], grad_sent[j]
        for level in range(levels):
            pairs = [
                (p * cores + c, (p ^ (1 << ((c + level) % levels))) * cores + c)
                for p in range(places)
                for c in range(cores)
            ]
            total = total + lax.ppermute(given, "dp", pairs).astype(F32)
            half_rows = total.shape[0] // 2
            if level < levels - 1:
                total, given = total[:half_rows], total[half_rows:].astype(BF16)
        grads.append(total.astype(BF16))
    pairs = [
        (flat(p, c, z), flat(z, c, p ^ turned(z, levels)))
        for p in range(places)
        for c in range(cores)
        for z in range(tensor_count)
    ]
    grad, policy_values = lax.optimization_barrier((jnp.concatenate(grads, axis=1), policy_values))
    grad_weight = lax.ppermute(grad, AXES, pairs).astype(F32)
    policy_values = pl.pallas_call(
        write_kernel,
        out_shape=jax.ShapeDtypeStruct(policy_values.shape, BF16),
        cost_estimate=pl.CostEstimate(flops=0, bytes_accessed=2**19, transcendentals=0),
        name="write",
    )(policy_values)
    return (policy_values.reshape(1, 1, slot_count, value_width), grad_weight)


def solution(mesh):
    in_specs = (
        P("dp", "tensor"),
        P("tensor"),
        P("tensor", None),
        P(),
        P("dp", None),
        P("dp", "tensor", None),
        P("dp", "tensor", None),
        P("dp", "tensor", None),
        P(("dp", "tensor")),
        P("dp", "tensor", None, None),
    )
    out_specs = (P("dp", "tensor", None, None), P(("dp", "tensor"), None))
    return jax.shard_map(
        on_device, mesh=mesh, in_specs=in_specs, out_specs=out_specs, check_vma=False
    )
```

```python
import functools
import math

import jax
import jax.numpy as jnp
from jax import lax
from jax.experimental import pallas as pl
from jax.experimental.pallas import tpu as pltpu
from jax.sharding import PartitionSpec as P

EPS = 1e-06
BETA = 1.0
AXES = ("dp", "tensor")
BF16 = jnp.bfloat16
F32 = jnp.float32
POWER_ROWS = 16
PARTS = 2


def dot(a, b):
    return jnp.dot(a, b, preferred_element_type=F32)


def dot_rows(a, b):
    return lax.dot_general(a, b, (((0,), (0,)), ((), ())), preferred_element_type=F32)


def swapped(array, dp_count):
    return lax.ppermute(array, "dp", [(i, i ^ 1) for i in range(dp_count)])


def turned(index, levels):
    return sum(((index >> i) & 1) << (levels - 1 - i) for i in range(levels))


def crossed(array, count, step):
    return lax.ppermute(array, "tensor", [(i, i ^ step) for i in range(count)])


def prepare_kernel(
    count, steps, at, x_ref, gain_ref, weight_ref, pol_ref, given_ref, kept_ref, *refs
):
    sent_refs, (rows_ref, total, square) = refs[:count], refs[count:]
    f = pl.program_id(0)
    own = x_ref.shape[0] // count
    levels = count.bit_length() - 1
    for i in range(count):
        source = jnp.bitwise_xor(at[0], turned(i, levels))
        rows_ref[i * own : (i + 1) * own, :] = x_ref[pl.ds(pl.multiple_of(source * own, own), own), :]
    wide = rows_ref[...].astype(F32)
    gained = (wide * pol_ref[...]).astype(BF16)

    @pl.when(f < steps // 2)
    def _():
        given_ref[...] = gained

    @pl.when(f >= steps // 2)
    def _():
        kept_ref[...] = gained

    part = dot((wide * gain_ref[...]).astype(BF16), weight_ref[...])
    squares = jnp.sum(wide * wide, axis=1, keepdims=True)

    @pl.when(f == 0)
    def _():
        total[...] = part
        square[...] = squares

    @pl.when(f > 0)
    def _():
        total[...] += part
        square[...] += squares

    @pl.when(f == steps - 1)
    def _():
        for i in range(count):
            sent = sent_refs[turned(i, levels)]
            sent[:own, :] = total[i * own : (i + 1) * own, :].astype(BF16)
            power = jnp.broadcast_to(square[i * own : (i + 1) * own, :], (own, 128)).T
            high = power[: POWER_ROWS // 2].astype(BF16).astype(F32)
            low = power[: POWER_ROWS // 2] - high
            sent[own:, :] = jnp.zeros((POWER_ROWS, sent.shape[1]), BF16)
            sent[own:, :own] = jnp.concatenate([high, low], axis=0).astype(BF16)


def row_kernel(
    count, span, model_width, lengths, bins, advantage, gap_ref, cot_ref, *refs
):
    ref_refs, (fixed_ref, pull_ref, scale_ref, row_at_ref) = refs[:count], refs[count:]
    own = pull_ref.shape[0]
    slots = row_at_ref.shape[1]
    row = lax.broadcasted_iota(jnp.int32, (own, slots), 0)
    slot = lax.broadcasted_iota(jnp.int32, (own, slots), 1)
    chosen = jnp.zeros((own, slots), jnp.bool_)
    size = jnp.ones((own, 128), F32)
    weight = jnp.zeros((own, 128), F32)
    start = jnp.int32(0)
    for s in range(lengths.shape[0]):
        end = start + lengths[s]
        inside = (row >= start) & (row < end)
        chosen = chosen | (inside & (slot - bins[s] * span == row - start))
        size = jnp.where(inside[:, :128], lengths[s].astype(F32), size)
        weight = jnp.where(inside[:, :128], advantage[s], weight)
        start = end
    row_at = jnp.where(chosen, 1.0, 0.0).astype(BF16)
    row_at_ref[...] = row_at
    importance = jnp.minimum(jnp.exp(jnp.broadcast_to(gap_ref[...], (128, own)).T), 2.0)
    coef_adv = (weight * importance / size).astype(BF16).astype(F32)
    coef_pull = (BETA / size).astype(BF16).astype(F32)
    total = ref_refs[0][...].astype(F32)
    for ref in ref_refs[1:]:
        total = total + ref[...].astype(F32)
    half = POWER_ROWS // 2
    square = total[own : own + 1, :own] + total[own + half : own + half + 1, :own]
    scale = lax.rsqrt(jnp.broadcast_to(square, (128, own)).T / model_width + EPS)
    reference = (total[:own] * scale[:, :1]).astype(BF16).astype(F32)
    upstream = dot(row_at, cot_ref[...])
    fixed_ref[...] = (coef_adv[:, :1] * upstream - coef_pull[:, :1] * reference) * scale[:, :1]
    pull_ref[...] = coef_pull * scale * scale
    scale_ref[...] = scale


def grad_kernel(factor, at, kept_ref, got_ref, slope_ref, slope_got_ref, *refs):
    *out_refs, grad = refs
    total = dot_rows(kept_ref[...], slope_ref[...]) + dot_rows(got_ref[...], slope_got_ref[...])
    grad[...] = total * factor
    rows = grad.shape[0] // at.shape[0]
    count = at.shape[0] // 2
    for s in range(2 * count):
        chunk = grad[pl.ds(pl.multiple_of(at[s] * rows, rows), rows), :]
        out_ref = out_refs[s // count]
        place = s % count
        out_ref[place * rows : (place + 1) * rows, :] = chunk.astype(out_ref.dtype)


def write_kernel(in_ref, out_ref):
    out_ref[...] = in_ref[...]


def on_device(
    tokens,
    ref_gain,
    ref_weight,
    pol_gain,
    pol_weight,
    lengths,
    bins,
    advantage,
    logprob_gap,
    cotangent,
):
    tensor_count = lax.axis_size("tensor")
    dp_count = lax.axis_size("dp")
    t = lax.axis_index("tensor")
    d = lax.axis_index("dp")
    cores = dp_count // tensor_count
    assert cores == 2
    places = dp_count // cores
    levels = places.bit_length() - 1
    assert 1 << levels == places == tensor_count
    place = d // cores
    core = d % cores
    group_rows, block = tokens.shape
    own_rows = group_rows // tensor_count
    slot_count = cotangent.shape[2]
    span_rows = slot_count // dp_count
    value_width = ref_weight.shape[1]
    model_width = pol_gain.shape[0]
    shard = pol_weight.shape[0]
    width = value_width // PARTS
    factor = 1.0 / math.sqrt(dp_count * tensor_count * lengths.shape[2])
    relative = place ^ t

    def flat(p, c, z):
        return (p * cores + c) * tensor_count + z

    def stage(number, held):
        pairs, is_getter = [], jnp.zeros((), jnp.bool_)
        for c in range(cores):
            holders = [0]
            for before in range(number):
                bit = 1 << ((c + before) % levels)
                holders = holders + [q ^ bit for q in holders]
            bit = 1 << ((c + number) % levels)
            for q in holders:
                pairs += [
                    (flat(q ^ z, c, z), flat(q ^ bit ^ z, c, z)) for z in range(tensor_count)
                ]
                is_getter = is_getter | ((core == c) & (relative == (q ^ bit)))
        return lax.ppermute(held, AXES, pairs), is_getter

    got, is_getter = stage(0, pol_weight)

    steps = 4
    feature_step = block // steps
    at = jnp.stack([t, (1 - core) * (steps // 2)]).astype(jnp.int32)
    sent_shape = (own_rows + POWER_ROWS, value_width)

    def at_step(f, at):
        return lax.rem(f + at[1], steps)

    prepared = pl.pallas_call(
        functools.partial(prepare_kernel, tensor_count, steps),
        grid_spec=pltpu.PrefetchScalarGridSpec(
            num_scalar_prefetch=1,
            grid=(steps,),
            in_specs=[
                pl.BlockSpec((group_rows, feature_step), lambda f, at: (0, at_step(f, at))),
                pl.BlockSpec((1, feature_step), lambda f, at: (0, at_step(f, at))),
                pl.BlockSpec((feature_step, value_width), lambda f, at: (at_step(f, at), 0)),
                pl.BlockSpec(
                    (1, feature_step), lambda f, at: (0, at[0] * steps + at_step(f, at))
                ),
            ],
            out_specs=[
                pl.BlockSpec(
                    (group_rows, feature_step), lambda f, at: (0, jnp.minimum(f, steps // 2 - 1))
                ),
                pl.BlockSpec(
                    (group_rows, feature_step), lambda f, at: (0, jnp.maximum(f - steps // 2, 0))
                ),
            ]
            + [pl.BlockSpec(sent_shape, lambda f, at: (0, 0))] * tensor_count,
            scratch_shapes=[
                pltpu.VMEM((group_rows, feature_step), BF16),
                pltpu.VMEM((group_rows, value_width), F32),
                pltpu.VMEM((group_rows, 1), F32),
            ],
        ),
        out_shape=[jax.ShapeDtypeStruct((group_rows, shard), BF16)] * 2
        + [jax.ShapeDtypeStruct(sent_shape, BF16)] * tensor_count,
        compiler_params=pltpu.CompilerParams(vmem_limit_bytes=56 * 2**20),
        cost_estimate=pl.CostEstimate(
            flops=2 * group_rows * block * value_width,
            bytes_accessed=8 * 2**20,
            transcendentals=0,
        ),
        name="prepare",
    )(at, tokens, ref_gain.reshape(1, block), ref_weight, pol_gain.reshape(1, model_width))
    given_rows, kept_rows, *ref_sent = prepared

    ref_got = [ref_sent[0]] + [
        crossed(ref_sent[k], tensor_count, k) for k in range(1, tensor_count)
    ]
    got_rows = swapped(given_rows, dp_count)

    cot = cotangent.reshape(slot_count, value_width)
    got, cot, kept_rows = lax.optimization_barrier((got, cot, kept_rows))
    parts = []
    for j in range(PARTS):
        cols = slice(j * width, (j + 1) * width)
        held_part = jnp.where(is_getter, got[:, cols], pol_weight[:, cols])
        for number in range(1, levels):
            got_part, is_getter_part = stage(number, held_part)
            if number < levels - 1:
                held_part = jnp.where(is_getter_part, got_part, held_part)
        parts.append((held_part, got_part, is_getter_part))
    got_cot = lax.all_to_all(cot, "dp", split_axis=0, concat_axis=0, tiled=True)

    def plane_bit(level):
        return jnp.where(core == 0, 1 << (level % levels), 1 << ((1 + level) % levels))

    chunk_at = []
    for i in range(places):
        away = sum(plane_bit(level) * ((i >> (levels - 1 - level)) & 1) for level in range(levels))
        chunk_at.append(place ^ away ^ turned(t, levels))
    chunk_at = jnp.stack(chunk_at).astype(jnp.int32)

    value_parts = []
    for j in range(PARTS):
        held_part, got_part, is_getter_part = parts[j]
        if j == 0:
            got_part, got_cot = lax.optimization_barrier((got_part, got_cot))
        weight = jnp.where(is_getter_part, got_part, held_part)
        value_given = dot(got_rows, weight).astype(BF16)
        value_got = swapped(value_given, dp_count).astype(F32)
        value_parts.append(dot(kept_rows, weight) + value_got)

    smem = pl.BlockSpec(memory_space=pltpu.SMEM)
    vmem = pl.BlockSpec(memory_space=pltpu.VMEM)
    fixed, pull, row_scale, row_at = pl.pallas_call(
        functools.partial(row_kernel, tensor_count, span_rows, model_width),
        in_specs=[smem] * 3 + [vmem] * (2 + tensor_count),
        out_specs=[vmem] * 4,
        out_shape=[
            jax.ShapeDtypeStruct((own_rows, value_width), F32),
            jax.ShapeDtypeStruct((own_rows, 128), F32),
            jax.ShapeDtypeStruct((own_rows, 128), F32),
            jax.ShapeDtypeStruct((own_rows, slot_count), BF16),
        ],
        compiler_params=pltpu.CompilerParams(vmem_limit_bytes=16 * 2**20),
        cost_estimate=pl.CostEstimate(
            flops=2 * own_rows * slot_count * value_width,
            bytes_accessed=2**21,
            transcendentals=0,
        ),
        name="rows",
    )(
        lengths.reshape(-1),
        bins.reshape(-1),
        advantage.reshape(-1),
        logprob_gap.reshape(1, own_rows),
        got_cot,
        *ref_got,
    )

    values, slopes = [], []
    for j in range(PARTS):
        total = value_parts[j]
        for level in range(levels):
            rows = total.shape[0] // 2
            sent = total[rows:].astype(BF16)
            total = total[:rows] + crossed(sent, tensor_count, 1 << level).astype(F32)
        values.append(total * row_scale[:, :1])

        cols = slice(j * width, (j + 1) * width)
        slope = (fixed[:, cols] + pull[:, :1] * total).astype(BF16)
        for level in reversed(range(levels)):
            slope = jnp.concatenate([slope, crossed(slope, tensor_count, 1 << level)], axis=0)
        slopes.append(slope)

    sent = dot_rows(row_at, jnp.concatenate(values, axis=1).astype(BF16)).astype(BF16)

    slopes[0], sent = lax.optimization_barrier((slopes[0], sent))
    policy_values = lax.all_to_all(sent, "dp", split_axis=0, concat_axis=0, tiled=True)

    grad_kept, grad_sent = [], []
    for j in range(PARTS):
        slopes_got = swapped(slopes[j], dp_count)
        chunks = pl.pallas_call(
            functools.partial(grad_kernel, factor),
            grid_spec=pltpu.PrefetchScalarGridSpec(
                num_scalar_prefetch=1,
                grid=(1,),
                in_specs=[
                    pl.BlockSpec((group_rows, shard), lambda i, at: (0, 0)),
                    pl.BlockSpec((group_rows, shard), lambda i, at: (0, 0)),
                    pl.BlockSpec((group_rows, width), lambda i, at: (0, 0)),
                    pl.BlockSpec((group_rows, width), lambda i, at: (0, 0)),
                ],
                out_specs=[pl.BlockSpec((shard // 2, width), lambda i, at: (0, 0))] * 2,
                scratch_shapes=[pltpu.VMEM((shard, width), F32)],
            ),
            out_shape=[
                jax.ShapeDtypeStruct((shard // 2, width), F32),
                jax.ShapeDtypeStruct((shard // 2, width), BF16),
            ],
            compiler_params=pltpu.CompilerParams(vmem_limit_bytes=32 * 2**20),
            cost_estimate=pl.CostEstimate(
                flops=4 * group_rows * shard * width,
                bytes_accessed=4 * 2**20,
                transcendentals=0,
            ),
            name="gradient",
        )(chunk_at, kept_rows, got_rows, slopes[j], slopes_got)
        grad_kept.append(chunks[0])
        grad_sent.append(chunks[1])
    grads = []
    for j in range(PARTS):
        total, given = grad_kept[j], grad_sent[j]
        for level in range(levels):
            pairs = [
                (p * cores + c, (p ^ (1 << ((c + level) % levels))) * cores + c)
                for p in range(places)
                for c in range(cores)
            ]
            total = total + lax.ppermute(given, "dp", pairs).astype(F32)
            half_rows = total.shape[0] // 2
            if level < levels - 1:
                total, given = total[:half_rows], total[half_rows:].astype(BF16)
        grads.append(total.astype(BF16))
    pairs = [
        (flat(p, c, z), flat(z, c, p ^ turned(z, levels)))
        for p in range(places)
        for c in range(cores)
        for z in range(tensor_count)
    ]
    grad, policy_values = lax.optimization_barrier((jnp.concatenate(grads, axis=1), policy_values))
    grad_weight = lax.ppermute(grad, AXES, pairs).astype(F32)
    policy_values = pl.pallas_call(
        write_kernel,
        out_shape=jax.ShapeDtypeStruct(policy_values.shape, BF16),
        cost_estimate=pl.CostEstimate(flops=0, bytes_accessed=2**19, transcendentals=0),
        name="write",
    )(policy_values)
    return (policy_values.reshape(1, 1, slot_count, value_width), grad_weight)


def solution(mesh):
    in_specs = (
        P("dp", "tensor"),
        P("tensor"),
        P("tensor", None),
        P(),
        P("dp", None),
        P("dp", "tensor", None),
        P("dp", "tensor", None),
        P("dp", "tensor", None),
        P(("dp", "tensor")),
        P("dp", "tensor", None, None),
    )
    out_specs = (P("dp", "tensor", None, None), P(("dp", "tensor"), None))
    return jax.shard_map(
        on_device, mesh=mesh, in_specs=in_specs, out_specs=out_specs, check_vma=False
    )
```

```python
import functools
import math

import jax
import jax.numpy as jnp
from jax import lax
from jax.experimental import pallas as pl
from jax.experimental.pallas import tpu as pltpu
from jax.sharding import PartitionSpec as P

EPS = 1e-06
BETA = 1.0
AXES = ("dp", "tensor")
BF16 = jnp.bfloat16
F32 = jnp.float32
POWER_ROWS = 16
PARTS = 2


def dot(a, b):
    return jnp.dot(a, b, preferred_element_type=F32)


def dot_rows(a, b):
    return lax.dot_general(a, b, (((0,), (0,)), ((), ())), preferred_element_type=F32)


def swapped(array, dp_count):
    return lax.ppermute(array, "dp", [(i, i ^ 1) for i in range(dp_count)])


def turned(index, levels):
    return sum(((index >> i) & 1) << (levels - 1 - i) for i in range(levels))


def crossed(array, count, step):
    return lax.ppermute(array, "tensor", [(i, i ^ step) for i in range(count)])


def prepare_kernel(
    count, steps, at, x_ref, gain_ref, weight_ref, pol_ref, given_ref, kept_ref, *refs
):
    sent_refs, (rows_ref, total, square) = refs[:count], refs[count:]
    f = pl.program_id(0)
    own = x_ref.shape[0] // count
    levels = count.bit_length() - 1
    for i in range(count):
        source = jnp.bitwise_xor(at[0], turned(i, levels))
        rows_ref[i * own : (i + 1) * own, :] = x_ref[pl.ds(pl.multiple_of(source * own, own), own), :]
    wide = rows_ref[...].astype(F32)
    gained = (wide * pol_ref[...]).astype(BF16)

    @pl.when(f < steps // 2)
    def _():
        given_ref[...] = gained

    @pl.when(f >= steps // 2)
    def _():
        kept_ref[...] = gained

    part = dot((wide * gain_ref[...]).astype(BF16), weight_ref[...])
    squares = jnp.sum(wide * wide, axis=1, keepdims=True)

    @pl.when(f == 0)
    def _():
        total[...] = part
        square[...] = squares

    @pl.when(f > 0)
    def _():
        total[...] += part
        square[...] += squares

    @pl.when(f == steps - 1)
    def _():
        for i in range(count):
            sent = sent_refs[turned(i, levels)]
            sent[:own, :] = total[i * own : (i + 1) * own, :].astype(BF16)
            power = jnp.broadcast_to(square[i * own : (i + 1) * own, :], (own, 128)).T
            high = power[: POWER_ROWS // 2].astype(BF16).astype(F32)
            low = power[: POWER_ROWS // 2] - high
            sent[own:, :] = jnp.zeros((POWER_ROWS, sent.shape[1]), BF16)
            sent[own:, :own] = jnp.concatenate([high, low], axis=0).astype(BF16)


def row_kernel(
    count, span, model_width, lengths, bins, advantage, gap_ref, cot_ref, *refs
):
    ref_refs, (fixed_ref, pull_ref, scale_ref, row_at_ref) = refs[:count], refs[count:]
    own = pull_ref.shape[0]
    slots = row_at_ref.shape[1]
    row = lax.broadcasted_iota(jnp.int32, (own, slots), 0)
    slot = lax.broadcasted_iota(jnp.int32, (own, slots), 1)
    chosen = jnp.zeros((own, slots), jnp.bool_)
    size = jnp.ones((own, 128), F32)
    weight = jnp.zeros((own, 128), F32)
    start = jnp.int32(0)
    for s in range(lengths.shape[0]):
        end = start + lengths[s]
        inside = (row >= start) & (row < end)
        chosen = chosen | (inside & (slot - bins[s] * span == row - start))
        size = jnp.where(inside[:, :128], lengths[s].astype(F32), size)
        weight = jnp.where(inside[:, :128], advantage[s], weight)
        start = end
    row_at = jnp.where(chosen, 1.0, 0.0).astype(BF16)
    row_at_ref[...] = row_at
    importance = jnp.minimum(jnp.exp(jnp.broadcast_to(gap_ref[...], (128, own)).T), 2.0)
    coef_adv = (weight * importance / size).astype(BF16).astype(F32)
    coef_pull = (BETA / size).astype(BF16).astype(F32)
    total = ref_refs[0][...].astype(F32)
    for ref in ref_refs[1:]:
        total = total + ref[...].astype(F32)
    half = POWER_ROWS // 2
    square = total[own : own + 1, :own] + total[own + half : own + half + 1, :own]
    scale = lax.rsqrt(jnp.broadcast_to(square, (128, own)).T / model_width + EPS)
    reference = (total[:own] * scale[:, :1]).astype(BF16).astype(F32)
    upstream = dot(row_at, cot_ref[...])
    fixed_ref[...] = (coef_adv[:, :1] * upstream - coef_pull[:, :1] * reference) * scale[:, :1]
    pull_ref[...] = coef_pull * scale * scale
    scale_ref[...] = scale


def grad_kernel(factor, at, kept_ref, got_ref, slope_ref, slope_got_ref, *refs):
    *out_refs, grad = refs
    total = dot_rows(kept_ref[...], slope_ref[...]) + dot_rows(got_ref[...], slope_got_ref[...])
    grad[...] = total * factor
    rows = grad.shape[0] // at.shape[0]
    count = at.shape[0] // 2
    for s in range(2 * count):
        chunk = grad[pl.ds(pl.multiple_of(at[s] * rows, rows), rows), :]
        out_ref = out_refs[s // count]
        place = s % count
        out_ref[place * rows : (place + 1) * rows, :] = chunk.astype(out_ref.dtype)


def write_kernel(in_ref, out_ref):
    out_ref[...] = in_ref[...]


def on_device(
    tokens,
    ref_gain,
    ref_weight,
    pol_gain,
    pol_weight,
    lengths,
    bins,
    advantage,
    logprob_gap,
    cotangent,
):
    tensor_count = lax.axis_size("tensor")
    dp_count = lax.axis_size("dp")
    t = lax.axis_index("tensor")
    d = lax.axis_index("dp")
    cores = dp_count // tensor_count
    assert cores == 2
    places = dp_count // cores
    levels = places.bit_length() - 1
    assert 1 << levels == places == tensor_count
    place = d // cores
    core = d % cores
    group_rows, block = tokens.shape
    own_rows = group_rows // tensor_count
    slot_count = cotangent.shape[2]
    span_rows = slot_count // dp_count
    value_width = ref_weight.shape[1]
    model_width = pol_gain.shape[0]
    shard = pol_weight.shape[0]
    width = value_width // PARTS
    factor = 1.0 / math.sqrt(dp_count * tensor_count * lengths.shape[2])
    relative = place ^ t

    def flat(p, c, z):
        return (p * cores + c) * tensor_count + z

    def stage(number, held):
        pairs, is_getter = [], jnp.zeros((), jnp.bool_)
        for c in range(cores):
            holders = [0]
            for before in range(number):
                bit = 1 << ((c + before) % levels)
                holders = holders + [q ^ bit for q in holders]
            bit = 1 << ((c + number) % levels)
            for q in holders:
                pairs += [
                    (flat(q ^ z, c, z), flat(q ^ bit ^ z, c, z)) for z in range(tensor_count)
                ]
                is_getter = is_getter | ((core == c) & (relative == (q ^ bit)))
        return lax.ppermute(held, AXES, pairs), is_getter

    got, is_getter = stage(0, pol_weight)

    steps = 4
    feature_step = block // steps
    at = jnp.stack([t, (1 - core) * (steps // 2)]).astype(jnp.int32)
    sent_shape = (own_rows + POWER_ROWS, value_width)

    def at_step(f, at):
        return lax.rem(f + at[1], steps)

    prepared = pl.pallas_call(
        functools.partial(prepare_kernel, tensor_count, steps),
        grid_spec=pltpu.PrefetchScalarGridSpec(
            num_scalar_prefetch=1,
            grid=(steps,),
            in_specs=[
                pl.BlockSpec((group_rows, feature_step), lambda f, at: (0, at_step(f, at))),
                pl.BlockSpec((1, feature_step), lambda f, at: (0, at_step(f, at))),
                pl.BlockSpec((feature_step, value_width), lambda f, at: (at_step(f, at), 0)),
                pl.BlockSpec(
                    (1, feature_step), lambda f, at: (0, at[0] * steps + at_step(f, at))
                ),
            ],
            out_specs=[
                pl.BlockSpec(
                    (group_rows, feature_step), lambda f, at: (0, jnp.minimum(f, steps // 2 - 1))
                ),
                pl.BlockSpec(
                    (group_rows, feature_step), lambda f, at: (0, jnp.maximum(f - steps // 2, 0))
                ),
            ]
            + [pl.BlockSpec(sent_shape, lambda f, at: (0, 0))] * tensor_count,
            scratch_shapes=[
                pltpu.VMEM((group_rows, feature_step), BF16),
                pltpu.VMEM((group_rows, value_width), F32),
                pltpu.VMEM((group_rows, 1), F32),
            ],
        ),
        out_shape=[jax.ShapeDtypeStruct((group_rows, shard), BF16)] * 2
        + [jax.ShapeDtypeStruct(sent_shape, BF16)] * tensor_count,
        compiler_params=pltpu.CompilerParams(vmem_limit_bytes=56 * 2**20),
        cost_estimate=pl.CostEstimate(
            flops=2 * group_rows * block * value_width,
            bytes_accessed=8 * 2**20,
            transcendentals=0,
        ),
        name="prepare",
    )(at, tokens, ref_gain.reshape(1, block), ref_weight, pol_gain.reshape(1, model_width))
    given_rows, kept_rows, *ref_sent = prepared

    ref_got = [ref_sent[0]] + [
        crossed(ref_sent[k], tensor_count, k) for k in range(1, tensor_count)
    ]
    got_rows = swapped(given_rows, dp_count)

    cot = cotangent.reshape(slot_count, value_width)
    got, cot, kept_rows = lax.optimization_barrier((got, cot, kept_rows))
    parts = []
    for j in range(PARTS):
        cols = slice(j * width, (j + 1) * width)
        held_part = jnp.where(is_getter, got[:, cols], pol_weight[:, cols])
        for number in range(1, levels):
            got_part, is_getter_part = stage(number, held_part)
            if number < levels - 1:
                held_part = jnp.where(is_getter_part, got_part, held_part)
        parts.append((held_part, got_part, is_getter_part))
    got_cot = lax.all_to_all(cot, "dp", split_axis=0, concat_axis=0, tiled=True)

    def plane_bit(level):
        return jnp.where(core == 0, 1 << (level % levels), 1 << ((1 + level) % levels))

    chunk_at = []
    for i in range(places):
        away = sum(plane_bit(level) * ((i >> (levels - 1 - level)) & 1) for level in range(levels))
        chunk_at.append(place ^ away ^ turned(t, levels))
    chunk_at = jnp.stack(chunk_at).astype(jnp.int32)

    value_parts = []
    for j in range(PARTS):
        held_part, got_part, is_getter_part = parts[j]
        if j == 0:
            got_part, got_cot = lax.optimization_barrier((got_part, got_cot))
        weight = jnp.where(is_getter_part, got_part, held_part)
        value_given = dot(got_rows, weight).astype(BF16)
        value_got = swapped(value_given, dp_count).astype(F32)
        value_parts.append(dot(kept_rows, weight) + value_got)

    tied = (value_parts[-1], lengths, bins, advantage, logprob_gap)
    value_parts[-1], lengths, bins, advantage, logprob_gap = lax.optimization_barrier(tied)
    smem = pl.BlockSpec(memory_space=pltpu.SMEM)
    vmem = pl.BlockSpec(memory_space=pltpu.VMEM)
    fixed, pull, row_scale, row_at = pl.pallas_call(
        functools.partial(row_kernel, tensor_count, span_rows, model_width),
        in_specs=[smem] * 3 + [vmem] * (2 + tensor_count),
        out_specs=[vmem] * 4,
        out_shape=[
            jax.ShapeDtypeStruct((own_rows, value_width), F32),
            jax.ShapeDtypeStruct((own_rows, 128), F32),
            jax.ShapeDtypeStruct((own_rows, 128), F32),
            jax.ShapeDtypeStruct((own_rows, slot_count), BF16),
        ],
        compiler_params=pltpu.CompilerParams(vmem_limit_bytes=16 * 2**20),
        cost_estimate=pl.CostEstimate(
            flops=2 * own_rows * slot_count * value_width,
            bytes_accessed=2**21,
            transcendentals=0,
        ),
        name="rows",
    )(
        lengths.reshape(-1),
        bins.reshape(-1),
        advantage.reshape(-1),
        logprob_gap.reshape(1, own_rows),
        got_cot,
        *ref_got,
    )

    values, slopes = [], []
    for j in range(PARTS):
        total = value_parts[j]
        for level in range(levels):
            rows = total.shape[0] // 2
            sent = total[rows:].astype(BF16)
            total = total[:rows] + crossed(sent, tensor_count, 1 << level).astype(F32)
        values.append(total * row_scale[:, :1])

        cols = slice(j * width, (j + 1) * width)
        slope = (fixed[:, cols] + pull[:, :1] * total).astype(BF16)
        for level in reversed(range(levels)):
            slope = jnp.concatenate([slope, crossed(slope, tensor_count, 1 << level)], axis=0)
        slopes.append(slope)

    sent = dot_rows(row_at, jnp.concatenate(values, axis=1).astype(BF16)).astype(BF16)

    slopes[0], sent = lax.optimization_barrier((slopes[0], sent))
    policy_values = lax.all_to_all(sent, "dp", split_axis=0, concat_axis=0, tiled=True)

    grad_kept, grad_sent = [], []
    for j in range(PARTS):
        slopes_got = swapped(slopes[j], dp_count)
        chunks = pl.pallas_call(
            functools.partial(grad_kernel, factor),
            grid_spec=pltpu.PrefetchScalarGridSpec(
                num_scalar_prefetch=1,
                grid=(1,),
                in_specs=[
                    pl.BlockSpec((group_rows, shard), lambda i, at: (0, 0)),
                    pl.BlockSpec((group_rows, shard), lambda i, at: (0, 0)),
                    pl.BlockSpec((group_rows, width), lambda i, at: (0, 0)),
                    pl.BlockSpec((group_rows, width), lambda i, at: (0, 0)),
                ],
                out_specs=[pl.BlockSpec((shard // 2, width), lambda i, at: (0, 0))] * 2,
                scratch_shapes=[pltpu.VMEM((shard, width), F32)],
            ),
            out_shape=[
                jax.ShapeDtypeStruct((shard // 2, width), F32),
                jax.ShapeDtypeStruct((shard // 2, width), BF16),
            ],
            compiler_params=pltpu.CompilerParams(vmem_limit_bytes=32 * 2**20),
            cost_estimate=pl.CostEstimate(
                flops=4 * group_rows * shard * width,
                bytes_accessed=4 * 2**20,
                transcendentals=0,
            ),
            name="gradient",
        )(chunk_at, kept_rows, got_rows, slopes[j], slopes_got)
        grad_kept.append(chunks[0])
        grad_sent.append(chunks[1])
    grads = []
    for j in range(PARTS):
        total, given = grad_kept[j], grad_sent[j]
        for level in range(levels):
            pairs = [
                (p * cores + c, (p ^ (1 << ((c + level) % levels))) * cores + c)
                for p in range(places)
                for c in range(cores)
            ]
            total = total + lax.ppermute(given, "dp", pairs).astype(F32)
            half_rows = total.shape[0] // 2
            if level < levels - 1:
                total, given = total[:half_rows], total[half_rows:].astype(BF16)
        grads.append(total.astype(BF16))
    pairs = [
        (flat(p, c, z), flat(z, c, p ^ turned(z, levels)))
        for p in range(places)
        for c in range(cores)
        for z in range(tensor_count)
    ]
    grad, policy_values = lax.optimization_barrier((jnp.concatenate(grads, axis=1), policy_values))
    grad_weight = lax.ppermute(grad, AXES, pairs).astype(F32)
    policy_values = pl.pallas_call(
        write_kernel,
        out_shape=jax.ShapeDtypeStruct(policy_values.shape, BF16),
        cost_estimate=pl.CostEstimate(flops=0, bytes_accessed=2**19, transcendentals=0),
        name="write",
    )(policy_values)
    return (policy_values.reshape(1, 1, slot_count, value_width), grad_weight)


def solution(mesh):
    in_specs = (
        P("dp", "tensor"),
        P("tensor"),
        P("tensor", None),
        P(),
        P("dp", None),
        P("dp", "tensor", None),
        P("dp", "tensor", None),
        P("dp", "tensor", None),
        P(("dp", "tensor")),
        P("dp", "tensor", None, None),
    )
    out_specs = (P("dp", "tensor", None, None), P(("dp", "tensor"), None))
    return jax.shard_map(
        on_device, mesh=mesh, in_specs=in_specs, out_specs=out_specs, check_vma=False
    )
```

```python
import functools
import math

import jax
import jax.numpy as jnp
from jax import lax
from jax.experimental import pallas as pl
from jax.experimental.pallas import tpu as pltpu
from jax.sharding import PartitionSpec as P

EPS = 1e-06
BETA = 1.0
AXES = ("dp", "tensor")
BF16 = jnp.bfloat16
F32 = jnp.float32
POWER_ROWS = 16
PARTS = 2


def dot(a, b):
    return jnp.dot(a, b, preferred_element_type=F32)


def dot_rows(a, b):
    return lax.dot_general(a, b, (((0,), (0,)), ((), ())), preferred_element_type=F32)


def swapped(array, dp_count):
    return lax.ppermute(array, "dp", [(i, i ^ 1) for i in range(dp_count)])


def turned(index, levels):
    return sum(((index >> i) & 1) << (levels - 1 - i) for i in range(levels))


def crossed(array, count, step):
    return lax.ppermute(array, "tensor", [(i, i ^ step) for i in range(count)])


def prepare_kernel(
    count, steps, at, x_ref, gain_ref, weight_ref, pol_ref, given_ref, kept_ref, *refs
):
    sent_refs, (rows_ref, total, square) = refs[:count], refs[count:]
    f = pl.program_id(0)
    own = x_ref.shape[0] // count
    levels = count.bit_length() - 1
    for i in range(count):
        source = jnp.bitwise_xor(at[0], turned(i, levels))
        rows_ref[i * own : (i + 1) * own, :] = x_ref[pl.ds(pl.multiple_of(source * own, own), own), :]
    wide = rows_ref[...].astype(F32)
    gained = (wide * pol_ref[...]).astype(BF16)

    @pl.when(f < steps // 2)
    def _():
        given_ref[...] = gained

    @pl.when(f >= steps // 2)
    def _():
        kept_ref[...] = gained

    part = dot((wide * gain_ref[...]).astype(BF16), weight_ref[...])
    squares = jnp.sum(wide * wide, axis=1, keepdims=True)

    @pl.when(f == 0)
    def _():
        total[...] = part
        square[...] = squares

    @pl.when(f > 0)
    def _():
        total[...] += part
        square[...] += squares

    @pl.when(f == steps - 1)
    def _():
        for i in range(count):
            sent = sent_refs[turned(i, levels)]
            sent[:own, :] = total[i * own : (i + 1) * own, :].astype(BF16)
            power = jnp.broadcast_to(square[i * own : (i + 1) * own, :], (own, 128)).T
            high = power[: POWER_ROWS // 2].astype(BF16).astype(F32)
            low = power[: POWER_ROWS // 2] - high
            sent[own:, :] = jnp.zeros((POWER_ROWS, sent.shape[1]), BF16)
            sent[own:, :own] = jnp.concatenate([high, low], axis=0).astype(BF16)


def row_kernel(
    count, span, model_width, lengths, bins, advantage, gap_ref, cot_ref, *refs
):
    ref_refs, (fixed_ref, pull_ref, scale_ref, row_at_ref) = refs[:count], refs[count:]
    own = pull_ref.shape[0]
    slots = row_at_ref.shape[1]
    row = lax.broadcasted_iota(jnp.int32, (own, slots), 0)
    slot = lax.broadcasted_iota(jnp.int32, (own, slots), 1)
    chosen = jnp.zeros((own, slots), jnp.bool_)
    size = jnp.ones((own, 128), F32)
    weight = jnp.zeros((own, 128), F32)
    start = jnp.int32(0)
    for s in range(lengths.shape[0]):
        end = start + lengths[s]
        inside = (row >= start) & (row < end)
        chosen = chosen | (inside & (slot - bins[s] * span == row - start))
        size = jnp.where(inside[:, :128], lengths[s].astype(F32), size)
        weight = jnp.where(inside[:, :128], advantage[s], weight)
        start = end
    row_at = jnp.where(chosen, 1.0, 0.0).astype(BF16)
    row_at_ref[...] = row_at
    importance = jnp.minimum(jnp.exp(jnp.broadcast_to(gap_ref[...], (128, own)).T), 2.0)
    coef_adv = (weight * importance / size).astype(BF16).astype(F32)
    coef_pull = (BETA / size).astype(BF16).astype(F32)
    total = ref_refs[0][...].astype(F32)
    for ref in ref_refs[1:]:
        total = total + ref[...].astype(F32)
    half = POWER_ROWS // 2
    square = total[own : own + 1, :own] + total[own + half : own + half + 1, :own]
    scale = lax.rsqrt(jnp.broadcast_to(square, (128, own)).T / model_width + EPS)
    reference = (total[:own] * scale[:, :1]).astype(BF16).astype(F32)
    upstream = dot(row_at, cot_ref[...])
    fixed_ref[...] = (coef_adv[:, :1] * upstream - coef_pull[:, :1] * reference) * scale[:, :1]
    pull_ref[...] = coef_pull * scale * scale
    scale_ref[...] = scale


def grad_kernel(factor, at, kept_ref, got_ref, slope_ref, slope_got_ref, *refs):
    *out_refs, grad = refs
    total = dot_rows(kept_ref[...], slope_ref[...]) + dot_rows(got_ref[...], slope_got_ref[...])
    grad[...] = total * factor
    rows = grad.shape[0] // at.shape[0]
    count = at.shape[0] // 2
    for s in range(2 * count):
        chunk = grad[pl.ds(pl.multiple_of(at[s] * rows, rows), rows), :]
        out_ref = out_refs[s // count]
        place = s % count
        out_ref[place * rows : (place + 1) * rows, :] = chunk.astype(out_ref.dtype)


def write_kernel(in_ref, out_ref):
    out_ref[...] = in_ref[...]


def on_device(
    tokens,
    ref_gain,
    ref_weight,
    pol_gain,
    pol_weight,
    lengths,
    bins,
    advantage,
    logprob_gap,
    cotangent,
):
    tensor_count = lax.axis_size("tensor")
    dp_count = lax.axis_size("dp")
    t = lax.axis_index("tensor")
    d = lax.axis_index("dp")
    cores = dp_count // tensor_count
    assert cores == 2
    places = dp_count // cores
    levels = places.bit_length() - 1
    assert 1 << levels == places == tensor_count
    place = d // cores
    core = d % cores
    group_rows, block = tokens.shape
    own_rows = group_rows // tensor_count
    slot_count = cotangent.shape[2]
    span_rows = slot_count // dp_count
    value_width = ref_weight.shape[1]
    model_width = pol_gain.shape[0]
    shard = pol_weight.shape[0]
    width = value_width // PARTS
    factor = 1.0 / math.sqrt(dp_count * tensor_count * lengths.shape[2])
    relative = place ^ t

    def flat(p, c, z):
        return (p * cores + c) * tensor_count + z

    def stage(number, held):
        pairs, is_getter = [], jnp.zeros((), jnp.bool_)
        for c in range(cores):
            holders = [0]
            for before in range(number):
                bit = 1 << ((c + before) % levels)
                holders = holders + [q ^ bit for q in holders]
            bit = 1 << ((c + number) % levels)
            for q in holders:
                pairs += [
                    (flat(q ^ z, c, z), flat(q ^ bit ^ z, c, z)) for z in range(tensor_count)
                ]
                is_getter = is_getter | ((core == c) & (relative == (q ^ bit)))
        return lax.ppermute(held, AXES, pairs), is_getter

    got, is_getter = stage(0, pol_weight)

    steps = 4
    feature_step = block // steps
    at = jnp.stack([t, (1 - core) * (steps // 2)]).astype(jnp.int32)
    sent_shape = (own_rows + POWER_ROWS, value_width)

    def at_step(f, at):
        return lax.rem(f + at[1], steps)

    prepared = pl.pallas_call(
        functools.partial(prepare_kernel, tensor_count, steps),
        grid_spec=pltpu.PrefetchScalarGridSpec(
            num_scalar_prefetch=1,
            grid=(steps,),
            in_specs=[
                pl.BlockSpec((group_rows, feature_step), lambda f, at: (0, at_step(f, at))),
                pl.BlockSpec((1, feature_step), lambda f, at: (0, at_step(f, at))),
                pl.BlockSpec((feature_step, value_width), lambda f, at: (at_step(f, at), 0)),
                pl.BlockSpec(
                    (1, feature_step), lambda f, at: (0, at[0] * steps + at_step(f, at))
                ),
            ],
            out_specs=[
                pl.BlockSpec(
                    (group_rows, feature_step), lambda f, at: (0, jnp.minimum(f, steps // 2 - 1))
                ),
                pl.BlockSpec(
                    (group_rows, feature_step), lambda f, at: (0, jnp.maximum(f - steps // 2, 0))
                ),
            ]
            + [pl.BlockSpec(sent_shape, lambda f, at: (0, 0))] * tensor_count,
            scratch_shapes=[
                pltpu.VMEM((group_rows, feature_step), BF16),
                pltpu.VMEM((group_rows, value_width), F32),
                pltpu.VMEM((group_rows, 1), F32),
            ],
        ),
        out_shape=[jax.ShapeDtypeStruct((group_rows, shard), BF16)] * 2
        + [jax.ShapeDtypeStruct(sent_shape, BF16)] * tensor_count,
        compiler_params=pltpu.CompilerParams(vmem_limit_bytes=56 * 2**20),
        cost_estimate=pl.CostEstimate(
            flops=2 * group_rows * block * value_width,
            bytes_accessed=8 * 2**20,
            transcendentals=0,
        ),
        name="prepare",
    )(at, tokens, ref_gain.reshape(1, block), ref_weight, pol_gain.reshape(1, model_width))
    given_rows, kept_rows, *ref_sent = prepared

    ref_got = [ref_sent[0]] + [
        crossed(ref_sent[k], tensor_count, k) for k in range(1, tensor_count)
    ]
    got_rows = swapped(given_rows, dp_count)

    cot = cotangent.reshape(slot_count, value_width)
    held = jnp.where(is_getter, got, pol_weight)
    held, cot, kept_rows = lax.optimization_barrier((held, cot, kept_rows))
    parts = []
    for j in range(PARTS):
        cols = slice(j * width, (j + 1) * width)
        held_part = held[:, cols]
        for number in range(1, levels):
            got_part, is_getter_part = stage(number, held_part)
            if number < levels - 1:
                held_part = jnp.where(is_getter_part, got_part, held_part)
        parts.append((held_part, got_part, is_getter_part))
    got_cot = lax.all_to_all(cot, "dp", split_axis=0, concat_axis=0, tiled=True)

    def plane_bit(level):
        return jnp.where(core == 0, 1 << (level % levels), 1 << ((1 + level) % levels))

    chunk_at = []
    for i in range(places):
        away = sum(plane_bit(level) * ((i >> (levels - 1 - level)) & 1) for level in range(levels))
        chunk_at.append(place ^ away ^ turned(t, levels))
    chunk_at = jnp.stack(chunk_at).astype(jnp.int32)

    value_parts = []
    for j in range(PARTS):
        held_part, got_part, is_getter_part = parts[j]
        if j == 0:
            got_part, got_cot = lax.optimization_barrier((got_part, got_cot))
        weight = jnp.where(is_getter_part, got_part, held_part)
        value_given = dot(got_rows, weight).astype(BF16)
        value_got = swapped(value_given, dp_count).astype(F32)
        value_parts.append(dot(kept_rows, weight) + value_got)

    tied = (value_parts[-1], lengths, bins, advantage, logprob_gap)
    value_parts[-1], lengths, bins, advantage, logprob_gap = lax.optimization_barrier(tied)
    smem = pl.BlockSpec(memory_space=pltpu.SMEM)
    vmem = pl.BlockSpec(memory_space=pltpu.VMEM)
    fixed, pull, row_scale, row_at = pl.pallas_call(
        functools.partial(row_kernel, tensor_count, span_rows, model_width),
        in_specs=[smem] * 3 + [vmem] * (2 + tensor_count),
        out_specs=[vmem] * 4,
        out_shape=[
            jax.ShapeDtypeStruct((own_rows, value_width), F32),
            jax.ShapeDtypeStruct((own_rows, 128), F32),
            jax.ShapeDtypeStruct((own_rows, 128), F32),
            jax.ShapeDtypeStruct((own_rows, slot_count), BF16),
        ],
        compiler_params=pltpu.CompilerParams(vmem_limit_bytes=16 * 2**20),
        cost_estimate=pl.CostEstimate(
            flops=2 * own_rows * slot_count * value_width,
            bytes_accessed=2**21,
            transcendentals=0,
        ),
        name="rows",
    )(
        lengths.reshape(-1),
        bins.reshape(-1),
        advantage.reshape(-1),
        logprob_gap.reshape(1, own_rows),
        got_cot,
        *ref_got,
    )

    values, slopes = [], []
    for j in range(PARTS):
        total = value_parts[j]
        for level in range(levels):
            rows = total.shape[0] // 2
            sent = total[rows:].astype(BF16)
            total = total[:rows] + crossed(sent, tensor_count, 1 << level).astype(F32)
        values.append(total * row_scale[:, :1])

        cols = slice(j * width, (j + 1) * width)
        slope = (fixed[:, cols] + pull[:, :1] * total).astype(BF16)
        for level in reversed(range(levels)):
            slope = jnp.concatenate([slope, crossed(slope, tensor_count, 1 << level)], axis=0)
        slopes.append(slope)

    sent = dot_rows(row_at, jnp.concatenate(values, axis=1).astype(BF16)).astype(BF16)

    slopes[0], sent = lax.optimization_barrier((slopes[0], sent))
    policy_values = lax.all_to_all(sent, "dp", split_axis=0, concat_axis=0, tiled=True)

    grad_kept, grad_sent = [], []
    for j in range(PARTS):
        slopes_got = swapped(slopes[j], dp_count)
        chunks = pl.pallas_call(
            functools.partial(grad_kernel, factor),
            grid_spec=pltpu.PrefetchScalarGridSpec(
                num_scalar_prefetch=1,
                grid=(1,),
                in_specs=[
                    pl.BlockSpec((group_rows, shard), lambda i, at: (0, 0)),
                    pl.BlockSpec((group_rows, shard), lambda i, at: (0, 0)),
                    pl.BlockSpec((group_rows, width), lambda i, at: (0, 0)),
                    pl.BlockSpec((group_rows, width), lambda i, at: (0, 0)),
                ],
                out_specs=[pl.BlockSpec((shard // 2, width), lambda i, at: (0, 0))] * 2,
                scratch_shapes=[pltpu.VMEM((shard, width), F32)],
            ),
            out_shape=[
                jax.ShapeDtypeStruct((shard // 2, width), F32),
                jax.ShapeDtypeStruct((shard // 2, width), BF16),
            ],
            compiler_params=pltpu.CompilerParams(vmem_limit_bytes=32 * 2**20),
            cost_estimate=pl.CostEstimate(
                flops=4 * group_rows * shard * width,
                bytes_accessed=4 * 2**20,
                transcendentals=0,
            ),
            name="gradient",
        )(chunk_at, kept_rows, got_rows, slopes[j], slopes_got)
        grad_kept.append(chunks[0])
        grad_sent.append(chunks[1])
    grads = []
    for j in range(PARTS):
        total, given = grad_kept[j], grad_sent[j]
        for level in range(levels):
            pairs = [
                (p * cores + c, (p ^ (1 << ((c + level) % levels))) * cores + c)
                for p in range(places)
                for c in range(cores)
            ]
            total = total + lax.ppermute(given, "dp", pairs).astype(F32)
            half_rows = total.shape[0] // 2
            if level < levels - 1:
                total, given = total[:half_rows], total[half_rows:].astype(BF16)
        grads.append(total.astype(BF16))
    pairs = [
        (flat(p, c, z), flat(z, c, p ^ turned(z, levels)))
        for p in range(places)
        for c in range(cores)
        for z in range(tensor_count)
    ]
    grad, policy_values = lax.optimization_barrier((jnp.concatenate(grads, axis=1), policy_values))
    grad_weight = lax.ppermute(grad, AXES, pairs).astype(F32)
    policy_values = pl.pallas_call(
        write_kernel,
        out_shape=jax.ShapeDtypeStruct(policy_values.shape, BF16),
        cost_estimate=pl.CostEstimate(flops=0, bytes_accessed=2**19, transcendentals=0),
        name="write",
    )(policy_values)
    return (policy_values.reshape(1, 1, slot_count, value_width), grad_weight)


def solution(mesh):
    in_specs = (
        P("dp", "tensor"),
        P("tensor"),
        P("tensor", None),
        P(),
        P("dp", None),
        P("dp", "tensor", None),
        P("dp", "tensor", None),
        P("dp", "tensor", None),
        P(("dp", "tensor")),
        P("dp", "tensor", None, None),
    )
    out_specs = (P("dp", "tensor", None, None), P(("dp", "tensor"), None))
    return jax.shard_map(
        on_device, mesh=mesh, in_specs=in_specs, out_specs=out_specs, check_vma=False
    )
```

```python
import functools
import math

import jax
import jax.numpy as jnp
from jax import lax
from jax.experimental import pallas as pl
from jax.experimental.pallas import tpu as pltpu
from jax.sharding import PartitionSpec as P

EPS = 1e-06
BETA = 1.0
AXES = ("dp", "tensor")
BF16 = jnp.bfloat16
F32 = jnp.float32
POWER_ROWS = 16
PARTS = 2


def dot(a, b):
    return jnp.dot(a, b, preferred_element_type=F32)


def dot_rows(a, b):
    return lax.dot_general(a, b, (((0,), (0,)), ((), ())), preferred_element_type=F32)


def swapped(array, dp_count):
    return lax.ppermute(array, "dp", [(i, i ^ 1) for i in range(dp_count)])


def turned(index, levels):
    return sum(((index >> i) & 1) << (levels - 1 - i) for i in range(levels))


def crossed(array, count, step):
    return lax.ppermute(array, "tensor", [(i, i ^ step) for i in range(count)])


def prepare_kernel(
    count, steps, at, x_ref, gain_ref, weight_ref, pol_ref, given_ref, kept_ref, *refs
):
    sent_refs, (rows_ref, total, square) = refs[:count], refs[count:]
    f = pl.program_id(0)
    own = x_ref.shape[0] // count
    levels = count.bit_length() - 1
    for i in range(count):
        source = jnp.bitwise_xor(at[0], turned(i, levels))
        rows_ref[i * own : (i + 1) * own, :] = x_ref[pl.ds(pl.multiple_of(source * own, own), own), :]
    wide = rows_ref[...].astype(F32)
    gained = (wide * pol_ref[...]).astype(BF16)

    @pl.when(f < steps // 2)
    def _():
        given_ref[...] = gained

    @pl.when(f >= steps // 2)
    def _():
        kept_ref[...] = gained

    part = dot((wide * gain_ref[...]).astype(BF16), weight_ref[...])
    squares = jnp.sum(wide * wide, axis=1, keepdims=True)

    @pl.when(f == 0)
    def _():
        total[...] = part
        square[...] = squares

    @pl.when(f > 0)
    def _():
        total[...] += part
        square[...] += squares

    @pl.when(f == steps - 1)
    def _():
        for i in range(count):
            sent = sent_refs[turned(i, levels)]
            sent[:own, :] = total[i * own : (i + 1) * own, :].astype(BF16)
            power = jnp.broadcast_to(square[i * own : (i + 1) * own, :], (own, 128)).T
            high = power[: POWER_ROWS // 2].astype(BF16).astype(F32)
            low = power[: POWER_ROWS // 2] - high
            sent[own:, :] = jnp.zeros((POWER_ROWS, sent.shape[1]), BF16)
            sent[own:, :own] = jnp.concatenate([high, low], axis=0).astype(BF16)


def row_kernel(
    count, span, model_width, lengths, bins, advantage, gap_ref, cot_ref, *refs
):
    ref_refs, (fixed_ref, pull_ref, scale_ref, row_at_ref) = refs[:count], refs[count:]
    own = pull_ref.shape[0]
    slots = row_at_ref.shape[1]
    row = lax.broadcasted_iota(jnp.int32, (own, slots), 0)
    slot = lax.broadcasted_iota(jnp.int32, (own, slots), 1)
    chosen = jnp.zeros((own, slots), jnp.bool_)
    size = jnp.ones((own, 128), F32)
    weight = jnp.zeros((own, 128), F32)
    start = jnp.int32(0)
    for s in range(lengths.shape[0]):
        end = start + lengths[s]
        inside = (row >= start) & (row < end)
        chosen = chosen | (inside & (slot - bins[s] * span == row - start))
        size = jnp.where(inside[:, :128], lengths[s].astype(F32), size)
        weight = jnp.where(inside[:, :128], advantage[s], weight)
        start = end
    row_at = jnp.where(chosen, 1.0, 0.0).astype(BF16)
    row_at_ref[...] = row_at
    importance = jnp.minimum(jnp.exp(jnp.broadcast_to(gap_ref[...], (128, own)).T), 2.0)
    coef_adv = (weight * importance / size).astype(BF16).astype(F32)
    coef_pull = (BETA / size).astype(BF16).astype(F32)
    total = ref_refs[0][...].astype(F32)
    for ref in ref_refs[1:]:
        total = total + ref[...].astype(F32)
    half = POWER_ROWS // 2
    square = total[own : own + 1, :own] + total[own + half : own + half + 1, :own]
    scale = lax.rsqrt(jnp.broadcast_to(square, (128, own)).T / model_width + EPS)
    reference = (total[:own] * scale[:, :1]).astype(BF16).astype(F32)
    upstream = dot(row_at, cot_ref[...])
    fixed_ref[...] = (coef_adv[:, :1] * upstream - coef_pull[:, :1] * reference) * scale[:, :1]
    pull_ref[...] = coef_pull * scale * scale
    scale_ref[...] = scale


def grad_kernel(factor, at, kept_ref, got_ref, slope_ref, slope_got_ref, *refs):
    *out_refs, grad = refs
    total = dot_rows(kept_ref[...], slope_ref[...]) + dot_rows(got_ref[...], slope_got_ref[...])
    grad[...] = total * factor
    rows = grad.shape[0] // at.shape[0]
    count = at.shape[0] // 2
    for s in range(2 * count):
        chunk = grad[pl.ds(pl.multiple_of(at[s] * rows, rows), rows), :]
        out_ref = out_refs[s // count]
        place = s % count
        out_ref[place * rows : (place + 1) * rows, :] = chunk.astype(out_ref.dtype)


def write_kernel(in_ref, out_ref):
    out_ref[...] = in_ref[...]


def on_device(
    tokens,
    ref_gain,
    ref_weight,
    pol_gain,
    pol_weight,
    lengths,
    bins,
    advantage,
    logprob_gap,
    cotangent,
):
    tensor_count = lax.axis_size("tensor")
    dp_count = lax.axis_size("dp")
    t = lax.axis_index("tensor")
    d = lax.axis_index("dp")
    cores = dp_count // tensor_count
    assert cores == 2
    places = dp_count // cores
    levels = places.bit_length() - 1
    assert 1 << levels == places == tensor_count
    place = d // cores
    core = d % cores
    group_rows, block = tokens.shape
    own_rows = group_rows // tensor_count
    slot_count = cotangent.shape[2]
    span_rows = slot_count // dp_count
    value_width = ref_weight.shape[1]
    model_width = pol_gain.shape[0]
    shard = pol_weight.shape[0]
    width = value_width // PARTS
    factor = 1.0 / math.sqrt(dp_count * tensor_count * lengths.shape[2])
    relative = place ^ t

    def flat(p, c, z):
        return (p * cores + c) * tensor_count + z

    def stage(number, held):
        pairs, is_getter = [], jnp.zeros((), jnp.bool_)
        for c in range(cores):
            holders = [0]
            for before in range(number):
                bit = 1 << ((c + before) % levels)
                holders = holders + [q ^ bit for q in holders]
            bit = 1 << ((c + number) % levels)
            for q in holders:
                pairs += [
                    (flat(q ^ z, c, z), flat(q ^ bit ^ z, c, z)) for z in range(tensor_count)
                ]
                is_getter = is_getter | ((core == c) & (relative == (q ^ bit)))
        return lax.ppermute(held, AXES, pairs), is_getter

    got, is_getter = stage(0, pol_weight)

    steps = 4
    feature_step = block // steps
    at = jnp.stack([t, (1 - core) * (steps // 2)]).astype(jnp.int32)
    sent_shape = (own_rows + POWER_ROWS, value_width)

    def at_step(f, at):
        return lax.rem(f + at[1], steps)

    prepared = pl.pallas_call(
        functools.partial(prepare_kernel, tensor_count, steps),
        grid_spec=pltpu.PrefetchScalarGridSpec(
            num_scalar_prefetch=1,
            grid=(steps,),
            in_specs=[
                pl.BlockSpec((group_rows, feature_step), lambda f, at: (0, at_step(f, at))),
                pl.BlockSpec((1, feature_step), lambda f, at: (0, at_step(f, at))),
                pl.BlockSpec((feature_step, value_width), lambda f, at: (at_step(f, at), 0)),
                pl.BlockSpec(
                    (1, feature_step), lambda f, at: (0, at[0] * steps + at_step(f, at))
                ),
            ],
            out_specs=[
                pl.BlockSpec(
                    (group_rows, feature_step), lambda f, at: (0, jnp.minimum(f, steps // 2 - 1))
                ),
                pl.BlockSpec(
                    (group_rows, feature_step), lambda f, at: (0, jnp.maximum(f - steps // 2, 0))
                ),
            ]
            + [pl.BlockSpec(sent_shape, lambda f, at: (0, 0))] * tensor_count,
            scratch_shapes=[
                pltpu.VMEM((group_rows, feature_step), BF16),
                pltpu.VMEM((group_rows, value_width), F32),
                pltpu.VMEM((group_rows, 1), F32),
            ],
        ),
        out_shape=[jax.ShapeDtypeStruct((group_rows, shard), BF16)] * 2
        + [jax.ShapeDtypeStruct(sent_shape, BF16)] * tensor_count,
        compiler_params=pltpu.CompilerParams(vmem_limit_bytes=56 * 2**20),
        cost_estimate=pl.CostEstimate(
            flops=2 * group_rows * block * value_width,
            bytes_accessed=8 * 2**20,
            transcendentals=0,
        ),
        name="prepare",
    )(at, tokens, ref_gain.reshape(1, block), ref_weight, pol_gain.reshape(1, model_width))
    given_rows, kept_rows, *ref_sent = prepared

    ref_got = [ref_sent[0]] + [
        crossed(ref_sent[k], tensor_count, k) for k in range(1, tensor_count)
    ]
    got_rows = swapped(given_rows, dp_count)

    cot = cotangent.reshape(slot_count, value_width)
    held = jnp.where(is_getter, got, pol_weight)
    held, cot, kept_rows = lax.optimization_barrier((held, cot, kept_rows))
    parts = []
    for j in range(PARTS):
        cols = slice(j * width, (j + 1) * width)
        held_part = held[:, cols]
        for number in range(1, levels):
            got_part, is_getter_part = stage(number, held_part)
            if number < levels - 1:
                held_part = jnp.where(is_getter_part, got_part, held_part)
        parts.append((held_part, got_part, is_getter_part))
    got_cot = lax.all_to_all(cot, "dp", split_axis=0, concat_axis=0, tiled=True)

    def plane_bit(level):
        return jnp.where(core == 0, 1 << (level % levels), 1 << ((1 + level) % levels))

    chunk_at = []
    for i in range(places):
        away = sum(plane_bit(level) * ((i >> (levels - 1 - level)) & 1) for level in range(levels))
        chunk_at.append(place ^ away ^ turned(t, levels))
    chunk_at = jnp.stack(chunk_at).astype(jnp.int32)

    value_parts = []
    for j in range(PARTS):
        held_part, got_part, is_getter_part = parts[j]
        weight = jnp.where(is_getter_part, got_part, held_part)
        value_given = dot(got_rows, weight).astype(BF16)
        value_got = swapped(value_given, dp_count)
        if j == 0:
            value_got, got_cot = lax.optimization_barrier((value_got, got_cot))
        value_parts.append(dot(kept_rows, weight) + value_got.astype(F32))

    tied = (value_parts[-1], lengths, bins, advantage, logprob_gap)
    value_parts[-1], lengths, bins, advantage, logprob_gap = lax.optimization_barrier(tied)
    smem = pl.BlockSpec(memory_space=pltpu.SMEM)
    vmem = pl.BlockSpec(memory_space=pltpu.VMEM)
    fixed, pull, row_scale, row_at = pl.pallas_call(
        functools.partial(row_kernel, tensor_count, span_rows, model_width),
        in_specs=[smem] * 3 + [vmem] * (2 + tensor_count),
        out_specs=[vmem] * 4,
        out_shape=[
            jax.ShapeDtypeStruct((own_rows, value_width), F32),
            jax.ShapeDtypeStruct((own_rows, 128), F32),
            jax.ShapeDtypeStruct((own_rows, 128), F32),
            jax.ShapeDtypeStruct((own_rows, slot_count), BF16),
        ],
        compiler_params=pltpu.CompilerParams(vmem_limit_bytes=16 * 2**20),
        cost_estimate=pl.CostEstimate(
            flops=2 * own_rows * slot_count * value_width,
            bytes_accessed=2**21,
            transcendentals=0,
        ),
        name="rows",
    )(
        lengths.reshape(-1),
        bins.reshape(-1),
        advantage.reshape(-1),
        logprob_gap.reshape(1, own_rows),
        got_cot,
        *ref_got,
    )

    values, slopes = [], []
    for j in range(PARTS):
        total = value_parts[j]
        for level in range(levels):
            rows = total.shape[0] // 2
            sent = total[rows:].astype(BF16)
            total = total[:rows] + crossed(sent, tensor_count, 1 << level).astype(F32)
        values.append(total * row_scale[:, :1])

        cols = slice(j * width, (j + 1) * width)
        slope = (fixed[:, cols] + pull[:, :1] * total).astype(BF16)
        for level in reversed(range(levels)):
            slope = jnp.concatenate([slope, crossed(slope, tensor_count, 1 << level)], axis=0)
        slopes.append(slope)

    sent = dot_rows(row_at, jnp.concatenate(values, axis=1).astype(BF16)).astype(BF16)

    slopes[0], sent = lax.optimization_barrier((slopes[0], sent))
    policy_values = lax.all_to_all(sent, "dp", split_axis=0, concat_axis=0, tiled=True)

    grad_kept, grad_sent = [], []
    for j in range(PARTS):
        slopes_got = swapped(slopes[j], dp_count)
        chunks = pl.pallas_call(
            functools.partial(grad_kernel, factor),
            grid_spec=pltpu.PrefetchScalarGridSpec(
                num_scalar_prefetch=1,
                grid=(1,),
                in_specs=[
                    pl.BlockSpec((group_rows, shard), lambda i, at: (0, 0)),
                    pl.BlockSpec((group_rows, shard), lambda i, at: (0, 0)),
                    pl.BlockSpec((group_rows, width), lambda i, at: (0, 0)),
                    pl.BlockSpec((group_rows, width), lambda i, at: (0, 0)),
                ],
                out_specs=[pl.BlockSpec((shard // 2, width), lambda i, at: (0, 0))] * 2,
                scratch_shapes=[pltpu.VMEM((shard, width), F32)],
            ),
            out_shape=[
                jax.ShapeDtypeStruct((shard // 2, width), F32),
                jax.ShapeDtypeStruct((shard // 2, width), BF16),
            ],
            compiler_params=pltpu.CompilerParams(vmem_limit_bytes=32 * 2**20),
            cost_estimate=pl.CostEstimate(
                flops=4 * group_rows * shard * width,
                bytes_accessed=4 * 2**20,
                transcendentals=0,
            ),
            name="gradient",
        )(chunk_at, kept_rows, got_rows, slopes[j], slopes_got)
        grad_kept.append(chunks[0])
        grad_sent.append(chunks[1])
    grads = []
    for j in range(PARTS):
        total, given = grad_kept[j], grad_sent[j]
        for level in range(levels):
            pairs = [
                (p * cores + c, (p ^ (1 << ((c + level) % levels))) * cores + c)
                for p in range(places)
                for c in range(cores)
            ]
            total = total + lax.ppermute(given, "dp", pairs).astype(F32)
            half_rows = total.shape[0] // 2
            if level < levels - 1:
                total, given = total[:half_rows], total[half_rows:].astype(BF16)
        grads.append(total.astype(BF16))
    pairs = [
        (flat(p, c, z), flat(z, c, p ^ turned(z, levels)))
        for p in range(places)
        for c in range(cores)
        for z in range(tensor_count)
    ]
    grad, policy_values = lax.optimization_barrier((jnp.concatenate(grads, axis=1), policy_values))
    grad_weight = lax.ppermute(grad, AXES, pairs).astype(F32)
    policy_values = pl.pallas_call(
        write_kernel,
        out_shape=jax.ShapeDtypeStruct(policy_values.shape, BF16),
        cost_estimate=pl.CostEstimate(flops=0, bytes_accessed=2**19, transcendentals=0),
        name="write",
    )(policy_values)
    return (policy_values.reshape(1, 1, slot_count, value_width), grad_weight)


def solution(mesh):
    in_specs = (
        P("dp", "tensor"),
        P("tensor"),
        P("tensor", None),
        P(),
        P("dp", None),
        P("dp", "tensor", None),
        P("dp", "tensor", None),
        P("dp", "tensor", None),
        P(("dp", "tensor")),
        P("dp", "tensor", None, None),
    )
    out_specs = (P("dp", "tensor", None, None), P(("dp", "tensor"), None))
    return jax.shard_map(
        on_device, mesh=mesh, in_specs=in_specs, out_specs=out_specs, check_vma=False
    )
```

```python
import functools
import math

import jax
import jax.numpy as jnp
from jax import lax
from jax.experimental import pallas as pl
from jax.experimental.pallas import tpu as pltpu
from jax.sharding import PartitionSpec as P

EPS = 1e-06
BETA = 1.0
AXES = ("dp", "tensor")
BF16 = jnp.bfloat16
F32 = jnp.float32
POWER_ROWS = 16
PARTS = 2


def dot(a, b):
    return jnp.dot(a, b, preferred_element_type=F32)


def dot_rows(a, b):
    return lax.dot_general(a, b, (((0,), (0,)), ((), ())), preferred_element_type=F32)


def swapped(array, dp_count):
    return lax.ppermute(array, "dp", [(i, i ^ 1) for i in range(dp_count)])


def turned(index, levels):
    return sum(((index >> i) & 1) << (levels - 1 - i) for i in range(levels))


def crossed(array, count, step):
    return lax.ppermute(array, "tensor", [(i, i ^ step) for i in range(count)])


def prepare_kernel(
    count, steps, at, x_ref, gain_ref, weight_ref, pol_ref, given_ref, kept_ref, *refs
):
    sent_refs, (rows_ref, total, square) = refs[:count], refs[count:]
    f = pl.program_id(0)
    own = x_ref.shape[0] // count
    levels = count.bit_length() - 1
    for i in range(count):
        source = jnp.bitwise_xor(at[0], turned(i, levels))
        rows_ref[i * own : (i + 1) * own, :] = x_ref[pl.ds(pl.multiple_of(source * own, own), own), :]
    wide = rows_ref[...].astype(F32)
    gained = (wide * pol_ref[...]).astype(BF16)

    @pl.when(f < steps // 2)
    def _():
        given_ref[...] = gained

    @pl.when(f >= steps // 2)
    def _():
        kept_ref[...] = gained

    part = dot((wide * gain_ref[...]).astype(BF16), weight_ref[...])
    squares = jnp.sum(wide * wide, axis=1, keepdims=True)

    @pl.when(f == 0)
    def _():
        total[...] = part
        square[...] = squares

    @pl.when(f > 0)
    def _():
        total[...] += part
        square[...] += squares

    @pl.when(f == steps - 1)
    def _():
        for i in range(count):
            sent = sent_refs[turned(i, levels)]
            sent[:own, :] = total[i * own : (i + 1) * own, :].astype(BF16)
            power = jnp.broadcast_to(square[i * own : (i + 1) * own, :], (own, 128)).T
            high = power[: POWER_ROWS // 2].astype(BF16).astype(F32)
            low = power[: POWER_ROWS // 2] - high
            sent[own:, :] = jnp.zeros((POWER_ROWS, sent.shape[1]), BF16)
            sent[own:, :own] = jnp.concatenate([high, low], axis=0).astype(BF16)


def row_kernel(
    count, span, model_width, lengths, bins, advantage, gap_ref, cot_ref, *refs
):
    ref_refs, (fixed_ref, pull_ref, scale_ref, row_at_ref) = refs[:count], refs[count:]
    own = pull_ref.shape[0]
    slots = row_at_ref.shape[1]
    row = lax.broadcasted_iota(jnp.int32, (own, slots), 0)
    slot = lax.broadcasted_iota(jnp.int32, (own, slots), 1)
    chosen = jnp.zeros((own, slots), jnp.bool_)
    size = jnp.ones((own, 128), F32)
    weight = jnp.zeros((own, 128), F32)
    start = jnp.int32(0)
    for s in range(lengths.shape[0]):
        end = start + lengths[s]
        inside = (row >= start) & (row < end)
        chosen = chosen | (inside & (slot - bins[s] * span == row - start))
        size = jnp.where(inside[:, :128], lengths[s].astype(F32), size)
        weight = jnp.where(inside[:, :128], advantage[s], weight)
        start = end
    row_at = jnp.where(chosen, 1.0, 0.0).astype(BF16)
    row_at_ref[...] = row_at
    importance = jnp.minimum(jnp.exp(jnp.broadcast_to(gap_ref[...], (128, own)).T), 2.0)
    coef_adv = (weight * importance / size).astype(BF16).astype(F32)
    coef_pull = (BETA / size).astype(BF16).astype(F32)
    total = ref_refs[0][...].astype(F32)
    for ref in ref_refs[1:]:
        total = total + ref[...].astype(F32)
    half = POWER_ROWS // 2
    square = total[own : own + 1, :own] + total[own + half : own + half + 1, :own]
    scale = lax.rsqrt(jnp.broadcast_to(square, (128, own)).T / model_width + EPS)
    reference = (total[:own] * scale[:, :1]).astype(BF16).astype(F32)
    upstream = dot(row_at, cot_ref[...])
    fixed_ref[...] = (coef_adv[:, :1] * upstream - coef_pull[:, :1] * reference) * scale[:, :1]
    pull_ref[...] = coef_pull * scale * scale
    scale_ref[...] = scale


def grad_kernel(factor, at, kept_ref, got_ref, slope_ref, slope_got_ref, *refs):
    *out_refs, grad = refs
    total = dot_rows(kept_ref[...], slope_ref[...]) + dot_rows(got_ref[...], slope_got_ref[...])
    grad[...] = total * factor
    rows = grad.shape[0] // at.shape[0]
    count = at.shape[0] // 2
    for s in range(2 * count):
        chunk = grad[pl.ds(pl.multiple_of(at[s] * rows, rows), rows), :]
        out_ref = out_refs[s // count]
        place = s % count
        out_ref[place * rows : (place + 1) * rows, :] = chunk.astype(out_ref.dtype)


def write_kernel(in_ref, out_ref):
    out_ref[...] = in_ref[...]


def on_device(
    tokens,
    ref_gain,
    ref_weight,
    pol_gain,
    pol_weight,
    lengths,
    bins,
    advantage,
    logprob_gap,
    cotangent,
):
    tensor_count = lax.axis_size("tensor")
    dp_count = lax.axis_size("dp")
    t = lax.axis_index("tensor")
    d = lax.axis_index("dp")
    cores = dp_count // tensor_count
    assert cores == 2
    places = dp_count // cores
    levels = places.bit_length() - 1
    assert 1 << levels == places == tensor_count
    place = d // cores
    core = d % cores
    group_rows, block = tokens.shape
    own_rows = group_rows // tensor_count
    slot_count = cotangent.shape[2]
    span_rows = slot_count // dp_count
    value_width = ref_weight.shape[1]
    model_width = pol_gain.shape[0]
    shard = pol_weight.shape[0]
    width = value_width // PARTS
    factor = 1.0 / math.sqrt(dp_count * tensor_count * lengths.shape[2])
    relative = place ^ t

    def flat(p, c, z):
        return (p * cores + c) * tensor_count + z

    def stage(number, held):
        pairs, is_getter = [], jnp.zeros((), jnp.bool_)
        for c in range(cores):
            holders = [0]
            for before in range(number):
                bit = 1 << ((c + before) % levels)
                holders = holders + [q ^ bit for q in holders]
            bit = 1 << ((c + number) % levels)
            for q in holders:
                pairs += [
                    (flat(q ^ z, c, z), flat(q ^ bit ^ z, c, z)) for z in range(tensor_count)
                ]
                is_getter = is_getter | ((core == c) & (relative == (q ^ bit)))
        return lax.ppermute(held, AXES, pairs), is_getter

    got, is_getter = stage(0, pol_weight)

    steps = 4
    feature_step = block // steps
    at = jnp.stack([t, (1 - core) * (steps // 2)]).astype(jnp.int32)
    sent_shape = (own_rows + POWER_ROWS, value_width)

    def at_step(f, at):
        return lax.rem(f + at[1], steps)

    prepared = pl.pallas_call(
        functools.partial(prepare_kernel, tensor_count, steps),
        grid_spec=pltpu.PrefetchScalarGridSpec(
            num_scalar_prefetch=1,
            grid=(steps,),
            in_specs=[
                pl.BlockSpec((group_rows, feature_step), lambda f, at: (0, at_step(f, at))),
                pl.BlockSpec((1, feature_step), lambda f, at: (0, at_step(f, at))),
                pl.BlockSpec((feature_step, value_width), lambda f, at: (at_step(f, at), 0)),
                pl.BlockSpec(
                    (1, feature_step), lambda f, at: (0, at[0] * steps + at_step(f, at))
                ),
            ],
            out_specs=[
                pl.BlockSpec(
                    (group_rows, feature_step), lambda f, at: (0, jnp.minimum(f, steps // 2 - 1))
                ),
                pl.BlockSpec(
                    (group_rows, feature_step), lambda f, at: (0, jnp.maximum(f - steps // 2, 0))
                ),
            ]
            + [pl.BlockSpec(sent_shape, lambda f, at: (0, 0))] * tensor_count,
            scratch_shapes=[
                pltpu.VMEM((group_rows, feature_step), BF16),
                pltpu.VMEM((group_rows, value_width), F32),
                pltpu.VMEM((group_rows, 1), F32),
            ],
        ),
        out_shape=[jax.ShapeDtypeStruct((group_rows, shard), BF16)] * 2
        + [jax.ShapeDtypeStruct(sent_shape, BF16)] * tensor_count,
        compiler_params=pltpu.CompilerParams(vmem_limit_bytes=56 * 2**20),
        cost_estimate=pl.CostEstimate(
            flops=2 * group_rows * block * value_width,
            bytes_accessed=8 * 2**20,
            transcendentals=0,
        ),
        name="prepare",
    )(at, tokens, ref_gain.reshape(1, block), ref_weight, pol_gain.reshape(1, model_width))
    given_rows, kept_rows, *ref_sent = prepared

    ref_got = [ref_sent[0]] + [
        crossed(ref_sent[k], tensor_count, k) for k in range(1, tensor_count)
    ]
    got_rows = swapped(given_rows, dp_count)

    cot = cotangent.reshape(slot_count, value_width)
    held = jnp.where(is_getter, got, pol_weight)
    held, cot, kept_rows = lax.optimization_barrier((held, cot, kept_rows))
    for number in range(1, levels):
        got, is_getter = stage(number, held)
        if number < levels - 1:
            held = jnp.where(is_getter, got, held)
    parts = []
    for j in range(PARTS):
        cols = slice(j * width, (j + 1) * width)
        parts.append((held[:, cols], got[:, cols], is_getter))
    got_cot = lax.all_to_all(cot, "dp", split_axis=0, concat_axis=0, tiled=True)

    def plane_bit(level):
        return jnp.where(core == 0, 1 << (level % levels), 1 << ((1 + level) % levels))

    chunk_at = []
    for i in range(places):
        away = sum(plane_bit(level) * ((i >> (levels - 1 - level)) & 1) for level in range(levels))
        chunk_at.append(place ^ away ^ turned(t, levels))
    chunk_at = jnp.stack(chunk_at).astype(jnp.int32)

    value_parts = []
    for j in range(PARTS):
        held_part, got_part, is_getter_part = parts[j]
        if j == 0:
            got_part, got_cot = lax.optimization_barrier((got_part, got_cot))
        weight = jnp.where(is_getter_part, got_part, held_part)
        value_given = dot(got_rows, weight).astype(BF16)
        value_got = swapped(value_given, dp_count).astype(F32)
        value_parts.append(dot(kept_rows, weight) + value_got)

    tied = (value_parts[-1], lengths, bins, advantage, logprob_gap)
    value_parts[-1], lengths, bins, advantage, logprob_gap = lax.optimization_barrier(tied)
    smem = pl.BlockSpec(memory_space=pltpu.SMEM)
    vmem = pl.BlockSpec(memory_space=pltpu.VMEM)
    fixed, pull, row_scale, row_at = pl.pallas_call(
        functools.partial(row_kernel, tensor_count, span_rows, model_width),
        in_specs=[smem] * 3 + [vmem] * (2 + tensor_count),
        out_specs=[vmem] * 4,
        out_shape=[
            jax.ShapeDtypeStruct((own_rows, value_width), F32),
            jax.ShapeDtypeStruct((own_rows, 128), F32),
            jax.ShapeDtypeStruct((own_rows, 128), F32),
            jax.ShapeDtypeStruct((own_rows, slot_count), BF16),
        ],
        compiler_params=pltpu.CompilerParams(vmem_limit_bytes=16 * 2**20),
        cost_estimate=pl.CostEstimate(
            flops=2 * own_rows * slot_count * value_width,
            bytes_accessed=2**21,
            transcendentals=0,
        ),
        name="rows",
    )(
        lengths.reshape(-1),
        bins.reshape(-1),
        advantage.reshape(-1),
        logprob_gap.reshape(1, own_rows),
        got_cot,
        *ref_got,
    )

    values, slopes = [], []
    for j in range(PARTS):
        total = value_parts[j]
        for level in range(levels):
            rows = total.shape[0] // 2
            sent = total[rows:].astype(BF16)
            total = total[:rows] + crossed(sent, tensor_count, 1 << level).astype(F32)
        values.append(total * row_scale[:, :1])

        cols = slice(j * width, (j + 1) * width)
        slope = (fixed[:, cols] + pull[:, :1] * total).astype(BF16)
        for level in reversed(range(levels)):
            slope = jnp.concatenate([slope, crossed(slope, tensor_count, 1 << level)], axis=0)
        slopes.append(slope)

    sent = dot_rows(row_at, jnp.concatenate(values, axis=1).astype(BF16)).astype(BF16)

    slopes[0], sent = lax.optimization_barrier((slopes[0], sent))
    policy_values = lax.all_to_all(sent, "dp", split_axis=0, concat_axis=0, tiled=True)

    grad_kept, grad_sent = [], []
    for j in range(PARTS):
        slopes_got = swapped(slopes[j], dp_count)
        chunks = pl.pallas_call(
            functools.partial(grad_kernel, factor),
            grid_spec=pltpu.PrefetchScalarGridSpec(
                num_scalar_prefetch=1,
                grid=(1,),
                in_specs=[
                    pl.BlockSpec((group_rows, shard), lambda i, at: (0, 0)),
                    pl.BlockSpec((group_rows, shard), lambda i, at: (0, 0)),
                    pl.BlockSpec((group_rows, width), lambda i, at: (0, 0)),
                    pl.BlockSpec((group_rows, width), lambda i, at: (0, 0)),
                ],
                out_specs=[pl.BlockSpec((shard // 2, width), lambda i, at: (0, 0))] * 2,
                scratch_shapes=[pltpu.VMEM((shard, width), F32)],
            ),
            out_shape=[
                jax.ShapeDtypeStruct((shard // 2, width), F32),
                jax.ShapeDtypeStruct((shard // 2, width), BF16),
            ],
            compiler_params=pltpu.CompilerParams(vmem_limit_bytes=32 * 2**20),
            cost_estimate=pl.CostEstimate(
                flops=4 * group_rows * shard * width,
                bytes_accessed=4 * 2**20,
                transcendentals=0,
            ),
            name="gradient",
        )(chunk_at, kept_rows, got_rows, slopes[j], slopes_got)
        grad_kept.append(chunks[0])
        grad_sent.append(chunks[1])
    grads = []
    for j in range(PARTS):
        total, given = grad_kept[j], grad_sent[j]
        for level in range(levels):
            pairs = [
                (p * cores + c, (p ^ (1 << ((c + level) % levels))) * cores + c)
                for p in range(places)
                for c in range(cores)
            ]
            total = total + lax.ppermute(given, "dp", pairs).astype(F32)
            half_rows = total.shape[0] // 2
            if level < levels - 1:
                total, given = total[:half_rows], total[half_rows:].astype(BF16)
        grads.append(total.astype(BF16))
    pairs = [
        (flat(p, c, z), flat(z, c, p ^ turned(z, levels)))
        for p in range(places)
        for c in range(cores)
        for z in range(tensor_count)
    ]
    grad, policy_values = lax.optimization_barrier((jnp.concatenate(grads, axis=1), policy_values))
    grad_weight = lax.ppermute(grad, AXES, pairs).astype(F32)
    policy_values = pl.pallas_call(
        write_kernel,
        out_shape=jax.ShapeDtypeStruct(policy_values.shape, BF16),
        cost_estimate=pl.CostEstimate(flops=0, bytes_accessed=2**19, transcendentals=0),
        name="write",
    )(policy_values)
    return (policy_values.reshape(1, 1, slot_count, value_width), grad_weight)


def solution(mesh):
    in_specs = (
        P("dp", "tensor"),
        P("tensor"),
        P("tensor", None),
        P(),
        P("dp", None),
        P("dp", "tensor", None),
        P("dp", "tensor", None),
        P("dp", "tensor", None),
        P(("dp", "tensor")),
        P("dp", "tensor", None, None),
    )
    out_specs = (P("dp", "tensor", None, None), P(("dp", "tensor"), None))
    return jax.shard_map(
        on_device, mesh=mesh, in_specs=in_specs, out_specs=out_specs, check_vma=False
    )
```

```python
import functools
import math

import jax
import jax.numpy as jnp
from jax import lax
from jax.experimental import pallas as pl
from jax.experimental.pallas import tpu as pltpu
from jax.sharding import PartitionSpec as P

EPS = 1e-06
BETA = 1.0
AXES = ("dp", "tensor")
BF16 = jnp.bfloat16
F32 = jnp.float32
POWER_ROWS = 16
PARTS = 2


def dot(a, b):
    return jnp.dot(a, b, preferred_element_type=F32)


def dot_rows(a, b):
    return lax.dot_general(a, b, (((0,), (0,)), ((), ())), preferred_element_type=F32)


def swapped(array, dp_count):
    return lax.ppermute(array, "dp", [(i, i ^ 1) for i in range(dp_count)])


def turned(index, levels):
    return sum(((index >> i) & 1) << (levels - 1 - i) for i in range(levels))


def crossed(array, count, step):
    return lax.ppermute(array, "tensor", [(i, i ^ step) for i in range(count)])


def prepare_kernel(
    count, steps, at, x_ref, gain_ref, weight_ref, pol_ref, given_ref, kept_ref, *refs
):
    sent_refs, (rows_ref, total, square) = refs[:count], refs[count:]
    f = pl.program_id(0)
    own = x_ref.shape[0] // count
    levels = count.bit_length() - 1
    for i in range(count):
        source = jnp.bitwise_xor(at[0], turned(i, levels))
        rows_ref[i * own : (i + 1) * own, :] = x_ref[pl.ds(pl.multiple_of(source * own, own), own), :]
    wide = rows_ref[...].astype(F32)
    gained = (wide * pol_ref[...]).astype(BF16)

    @pl.when(f < steps // 2)
    def _():
        given_ref[...] = gained

    @pl.when(f >= steps // 2)
    def _():
        kept_ref[...] = gained

    part = dot((wide * gain_ref[...]).astype(BF16), weight_ref[...])
    squares = jnp.sum(wide * wide, axis=1, keepdims=True)

    @pl.when(f == 0)
    def _():
        total[...] = part
        square[...] = squares

    @pl.when(f > 0)
    def _():
        total[...] += part
        square[...] += squares

    @pl.when(f == steps - 1)
    def _():
        for i in range(count):
            sent = sent_refs[turned(i, levels)]
            sent[:own, :] = total[i * own : (i + 1) * own, :].astype(BF16)
            power = jnp.broadcast_to(square[i * own : (i + 1) * own, :], (own, 128)).T
            high = power[: POWER_ROWS // 2].astype(BF16).astype(F32)
            low = power[: POWER_ROWS // 2] - high
            sent[own:, :] = jnp.zeros((POWER_ROWS, sent.shape[1]), BF16)
            sent[own:, :own] = jnp.concatenate([high, low], axis=0).astype(BF16)


def row_kernel(
    count, span, model_width, lengths, bins, advantage, gap_ref, cot_ref, *refs
):
    ref_refs, (fixed_ref, pull_ref, scale_ref, row_at_ref) = refs[:count], refs[count:]
    own = pull_ref.shape[0]
    slots = row_at_ref.shape[1]
    row = lax.broadcasted_iota(jnp.int32, (own, slots), 0)
    slot = lax.broadcasted_iota(jnp.int32, (own, slots), 1)
    chosen = jnp.zeros((own, slots), jnp.bool_)
    size = jnp.ones((own, 128), F32)
    weight = jnp.zeros((own, 128), F32)
    start = jnp.int32(0)
    for s in range(lengths.shape[0]):
        end = start + lengths[s]
        inside = (row >= start) & (row < end)
        chosen = chosen | (inside & (slot - bins[s] * span == row - start))
        size = jnp.where(inside[:, :128], lengths[s].astype(F32), size)
        weight = jnp.where(inside[:, :128], advantage[s], weight)
        start = end
    row_at = jnp.where(chosen, 1.0, 0.0).astype(BF16)
    row_at_ref[...] = row_at
    importance = jnp.minimum(jnp.exp(jnp.broadcast_to(gap_ref[...], (128, own)).T), 2.0)
    coef_adv = (weight * importance / size).astype(BF16).astype(F32)
    coef_pull = (BETA / size).astype(BF16).astype(F32)
    total = ref_refs[0][...].astype(F32)
    for ref in ref_refs[1:]:
        total = total + ref[...].astype(F32)
    half = POWER_ROWS // 2
    square = total[own : own + 1, :own] + total[own + half : own + half + 1, :own]
    scale = lax.rsqrt(jnp.broadcast_to(square, (128, own)).T / model_width + EPS)
    reference = (total[:own] * scale[:, :1]).astype(BF16).astype(F32)
    upstream = dot(row_at, cot_ref[...])
    fixed_ref[...] = (coef_adv[:, :1] * upstream - coef_pull[:, :1] * reference) * scale[:, :1]
    pull_ref[...] = coef_pull * scale * scale
    scale_ref[...] = scale


def grad_kernel(factor, at, kept_ref, got_ref, slope_ref, slope_got_ref, *refs):
    *out_refs, grad = refs
    total = dot_rows(kept_ref[...], slope_ref[...]) + dot_rows(got_ref[...], slope_got_ref[...])
    grad[...] = total * factor
    rows = grad.shape[0] // at.shape[0]
    count = at.shape[0] // 2
    for s in range(2 * count):
        chunk = grad[pl.ds(pl.multiple_of(at[s] * rows, rows), rows), :]
        out_ref = out_refs[s // count]
        place = s % count
        out_ref[place * rows : (place + 1) * rows, :] = chunk.astype(out_ref.dtype)


def write_kernel(in_ref, out_ref):
    out_ref[...] = in_ref[...]


def on_device(
    tokens,
    ref_gain,
    ref_weight,
    pol_gain,
    pol_weight,
    lengths,
    bins,
    advantage,
    logprob_gap,
    cotangent,
):
    tensor_count = lax.axis_size("tensor")
    dp_count = lax.axis_size("dp")
    t = lax.axis_index("tensor")
    d = lax.axis_index("dp")
    cores = dp_count // tensor_count
    assert cores == 2
    places = dp_count // cores
    levels = places.bit_length() - 1
    assert 1 << levels == places == tensor_count
    place = d // cores
    core = d % cores
    group_rows, block = tokens.shape
    own_rows = group_rows // tensor_count
    slot_count = cotangent.shape[2]
    span_rows = slot_count // dp_count
    value_width = ref_weight.shape[1]
    model_width = pol_gain.shape[0]
    shard = pol_weight.shape[0]
    width = value_width // PARTS
    factor = 1.0 / math.sqrt(dp_count * tensor_count * lengths.shape[2])
    relative = place ^ t

    def flat(p, c, z):
        return (p * cores + c) * tensor_count + z

    def stage(number, held):
        pairs, is_getter = [], jnp.zeros((), jnp.bool_)
        for c in range(cores):
            holders = [0]
            for before in range(number):
                bit = 1 << ((c + before) % levels)
                holders = holders + [q ^ bit for q in holders]
            bit = 1 << ((c + number) % levels)
            for q in holders:
                pairs += [
                    (flat(q ^ z, c, z), flat(q ^ bit ^ z, c, z)) for z in range(tensor_count)
                ]
                is_getter = is_getter | ((core == c) & (relative == (q ^ bit)))
        return lax.ppermute(held, AXES, pairs), is_getter

    got, is_getter = stage(0, pol_weight)

    steps = 4
    feature_step = block // steps
    at = jnp.stack([t, (1 - core) * (steps // 2)]).astype(jnp.int32)
    sent_shape = (own_rows + POWER_ROWS, value_width)

    def at_step(f, at):
        return lax.rem(f + at[1], steps)

    prepared = pl.pallas_call(
        functools.partial(prepare_kernel, tensor_count, steps),
        grid_spec=pltpu.PrefetchScalarGridSpec(
            num_scalar_prefetch=1,
            grid=(steps,),
            in_specs=[
                pl.BlockSpec((group_rows, feature_step), lambda f, at: (0, at_step(f, at))),
                pl.BlockSpec((1, feature_step), lambda f, at: (0, at_step(f, at))),
                pl.BlockSpec((feature_step, value_width), lambda f, at: (at_step(f, at), 0)),
                pl.BlockSpec(
                    (1, feature_step), lambda f, at: (0, at[0] * steps + at_step(f, at))
                ),
            ],
            out_specs=[
                pl.BlockSpec(
                    (group_rows, feature_step), lambda f, at: (0, jnp.minimum(f, steps // 2 - 1))
                ),
                pl.BlockSpec(
                    (group_rows, feature_step), lambda f, at: (0, jnp.maximum(f - steps // 2, 0))
                ),
            ]
            + [pl.BlockSpec(sent_shape, lambda f, at: (0, 0))] * tensor_count,
            scratch_shapes=[
                pltpu.VMEM((group_rows, feature_step), BF16),
                pltpu.VMEM((group_rows, value_width), F32),
                pltpu.VMEM((group_rows, 1), F32),
            ],
        ),
        out_shape=[jax.ShapeDtypeStruct((group_rows, shard), BF16)] * 2
        + [jax.ShapeDtypeStruct(sent_shape, BF16)] * tensor_count,
        compiler_params=pltpu.CompilerParams(vmem_limit_bytes=56 * 2**20),
        cost_estimate=pl.CostEstimate(
            flops=2 * group_rows * block * value_width,
            bytes_accessed=8 * 2**20,
            transcendentals=0,
        ),
        name="prepare",
    )(at, tokens, ref_gain.reshape(1, block), ref_weight, pol_gain.reshape(1, model_width))
    given_rows, kept_rows, *ref_sent = prepared

    ref_got = [ref_sent[0]] + [
        crossed(ref_sent[k], tensor_count, k) for k in range(1, tensor_count)
    ]
    got_rows = swapped(given_rows, dp_count)

    cot = cotangent.reshape(slot_count, value_width)
    held = jnp.where(is_getter, got, pol_weight)
    held, cot, kept_rows = lax.optimization_barrier((held, cot, kept_rows))
    for number in range(1, levels):
        got, is_getter = stage(number, held)
        if number < levels - 1:
            held = jnp.where(is_getter, got, held)
    weight_all = lax.optimization_barrier(jnp.where(is_getter, got, held))
    got_cot = lax.all_to_all(cot, "dp", split_axis=0, concat_axis=0, tiled=True)

    def plane_bit(level):
        return jnp.where(core == 0, 1 << (level % levels), 1 << ((1 + level) % levels))

    chunk_at = []
    for i in range(places):
        away = sum(plane_bit(level) * ((i >> (levels - 1 - level)) & 1) for level in range(levels))
        chunk_at.append(place ^ away ^ turned(t, levels))
    chunk_at = jnp.stack(chunk_at).astype(jnp.int32)

    value_parts = []
    for j in range(PARTS):
        weight = weight_all[:, j * width : (j + 1) * width]
        if j == 0:
            weight, got_cot = lax.optimization_barrier((weight, got_cot))
        value_given = dot(got_rows, weight).astype(BF16)
        value_got = swapped(value_given, dp_count).astype(F32)
        value_parts.append(dot(kept_rows, weight) + value_got)

    tied = (value_parts[-1], lengths, bins, advantage, logprob_gap)
    value_parts[-1], lengths, bins, advantage, logprob_gap = lax.optimization_barrier(tied)
    smem = pl.BlockSpec(memory_space=pltpu.SMEM)
    vmem = pl.BlockSpec(memory_space=pltpu.VMEM)
    fixed, pull, row_scale, row_at = pl.pallas_call(
        functools.partial(row_kernel, tensor_count, span_rows, model_width),
        in_specs=[smem] * 3 + [vmem] * (2 + tensor_count),
        out_specs=[vmem] * 4,
        out_shape=[
            jax.ShapeDtypeStruct((own_rows, value_width), F32),
            jax.ShapeDtypeStruct((own_rows, 128), F32),
            jax.ShapeDtypeStruct((own_rows, 128), F32),
            jax.ShapeDtypeStruct((own_rows, slot_count), BF16),
        ],
        compiler_params=pltpu.CompilerParams(vmem_limit_bytes=16 * 2**20),
        cost_estimate=pl.CostEstimate(
            flops=2 * own_rows * slot_count * value_width,
            bytes_accessed=2**21,
            transcendentals=0,
        ),
        name="rows",
    )(
        lengths.reshape(-1),
        bins.reshape(-1),
        advantage.reshape(-1),
        logprob_gap.reshape(1, own_rows),
        got_cot,
        *ref_got,
    )

    values, slopes = [], []
    for j in range(PARTS):
        total = value_parts[j]
        for level in range(levels):
            rows = total.shape[0] // 2
            sent = total[rows:].astype(BF16)
            total = total[:rows] + crossed(sent, tensor_count, 1 << level).astype(F32)
        values.append(total * row_scale[:, :1])

        cols = slice(j * width, (j + 1) * width)
        slope = (fixed[:, cols] + pull[:, :1] * total).astype(BF16)
        for level in reversed(range(levels)):
            slope = jnp.concatenate([slope, crossed(slope, tensor_count, 1 << level)], axis=0)
        slopes.append(slope)

    sent = dot_rows(row_at, jnp.concatenate(values, axis=1).astype(BF16)).astype(BF16)

    slopes[0], sent = lax.optimization_barrier((slopes[0], sent))
    policy_values = lax.all_to_all(sent, "dp", split_axis=0, concat_axis=0, tiled=True)

    grad_kept, grad_sent = [], []
    for j in range(PARTS):
        slopes_got = swapped(slopes[j], dp_count)
        chunks = pl.pallas_call(
            functools.partial(grad_kernel, factor),
            grid_spec=pltpu.PrefetchScalarGridSpec(
                num_scalar_prefetch=1,
                grid=(1,),
                in_specs=[
                    pl.BlockSpec((group_rows, shard), lambda i, at: (0, 0)),
                    pl.BlockSpec((group_rows, shard), lambda i, at: (0, 0)),
                    pl.BlockSpec((group_rows, width), lambda i, at: (0, 0)),
                    pl.BlockSpec((group_rows, width), lambda i, at: (0, 0)),
                ],
                out_specs=[pl.BlockSpec((shard // 2, width), lambda i, at: (0, 0))] * 2,
                scratch_shapes=[pltpu.VMEM((shard, width), F32)],
            ),
            out_shape=[
                jax.ShapeDtypeStruct((shard // 2, width), F32),
                jax.ShapeDtypeStruct((shard // 2, width), BF16),
            ],
            compiler_params=pltpu.CompilerParams(vmem_limit_bytes=32 * 2**20),
            cost_estimate=pl.CostEstimate(
                flops=4 * group_rows * shard * width,
                bytes_accessed=4 * 2**20,
                transcendentals=0,
            ),
            name="gradient",
        )(chunk_at, kept_rows, got_rows, slopes[j], slopes_got)
        grad_kept.append(chunks[0])
        grad_sent.append(chunks[1])
    grads = []
    for j in range(PARTS):
        total, given = grad_kept[j], grad_sent[j]
        for level in range(levels):
            pairs = [
                (p * cores + c, (p ^ (1 << ((c + level) % levels))) * cores + c)
                for p in range(places)
                for c in range(cores)
            ]
            total = total + lax.ppermute(given, "dp", pairs).astype(F32)
            half_rows = total.shape[0] // 2
            if level < levels - 1:
                total, given = total[:half_rows], total[half_rows:].astype(BF16)
        grads.append(total.astype(BF16))
    pairs = [
        (flat(p, c, z), flat(z, c, p ^ turned(z, levels)))
        for p in range(places)
        for c in range(cores)
        for z in range(tensor_count)
    ]
    grad, policy_values = lax.optimization_barrier((jnp.concatenate(grads, axis=1), policy_values))
    grad_weight = lax.ppermute(grad, AXES, pairs).astype(F32)
    policy_values = pl.pallas_call(
        write_kernel,
        out_shape=jax.ShapeDtypeStruct(policy_values.shape, BF16),
        cost_estimate=pl.CostEstimate(flops=0, bytes_accessed=2**19, transcendentals=0),
        name="write",
    )(policy_values)
    return (policy_values.reshape(1, 1, slot_count, value_width), grad_weight)


def solution(mesh):
    in_specs = (
        P("dp", "tensor"),
        P("tensor"),
        P("tensor", None),
        P(),
        P("dp", None),
        P("dp", "tensor", None),
        P("dp", "tensor", None),
        P("dp", "tensor", None),
        P(("dp", "tensor")),
        P("dp", "tensor", None, None),
    )
    out_specs = (P("dp", "tensor", None, None), P(("dp", "tensor"), None))
    return jax.shard_map(
        on_device, mesh=mesh, in_specs=in_specs, out_specs=out_specs, check_vma=False
    )
```
